32 devices in a mesh: seq: 8 (over y, x, core), grp: 4 (over z).
Axes of the slice: x: 2, y: 2, z: 4, core: 2. Of those that a mesh axis runs over, the one named last changes fastest.
Arguments:
- tokens: bfloat16 [3072, 768], P('seq'), may hold values from -6 to 6
- cotangent: bfloat16 [3072, 768], P('seq'), may hold values from -6 to 6
- entry_weight: bfloat16 [768, 2304], replicated, may hold values from -0.21875 to 0.21875
- exit_weight: bfloat16 [768, 768], replicated, may hold values from -3.5 to 3.5
- up_weight: bfloat16 [768, 3072], replicated, may hold values from -0.21875 to 0.21875
- down_weight: bfloat16 [3072, 768], replicated, may hold values from -0.109375 to 0.109375
- first_gain: float32 [768], replicated, may hold values from 0.5 to 1.5
- first_bias: float32 [768], replicated, may hold values from -3 to 3
- second_gain: float32 [768], replicated, may hold values from 0.5 to 1.5
- second_bias: float32 [768], replicated, may hold values from -3 to 3
- dilations: int32 [4], replicated, may hold values from 2 to 8, as said below
- offsets: int32 [4, 12], replicated, may hold values from 0 to 7, as said below
Outputs:
- output: bfloat16 [3072, 768], P('seq')
- token_grad: bfloat16 [3072, 768], P('seq')
- entry_grad: float32 [768, 2304], P('seq')
- exit_grad: float32 [768, 768], P('seq')
- up_grad: float32 [768, 3072], P('seq')
- down_grad: float32 [3072, 768], P('seq')
- first_gain_grad: float32 [768], P('seq')
- first_bias_grad: float32 [768], P('seq')
- second_gain_grad: float32 [768], P('seq')
- second_bias_grad: float32 [768], P('seq')
The draws below stay inside these ranges and needn't reach their ends.
Inputs may be any that keep to these rules, and one draw needn't show every extreme that they name: `dilations`: every rate is one of 2, 3, 4, 6 and 8; some group has 2 and another 8. offsets[g, h] lies in 0 to dilations[g] - 1; in every group one head has offset 0 and another dilations[g] - 1.
All inputs are finite; a program needn't handle non-finite values.
Results may differ from the reference program's by a relative error of at most 0.013.
Values may be sent and summed in bfloat16 or wider, within the bound.
A program may use at most 320 MiB of HBM per device.

```python
import jax
import jax.numpy as jnp
from jax import lax

D = 768
HEADS = 12
HEAD_DIM = 64
FF = 3072
TOK_DEV = 384
RATE_MIN = 2
RATE_MAX = 8
SEQ_LEN = 3072
N_SEQ = 8
N_GRP = 4


def plan_rates(key):
    order = jax.random.permutation(jax.random.fold_in(key, 11), N_GRP).astype(jnp.int32)
    picks = jax.random.randint(jax.random.fold_in(key, 12), (N_GRP,), 0, 5)
    choices_row = jnp.stack([jnp.int32(RATE_MIN), jnp.int32(3 * RATE_MIN // 2), jnp.int32(2 * RATE_MIN), jnp.int32(3 * RATE_MIN), jnp.int32(RATE_MAX)])
    others = jnp.sum(jnp.where(picks[:, None] == jnp.arange(5, dtype=jnp.int32)[None, :], choices_row[None, :], 0), axis=1)
    rates = jnp.where(order == 0, RATE_MIN, jnp.where(order == 1, RATE_MAX, others))
    return rates.astype(jnp.int32)


def draw_dilations(key, part):
    limits = plan_rates(key)
    return limits.astype(jnp.int32)


def draw_offsets(key, part):
    limits = plan_rates(key)
    key = jax.random.fold_in(key, 2)
    high_key, low_key, drawn_key = jax.random.split(key, 3)
    drawn_base = jax.random.randint(drawn_key, (N_GRP, HEADS), 0, limits[:, None])
    top_head = jax.random.randint(high_key, (N_GRP, 1), 0, HEADS)
    bottom_head = (top_head + 1 + jax.random.randint(low_key, (N_GRP, 1), 0, HEADS - 1)) % HEADS
    head_ids = jnp.arange(HEADS, dtype=jnp.int32)[None, :]
    chosen = jnp.where(head_ids == top_head, limits[:, None] - 1, drawn_base)
    return jnp.where(head_ids == bottom_head, 0, chosen).astype(jnp.int32)


def block_scale(stream_key, dims, cuts, least, high):
    def one(dim, shards_of):
        draws = jax.random.uniform(jax.random.fold_in(jax.random.fold_in(stream_key, 6), dim), (shards_of,), jnp.float32, least / len(cuts), high / len(cuts))
        return jnp.repeat(jnp.exp(draws), dims[dim] // shards_of).reshape((-1,) + (1,) * (len(dims) - dim - 1))

    loudness = one(*cuts[0])
    for cut in cuts[1:]:
        loudness = loudness * one(*cut)
    return loudness


def noise(own_key, shape, width, most, cuts=(), kind=jnp.bfloat16):
    values = width * jax.random.normal(own_key, shape, jnp.float32)
    if cuts:
        values = values * block_scale(own_key, shape, cuts, -0.22, 0.18)
    return jnp.clip(values, -most, most).astype(kind)


def setup_inputs(seed: int = 0) -> dict:
    seeds = jax.random.split(jax.random.key(seed), 13)
    return {
        "tokens": noise(seeds[0], (SEQ_LEN, D), 1.0, 6.0, ((0, 8),)),
        "cotangent": noise(seeds[1], (SEQ_LEN, D), 1.0, 6.0, ((0, 8),)),
        "entry_weight": noise(seeds[2], (D, 3 * D), D ** -0.5, 0.21875),
        "exit_weight": noise(seeds[3], (D, D), (max(1, D // 256)) ** -0.5, 3.5),
        "up_weight": noise(seeds[4], (D, FF), D ** -0.5, 0.21875),
        "down_weight": noise(seeds[5], (FF, D), FF ** -0.5, 0.109375),
        "first_gain": jnp.clip(1.0 + 0.1 * jax.random.normal(seeds[6], (D,), jnp.float32), 0.5, 1.5),
        "first_bias": noise(seeds[7], (D,), 0.3, 3.0, (), jnp.float32),
        "second_gain": jnp.clip(1.0 + 0.1 * jax.random.normal(seeds[8], (D,), jnp.float32), 0.5, 1.5),
        "second_bias": noise(seeds[9], (D,), 0.3, 3.0, (), jnp.float32),
        "dilations": draw_dilations(jax.random.fold_in(seeds[12], 71), 0),
        "offsets": draw_offsets(jax.random.fold_in(seeds[12], 71), 0),
    }


@jax.custom_vjp
def low(v):
    return lax.optimization_barrier(v.astype(jnp.bfloat16)).astype(jnp.float32)

@jax.custom_vjp
def low_back(v):
    return v

def low_keep(v):
    return (low(v), None)

def low_pass(kept, grad):
    return (grad,)

def back_keep(v):
    return (v, None)

def back_low(kept, grad):
    return (low(grad),)
low.defvjp(low_keep, low_pass)
low_back.defvjp(back_keep, back_low)
EPS = 1e-05
PRECISE = lax.Precision.HIGHEST

def layer_norm(values, gain_vec, bias_vec):
    centered = values - lax.optimization_barrier(jnp.mean(values, axis=1, keepdims=True))
    variance = lax.optimization_barrier(jnp.mean(centered * centered, axis=1, keepdims=True))
    return centered * lax.rsqrt(variance + EPS) * gain_vec + bias_vec

def local_terms(queries, keys_in, values_in, score_scale):
    blocks = queries.shape[0] // TOK_DEV
    block_shape = (blocks, TOK_DEV, HEADS, HEAD_DIM)
    positions = jnp.arange(TOK_DEV, dtype=jnp.int32)
    causal = positions[:, None] >= positions[None, :]

    def one_block(items):
        query_block, key_block, value_block = items
        scores = low_back(jnp.einsum('ihd,jhd->hij', query_block, key_block, precision=PRECISE) * score_scale)
        weights = jnp.where(causal[None], jnp.exp(scores), 0.0)
        numerators = jnp.einsum('hij,jhd->ihd', low(weights), value_block, precision=PRECISE)
        return (numerators, lax.optimization_barrier(jnp.sum(weights, axis=2)).T)
    numerators, denominators = lax.map(jax.checkpoint(one_block), (queries.reshape(block_shape), keys_in.reshape(block_shape), values_in.reshape(block_shape)))
    return (numerators.reshape(-1, HEADS, HEAD_DIM), denominators.reshape(-1, HEADS))

def pattern_terms(queries, keys_in, values_in, dilation, head_offsets, segment, score_scale):
    seq_total = queries.shape[0]
    capacity = seq_total // RATE_MIN
    step_ids = jnp.arange(capacity, dtype=jnp.int32)

    def one_head(items):
        query_head, key_head, value_head, offset_head = items
        row_live = step_ids < seq_total // dilation
        places = jnp.minimum(offset_head + dilation * step_ids, seq_total - 1).astype(jnp.int32)
        picked_q = query_head[places]
        picked_k = key_head[places]
        picked_v = value_head[places]
        scores = low_back(jnp.dot(picked_q, picked_k.T, precision=PRECISE) * score_scale)
        allowed = row_live[:, None] & row_live[None, :] & (places[None, :] <= places[:, None]) & (places[None, :] // segment == places[:, None] // segment)
        weights = jnp.where(allowed, jnp.exp(scores), 0.0)
        row_den = lax.optimization_barrier(jnp.sum(weights, axis=1))
        row_num = jnp.dot(low(weights), picked_v, precision=PRECISE)
        full_num = jnp.zeros((seq_total, HEAD_DIM), jnp.float32).at[places].add(row_num)
        full_den = jnp.zeros((seq_total,), jnp.float32).at[places].add(row_den)
        return (full_num, full_den)
    numerators, denominators = lax.map(jax.checkpoint(one_head), (queries.transpose(1, 0, 2), keys_in.transpose(1, 0, 2), values_in.transpose(1, 0, 2), head_offsets))
    return (numerators.transpose(1, 0, 2), denominators.T)

def reference(tokens, cotangent, entry_weight, exit_weight, up_weight, down_weight, first_gain, first_bias, second_gain, second_bias, dilations, offsets):
    seq_total = TOK_DEV * N_SEQ
    score_scale = HEAD_DIM ** (-0.5)

    def forward(inputs, entry_mat, exit_mat, up_mat, down_mat, gain_one, bias_one, gain_two, bias_two):
        normed_one = layer_norm(inputs, gain_one, bias_one)
        packed = low_back(low(jnp.dot(low(normed_one), entry_mat, precision=PRECISE)))
        queries = packed[:, :D].reshape(seq_total, HEADS, HEAD_DIM)
        keys_all = packed[:, D:2 * D].reshape(seq_total, HEADS, HEAD_DIM)
        values_all = packed[:, 2 * D:].reshape(seq_total, HEADS, HEAD_DIM)
        numerators, denominators = local_terms(queries, keys_all, values_all, score_scale)
        for group_idx in range(N_GRP):
            dilation = dilations[group_idx]
            segment = seq_total * dilation // RATE_MAX
            part_num, part_den = pattern_terms(queries, keys_all, values_all, dilation, offsets[group_idx], segment, score_scale)
            numerators = numerators + part_num
            denominators = denominators + part_den
        numerators = low_back(numerators)
        mixed = low_back(low(numerators / denominators[:, :, None])).reshape(seq_total, D)
        branch = low_back(jnp.dot(mixed, exit_mat, precision=PRECISE))
        middle = inputs + branch
        normed_two = layer_norm(middle, gain_two, bias_two)
        hidden = low_back(jnp.dot(low(normed_two), up_mat, precision=PRECISE))
        active = low(jax.nn.gelu(hidden, approximate=False))
        return middle + jnp.dot(active, down_mat, precision=PRECISE)
    result, pullback = jax.vjp(forward, tokens.astype(jnp.float32), entry_weight.astype(jnp.float32), exit_weight.astype(jnp.float32), up_weight.astype(jnp.float32), down_weight.astype(jnp.float32), first_gain, first_bias, second_gain, second_bias)
    grads = pullback(cotangent.astype(jnp.float32))
    return (result.astype(jnp.bfloat16), grads[0].astype(jnp.bfloat16), grads[1], grads[2], grads[3], grads[4], grads[5], grads[6], grads[7], grads[8])
```

```python
from functools import partial

import jax
import jax.numpy as jnp
from jax import lax
from jax.experimental import pallas as pl
from jax.experimental.pallas import tpu as pltpu
from jax.sharding import PartitionSpec as P

RATE_MIN = 2
RATE_MAX = 8


EPS = 1e-05
PRECISE = lax.Precision.HIGHEST


def norm_forward(values, gain_vec, bias_vec):
    centered = values - jnp.mean(values, axis=1, keepdims=True)
    inverse = lax.rsqrt(jnp.mean(centered * centered, axis=1, keepdims=True) + EPS)
    plain = centered * inverse
    return (plain * gain_vec + bias_vec, plain, inverse)


def norm_backward(upstream, plain, inverse, gain_vec):
    scaled = upstream * gain_vec
    inner = (
        scaled
        - jnp.mean(scaled, axis=1, keepdims=True)
        - plain * jnp.mean(scaled * plain, axis=1, keepdims=True)
    )
    return (inverse * inner, jnp.sum(upstream * plain, axis=0), jnp.sum(upstream, axis=0))


def key_weights(query_sp, query_pos, key_block, first_row, geometry):
    local_len, capacity, dilation, segment, head_offs, score_scale = geometry
    key_count = key_block.shape[0]
    key_heads = key_block.reshape(key_count, query_sp.shape[1], query_sp.shape[2])
    scores = (
        jnp.einsum("ihd,jhd->hij", query_sp, key_heads, preferred_element_type=jnp.float32)
        * score_scale
    )
    key_index = first_row + jnp.arange(key_count, dtype=jnp.int32)
    source = key_index // capacity
    within = key_index - source * capacity
    key_pos = source[None, :] * local_len + head_offs[:, None] + dilation * within[None, :]
    key_live = within < local_len // dilation
    earlier = key_pos[:, None, :] <= query_pos[:, :, None]
    segment_match = key_pos[:, None, :] // segment == query_pos[:, :, None] // segment
    allowed = earlier & segment_match & key_live[None, None, :]
    return (jnp.where(allowed, jnp.exp(scores), 0.0), key_heads)


def forward_block(running, pieces, first_row, query_sp, query_pos, geometry):
    numerator, denominator = running
    key_block, value_block = pieces
    weights, key_heads = key_weights(query_sp, query_pos, key_block, first_row, geometry)
    value_heads = value_block.reshape(key_heads.shape)
    numerator = numerator + jnp.einsum(
        "hij,jhd->hid",
        weights.astype(jnp.bfloat16),
        value_heads,
        preferred_element_type=jnp.float32,
    )
    return (numerator, denominator + jnp.sum(weights, axis=2))


def blockwise(step_fn, running, pieces, first_row, block_rows):
    total_rows = pieces[0].shape[0]
    if total_rows > block_rows and total_rows % block_rows == 0:
        number = total_rows // block_rows
        stacked_first = pieces[0].reshape(number, block_rows, pieces[0].shape[1])
        stacked_second = pieces[1].reshape(number, block_rows, pieces[1].shape[1])
        block_starts = first_row + block_rows * jnp.arange(number, dtype=jnp.int32)

        def advance(state, items):
            return (step_fn(state, (items[0], items[1]), items[2]), None)

        running, _ = lax.scan(advance, running, (stacked_first, stacked_second, block_starts))
        return running
    return step_fn(running, pieces, first_row)


def backward_block(running, items, query_sp, query_pos, grad_sp, shift_sp, geometry):
    key_block, value_block, first_row = items
    score_scale = geometry[5]
    weights, key_heads = key_weights(query_sp, query_pos, key_block, first_row, geometry)
    key_count = key_block.shape[0]
    value_heads = value_block.reshape(key_heads.shape)
    pressure = jnp.einsum("ihd,jhd->hij", grad_sp, value_heads, preferred_element_type=jnp.float32)
    slopes = (weights * (pressure - shift_sp[:, :, None])).astype(jnp.bfloat16)
    running = (
        running
        + jnp.einsum("hij,jhd->ihd", slopes, key_heads, preferred_element_type=jnp.float32)
        * score_scale
    )
    grad_keys = (
        jnp.einsum("hij,ihd->jhd", slopes, query_sp, preferred_element_type=jnp.float32)
        * score_scale
    )
    grad_values = jnp.einsum(
        "hij,ihd->jhd", weights.astype(jnp.bfloat16), grad_sp, preferred_element_type=jnp.float32
    )
    return (running, (grad_keys.reshape(key_count, -1), grad_values.reshape(key_count, -1)))


def local_weights(query_heads, key_heads, score_scale):
    local_len = query_heads.shape[0]
    scores = (
        jnp.einsum("ihd,jhd->hij", query_heads, key_heads, preferred_element_type=jnp.float32)
        * score_scale
    )
    positions = jnp.arange(local_len, dtype=jnp.int32)
    causal = positions[:, None] >= positions[None, :]
    return jnp.where(causal[None], jnp.exp(scores), 0.0)


def on_device(
    tokens,
    cotangent,
    entry_weight,
    exit_weight,
    up_weight,
    down_weight,
    first_gain,
    first_bias,
    second_gain,
    second_bias,
    dilations,
    offsets,
):
    local_len, width_model = tokens.shape
    head_count = offsets.shape[1]
    head_size = width_model // head_count
    score_scale = head_size ** (-0.5)
    capacity = local_len // RATE_MIN
    group_idx = lax.axis_index("grp")
    seq_index = lax.axis_index("seq")
    seq_count = lax.axis_size("seq")
    dilation = lax.dynamic_index_in_dim(dilations, group_idx, 0, keepdims=False)
    head_offs = lax.dynamic_index_in_dim(offsets, group_idx, 0, keepdims=False)
    segment = local_len * seq_count * dilation // RATE_MAX
    step_ids = jnp.arange(capacity, dtype=jnp.int32)
    row_live = step_ids < local_len // dilation
    local_rows = jnp.minimum(head_offs[:, None] + dilation * step_ids[None, :], local_len - 1)
    query_pos = jnp.where(
        row_live[None, :],
        seq_index * local_len + head_offs[:, None] + dilation * step_ids[None, :],
        -1,
    )
    geometry = (local_len, capacity, dilation, segment, head_offs, score_scale)
    head_shape = (local_len, head_count, head_size)
    selector = local_rows[:, :, None] == jnp.arange(local_len, dtype=jnp.int32)[None, None, :]
    select_low = selector.astype(jnp.bfloat16)
    select_full = selector.astype(jnp.float32)

    def pick(array_in):
        return jnp.einsum(
            "hci,ihd->chd", select_low, array_in, preferred_element_type=jnp.float32
        ).astype(jnp.bfloat16)

    def place_back(sparse_in):
        return jnp.einsum("hci,chd->ihd", select_full, sparse_in, precision=PRECISE)

    inputs = tokens.astype(jnp.float32)
    normed_one, plain_one, inverse_one = norm_forward(inputs, first_gain, first_bias)
    normed_low = normed_one.astype(jnp.bfloat16)
    packed = jnp.dot(normed_low, entry_weight, preferred_element_type=jnp.float32).astype(
        jnp.bfloat16
    )
    query_heads = packed[:, :width_model].reshape(head_shape)
    key_heads = packed[:, width_model : 2 * width_model].reshape(head_shape)
    value_heads = packed[:, 2 * width_model :].reshape(head_shape)
    query_sp = pick(query_heads)
    key_sp = pick(key_heads).reshape(capacity, width_model)
    value_sp = pick(value_heads).reshape(capacity, width_model)
    empty_state = (
        jnp.zeros((head_count, capacity, head_size), jnp.float32),
        jnp.zeros((head_count, capacity), jnp.float32),
    )
    forward_step = partial(forward_block, query_sp=query_sp, query_pos=query_pos, geometry=geometry)
    numerator, denominator = blockwise(
        forward_step,
        empty_state,
        (
            lax.all_gather(key_sp, "seq", axis=0, tiled=True),
            lax.all_gather(value_sp, "seq", axis=0, tiled=True),
        ),
        jnp.int32(0),
        8 * capacity,
    )

    def local_part(query_in, key_in, value_in):
        weights = local_weights(query_in, key_in, score_scale)
        local_num = jnp.einsum(
            "hij,jhd->ihd",
            weights.astype(jnp.bfloat16),
            value_in,
            preferred_element_type=jnp.float32,
        )
        return (local_num, jnp.sum(weights, axis=2).T)

    def local_none(query_in, key_in, value_in):
        return (jnp.zeros(head_shape, jnp.float32), jnp.zeros((local_len, head_count), jnp.float32))

    local_num, local_den = lax.cond(
        group_idx == 0, local_part, local_none, query_heads, key_heads, value_heads
    )
    numerator_full = (
        jnp.einsum("hci,hcd->ihd", select_full, numerator, precision=PRECISE) + local_num
    )
    denominator_full = (
        jnp.einsum("hci,hc->ih", select_full, denominator, precision=PRECISE) + local_den
    )
    merged_num, merged_den = lax.psum(
        (numerator_full.reshape(local_len, width_model), denominator_full), "grp"
    )
    attention = merged_num.reshape(head_shape) / merged_den[:, :, None]
    mixed = attention.reshape(local_len, width_model).astype(jnp.bfloat16)
    middle = inputs + jnp.dot(mixed, exit_weight, preferred_element_type=jnp.float32)
    normed_two, plain_two, inverse_two = norm_forward(middle, second_gain, second_bias)
    normed_two_low = normed_two.astype(jnp.bfloat16)
    hidden = jnp.dot(normed_two_low, up_weight, preferred_element_type=jnp.float32)
    active = jax.nn.gelu(hidden, approximate=False).astype(jnp.bfloat16)
    output = (middle + jnp.dot(active, down_weight, preferred_element_type=jnp.float32)).astype(
        jnp.bfloat16
    )
    down_grad = jnp.dot(active.T, cotangent, preferred_element_type=jnp.float32)
    grad_active = jnp.dot(cotangent, down_weight.T, preferred_element_type=jnp.float32)
    _, gelu_pull = jax.vjp(partial(jax.nn.gelu, approximate=False), hidden)
    grad_hidden = gelu_pull(grad_active)[0].astype(jnp.bfloat16)
    up_grad = jnp.dot(normed_two_low.T, grad_hidden, preferred_element_type=jnp.float32)
    grad_normed_two = jnp.dot(grad_hidden, up_weight.T, preferred_element_type=jnp.float32)
    grad_plain_two, second_gain_grad, second_bias_grad = norm_backward(
        grad_normed_two, plain_two, inverse_two, second_gain
    )
    grad_middle = cotangent.astype(jnp.float32) + grad_plain_two
    grad_branch = grad_middle.astype(jnp.bfloat16)
    exit_grad = jnp.dot(mixed.T, grad_branch, preferred_element_type=jnp.float32)
    grad_mixed_low = lax.optimization_barrier(
        jnp.dot(grad_branch, exit_weight.T, preferred_element_type=jnp.float32).astype(jnp.bfloat16)
    )
    grad_mixed = grad_mixed_low.astype(jnp.float32).reshape(head_shape)
    grad_numer = (grad_mixed / merged_den[:, :, None]).astype(jnp.bfloat16)
    row_shift = jnp.sum(grad_mixed * attention, axis=2) / merged_den
    grad_sp = pick(grad_numer)
    shift_sp = jnp.einsum("hci,ih->hc", select_full, row_shift, precision=PRECISE)
    back_keys, back_values = (
        lax.all_gather(key_sp, "seq", axis=0, tiled=True),
        lax.all_gather(value_sp, "seq", axis=0, tiled=True),
    )
    block_rows = 8 * capacity
    number = back_keys.shape[0] // block_rows
    stacked_keys = back_keys.reshape(number, block_rows, width_model)
    stacked_values = back_values.reshape(number, block_rows, width_model)
    block_starts = block_rows * jnp.arange(number, dtype=jnp.int32)
    empty_query = jnp.zeros((capacity, head_count, head_size), jnp.float32)
    back_step = partial(
        backward_block,
        query_sp=query_sp,
        query_pos=query_pos,
        grad_sp=grad_sp,
        shift_sp=shift_sp,
        geometry=geometry,
    )
    grad_query_sp, (grad_key_all, grad_value_all) = lax.scan(
        back_step, empty_query, (stacked_keys, stacked_values, block_starts)
    )
    own_keys, own_values = (
        lax.psum_scatter(
            grad_key_all.reshape(-1, width_model), "seq", scatter_dimension=0, tiled=True
        ),
        lax.psum_scatter(
            grad_value_all.reshape(-1, width_model), "seq", scatter_dimension=0, tiled=True
        ),
    )

    def local_grads(query_in, key_in, value_in, grad_in, shift_in):
        weights = local_weights(query_in, key_in, score_scale)
        pressure = jnp.einsum("ihd,jhd->hij", grad_in, value_in, preferred_element_type=jnp.float32)
        slopes = (weights * (pressure - shift_in.T[:, :, None])).astype(jnp.bfloat16)
        grad_query = (
            jnp.einsum("hij,jhd->ihd", slopes, key_in, preferred_element_type=jnp.float32)
            * score_scale
        )
        grad_key = (
            jnp.einsum("hij,ihd->jhd", slopes, query_in, preferred_element_type=jnp.float32)
            * score_scale
        )
        grad_value = jnp.einsum(
            "hij,ihd->jhd",
            weights.astype(jnp.bfloat16),
            grad_in,
            preferred_element_type=jnp.float32,
        )
        return (grad_query, grad_key, grad_value)

    def local_skip(query_in, key_in, value_in, grad_in, shift_in):
        zeros_heads = jnp.zeros(head_shape, jnp.float32)
        return (zeros_heads, zeros_heads, zeros_heads)

    local_dq, local_dk, local_dv = lax.cond(
        group_idx == 0,
        local_grads,
        local_skip,
        query_heads,
        key_heads,
        value_heads,
        grad_numer,
        row_shift,
    )
    grad_query_full = place_back(grad_query_sp) + local_dq
    grad_key_full = place_back(own_keys.reshape(capacity, head_count, head_size)) + local_dk
    grad_value_full = place_back(own_values.reshape(capacity, head_count, head_size)) + local_dv
    grad_packed = jnp.concatenate(
        [
            grad_query_full.reshape(local_len, width_model),
            grad_key_full.reshape(local_len, width_model),
            grad_value_full.reshape(local_len, width_model),
        ],
        axis=1,
    )
    summed = lax.psum(grad_packed, "grp").astype(jnp.bfloat16)
    entry_grad = jnp.dot(normed_low.T, summed, preferred_element_type=jnp.float32)
    grad_normed_one = jnp.dot(summed, entry_weight.T, preferred_element_type=jnp.float32)
    grad_plain_one, first_gain_grad, first_bias_grad = norm_backward(
        grad_normed_one, plain_one, inverse_one, first_gain
    )
    token_grad = (grad_middle + grad_plain_one).astype(jnp.bfloat16)
    shards = (
        lax.psum_scatter(entry_grad, "seq", scatter_dimension=0, tiled=True),
        lax.psum_scatter(exit_grad, "seq", scatter_dimension=0, tiled=True),
        lax.psum_scatter(up_grad, "seq", scatter_dimension=0, tiled=True),
        lax.psum_scatter(down_grad, "seq", scatter_dimension=0, tiled=True),
        lax.psum_scatter(first_gain_grad, "seq", scatter_dimension=0, tiled=True),
        lax.psum_scatter(first_bias_grad, "seq", scatter_dimension=0, tiled=True),
        lax.psum_scatter(second_gain_grad, "seq", scatter_dimension=0, tiled=True),
        lax.psum_scatter(second_bias_grad, "seq", scatter_dimension=0, tiled=True),
    )
    return (
        output,
        token_grad,
        shards[0],
        shards[1],
        shards[2],
        shards[3],
        shards[4],
        shards[5],
        shards[6],
        shards[7],
    )


MESH = pl.DeviceIdType.MESH
LANES = 128
LOG2E = 1.4426950408889634
F32 = jnp.float32
BF16 = jnp.bfloat16


def dot_nn(left, right):
    return lax.dot_general(left, right, (((1,), (0,)), ((), ())), preferred_element_type=F32)


def dot_nt(left, right):
    return lax.dot_general(left, right, (((1,), (1,)), ((), ())), preferred_element_type=F32)


def dot_tn(left, right):
    return lax.dot_general(left, right, (((0,), (0,)), ((), ())), preferred_element_type=F32)


def lane_ids(width):
    return lax.broadcasted_iota(jnp.int32, (1, width), 1)


def slot_mask(slot, width=256):
    ids = lane_ids(width)
    return jnp.where((ids >= 64 * slot) & (ids < 64 * slot + 64), 1.0, 0.0).astype(F32)


def join_halves(low_part, high_part):
    return jnp.where(lane_ids(LANES) < 64, low_part, high_part)


def swap_halves(tile):
    return pltpu.roll(tile, 64, axis=1)


def layer_kernel(
    sizes,
    dil_ref,
    off_ref,
    tok_ref,
    cot_ref,
    gain1_ref,
    bias1_ref,
    gain2_ref,
    bias2_ref,
    entry_hbm,
    exit_hbm,
    up_hbm,
    down_hbm,
    out_ref,
    tgrad_ref,
    oentry_ref,
    oexit_ref,
    oup_ref,
    odown_ref,
    ostat_ref,
    win,
    exit_all,
    exit_win,
    up_all,
    down_all,
    n1,
    n2,
    plain2,
    inv2,
    middle,
    gmid,
    gbranch,
    mixed,
    active,
    ghid,
    gn2,
    member,
    masks,
    kv,
    qb,
    dob,
    qmask,
    shift,
    invden,
    att,
    acc_a,
    acc_b,
    acc_c,
    zmix,
    zdq,
    zdkv,
    stat,
    pc_down,
    r1_down,
    y_down,
    r2_down,
    ag_down,
    pc_up,
    r1_up,
    y_up,
    r2_up,
    ag_up,
    pc_entry,
    r1_entry,
    y_entry,
    r2_entry,
    ag_entry,
    load_sem,
    kv_ssem,
    kv_rsem,
    q_ssem,
    q_rsem,
    do_ssem,
    do_rsem,
    zm_ssem,
    zm_rsem,
    zq_ssem,
    zq_rsem,
    zk_ssem,
    zk_rsem,
    rs_s1,
    rs_r1,
    rs_s2,
    rs_r2,
    rs_zs,
    rs_zr,
    st_ssem,
    st_rsem,
):
    T, D, HEADS, E, FF, NSEQ, NGRP = sizes
    scale = E ** (-0.5)
    exp_scale = scale * LOG2E
    s = lax.axis_index("seq")
    g = lax.axis_index("grp")
    chip = s // 2
    core = s % 2
    sib = s + 1 - 2 * core
    odd = g % 2
    chips = NSEQ // 2
    part = D // NGRP
    is_odd = odd == 1

    def to_seq(peer, src, dst, ssem, rsem):
        return pltpu.make_async_remote_copy(
            src_ref=src,
            dst_ref=dst,
            send_sem=ssem,
            recv_sem=rsem,
            device_id={"seq": peer},
            device_id_type=MESH,
        )

    def to_grp(peer, src, dst, ssem, rsem):
        return pltpu.make_async_remote_copy(
            src_ref=src,
            dst_ref=dst,
            send_sem=ssem,
            recv_sem=rsem,
            device_id={"grp": peer},
            device_id_type=MESH,
        )

    loads = []
    for t in range(3):
        first = pl.multiple_of(t * D + part * g - 64 * odd, LANES)
        loads.append(
            pltpu.make_async_copy(entry_hbm.at[:, pl.ds(first, 256)], win.at[t], load_sem.at[t])
        )
    loads.append(pltpu.make_async_copy(down_hbm, down_all, load_sem.at[3]))
    loads.append(pltpu.make_async_copy(exit_hbm, exit_all, load_sem.at[4]))
    loads.append(
        pltpu.make_async_copy(
            exit_hbm.at[pl.ds(pl.multiple_of(part * g, 64), part), :],
            exit_win.at[pl.ds(64, part), :],
            load_sem.at[5],
        )
    )
    loads.append(pltpu.make_async_copy(up_hbm, up_all, load_sem.at[6]))
    for load in loads:
        load.start()
    entry_all = up_all.at[:, 0 : 3 * D]
    late_load = pltpu.make_async_copy(entry_hbm, entry_all, load_sem.at[7])

    barrier = pltpu.get_barrier_semaphore()
    for step in range(1, NSEQ):
        pl.semaphore_signal(
            barrier, inc=1, device_id={"seq": lax.rem(s + step, NSEQ)}, device_id_type=MESH
        )
    for step in range(1, NGRP):
        pl.semaphore_signal(
            barrier, inc=1, device_id={"grp": lax.rem(g + step, NGRP)}, device_id_type=MESH
        )

    rows = 96

    def norm_one(i, carry):
        at = pl.ds(pl.multiple_of(i * rows, rows), rows)
        value = tok_ref[at, :].astype(F32)
        centered = value - jnp.mean(value, axis=1, keepdims=True)
        inverse = lax.rsqrt(jnp.mean(centered * centered, axis=1, keepdims=True) + EPS)
        n1[at, :] = (centered * inverse * gain1_ref[...] + bias1_ref[...]).astype(BF16)
        return carry

    lax.fori_loop(0, T // rows, norm_one, 0)
    exit_win[0:64, :] = jnp.zeros((64, D), BF16)

    for t in range(3):
        loads[t].wait()
    lane256 = lane_ids(256)
    q_raw = dot_nn(n1[...], win[0])
    k_raw = dot_nn(n1[...], win[1])
    v_raw = dot_nn(n1[...], win[2])
    q_own = jnp.where(is_odd, pltpu.roll(q_raw, 192, axis=1), q_raw)
    k_own = jnp.where(is_odd, pltpu.roll(k_raw, 192, axis=1), k_raw)
    v_own = jnp.where(is_odd, v_raw, pltpu.roll(v_raw, 64, axis=1))
    q_own = jnp.where(lane256 < 192, q_own, 0.0)
    qb[s] = q_own.astype(BF16)
    for h in range(3):
        qmask[h] = (q_own * slot_mask(h)).astype(BF16)
    kv[s, :, 0:128] = k_own[:, 0:128].astype(BF16)
    kv[s, :, 128:256] = join_halves(k_own[:, 128:256], v_own[:, 0:128]).astype(BF16)
    kv[s, :, 256:384] = v_own[:, 128:256].astype(BF16)

    pl.semaphore_wait(barrier, NSEQ - 1 + NGRP - 1)

    sends = []

    def start_when(cond, copy):
        @pl.when(cond)
        def _():
            copy.start()

        sends.append((cond, copy))

    for d in range(1, chips):
        up_to = lax.rem(s + 2 * d, NSEQ)
        start_when(
            chip + d < chips,
            to_seq(up_to, kv.at[s], kv.at[s], kv_ssem.at[d - 1], kv_rsem.at[s]),
        )
    start_when(core == 0, to_seq(sib, kv.at[s], kv.at[s], kv_ssem.at[3], kv_rsem.at[s]))
    for d in range(1, chips):
        down_to = lax.rem(s - 2 * d + NSEQ, NSEQ)
        start_when(
            chip - d >= 0,
            to_seq(down_to, qb.at[s], qb.at[s], q_ssem.at[d - 1], q_rsem.at[s]),
        )
    start_when(core == 1, to_seq(sib, qb.at[s], qb.at[s], q_ssem.at[3], q_rsem.at[s]))

    lane128 = lane_ids(LANES)
    rate_row = jnp.ones((1, LANES), F32)
    for i in range(NGRP):
        rate_row = jnp.where(lane128 == i, dil_ref[i].astype(F32), rate_row)
    local_pos = lax.broadcasted_iota(jnp.int32, (T, 1), 0).astype(F32)
    residue = local_pos - rate_row * jnp.floor((local_pos + 0.5) / rate_row)
    for h in range(3):
        off_row = jnp.full((1, LANES), -1.0, F32)
        for i in range(NGRP):
            off_row = jnp.where(
                lane128 == i, off_ref[i * HEADS + 3 * g + h].astype(F32), off_row
            )
        member[h] = jnp.where(residue == off_row, 1.0, 0.0).astype(BF16)
    per_segment = rate_row * (T * NSEQ // RATE_MAX)

    def segment_of(block):
        return jnp.floor((jnp.full((1, LANES), block * T, jnp.int32).astype(F32) + 0.5) / per_segment)

    own_segment = segment_of(s)

    def build_mask(i, carry):
        b = i // 3
        h = i - 3 * b
        same = jnp.where(segment_of(b) == own_segment, 1.0, 0.0)
        count = dot_nt((member[h].astype(F32) * same).astype(BF16), member[h])
        masks[b, h] = count.astype(BF16)

        @pl.when(b == s)
        def _():
            row_id = lax.broadcasted_iota(jnp.int32, (T, T), 0)
            col_id = lax.broadcasted_iota(jnp.int32, (T, T), 1)
            masks[b, h] = jnp.where(col_id <= row_id, count + 1.0, 0.0).astype(BF16)
            masks[NSEQ, h] = jnp.where(row_id <= col_id, count + 1.0, 0.0).astype(BF16)

        return carry

    lax.fori_loop(0, 3 * NSEQ, build_mask, 0)

    loads[3].wait()

    def cot_times_down(i, carry):
        at = pl.ds(pl.multiple_of(i * T, T), T)
        ghid[:, at] = dot_nt(cot_ref[...], down_all[at, :]).astype(BF16)
        return carry

    lax.fori_loop(0, FF // T, cot_times_down, 0)

    acc_a[...] = jnp.zeros_like(acc_a)
    den = shift
    den[...] = jnp.zeros_like(den)

    def forward_step(j, carry):
        jj = j - 1 - core
        d = jj // 2 + 1
        which = jj % 2
        far = jnp.where(which == 0, s - 2 * d, sib - 2 * d)
        b = jnp.where(j == 0, s, jnp.where(jj < 0, s - 1, far))

        @pl.when(j > 0)
        def _():
            to_seq(sib, kv.at[b], kv.at[b], kv_ssem.at[0], kv_rsem.at[b]).wait_recv()

        @pl.when((jj >= 0) & (which == 0))
        def _():
            to_seq(sib, kv.at[b], kv.at[b], kv_ssem.at[3 + d], kv_rsem.at[b]).start()

        for h in range(3):
            score = dot_nt(qmask[h], kv[b, :, 0:256])
            weight = jnp.exp2(score * exp_scale) * masks[b, h].astype(F32)
            den[h] += weight[:, 0:128] + weight[:, 128:256] + weight[:, 256:384]
            low_weight = weight.astype(BF16)
            masks[b, h] = low_weight
            acc_a[...] += dot_nn(low_weight, kv[b, :, 128:384]) * slot_mask(h + 1)
        return carry

    lax.fori_loop(0, s + 1, forward_step, 0)

    inv_all = jnp.zeros((T, 256), F32)
    for h in range(3):
        inv_all = jnp.where(
            slot_mask(h + 1) > 0.5, 1.0 / jnp.sum(den[h], axis=1, keepdims=True), inv_all
        )
    invden[...] = inv_all
    att_own = acc_a[...] * inv_all
    att[...] = att_own

    def pack(target, tile_low, tile_high):
        target[0:T, :] = tile_high.astype(BF16)
        half = T // 2
        target[T : T + half, :] = join_halves(
            swap_halves(tile_low[half:T]), tile_low[0:half]
        ).astype(BF16)

    def unpack_pair(first, second, place):
        half = T // 2
        a_high = first[0:T, :].astype(F32)
        a_rest = first[T : T + half, :].astype(F32)
        b_high = second[0:T, :].astype(F32)
        b_rest = second[T : T + half, :].astype(F32)
        place(2, slice(0, T), b_high)
        swapped = swap_halves(a_high)
        place(0, slice(0, half), join_halves(swap_halves(a_rest), swapped[0:half]))
        place(0, slice(half, T), join_halves(a_rest, swapped[half:T]))
        place(1, slice(0, half), join_halves(swapped[0:half], b_rest))
        place(1, slice(half, T), join_halves(swapped[half:T], swap_halves(b_rest)))

    def chain_start(at, ssem, rsem):
        start_when(g + 1 < NGRP, to_grp(lax.rem(g + 1, NGRP), at(g), at(g), ssem.at[0, 0], rsem.at[g]))
        start_when(
            g >= 1, to_grp(lax.rem(g + NGRP - 1, NGRP), at(g), at(g), ssem.at[0, 1], rsem.at[g])
        )

    def chain_step(d, at, ssem, rsem):
        right = lax.rem(g + 1, NGRP)
        left = lax.rem(g + NGRP - 1, NGRP)
        lower = lax.rem(g - d + NGRP, NGRP)
        upper = lax.rem(g + d, NGRP)

        @pl.when(g - d >= 0)
        def _():
            to_grp(right, at(lower), at(lower), ssem.at[0, 0], rsem.at[lower]).wait_recv()

        if d < NGRP - 1:
            start_when(
                (g - d >= 0) & (g + 1 < NGRP),
                to_grp(right, at(lower), at(lower), ssem.at[d, 0], rsem.at[lower]),
            )

        @pl.when(g + d < NGRP)
        def _():
            to_grp(left, at(upper), at(upper), ssem.at[0, 1], rsem.at[upper]).wait_recv()

        if d < NGRP - 1:
            start_when(
                (g + d < NGRP) & (g >= 1),
                to_grp(left, at(upper), at(upper), ssem.at[d, 1], rsem.at[upper]),
            )

    pack(zmix.at[g], att_own[:, 0:128], att_own[:, 128:256])
    chain_start(lambda i: zmix.at[i], zm_ssem, zm_rsem)

    for d in range(1, chips):
        slot = lax.rem(s + 2 * d, NSEQ)

        @pl.when(chip + d < chips)
        def _():
            to_seq(sib, qb.at[slot], qb.at[slot], q_ssem.at[0], q_rsem.at[slot]).wait_recv()

        start_when(
            chip + d < chips,
            to_seq(sib, qb.at[slot], qb.at[slot], q_ssem.at[3 + d], q_rsem.at[slot]),
        )

    for d in range(1, NGRP):
        chain_step(d, lambda i: zmix.at[i], zm_ssem, zm_rsem)

    def place_mixed(pair):
        def place(tile, at, value):
            first = pair * 2 * part + tile * LANES
            mixed[at, first : first + LANES] = value.astype(BF16)

        return place

    for pair in range(NGRP // 2):
        unpack_pair(zmix.at[2 * pair], zmix.at[2 * pair + 1], place_mixed(pair))

    loads[4].wait()
    middle[...] = tok_ref[...].astype(F32) + dot_nn(mixed[...], exit_all[...])

    def norm_two(i, carry):
        at = pl.ds(pl.multiple_of(i * rows, rows), rows)
        value = middle[at, :]
        centered = value - jnp.mean(value, axis=1, keepdims=True)
        inverse = lax.rsqrt(jnp.mean(centered * centered, axis=1, keepdims=True) + EPS)
        plain = centered * inverse
        plain2[at, :] = plain
        inv2[at, :] = jnp.broadcast_to(inverse, (rows, LANES))
        n2[at, :] = (plain * gain2_ref[...] + bias2_ref[...]).astype(BF16)
        return carry

    lax.fori_loop(0, T // rows, norm_two, 0)

    loads[6].wait()
    gn2[...] = jnp.zeros_like(gn2)

    def feed_forward(i, carry):
        at = pl.ds(pl.multiple_of(i * T, T), T)
        hidden = dot_nn(n2[...], up_all[:, at])
        cdf = 0.5 + 0.5 * lax.erf(hidden * (0.5**0.5))
        active[:, at] = (hidden * cdf).astype(BF16)
        density = jnp.exp2(hidden * hidden * (-0.5 * LOG2E)) * 0.3989422804014327
        low_grad = (ghid[:, at].astype(F32) * (cdf + hidden * density)).astype(BF16)
        ghid[:, at] = low_grad
        gn2[...] += dot_nt(low_grad, up_all[:, at])
        return carry

    lax.fori_loop(0, FF // T, feed_forward, 0)
    late_load.start()

    stat[s] = jnp.zeros((8, D), F32)

    def norm_two_back(i, carry):
        at = pl.ds(pl.multiple_of(i * rows, rows), rows)
        upstream = gn2[at, :]
        plain = plain2[at, :]
        scaled = upstream * gain2_ref[...]
        inner = (
            scaled
            - jnp.mean(scaled, axis=1, keepdims=True)
            - plain * jnp.mean(scaled * plain, axis=1, keepdims=True)
        )
        grad = cot_ref[at, :].astype(F32) + inv2[at, 0:1] * inner
        gmid[at, :] = grad
        gbranch[at, :] = grad.astype(BF16)
        stat[s, 0:1, :] += jnp.sum(upstream * plain, axis=0, keepdims=True)
        stat[s, 1:2, :] += jnp.sum(upstream, axis=0, keepdims=True)
        return carry

    lax.fori_loop(0, T // rows, norm_two_back, 0)

    loads[5].wait()
    gmix = dot_nt(gbranch[...], exit_win[...]).astype(BF16).astype(F32)
    numer_grad = gmix * invden[...]
    product = numer_grad * att[...]
    for h in range(3):
        value = jnp.sum(product * slot_mask(h + 1), axis=1, keepdims=True)
        shift[h] = jnp.broadcast_to(value, (T, LANES))
        high = value.astype(BF16).astype(F32)
        low = value - high
        numer_grad = jnp.where(lane256 == 2 * h, high, numer_grad)
        numer_grad = jnp.where(lane256 == 2 * h + 1, low, numer_grad)
    dob[s] = numer_grad.astype(BF16)

    for d in range(1, chips):
        down_to = lax.rem(s - 2 * d + NSEQ, NSEQ)
        start_when(
            chip - d >= 0,
            to_seq(down_to, dob.at[s], dob.at[s], do_ssem.at[d - 1], do_rsem.at[s]),
        )
    start_when(core == 1, to_seq(sib, dob.at[s], dob.at[s], do_ssem.at[3], do_rsem.at[s]))

    width = part + 64
    up_grad = dot_tn(n2[...], ghid[:, pl.ds(pl.multiple_of(g * D, LANES), D)])
    for t in range(NSEQ):
        pc_up[t % 2, t // 2] = up_grad[96 * t : 96 * t + 96, :].astype(BF16)

    @pl.when(g < 3)
    def _():
        cols = pl.ds(pl.multiple_of(lax.rem(g, 3) * width, LANES), width)

        def down_piece(t, carry):
            at = pl.ds(pl.multiple_of(t * T, T), T)
            pc_down[t % 2, t // 2] = dot_tn(active[:, at], cot_ref[:, cols]).astype(BF16)
            return carry

        lax.fori_loop(0, NSEQ, down_piece, 0)

    @pl.when(g == 3)
    def _():
        exit_grad = dot_tn(mixed[...], gbranch[...]).astype(BF16)
        for t in range(NSEQ):
            for i in range(3):
                pc_down[t % 2, t // 2, 96 * i : 96 * i + 96, :] = exit_grad[
                    96 * t : 96 * t + 96, width * i : width * i + width
                ]
            pc_down[t % 2, t // 2, 288:384, :] = jnp.zeros((96, width), BF16)

    def reduce_start(i, pieces, first_in):
        start_when(
            core >= 0,
            to_seq(sib, pieces.at[1 - core], first_in, rs_s1.at[i], rs_r1.at[i]),
        )

    def reduce_pass(i, pieces, first_in, total, second_in):
        to_seq(sib, pieces.at[core], first_in, rs_s1.at[i], rs_r1.at[i]).wait_recv()
        for cc in range(chips):
            total[cc] = (pieces[core, cc].astype(F32) + first_in[cc].astype(F32)).astype(BF16)
        for d in range(1, chips):
            to_chip = lax.rem(chip + d, chips)
            start_when(
                core >= 0,
                to_seq(
                    2 * to_chip + core,
                    total.at[to_chip],
                    second_in.at[chip],
                    rs_s2.at[i, d - 1],
                    rs_r2.at[i, chip],
                ),
            )

    def reduce_end(i, total, second_in, gathered):
        result = total[chip].astype(F32)
        for d in range(1, chips):
            slot = lax.rem(chip + d, chips)
            to_seq(
                sib, second_in.at[slot], second_in.at[slot], rs_s1.at[i], rs_r2.at[i, slot]
            ).wait_recv()
            result = result + second_in[slot].astype(F32)
        gathered[g] = result.astype(BF16)
        chain_start(lambda j: gathered.at[j], rs_zs.at[i], rs_zr.at[i])

    reduce_start(0, pc_up, r1_up)
    reduce_start(1, pc_down, r1_down)

    for h in range(3):
        qmask[h] = (dob[s].astype(F32) * slot_mask(h + 1)).astype(BF16)
    acc_a[...] = jnp.zeros_like(acc_a)

    def query_side(b, carry):
        for h in range(3):
            pressure = dot_nt(qmask[h], kv[b, :, 128:384])
            row_shift = shift[h]
            row_shift = jnp.concatenate([row_shift, row_shift, row_shift], axis=1)
            slope = (masks[b, h].astype(F32) * (pressure - row_shift)).astype(BF16)
            acc_a[...] += dot_nn(slope, kv[b, :, 0:256]) * slot_mask(h)
        return carry

    lax.fori_loop(0, s + 1, query_side, 0)
    dq = pltpu.roll(acc_a[...] * scale, 64, axis=1)
    pack(zdq.at[g], dq[:, 0:128], dq[:, 128:256])
    chain_start(lambda i: zdq.at[i], zq_ssem, zq_rsem)

    reduce_pass(0, pc_up, r1_up, y_up, r2_up)
    reduce_pass(1, pc_down, r1_down, y_down, r2_down)

    acc_b[...] = jnp.zeros_like(acc_b)
    acc_c[...] = jnp.zeros_like(acc_c)
    v_tile = kv[s, :, 128:384].astype(F32)
    k_tile = kv[s, :, 0:256].astype(F32)
    for h in range(3):
        qmask[h] = (k_tile * slot_mask(h)).astype(BF16)
        minus = jnp.where((lane256 == 2 * h) | (lane256 == 2 * h + 1), -1.0, 0.0)
        qmask[3 + h] = (v_tile * slot_mask(h + 1) + minus).astype(BF16)

    def key_side(j, carry):
        jj = j - 2 + core
        d = jj // 2 + 1
        which = jj % 2
        far = jnp.where(which == 0, s + 2 * d, sib + 2 * d)
        b = jnp.where(j == 0, s, jnp.where(jj < 0, s + 1, far))

        @pl.when(j > 0)
        def _():
            to_seq(sib, dob.at[b], dob.at[b], do_ssem.at[0], do_rsem.at[b]).wait_recv()

        @pl.when((jj >= 0) & (which == 0))
        def _():
            to_seq(sib, dob.at[b], dob.at[b], do_ssem.at[3 + d], do_rsem.at[b]).start()

        @pl.when((j > 0) & ((jj < 0) | (which == 1)))
        def _():
            to_seq(sib, qb.at[b], qb.at[b], q_ssem.at[0], q_rsem.at[b]).wait_recv()

        at = jnp.where(j == 0, NSEQ, b)
        for h in range(3):
            score = dot_nt(qmask[h], qb[b])
            weight = jnp.exp2(score * exp_scale) * masks[at, h].astype(F32)
            pressure = dot_nt(qmask[3 + h], dob[b])
            slope = (weight * pressure).astype(BF16)
            acc_b[...] += dot_nn(slope, qb[b]) * slot_mask(h)
            acc_c[...] += dot_nn(weight.astype(BF16), dob[b]) * slot_mask(h + 1)
        return carry

    lax.fori_loop(0, NSEQ - s, key_side, 0)

    dk = pltpu.roll(acc_b[...] * scale, 64, axis=1)
    pack(zdkv.at[g, 0], dk[:, 0:128], dk[:, 128:256])
    dv = acc_c[...]
    pack(zdkv.at[g, 1], dv[:, 0:128], dv[:, 128:256])
    chain_start(lambda i: zdkv.at[i], zk_ssem, zk_rsem)

    dfull = ghid.at[:, 0 : 3 * D]
    dpack = ghid.at[:, 3 * D : 3 * D + 640]
    dpack[:, 0:128] = join_halves(swap_halves(dq[:, 0:128]), swap_halves(dq[:, 128:256])).astype(BF16)
    dpack[:, 128:256] = join_halves(swap_halves(dq[:, 128:256]), dk[:, 0:128]).astype(BF16)
    dpack[:, 256:384] = dk[:, 128:256].astype(BF16)
    dpack[:, 384:512] = join_halves(swap_halves(dv[:, 0:128]), swap_halves(dv[:, 128:256])).astype(BF16)
    dpack[:, 512:640] = join_halves(swap_halves(dv[:, 128:256]), jnp.zeros((T, LANES), F32)).astype(BF16)
    entry_grad = dot_tn(n1[...], dpack[...])
    for t in range(NSEQ):
        pc_entry[t % 2, t // 2] = entry_grad[96 * t : 96 * t + 96, :].astype(BF16)
    reduce_start(2, pc_entry, r1_entry)

    reduce_end(0, y_up, r2_up, ag_up)
    reduce_end(1, y_down, r2_down, ag_down)
    for d in range(1, NGRP):
        chain_step(d, lambda i: zdq.at[i], zq_ssem, zq_rsem)
    reduce_pass(2, pc_entry, r1_entry, y_entry, r2_entry)
    for d in range(1, NGRP):
        chain_step(d, lambda i: zdkv.at[i], zk_ssem, zk_rsem)

    def place_grad(first_col):
        def place(tile, at, value):
            first = first_col + tile * LANES
            dfull[at, first : first + LANES] = value.astype(BF16)

        return place

    for pair in range(NGRP // 2):
        first_col = pair * 2 * part
        unpack_pair(zdq.at[2 * pair], zdq.at[2 * pair + 1], place_grad(first_col))
        for t in range(2):
            unpack_pair(
                zdkv.at[2 * pair, t], zdkv.at[2 * pair + 1, t], place_grad((t + 1) * D + first_col)
            )

    out_ref[...] = (middle[...] + dot_nn(active[...], down_all[...])).astype(BF16)
    reduce_end(2, y_entry, r2_entry, ag_entry)
    late_load.wait()
    gn2[...] = dot_nt(dfull[...], up_all[:, 0 : 3 * D])

    def norm_one_back(i, carry):
        at = pl.ds(pl.multiple_of(i * rows, rows), rows)
        value = tok_ref[at, :].astype(F32)
        centered = value - jnp.mean(value, axis=1, keepdims=True)
        inverse = lax.rsqrt(jnp.mean(centered * centered, axis=1, keepdims=True) + EPS)
        plain = centered * inverse
        upstream = gn2[at, :]
        scaled = upstream * gain1_ref[...]
        inner = (
            scaled
            - jnp.mean(scaled, axis=1, keepdims=True)
            - plain * jnp.mean(scaled * plain, axis=1, keepdims=True)
        )
        tgrad_ref[at, :] = (gmid[at, :] + inverse * inner).astype(BF16)
        stat[s, 2:3, :] += jnp.sum(upstream * plain, axis=0, keepdims=True)
        stat[s, 3:4, :] += jnp.sum(upstream, axis=0, keepdims=True)
        return carry

    lax.fori_loop(0, T // rows, norm_one_back, 0)
    for step in range(1, NSEQ):
        peer = lax.rem(s + step, NSEQ)
        start_when(
            core >= 0, to_seq(peer, stat.at[s], stat.at[s], st_ssem.at[step - 1], st_rsem.at[s])
        )

    for d in range(1, NGRP):
        chain_step(d, lambda i: ag_up.at[i], rs_zs.at[0], rs_zr.at[0])
    for i in range(NGRP):
        oup_ref[:, D * i : D * i + D] = ag_up[i]
    for d in range(1, NGRP):
        chain_step(d, lambda i: ag_down.at[i], rs_zs.at[1], rs_zr.at[1])
    for i in range(3):
        odown_ref[:, width * i : width * i + width] = ag_down[i]
        oexit_ref[:, width * i : width * i + width] = ag_down[3, 96 * i : 96 * i + 96, :]
    for d in range(1, NGRP):
        chain_step(d, lambda i: ag_entry.at[i], rs_zs.at[2], rs_zr.at[2])
    for pair in range(NGRP // 2):
        a = ag_entry[2 * pair].astype(F32)
        b = ag_entry[2 * pair + 1].astype(F32)
        first = pair * 2 * part
        tiles = (
            (0, a[:, 0:128]),
            (1, join_halves(a[:, 128:256], swap_halves(b[:, 0:128]))),
            (2, join_halves(swap_halves(b[:, 0:128]), swap_halves(b[:, 128:256]))),
            (6, join_halves(swap_halves(a[:, 128:256]), swap_halves(a[:, 256:384]))),
            (7, join_halves(swap_halves(a[:, 256:384]), b[:, 128:256])),
            (8, b[:, 256:384]),
            (12, a[:, 384:512]),
            (13, join_halves(a[:, 512:640], swap_halves(b[:, 384:512]))),
            (14, join_halves(swap_halves(b[:, 384:512]), swap_halves(b[:, 512:640]))),
        )
        for tile, value in tiles:
            at = tile * LANES + first
            oentry_ref[:, at : at + LANES] = value.astype(BF16)

    for step in range(1, NSEQ):
        slot = lax.rem(s + step, NSEQ)
        to_seq(sib, stat.at[slot], stat.at[slot], st_ssem.at[0], st_rsem.at[slot]).wait_recv()
    total_stat = stat[0]
    for i in range(1, NSEQ):
        total_stat = total_stat + stat[i]
    ostat_ref[...] = total_stat

    for cond, copy in sends:

        @pl.when(cond)
        def _(copy=copy):
            copy.wait_send()

    for d in range(1, chips):

        @pl.when(chip - d >= 0)
        def _(d=d):
            slot = lax.rem(s - 2 * d + NSEQ, NSEQ)
            to_seq(sib, kv.at[slot], kv.at[slot], kv_ssem.at[3 + d], kv_rsem.at[slot]).wait_send()

        @pl.when(chip + d < chips)
        def _(d=d):
            slot = lax.rem(s + 2 * d, NSEQ)
            to_seq(sib, dob.at[slot], dob.at[slot], do_ssem.at[3 + d], do_rsem.at[slot]).wait_send()


def fast_on_device(
    seq_count,
    tokens,
    cotangent,
    entry_weight,
    exit_weight,
    up_weight,
    down_weight,
    first_gain,
    first_bias,
    second_gain,
    second_bias,
    dilations,
    offsets,
):
    T, D = tokens.shape
    NGRP, HEADS = offsets.shape
    FF = up_weight.shape[1]
    E = D // HEADS
    NSEQ = seq_count
    chips = NSEQ // 2
    sizes = (T, D, HEADS, E, FF, NSEQ, NGRP)
    share = T * 3 // 2
    vmem = pl.BlockSpec(memory_space=pltpu.VMEM)
    smem = pl.BlockSpec(memory_space=pltpu.SMEM)
    anywhere = pl.BlockSpec(memory_space=pl.ANY)
    dma = pltpu.SemaphoreType.DMA
    scratch = [
        pltpu.VMEM((3, D, 256), BF16),
        pltpu.VMEM((D, D), BF16),
        pltpu.VMEM((256, D), BF16),
        pltpu.VMEM((D, FF), BF16),
        pltpu.VMEM((FF, D), BF16),
        pltpu.VMEM((T, D), BF16),
        pltpu.VMEM((T, D), BF16),
        pltpu.VMEM((T, D), F32),
        pltpu.VMEM((T, LANES), F32),
        pltpu.VMEM((T, D), F32),
        pltpu.VMEM((T, D), F32),
        pltpu.VMEM((T, D), BF16),
        pltpu.VMEM((T, D), BF16),
        pltpu.VMEM((T, FF), BF16),
        pltpu.VMEM((T, FF), BF16),
        pltpu.VMEM((T, D), F32),
        pltpu.VMEM((3, T, LANES), BF16),
        pltpu.VMEM((NSEQ + 1, 3, T, T), BF16),
        pltpu.VMEM((NSEQ, T, 384), BF16),
        pltpu.VMEM((NSEQ, T, 256), BF16),
        pltpu.VMEM((NSEQ, T, 256), BF16),
        pltpu.VMEM((6, T, 256), BF16),
        pltpu.VMEM((3, T, LANES), F32),
        pltpu.VMEM((T, 256), F32),
        pltpu.VMEM((T, 256), F32),
        pltpu.VMEM((T, 256), F32),
        pltpu.VMEM((T, 256), F32),
        pltpu.VMEM((T, 256), F32),
        pltpu.VMEM((NGRP, share, LANES), BF16),
        pltpu.VMEM((NGRP, share, LANES), BF16),
        pltpu.VMEM((NGRP, 2, share, LANES), BF16),
        pltpu.VMEM((NSEQ, 8, D), F32),
    ]
    for rows, cols in ((T, 256), (96, D), (96, 640)):
        scratch += [
            pltpu.VMEM((2, chips, rows, cols), BF16),
            pltpu.VMEM((chips, rows, cols), BF16),
            pltpu.VMEM((chips, rows, cols), BF16),
            pltpu.VMEM((chips, rows, cols), BF16),
            pltpu.VMEM((NGRP, rows, cols), BF16),
        ]
    scratch += [
        dma((8,)),
        dma((7,)),
        dma((NSEQ,)),
        dma((7,)),
        dma((NSEQ,)),
        dma((7,)),
        dma((NSEQ,)),
        dma((3, 2)),
        dma((NGRP,)),
        dma((3, 2)),
        dma((NGRP,)),
        dma((3, 2)),
        dma((NGRP,)),
        dma((3,)),
        dma((3,)),
        dma((3, 3)),
        dma((3, chips)),
        dma((3, 3, 2)),
        dma((3, NGRP)),
        dma((NSEQ - 1,)),
        dma((NSEQ,)),
    ]
    out_shape = (
        jax.ShapeDtypeStruct((T, D), BF16),
        jax.ShapeDtypeStruct((T, D), BF16),
        jax.ShapeDtypeStruct((96, 3 * D), BF16),
        jax.ShapeDtypeStruct((96, D), BF16),
        jax.ShapeDtypeStruct((96, FF), BF16),
        jax.ShapeDtypeStruct((T, D), BF16),
        jax.ShapeDtypeStruct((8, D), F32),
    )
    output, token_grad, entry_grad, exit_grad, up_grad, down_grad, stats = pl.pallas_call(
        partial(layer_kernel, sizes),
        out_shape=out_shape,
        in_specs=[smem] * 2 + [vmem] * 6 + [anywhere] * 4,
        out_specs=tuple([vmem] * 7),
        scratch_shapes=scratch,
        compiler_params=pltpu.CompilerParams(
            collective_id=0, has_side_effects=True, vmem_limit_bytes=63 * 1024 * 1024
        ),
        name="layer",
    )(
        dilations,
        offsets.reshape(-1),
        tokens,
        cotangent,
        first_gain.reshape(1, D),
        first_bias.reshape(1, D),
        second_gain.reshape(1, D),
        second_bias.reshape(1, D),
        entry_weight,
        exit_weight,
        up_weight,
        down_weight,
    )
    start = lax.axis_index("seq") * (D // NSEQ)
    own = lax.dynamic_slice_in_dim(stats, start, D // NSEQ, 1)
    return (
        output,
        token_grad,
        entry_grad.astype(F32),
        exit_grad.astype(F32),
        up_grad.astype(F32),
        down_grad.astype(F32),
        own[2],
        own[3],
        own[0],
        own[1],
    )


def solution(mesh):
    seq_count = mesh.shape["seq"]
    fast = seq_count == 8 and mesh.shape["grp"] == 4
    return jax.shard_map(
        partial(fast_on_device, seq_count) if fast else on_device,
        mesh=mesh,
        in_specs=(P("seq", None), P("seq", None), P(), P(), P(), P(), P(), P(), P(), P(), P(), P()),
        out_specs=(
            P("seq", None),
            P("seq", None),
            P("seq", None),
            P("seq", None),
            P("seq", None),
            P("seq", None),
            P("seq"),
            P("seq"),
            P("seq"),
            P("seq"),
        ),
        check_vma=False,
    )
```

```python
from functools import partial

import jax
import jax.numpy as jnp
from jax import lax
from jax.experimental import pallas as pl
from jax.experimental.pallas import tpu as pltpu
from jax.sharding import PartitionSpec as P

RATE_MIN = 2
RATE_MAX = 8


EPS = 1e-05
PRECISE = lax.Precision.HIGHEST


def norm_forward(values, gain_vec, bias_vec):
    centered = values - jnp.mean(values, axis=1, keepdims=True)
    inverse = lax.rsqrt(jnp.mean(centered * centered, axis=1, keepdims=True) + EPS)
    plain = centered * inverse
    return (plain * gain_vec + bias_vec, plain, inverse)


def norm_backward(upstream, plain, inverse, gain_vec):
    scaled = upstream * gain_vec
    inner = (
        scaled
        - jnp.mean(scaled, axis=1, keepdims=True)
        - plain * jnp.mean(scaled * plain, axis=1, keepdims=True)
    )
    return (inverse * inner, jnp.sum(upstream * plain, axis=0), jnp.sum(upstream, axis=0))


def key_weights(query_sp, query_pos, key_block, first_row, geometry):
    local_len, capacity, dilation, segment, head_offs, score_scale = geometry
    key_count = key_block.shape[0]
    key_heads = key_block.reshape(key_count, query_sp.shape[1], query_sp.shape[2])
    scores = (
        jnp.einsum("ihd,jhd->hij", query_sp, key_heads, preferred_element_type=jnp.float32)
        * score_scale
    )
    key_index = first_row + jnp.arange(key_count, dtype=jnp.int32)
    source = key_index // capacity
    within = key_index - source * capacity
    key_pos = source[None, :] * local_len + head_offs[:, None] + dilation * within[None, :]
    key_live = within < local_len // dilation
    earlier = key_pos[:, None, :] <= query_pos[:, :, None]
    segment_match = key_pos[:, None, :] // segment == query_pos[:, :, None] // segment
    allowed = earlier & segment_match & key_live[None, None, :]
    return (jnp.where(allowed, jnp.exp(scores), 0.0), key_heads)


def forward_block(running, pieces, first_row, query_sp, query_pos, geometry):
    numerator, denominator = running
    key_block, value_block = pieces
    weights, key_heads = key_weights(query_sp, query_pos, key_block, first_row, geometry)
    value_heads = value_block.reshape(key_heads.shape)
    numerator = numerator + jnp.einsum(
        "hij,jhd->hid",
        weights.astype(jnp.bfloat16),
        value_heads,
        preferred_element_type=jnp.float32,
    )
    return (numerator, denominator + jnp.sum(weights, axis=2))


def blockwise(step_fn, running, pieces, first_row, block_rows):
    total_rows = pieces[0].shape[0]
    if total_rows > block_rows and total_rows % block_rows == 0:
        number = total_rows // block_rows
        stacked_first = pieces[0].reshape(number, block_rows, pieces[0].shape[1])
        stacked_second = pieces[1].reshape(number, block_rows, pieces[1].shape[1])
        block_starts = first_row + block_rows * jnp.arange(number, dtype=jnp.int32)

        def advance(state, items):
            return (step_fn(state, (items[0], items[1]), items[2]), None)

        running, _ = lax.scan(advance, running, (stacked_first, stacked_second, block_starts))
        return running
    return step_fn(running, pieces, first_row)


def backward_block(running, items, query_sp, query_pos, grad_sp, shift_sp, geometry):
    key_block, value_block, first_row = items
    score_scale = geometry[5]
    weights, key_heads = key_weights(query_sp, query_pos, key_block, first_row, geometry)
    key_count = key_block.shape[0]
    value_heads = value_block.reshape(key_heads.shape)
    pressure = jnp.einsum("ihd,jhd->hij", grad_sp, value_heads, preferred_element_type=jnp.float32)
    slopes = (weights * (pressure - shift_sp[:, :, None])).astype(jnp.bfloat16)
    running = (
        running
        + jnp.einsum("hij,jhd->ihd", slopes, key_heads, preferred_element_type=jnp.float32)
        * score_scale
    )
    grad_keys = (
        jnp.einsum("hij,ihd->jhd", slopes, query_sp, preferred_element_type=jnp.float32)
        * score_scale
    )
    grad_values = jnp.einsum(
        "hij,ihd->jhd", weights.astype(jnp.bfloat16), grad_sp, preferred_element_type=jnp.float32
    )
    return (running, (grad_keys.reshape(key_count, -1), grad_values.reshape(key_count, -1)))


def local_weights(query_heads, key_heads, score_scale):
    local_len = query_heads.shape[0]
    scores = (
        jnp.einsum("ihd,jhd->hij", query_heads, key_heads, preferred_element_type=jnp.float32)
        * score_scale
    )
    positions = jnp.arange(local_len, dtype=jnp.int32)
    causal = positions[:, None] >= positions[None, :]
    return jnp.where(causal[None], jnp.exp(scores), 0.0)


def on_device(
    tokens,
    cotangent,
    entry_weight,
    exit_weight,
    up_weight,
    down_weight,
    first_gain,
    first_bias,
    second_gain,
    second_bias,
    dilations,
    offsets,
):
    local_len, width_model = tokens.shape
    head_count = offsets.shape[1]
    head_size = width_model // head_count
    score_scale = head_size ** (-0.5)
    capacity = local_len // RATE_MIN
    group_idx = lax.axis_index("grp")
    seq_index = lax.axis_index("seq")
    seq_count = lax.axis_size("seq")
    dilation = lax.dynamic_index_in_dim(dilations, group_idx, 0, keepdims=False)
    head_offs = lax.dynamic_index_in_dim(offsets, group_idx, 0, keepdims=False)
    segment = local_len * seq_count * dilation // RATE_MAX
    step_ids = jnp.arange(capacity, dtype=jnp.int32)
    row_live = step_ids < local_len // dilation
    local_rows = jnp.minimum(head_offs[:, None] + dilation * step_ids[None, :], local_len - 1)
    query_pos = jnp.where(
        row_live[None, :],
        seq_index * local_len + head_offs[:, None] + dilation * step_ids[None, :],
        -1,
    )
    geometry = (local_len, capacity, dilation, segment, head_offs, score_scale)
    head_shape = (local_len, head_count, head_size)
    selector = local_rows[:, :, None] == jnp.arange(local_len, dtype=jnp.int32)[None, None, :]
    select_low = selector.astype(jnp.bfloat16)
    select_full = selector.astype(jnp.float32)

    def pick(array_in):
        return jnp.einsum(
            "hci,ihd->chd", select_low, array_in, preferred_element_type=jnp.float32
        ).astype(jnp.bfloat16)

    def place_back(sparse_in):
        return jnp.einsum("hci,chd->ihd", select_full, sparse_in, precision=PRECISE)

    inputs = tokens.astype(jnp.float32)
    normed_one, plain_one, inverse_one = norm_forward(inputs, first_gain, first_bias)
    normed_low = normed_one.astype(jnp.bfloat16)
    packed = jnp.dot(normed_low, entry_weight, preferred_element_type=jnp.float32).astype(
        jnp.bfloat16
    )
    query_heads = packed[:, :width_model].reshape(head_shape)
    key_heads = packed[:, width_model : 2 * width_model].reshape(head_shape)
    value_heads = packed[:, 2 * width_model :].reshape(head_shape)
    query_sp = pick(query_heads)
    key_sp = pick(key_heads).reshape(capacity, width_model)
    value_sp = pick(value_heads).reshape(capacity, width_model)
    empty_state = (
        jnp.zeros((head_count, capacity, head_size), jnp.float32),
        jnp.zeros((head_count, capacity), jnp.float32),
    )
    forward_step = partial(forward_block, query_sp=query_sp, query_pos=query_pos, geometry=geometry)
    numerator, denominator = blockwise(
        forward_step,
        empty_state,
        (
            lax.all_gather(key_sp, "seq", axis=0, tiled=True),
            lax.all_gather(value_sp, "seq", axis=0, tiled=True),
        ),
        jnp.int32(0),
        8 * capacity,
    )

    def local_part(query_in, key_in, value_in):
        weights = local_weights(query_in, key_in, score_scale)
        local_num = jnp.einsum(
            "hij,jhd->ihd",
            weights.astype(jnp.bfloat16),
            value_in,
            preferred_element_type=jnp.float32,
        )
        return (local_num, jnp.sum(weights, axis=2).T)

    def local_none(query_in, key_in, value_in):
        return (jnp.zeros(head_shape, jnp.float32), jnp.zeros((local_len, head_count), jnp.float32))

    local_num, local_den = lax.cond(
        group_idx == 0, local_part, local_none, query_heads, key_heads, value_heads
    )
    numerator_full = (
        jnp.einsum("hci,hcd->ihd", select_full, numerator, precision=PRECISE) + local_num
    )
    denominator_full = (
        jnp.einsum("hci,hc->ih", select_full, denominator, precision=PRECISE) + local_den
    )
    merged_num, merged_den = lax.psum(
        (numerator_full.reshape(local_len, width_model), denominator_full), "grp"
    )
    attention = merged_num.reshape(head_shape) / merged_den[:, :, None]
    mixed = attention.reshape(local_len, width_model).astype(jnp.bfloat16)
    middle = inputs + jnp.dot(mixed, exit_weight, preferred_element_type=jnp.float32)
    normed_two, plain_two, inverse_two = norm_forward(middle, second_gain, second_bias)
    normed_two_low = normed_two.astype(jnp.bfloat16)
    hidden = jnp.dot(normed_two_low, up_weight, preferred_element_type=jnp.float32)
    active = jax.nn.gelu(hidden, approximate=False).astype(jnp.bfloat16)
    output = (middle + jnp.dot(active, down_weight, preferred_element_type=jnp.float32)).astype(
        jnp.bfloat16
    )
    down_grad = jnp.dot(active.T, cotangent, preferred_element_type=jnp.float32)
    grad_active = jnp.dot(cotangent, down_weight.T, preferred_element_type=jnp.float32)
    _, gelu_pull = jax.vjp(partial(jax.nn.gelu, approximate=False), hidden)
    grad_hidden = gelu_pull(grad_active)[0].astype(jnp.bfloat16)
    up_grad = jnp.dot(normed_two_low.T, grad_hidden, preferred_element_type=jnp.float32)
    grad_normed_two = jnp.dot(grad_hidden, up_weight.T, preferred_element_type=jnp.float32)
    grad_plain_two, second_gain_grad, second_bias_grad = norm_backward(
        grad_normed_two, plain_two, inverse_two, second_gain
    )
    grad_middle = cotangent.astype(jnp.float32) + grad_plain_two
    grad_branch = grad_middle.astype(jnp.bfloat16)
    exit_grad = jnp.dot(mixed.T, grad_branch, preferred_element_type=jnp.float32)
    grad_mixed_low = lax.optimization_barrier(
        jnp.dot(grad_branch, exit_weight.T, preferred_element_type=jnp.float32).astype(jnp.bfloat16)
    )
    grad_mixed = grad_mixed_low.astype(jnp.float32).reshape(head_shape)
    grad_numer = (grad_mixed / merged_den[:, :, None]).astype(jnp.bfloat16)
    row_shift = jnp.sum(grad_mixed * attention, axis=2) / merged_den
    grad_sp = pick(grad_numer)
    shift_sp = jnp.einsum("hci,ih->hc", select_full, row_shift, precision=PRECISE)
    back_keys, back_values = (
        lax.all_gather(key_sp, "seq", axis=0, tiled=True),
        lax.all_gather(value_sp, "seq", axis=0, tiled=True),
    )
    block_rows = 8 * capacity
    number = back_keys.shape[0] // block_rows
    stacked_keys = back_keys.reshape(number, block_rows, width_model)
    stacked_values = back_values.reshape(number, block_rows, width_model)
    block_starts = block_rows * jnp.arange(number, dtype=jnp.int32)
    empty_query = jnp.zeros((capacity, head_count, head_size), jnp.float32)
    back_step = partial(
        backward_block,
        query_sp=query_sp,
        query_pos=query_pos,
        grad_sp=grad_sp,
        shift_sp=shift_sp,
        geometry=geometry,
    )
    grad_query_sp, (grad_key_all, grad_value_all) = lax.scan(
        back_step, empty_query, (stacked_keys, stacked_values, block_starts)
    )
    own_keys, own_values = (
        lax.psum_scatter(
            grad_key_all.reshape(-1, width_model), "seq", scatter_dimension=0, tiled=True
        ),
        lax.psum_scatter(
            grad_value_all.reshape(-1, width_model), "seq", scatter_dimension=0, tiled=True
        ),
    )

    def local_grads(query_in, key_in, value_in, grad_in, shift_in):
        weights = local_weights(query_in, key_in, score_scale)
        pressure = jnp.einsum("ihd,jhd->hij", grad_in, value_in, preferred_element_type=jnp.float32)
        slopes = (weights * (pressure - shift_in.T[:, :, None])).astype(jnp.bfloat16)
        grad_query = (
            jnp.einsum("hij,jhd->ihd", slopes, key_in, preferred_element_type=jnp.float32)
            * score_scale
        )
        grad_key = (
            jnp.einsum("hij,ihd->jhd", slopes, query_in, preferred_element_type=jnp.float32)
            * score_scale
        )
        grad_value = jnp.einsum(
            "hij,ihd->jhd",
            weights.astype(jnp.bfloat16),
            grad_in,
            preferred_element_type=jnp.float32,
        )
        return (grad_query, grad_key, grad_value)

    def local_skip(query_in, key_in, value_in, grad_in, shift_in):
        zeros_heads = jnp.zeros(head_shape, jnp.float32)
        return (zeros_heads, zeros_heads, zeros_heads)

    local_dq, local_dk, local_dv = lax.cond(
        group_idx == 0,
        local_grads,
        local_skip,
        query_heads,
        key_heads,
        value_heads,
        grad_numer,
        row_shift,
    )
    grad_query_full = place_back(grad_query_sp) + local_dq
    grad_key_full = place_back(own_keys.reshape(capacity, head_count, head_size)) + local_dk
    grad_value_full = place_back(own_values.reshape(capacity, head_count, head_size)) + local_dv
    grad_packed = jnp.concatenate(
        [
            grad_query_full.reshape(local_len, width_model),
            grad_key_full.reshape(local_len, width_model),
            grad_value_full.reshape(local_len, width_model),
        ],
        axis=1,
    )
    summed = lax.psum(grad_packed, "grp").astype(jnp.bfloat16)
    entry_grad = jnp.dot(normed_low.T, summed, preferred_element_type=jnp.float32)
    grad_normed_one = jnp.dot(summed, entry_weight.T, preferred_element_type=jnp.float32)
    grad_plain_one, first_gain_grad, first_bias_grad = norm_backward(
        grad_normed_one, plain_one, inverse_one, first_gain
    )
    token_grad = (grad_middle + grad_plain_one).astype(jnp.bfloat16)
    shards = (
        lax.psum_scatter(entry_grad, "seq", scatter_dimension=0, tiled=True),
        lax.psum_scatter(exit_grad, "seq", scatter_dimension=0, tiled=True),
        lax.psum_scatter(up_grad, "seq", scatter_dimension=0, tiled=True),
        lax.psum_scatter(down_grad, "seq", scatter_dimension=0, tiled=True),
        lax.psum_scatter(first_gain_grad, "seq", scatter_dimension=0, tiled=True),
        lax.psum_scatter(first_bias_grad, "seq", scatter_dimension=0, tiled=True),
        lax.psum_scatter(second_gain_grad, "seq", scatter_dimension=0, tiled=True),
        lax.psum_scatter(second_bias_grad, "seq", scatter_dimension=0, tiled=True),
    )
    return (
        output,
        token_grad,
        shards[0],
        shards[1],
        shards[2],
        shards[3],
        shards[4],
        shards[5],
        shards[6],
        shards[7],
    )


MESH = pl.DeviceIdType.MESH
LANES = 128
LOG2E = 1.4426950408889634
F32 = jnp.float32
BF16 = jnp.bfloat16


def dot_nn(left, right):
    return lax.dot_general(left, right, (((1,), (0,)), ((), ())), preferred_element_type=F32)


def dot_nt(left, right):
    return lax.dot_general(left, right, (((1,), (1,)), ((), ())), preferred_element_type=F32)


def dot_tn(left, right):
    return lax.dot_general(left, right, (((0,), (0,)), ((), ())), preferred_element_type=F32)


def lane_ids(width):
    return lax.broadcasted_iota(jnp.int32, (1, width), 1)


def slot_mask(slot, width=256):
    ids = lane_ids(width)
    return jnp.where((ids >= 64 * slot) & (ids < 64 * slot + 64), 1.0, 0.0).astype(F32)


def join_halves(low_part, high_part):
    return jnp.where(lane_ids(LANES) < 64, low_part, high_part)


def swap_halves(tile):
    return pltpu.roll(tile, 64, axis=1)


def layer_kernel(
    sizes,
    dil_ref,
    off_ref,
    tok_ref,
    cot_ref,
    gain1_ref,
    bias1_ref,
    gain2_ref,
    bias2_ref,
    entry_hbm,
    exit_hbm,
    up_hbm,
    down_hbm,
    out_ref,
    tgrad_ref,
    oentry_ref,
    oexit_ref,
    oup_ref,
    odown_ref,
    ostat_ref,
    win,
    exit_all,
    exit_win,
    up_all,
    down_all,
    n1,
    n2,
    plain2,
    inv2,
    middle,
    gmid,
    gbranch,
    mixed,
    active,
    ghid,
    gn2,
    member,
    masks,
    kv,
    qb,
    dob,
    qmask,
    shift,
    invden,
    att,
    acc_a,
    acc_b,
    acc_c,
    zmix,
    zdq,
    zdkv,
    stat,
    pc_down,
    r1_down,
    y_down,
    r2_down,
    ag_down,
    pc_up,
    r1_up,
    y_up,
    r2_up,
    ag_up,
    pc_entry,
    r1_entry,
    y_entry,
    r2_entry,
    ag_entry,
    load_sem,
    kv_ssem,
    kv_rsem,
    q_ssem,
    q_rsem,
    do_ssem,
    do_rsem,
    zm_ssem,
    zm_rsem,
    zq_ssem,
    zq_rsem,
    zk_ssem,
    zk_rsem,
    rs_s1,
    rs_r1,
    rs_s2,
    rs_r2,
    rs_zs,
    rs_zr,
    st_ssem,
    st_rsem,
):
    T, D, HEADS, E, FF, NSEQ, NGRP = sizes
    scale = E ** (-0.5)
    exp_scale = scale * LOG2E
    s = lax.axis_index("seq")
    g = lax.axis_index("grp")
    chip = s // 2
    core = s % 2
    sib = s + 1 - 2 * core
    odd = g % 2
    chips = NSEQ // 2
    part = D // NGRP
    is_odd = odd == 1
    gain1 = gain1_ref[...].reshape(1, D)
    bias1 = bias1_ref[...].reshape(1, D)
    gain2 = gain2_ref[...].reshape(1, D)
    bias2 = bias2_ref[...].reshape(1, D)

    def to_seq(peer, src, dst, ssem, rsem):
        return pltpu.make_async_remote_copy(
            src_ref=src,
            dst_ref=dst,
            send_sem=ssem,
            recv_sem=rsem,
            device_id={"seq": peer},
            device_id_type=MESH,
        )

    def to_grp(peer, src, dst, ssem, rsem):
        return pltpu.make_async_remote_copy(
            src_ref=src,
            dst_ref=dst,
            send_sem=ssem,
            recv_sem=rsem,
            device_id={"grp": peer},
            device_id_type=MESH,
        )

    loads = []
    for t in range(3):
        first = pl.multiple_of(t * D + part * g - 64 * odd, LANES)
        loads.append(
            pltpu.make_async_copy(entry_hbm.at[:, pl.ds(first, 256)], win.at[t], load_sem.at[t])
        )
    loads.append(pltpu.make_async_copy(down_hbm, down_all, load_sem.at[3]))
    loads.append(pltpu.make_async_copy(exit_hbm, exit_all, load_sem.at[4]))
    loads.append(
        pltpu.make_async_copy(
            exit_hbm.at[pl.ds(pl.multiple_of(part * g, 64), part), :],
            exit_win.at[pl.ds(64, part), :],
            load_sem.at[5],
        )
    )
    loads.append(pltpu.make_async_copy(up_hbm, up_all, load_sem.at[6]))
    for load in loads:
        load.start()
    entry_all = up_all.at[:, 0 : 3 * D]
    late_load = pltpu.make_async_copy(entry_hbm, entry_all, load_sem.at[7])

    barrier = pltpu.get_barrier_semaphore()
    for step in range(1, NSEQ):
        pl.semaphore_signal(
            barrier, inc=1, device_id={"seq": lax.rem(s + step, NSEQ)}, device_id_type=MESH
        )
    for step in range(1, NGRP):
        pl.semaphore_signal(
            barrier, inc=1, device_id={"grp": lax.rem(g + step, NGRP)}, device_id_type=MESH
        )

    rows = 96

    def norm_one(i, carry):
        at = pl.ds(pl.multiple_of(i * rows, rows), rows)
        value = tok_ref[at, :].astype(F32)
        centered = value - jnp.mean(value, axis=1, keepdims=True)
        inverse = lax.rsqrt(jnp.mean(centered * centered, axis=1, keepdims=True) + EPS)
        n1[at, :] = (centered * inverse * gain1 + bias1).astype(BF16)
        return carry

    lax.fori_loop(0, T // rows, norm_one, 0)
    exit_win[0:64, :] = jnp.zeros((64, D), BF16)

    for t in range(3):
        loads[t].wait()
    lane256 = lane_ids(256)
    q_raw = dot_nn(n1[...], win[0])
    k_raw = dot_nn(n1[...], win[1])
    v_raw = dot_nn(n1[...], win[2])
    q_own = jnp.where(is_odd, pltpu.roll(q_raw, 192, axis=1), q_raw)
    k_own = jnp.where(is_odd, pltpu.roll(k_raw, 192, axis=1), k_raw)
    v_own = jnp.where(is_odd, v_raw, pltpu.roll(v_raw, 64, axis=1))
    q_own = jnp.where(lane256 < 192, q_own, 0.0)
    qb[s] = q_own.astype(BF16)
    for h in range(3):
        qmask[h] = (q_own * slot_mask(h)).astype(BF16)
    kv[s, :, 0:128] = k_own[:, 0:128].astype(BF16)
    kv[s, :, 128:256] = join_halves(k_own[:, 128:256], v_own[:, 0:128]).astype(BF16)
    kv[s, :, 256:384] = v_own[:, 128:256].astype(BF16)

    pl.semaphore_wait(barrier, NSEQ - 1 + NGRP - 1)

    sends = []

    def start_when(cond, copy):
        @pl.when(cond)
        def _():
            copy.start()

        sends.append((cond, copy))

    for d in range(1, chips):
        up_to = lax.rem(s + 2 * d, NSEQ)
        start_when(
            chip + d < chips,
            to_seq(up_to, kv.at[s], kv.at[s], kv_ssem.at[d - 1], kv_rsem.at[s]),
        )
    start_when(core == 0, to_seq(sib, kv.at[s], kv.at[s], kv_ssem.at[3], kv_rsem.at[s]))
    for d in range(1, chips):
        down_to = lax.rem(s - 2 * d + NSEQ, NSEQ)
        start_when(
            chip - d >= 0,
            to_seq(down_to, qb.at[s], qb.at[s], q_ssem.at[d - 1], q_rsem.at[s]),
        )
    start_when(core == 1, to_seq(sib, qb.at[s], qb.at[s], q_ssem.at[3], q_rsem.at[s]))

    lane128 = lane_ids(LANES)
    rate_row = jnp.ones((1, LANES), F32)
    for i in range(NGRP):
        rate_row = jnp.where(lane128 == i, dil_ref[i].astype(F32), rate_row)
    local_pos = lax.broadcasted_iota(jnp.int32, (T, 1), 0).astype(F32)
    residue = local_pos - rate_row * jnp.floor((local_pos + 0.5) / rate_row)
    for h in range(3):
        off_row = jnp.full((1, LANES), -1.0, F32)
        for i in range(NGRP):
            off_row = jnp.where(
                lane128 == i, off_ref[i, 3 * g + h].astype(F32), off_row
            )
        member[h] = jnp.where(residue == off_row, 1.0, 0.0).astype(BF16)
    per_segment = rate_row * (T * NSEQ // RATE_MAX)

    def segment_of(block):
        return jnp.floor((jnp.full((1, LANES), block * T, jnp.int32).astype(F32) + 0.5) / per_segment)

    own_segment = segment_of(s)

    def build_mask(i, carry):
        b = i // 3
        h = i - 3 * b
        same = jnp.where(segment_of(b) == own_segment, 1.0, 0.0)
        count = dot_nt((member[h].astype(F32) * same).astype(BF16), member[h])
        masks[b, h] = count.astype(BF16)

        @pl.when(b == s)
        def _():
            row_id = lax.broadcasted_iota(jnp.int32, (T, T), 0)
            col_id = lax.broadcasted_iota(jnp.int32, (T, T), 1)
            masks[b, h] = jnp.where(col_id <= row_id, count + 1.0, 0.0).astype(BF16)
            masks[NSEQ, h] = jnp.where(row_id <= col_id, count + 1.0, 0.0).astype(BF16)

        return carry

    lax.fori_loop(0, 3 * NSEQ, build_mask, 0)

    loads[3].wait()

    def cot_times_down(i, carry):
        at = pl.ds(pl.multiple_of(i * T, T), T)
        ghid[:, at] = dot_nt(cot_ref[...], down_all[at, :]).astype(BF16)
        return carry

    lax.fori_loop(0, FF // T, cot_times_down, 0)

    acc_a[...] = jnp.zeros_like(acc_a)
    den = shift
    den[...] = jnp.zeros_like(den)

    def forward_step(j, carry):
        jj = j - 1 - core
        d = jj // 2 + 1
        which = jj % 2
        far = jnp.where(which == 0, s - 2 * d, sib - 2 * d)
        b = jnp.where(j == 0, s, jnp.where(jj < 0, s - 1, far))

        @pl.when(j > 0)
        def _():
            to_seq(sib, kv.at[b], kv.at[b], kv_ssem.at[0], kv_rsem.at[b]).wait_recv()

        @pl.when((jj >= 0) & (which == 0))
        def _():
            to_seq(sib, kv.at[b], kv.at[b], kv_ssem.at[3 + d], kv_rsem.at[b]).start()

        for h in range(3):
            score = dot_nt(qmask[h], kv[b, :, 0:256])
            weight = jnp.exp2(score * exp_scale) * masks[b, h].astype(F32)
            den[h] += weight[:, 0:128] + weight[:, 128:256] + weight[:, 256:384]
            low_weight = weight.astype(BF16)
            masks[b, h] = low_weight
            acc_a[...] += dot_nn(low_weight, kv[b, :, 128:384]) * slot_mask(h + 1)
        return carry

    lax.fori_loop(0, s + 1, forward_step, 0)

    inv_all = jnp.zeros((T, 256), F32)
    for h in range(3):
        inv_all = jnp.where(
            slot_mask(h + 1) > 0.5, 1.0 / jnp.sum(den[h], axis=1, keepdims=True), inv_all
        )
    invden[...] = inv_all
    att_own = acc_a[...] * inv_all
    att[...] = att_own

    def pack(target, tile_low, tile_high):
        target[0:T, :] = tile_high.astype(BF16)
        half = T // 2
        target[T : T + half, :] = join_halves(
            swap_halves(tile_low[half:T]), tile_low[0:half]
        ).astype(BF16)

    def unpack_pair(first, second, place):
        half = T // 2
        a_high = first[0:T, :].astype(F32)
        a_rest = first[T : T + half, :].astype(F32)
        b_high = second[0:T, :].astype(F32)
        b_rest = second[T : T + half, :].astype(F32)
        place(2, slice(0, T), b_high)
        swapped = swap_halves(a_high)
        place(0, slice(0, half), join_halves(swap_halves(a_rest), swapped[0:half]))
        place(0, slice(half, T), join_halves(a_rest, swapped[half:T]))
        place(1, slice(0, half), join_halves(swapped[0:half], b_rest))
        place(1, slice(half, T), join_halves(swapped[half:T], swap_halves(b_rest)))

    def chain_start(at, ssem, rsem):
        start_when(g + 1 < NGRP, to_grp(lax.rem(g + 1, NGRP), at(g), at(g), ssem.at[0, 0], rsem.at[g]))
        start_when(
            g >= 1, to_grp(lax.rem(g + NGRP - 1, NGRP), at(g), at(g), ssem.at[0, 1], rsem.at[g])
        )

    def chain_step(d, at, ssem, rsem):
        right = lax.rem(g + 1, NGRP)
        left = lax.rem(g + NGRP - 1, NGRP)
        lower = lax.rem(g - d + NGRP, NGRP)
        upper = lax.rem(g + d, NGRP)

        @pl.when(g - d >= 0)
        def _():
            to_grp(right, at(lower), at(lower), ssem.at[0, 0], rsem.at[lower]).wait_recv()

        if d < NGRP - 1:
            start_when(
                (g - d >= 0) & (g + 1 < NGRP),
                to_grp(right, at(lower), at(lower), ssem.at[d, 0], rsem.at[lower]),
            )

        @pl.when(g + d < NGRP)
        def _():
            to_grp(left, at(upper), at(upper), ssem.at[0, 1], rsem.at[upper]).wait_recv()

        if d < NGRP - 1:
            start_when(
                (g + d < NGRP) & (g >= 1),
                to_grp(left, at(upper), at(upper), ssem.at[d, 1], rsem.at[upper]),
            )

    pack(zmix.at[g], att_own[:, 0:128], att_own[:, 128:256])
    chain_start(lambda i: zmix.at[i], zm_ssem, zm_rsem)

    for d in range(1, chips):
        slot = lax.rem(s + 2 * d, NSEQ)

        @pl.when(chip + d < chips)
        def _():
            to_seq(sib, qb.at[slot], qb.at[slot], q_ssem.at[0], q_rsem.at[slot]).wait_recv()

        start_when(
            chip + d < chips,
            to_seq(sib, qb.at[slot], qb.at[slot], q_ssem.at[3 + d], q_rsem.at[slot]),
        )

    for d in range(1, NGRP):
        chain_step(d, lambda i: zmix.at[i], zm_ssem, zm_rsem)

    def place_mixed(pair):
        def place(tile, at, value):
            first = pair * 2 * part + tile * LANES
            mixed[at, first : first + LANES] = value.astype(BF16)

        return place

    for pair in range(NGRP // 2):
        unpack_pair(zmix.at[2 * pair], zmix.at[2 * pair + 1], place_mixed(pair))

    loads[4].wait()
    middle[...] = tok_ref[...].astype(F32) + dot_nn(mixed[...], exit_all[...])

    def norm_two(i, carry):
        at = pl.ds(pl.multiple_of(i * rows, rows), rows)
        value = middle[at, :]
        centered = value - jnp.mean(value, axis=1, keepdims=True)
        inverse = lax.rsqrt(jnp.mean(centered * centered, axis=1, keepdims=True) + EPS)
        plain = centered * inverse
        plain2[at, :] = plain
        inv2[at, :] = jnp.broadcast_to(inverse, (rows, LANES))
        n2[at, :] = (plain * gain2 + bias2).astype(BF16)
        return carry

    lax.fori_loop(0, T // rows, norm_two, 0)

    loads[6].wait()
    gn2[...] = jnp.zeros_like(gn2)

    def feed_forward(i, carry):
        at = pl.ds(pl.multiple_of(i * T, T), T)
        hidden = dot_nn(n2[...], up_all[:, at])
        cdf = 0.5 + 0.5 * lax.erf(hidden * (0.5**0.5))
        active[:, at] = (hidden * cdf).astype(BF16)
        density = jnp.exp2(hidden * hidden * (-0.5 * LOG2E)) * 0.3989422804014327
        low_grad = (ghid[:, at].astype(F32) * (cdf + hidden * density)).astype(BF16)
        ghid[:, at] = low_grad
        gn2[...] += dot_nt(low_grad, up_all[:, at])
        return carry

    lax.fori_loop(0, FF // T, feed_forward, 0)
    late_load.start()

    stat[s] = jnp.zeros((8, D), F32)

    def norm_two_back(i, carry):
        at = pl.ds(pl.multiple_of(i * rows, rows), rows)
        upstream = gn2[at, :]
        plain = plain2[at, :]
        scaled = upstream * gain2
        inner = (
            scaled
            - jnp.mean(scaled, axis=1, keepdims=True)
            - plain * jnp.mean(scaled * plain, axis=1, keepdims=True)
        )
        grad = cot_ref[at, :].astype(F32) + inv2[at, 0:1] * inner
        gmid[at, :] = grad
        gbranch[at, :] = grad.astype(BF16)
        stat[s, 0:1, :] += jnp.sum(upstream * plain, axis=0, keepdims=True)
        stat[s, 1:2, :] += jnp.sum(upstream, axis=0, keepdims=True)
        return carry

    lax.fori_loop(0, T // rows, norm_two_back, 0)

    loads[5].wait()
    gmix = dot_nt(gbranch[...], exit_win[...]).astype(BF16).astype(F32)
    numer_grad = gmix * invden[...]
    product = numer_grad * att[...]
    for h in range(3):
        value = jnp.sum(product * slot_mask(h + 1), axis=1, keepdims=True)
        shift[h] = jnp.broadcast_to(value, (T, LANES))
        high = value.astype(BF16).astype(F32)
        low = value - high
        numer_grad = jnp.where(lane256 == 2 * h, high, numer_grad)
        numer_grad = jnp.where(lane256 == 2 * h + 1, low, numer_grad)
    dob[s] = numer_grad.astype(BF16)

    for d in range(1, chips):
        down_to = lax.rem(s - 2 * d + NSEQ, NSEQ)
        start_when(
            chip - d >= 0,
            to_seq(down_to, dob.at[s], dob.at[s], do_ssem.at[d - 1], do_rsem.at[s]),
        )
    start_when(core == 1, to_seq(sib, dob.at[s], dob.at[s], do_ssem.at[3], do_rsem.at[s]))

    width = part + 64
    up_grad = dot_tn(n2[...], ghid[:, pl.ds(pl.multiple_of(g * D, LANES), D)])
    for t in range(NSEQ):
        pc_up[t % 2, t // 2] = up_grad[96 * t : 96 * t + 96, :].astype(BF16)

    @pl.when(g < 3)
    def _():
        cols = pl.ds(pl.multiple_of(lax.rem(g, 3) * width, LANES), width)

        def down_piece(t, carry):
            at = pl.ds(pl.multiple_of(t * T, T), T)
            pc_down[t % 2, t // 2] = dot_tn(active[:, at], cot_ref[:, cols]).astype(BF16)
            return carry

        lax.fori_loop(0, NSEQ, down_piece, 0)

    @pl.when(g == 3)
    def _():
        exit_grad = dot_tn(mixed[...], gbranch[...]).astype(BF16)
        for t in range(NSEQ):
            for i in range(3):
                pc_down[t % 2, t // 2, 96 * i : 96 * i + 96, :] = exit_grad[
                    96 * t : 96 * t + 96, width * i : width * i + width
                ]
            pc_down[t % 2, t // 2, 288:384, :] = jnp.zeros((96, width), BF16)

    def reduce_start(i, pieces, first_in):
        start_when(
            core >= 0,
            to_seq(sib, pieces.at[1 - core], first_in, rs_s1.at[i], rs_r1.at[i]),
        )

    def reduce_pass(i, pieces, first_in, total, second_in):
        to_seq(sib, pieces.at[core], first_in, rs_s1.at[i], rs_r1.at[i]).wait_recv()
        for cc in range(chips):
            total[cc] = (pieces[core, cc].astype(F32) + first_in[cc].astype(F32)).astype(BF16)
        for d in range(1, chips):
            to_chip = lax.rem(chip + d, chips)
            start_when(
                core >= 0,
                to_seq(
                    2 * to_chip + core,
                    total.at[to_chip],
                    second_in.at[chip],
                    rs_s2.at[i, d - 1],
                    rs_r2.at[i, chip],
                ),
            )

    def reduce_end(i, total, second_in, gathered):
        result = total[chip].astype(F32)
        for d in range(1, chips):
            slot = lax.rem(chip + d, chips)
            to_seq(
                sib, second_in.at[slot], second_in.at[slot], rs_s1.at[i], rs_r2.at[i, slot]
            ).wait_recv()
            result = result + second_in[slot].astype(F32)
        gathered[g] = result.astype(BF16)
        chain_start(lambda j: gathered.at[j], rs_zs.at[i], rs_zr.at[i])

    reduce_start(0, pc_up, r1_up)
    reduce_start(1, pc_down, r1_down)

    for h in range(3):
        qmask[h] = (dob[s].astype(F32) * slot_mask(h + 1)).astype(BF16)
    acc_a[...] = jnp.zeros_like(acc_a)

    def query_side(b, carry):
        for h in range(3):
            pressure = dot_nt(qmask[h], kv[b, :, 128:384])
            row_shift = shift[h]
            row_shift = jnp.concatenate([row_shift, row_shift, row_shift], axis=1)
            slope = (masks[b, h].astype(F32) * (pressure - row_shift)).astype(BF16)
            acc_a[...] += dot_nn(slope, kv[b, :, 0:256]) * slot_mask(h)
        return carry

    lax.fori_loop(0, s + 1, query_side, 0)
    dq = pltpu.roll(acc_a[...] * scale, 64, axis=1)
    pack(zdq.at[g], dq[:, 0:128], dq[:, 128:256])
    chain_start(lambda i: zdq.at[i], zq_ssem, zq_rsem)

    reduce_pass(0, pc_up, r1_up, y_up, r2_up)
    reduce_pass(1, pc_down, r1_down, y_down, r2_down)

    acc_b[...] = jnp.zeros_like(acc_b)
    acc_c[...] = jnp.zeros_like(acc_c)
    v_tile = kv[s, :, 128:384].astype(F32)
    k_tile = kv[s, :, 0:256].astype(F32)
    for h in range(3):
        qmask[h] = (k_tile * slot_mask(h)).astype(BF16)
        minus = jnp.where((lane256 == 2 * h) | (lane256 == 2 * h + 1), -1.0, 0.0)
        qmask[3 + h] = (v_tile * slot_mask(h + 1) + minus).astype(BF16)

    def key_side(j, carry):
        jj = j - 2 + core
        d = jj // 2 + 1
        which = jj % 2
        far = jnp.where(which == 0, s + 2 * d, sib + 2 * d)
        b = jnp.where(j == 0, s, jnp.where(jj < 0, s + 1, far))

        @pl.when(j > 0)
        def _():
            to_seq(sib, dob.at[b], dob.at[b], do_ssem.at[0], do_rsem.at[b]).wait_recv()

        @pl.when((jj >= 0) & (which == 0))
        def _():
            to_seq(sib, dob.at[b], dob.at[b], do_ssem.at[3 + d], do_rsem.at[b]).start()

        @pl.when((j > 0) & ((jj < 0) | (which == 1)))
        def _():
            to_seq(sib, qb.at[b], qb.at[b], q_ssem.at[0], q_rsem.at[b]).wait_recv()

        at = jnp.where(j == 0, NSEQ, b)
        for h in range(3):
            score = dot_nt(qmask[h], qb[b])
            weight = jnp.exp2(score * exp_scale) * masks[at, h].astype(F32)
            pressure = dot_nt(qmask[3 + h], dob[b])
            slope = (weight * pressure).astype(BF16)
            acc_b[...] += dot_nn(slope, qb[b]) * slot_mask(h)
            acc_c[...] += dot_nn(weight.astype(BF16), dob[b]) * slot_mask(h + 1)
        return carry

    lax.fori_loop(0, NSEQ - s, key_side, 0)

    dk = pltpu.roll(acc_b[...] * scale, 64, axis=1)
    pack(zdkv.at[g, 0], dk[:, 0:128], dk[:, 128:256])
    dv = acc_c[...]
    pack(zdkv.at[g, 1], dv[:, 0:128], dv[:, 128:256])
    chain_start(lambda i: zdkv.at[i], zk_ssem, zk_rsem)

    dfull = ghid.at[:, 0 : 3 * D]
    dpack = ghid.at[:, 3 * D : 3 * D + 640]
    dpack[:, 0:128] = join_halves(swap_halves(dq[:, 0:128]), swap_halves(dq[:, 128:256])).astype(BF16)
    dpack[:, 128:256] = join_halves(swap_halves(dq[:, 128:256]), dk[:, 0:128]).astype(BF16)
    dpack[:, 256:384] = dk[:, 128:256].astype(BF16)
    dpack[:, 384:512] = join_halves(swap_halves(dv[:, 0:128]), swap_halves(dv[:, 128:256])).astype(BF16)
    dpack[:, 512:640] = join_halves(swap_halves(dv[:, 128:256]), jnp.zeros((T, LANES), F32)).astype(BF16)
    entry_grad = dot_tn(n1[...], dpack[...])
    for t in range(NSEQ):
        pc_entry[t % 2, t // 2] = entry_grad[96 * t : 96 * t + 96, :].astype(BF16)
    reduce_start(2, pc_entry, r1_entry)

    reduce_end(0, y_up, r2_up, ag_up)
    reduce_end(1, y_down, r2_down, ag_down)
    for d in range(1, NGRP):
        chain_step(d, lambda i: zdq.at[i], zq_ssem, zq_rsem)
    reduce_pass(2, pc_entry, r1_entry, y_entry, r2_entry)
    for d in range(1, NGRP):
        chain_step(d, lambda i: zdkv.at[i], zk_ssem, zk_rsem)

    def place_grad(first_col):
        def place(tile, at, value):
            first = first_col + tile * LANES
            dfull[at, first : first + LANES] = value.astype(BF16)

        return place

    for pair in range(NGRP // 2):
        first_col = pair * 2 * part
        unpack_pair(zdq.at[2 * pair], zdq.at[2 * pair + 1], place_grad(first_col))
        for t in range(2):
            unpack_pair(
                zdkv.at[2 * pair, t], zdkv.at[2 * pair + 1, t], place_grad((t + 1) * D + first_col)
            )

    out_ref[...] = (middle[...] + dot_nn(active[...], down_all[...])).astype(BF16)
    reduce_end(2, y_entry, r2_entry, ag_entry)
    late_load.wait()
    gn2[...] = dot_nt(dfull[...], up_all[:, 0 : 3 * D])

    def norm_one_back(i, carry):
        at = pl.ds(pl.multiple_of(i * rows, rows), rows)
        value = tok_ref[at, :].astype(F32)
        centered = value - jnp.mean(value, axis=1, keepdims=True)
        inverse = lax.rsqrt(jnp.mean(centered * centered, axis=1, keepdims=True) + EPS)
        plain = centered * inverse
        upstream = gn2[at, :]
        scaled = upstream * gain1
        inner = (
            scaled
            - jnp.mean(scaled, axis=1, keepdims=True)
            - plain * jnp.mean(scaled * plain, axis=1, keepdims=True)
        )
        tgrad_ref[at, :] = (gmid[at, :] + inverse * inner).astype(BF16)
        stat[s, 2:3, :] += jnp.sum(upstream * plain, axis=0, keepdims=True)
        stat[s, 3:4, :] += jnp.sum(upstream, axis=0, keepdims=True)
        return carry

    lax.fori_loop(0, T // rows, norm_one_back, 0)
    for step in range(1, NSEQ):
        peer = lax.rem(s + step, NSEQ)
        start_when(
            core >= 0, to_seq(peer, stat.at[s], stat.at[s], st_ssem.at[step - 1], st_rsem.at[s])
        )

    for d in range(1, NGRP):
        chain_step(d, lambda i: ag_up.at[i], rs_zs.at[0], rs_zr.at[0])
    for i in range(NGRP):
        oup_ref[:, D * i : D * i + D] = ag_up[i]
    for d in range(1, NGRP):
        chain_step(d, lambda i: ag_down.at[i], rs_zs.at[1], rs_zr.at[1])
    for i in range(3):
        odown_ref[:, width * i : width * i + width] = ag_down[i]
        oexit_ref[:, width * i : width * i + width] = ag_down[3, 96 * i : 96 * i + 96, :]
    for d in range(1, NGRP):
        chain_step(d, lambda i: ag_entry.at[i], rs_zs.at[2], rs_zr.at[2])
    for pair in range(NGRP // 2):
        a = ag_entry[2 * pair].astype(F32)
        b = ag_entry[2 * pair + 1].astype(F32)
        first = pair * 2 * part
        tiles = (
            (0, a[:, 0:128]),
            (1, join_halves(a[:, 128:256], swap_halves(b[:, 0:128]))),
            (2, join_halves(swap_halves(b[:, 0:128]), swap_halves(b[:, 128:256]))),
            (6, join_halves(swap_halves(a[:, 128:256]), swap_halves(a[:, 256:384]))),
            (7, join_halves(swap_halves(a[:, 256:384]), b[:, 128:256])),
            (8, b[:, 256:384]),
            (12, a[:, 384:512]),
            (13, join_halves(a[:, 512:640], swap_halves(b[:, 384:512]))),
            (14, join_halves(swap_halves(b[:, 384:512]), swap_halves(b[:, 512:640]))),
        )
        for tile, value in tiles:
            at = tile * LANES + first
            oentry_ref[:, at : at + LANES] = value.astype(BF16)

    for step in range(1, NSEQ):
        slot = lax.rem(s + step, NSEQ)
        to_seq(sib, stat.at[slot], stat.at[slot], st_ssem.at[0], st_rsem.at[slot]).wait_recv()
    total_stat = stat[0]
    for i in range(1, NSEQ):
        total_stat = total_stat + stat[i]
    ostat_ref[...] = total_stat

    for cond, copy in sends:

        @pl.when(cond)
        def _(copy=copy):
            copy.wait_send()

    for d in range(1, chips):

        @pl.when(chip - d >= 0)
        def _(d=d):
            slot = lax.rem(s - 2 * d + NSEQ, NSEQ)
            to_seq(sib, kv.at[slot], kv.at[slot], kv_ssem.at[3 + d], kv_rsem.at[slot]).wait_send()

        @pl.when(chip + d < chips)
        def _(d=d):
            slot = lax.rem(s + 2 * d, NSEQ)
            to_seq(sib, dob.at[slot], dob.at[slot], do_ssem.at[3 + d], do_rsem.at[slot]).wait_send()


def finish_kernel(
    out_in,
    tgrad_in,
    entry_in,
    exit_in,
    up_in,
    down_in,
    stat_in,
    out_hbm,
    tgrad_hbm,
    entry_hbm,
    exit_hbm,
    up_hbm,
    down_hbm,
    fgain_ref,
    fbias_ref,
    sgain_ref,
    sbias_ref,
    out_low,
    tgrad_low,
    down_low,
    up_low,
    entry_low,
    exit_low,
    stat_low,
    down_full,
    up_full,
    entry_full,
    exit_full,
    sems,
):
    plans = (
        (down_in, down_low, down_full, down_hbm),
        (up_in, up_low, up_full, up_hbm),
        (entry_in, entry_low, entry_full, entry_hbm),
        (exit_in, exit_low, exit_full, exit_hbm),
        (out_in, out_low, out_low, out_hbm),
        (tgrad_in, tgrad_low, tgrad_low, tgrad_hbm),
    )
    loads = [
        pltpu.make_async_copy(source, low, sems.at[6 + i])
        for i, (source, low, _, _) in enumerate(plans)
    ]
    stat_load = pltpu.make_async_copy(stat_in, stat_low, sems.at[12])
    for copy in [*loads, stat_load]:
        copy.start()
    copies = []
    for i, (_, low, full, target) in enumerate(plans):
        loads[i].wait()
        if full is not low:
            full[...] = low[...].astype(F32)
        copy = pltpu.make_async_copy(full, target, sems.at[i])
        copy.start()
        copies.append(copy)
    stat_load.wait()
    width = stat_low.shape[1]
    part = fgain_ref.shape[0]
    first = lax.axis_index("seq") * part
    turned = pltpu.roll(stat_low[...], lax.rem(width - first, width), axis=1)
    fgain_ref[...] = turned[2:3, 0:part].reshape(part)
    fbias_ref[...] = turned[3:4, 0:part].reshape(part)
    sgain_ref[...] = turned[0:1, 0:part].reshape(part)
    sbias_ref[...] = turned[1:2, 0:part].reshape(part)
    for copy in copies:
        copy.wait()


def fast_on_device(
    seq_count,
    tokens,
    cotangent,
    entry_weight,
    exit_weight,
    up_weight,
    down_weight,
    first_gain,
    first_bias,
    second_gain,
    second_bias,
    dilations,
    offsets,
):
    T, D = tokens.shape
    NGRP, HEADS = offsets.shape
    FF = up_weight.shape[1]
    E = D // HEADS
    NSEQ = seq_count
    chips = NSEQ // 2
    sizes = (T, D, HEADS, E, FF, NSEQ, NGRP)
    share = T * 3 // 2
    vmem = pl.BlockSpec(memory_space=pltpu.VMEM)
    smem = pl.BlockSpec(memory_space=pltpu.SMEM)
    anywhere = pl.BlockSpec(memory_space=pl.ANY)
    dma = pltpu.SemaphoreType.DMA
    scratch = [
        pltpu.VMEM((3, D, 256), BF16),
        pltpu.VMEM((D, D), BF16),
        pltpu.VMEM((256, D), BF16),
        pltpu.VMEM((D, FF), BF16),
        pltpu.VMEM((FF, D), BF16),
        pltpu.VMEM((T, D), BF16),
        pltpu.VMEM((T, D), BF16),
        pltpu.VMEM((T, D), F32),
        pltpu.VMEM((T, LANES), F32),
        pltpu.VMEM((T, D), F32),
        pltpu.VMEM((T, D), F32),
        pltpu.VMEM((T, D), BF16),
        pltpu.VMEM((T, D), BF16),
        pltpu.VMEM((T, FF), BF16),
        pltpu.VMEM((T, FF), BF16),
        pltpu.VMEM((T, D), F32),
        pltpu.VMEM((3, T, LANES), BF16),
        pltpu.VMEM((NSEQ + 1, 3, T, T), BF16),
        pltpu.VMEM((NSEQ, T, 384), BF16),
        pltpu.VMEM((NSEQ, T, 256), BF16),
        pltpu.VMEM((NSEQ, T, 256), BF16),
        pltpu.VMEM((6, T, 256), BF16),
        pltpu.VMEM((3, T, LANES), F32),
        pltpu.VMEM((T, 256), F32),
        pltpu.VMEM((T, 256), F32),
        pltpu.VMEM((T, 256), F32),
        pltpu.VMEM((T, 256), F32),
        pltpu.VMEM((T, 256), F32),
        pltpu.VMEM((NGRP, share, LANES), BF16),
        pltpu.VMEM((NGRP, share, LANES), BF16),
        pltpu.VMEM((NGRP, 2, share, LANES), BF16),
        pltpu.VMEM((NSEQ, 8, D), F32),
    ]
    for rows, cols in ((T, 256), (96, D), (96, 640)):
        scratch += [
            pltpu.VMEM((2, chips, rows, cols), BF16),
            pltpu.VMEM((chips, rows, cols), BF16),
            pltpu.VMEM((chips, rows, cols), BF16),
            pltpu.VMEM((chips, rows, cols), BF16),
            pltpu.VMEM((NGRP, rows, cols), BF16),
        ]
    scratch += [
        dma((8,)),
        dma((7,)),
        dma((NSEQ,)),
        dma((7,)),
        dma((NSEQ,)),
        dma((7,)),
        dma((NSEQ,)),
        dma((3, 2)),
        dma((NGRP,)),
        dma((3, 2)),
        dma((NGRP,)),
        dma((3, 2)),
        dma((NGRP,)),
        dma((3,)),
        dma((3,)),
        dma((3, 3)),
        dma((3, chips)),
        dma((3, 3, 2)),
        dma((3, NGRP)),
        dma((NSEQ - 1,)),
        dma((NSEQ,)),
    ]
    out_shape = (
        jax.ShapeDtypeStruct((T, D), BF16),
        jax.ShapeDtypeStruct((T, D), BF16),
        jax.ShapeDtypeStruct((96, 3 * D), BF16),
        jax.ShapeDtypeStruct((96, D), BF16),
        jax.ShapeDtypeStruct((96, FF), BF16),
        jax.ShapeDtypeStruct((T, D), BF16),
        jax.ShapeDtypeStruct((8, D), F32),
    )
    output, token_grad, entry_grad, exit_grad, up_grad, down_grad, stats = pl.pallas_call(
        partial(layer_kernel, sizes),
        out_shape=out_shape,
        in_specs=[smem] * 2 + [vmem] * 6 + [anywhere] * 4,
        out_specs=tuple([vmem] * 7),
        scratch_shapes=scratch,
        compiler_params=pltpu.CompilerParams(
            collective_id=0, has_side_effects=True, vmem_limit_bytes=63 * 1024 * 1024
        ),
        name="layer",
    )(
        dilations,
        offsets,
        tokens,
        cotangent,
        first_gain,
        first_bias,
        second_gain,
        second_bias,
        entry_weight,
        exit_weight,
        up_weight,
        down_weight,
    )
    part = D // NSEQ
    finish_shape = (
        jax.ShapeDtypeStruct((T, D), BF16),
        jax.ShapeDtypeStruct((T, D), BF16),
        jax.ShapeDtypeStruct((part, 3 * D), F32),
        jax.ShapeDtypeStruct((part, D), F32),
        jax.ShapeDtypeStruct((part, FF), F32),
        jax.ShapeDtypeStruct((T, D), F32),
    ) + tuple([jax.ShapeDtypeStruct((part,), F32)] * 4)
    return pl.pallas_call(
        finish_kernel,
        out_shape=finish_shape,
        in_specs=[anywhere] * 7,
        out_specs=tuple([anywhere] * 6 + [vmem] * 4),
        scratch_shapes=[
            pltpu.VMEM((T, D), BF16),
            pltpu.VMEM((T, D), BF16),
            pltpu.VMEM((T, D), BF16),
            pltpu.VMEM((part, FF), BF16),
            pltpu.VMEM((part, 3 * D), BF16),
            pltpu.VMEM((part, D), BF16),
            pltpu.VMEM((8, D), F32),
            pltpu.VMEM((T, D), F32),
            pltpu.VMEM((part, FF), F32),
            pltpu.VMEM((part, 3 * D), F32),
            pltpu.VMEM((part, D), F32),
            dma((13,)),
        ],
        compiler_params=pltpu.CompilerParams(vmem_limit_bytes=62 * 1024 * 1024),
        name="finish",
    )(output, token_grad, entry_grad, exit_grad, up_grad, down_grad, stats)


def solution(mesh):
    seq_count = mesh.shape["seq"]
    fast = seq_count == 8 and mesh.shape["grp"] == 4
    return jax.shard_map(
        partial(fast_on_device, seq_count) if fast else on_device,
        mesh=mesh,
        in_specs=(P("seq", None), P("seq", None), P(), P(), P(), P(), P(), P(), P(), P(), P(), P()),
        out_specs=(
            P("seq", None),
            P("seq", None),
            P("seq", None),
            P("seq", None),
            P("seq", None),
            P("seq", None),
            P("seq"),
            P("seq"),
            P("seq"),
            P("seq"),
        ),
        check_vma=False,
    )
```

```python
from functools import partial

import jax
import jax.numpy as jnp
from jax import lax
from jax.experimental import pallas as pl
from jax.experimental.pallas import tpu as pltpu
from jax.sharding import PartitionSpec as P

RATE_MIN = 2
RATE_MAX = 8


EPS = 1e-05
PRECISE = lax.Precision.HIGHEST


def norm_forward(values, gain_vec, bias_vec):
    centered = values - jnp.mean(values, axis=1, keepdims=True)
    inverse = lax.rsqrt(jnp.mean(centered * centered, axis=1, keepdims=True) + EPS)
    plain = centered * inverse
    return (plain * gain_vec + bias_vec, plain, inverse)


def norm_backward(upstream, plain, inverse, gain_vec):
    scaled = upstream * gain_vec
    inner = (
        scaled
        - jnp.mean(scaled, axis=1, keepdims=True)
        - plain * jnp.mean(scaled * plain, axis=1, keepdims=True)
    )
    return (inverse * inner, jnp.sum(upstream * plain, axis=0), jnp.sum(upstream, axis=0))


def key_weights(query_sp, query_pos, key_block, first_row, geometry):
    local_len, capacity, dilation, segment, head_offs, score_scale = geometry
    key_count = key_block.shape[0]
    key_heads = key_block.reshape(key_count, query_sp.shape[1], query_sp.shape[2])
    scores = (
        jnp.einsum("ihd,jhd->hij", query_sp, key_heads, preferred_element_type=jnp.float32)
        * score_scale
    )
    key_index = first_row + jnp.arange(key_count, dtype=jnp.int32)
    source = key_index // capacity
    within = key_index - source * capacity
    key_pos = source[None, :] * local_len + head_offs[:, None] + dilation * within[None, :]
    key_live = within < local_len // dilation
    earlier = key_pos[:, None, :] <= query_pos[:, :, None]
    segment_match = key_pos[:, None, :] // segment == query_pos[:, :, None] // segment
    allowed = earlier & segment_match & key_live[None, None, :]
    return (jnp.where(allowed, jnp.exp(scores), 0.0), key_heads)


def forward_block(running, pieces, first_row, query_sp, query_pos, geometry):
    numerator, denominator = running
    key_block, value_block = pieces
    weights, key_heads = key_weights(query_sp, query_pos, key_block, first_row, geometry)
    value_heads = value_block.reshape(key_heads.shape)
    numerator = numerator + jnp.einsum(
        "hij,jhd->hid",
        weights.astype(jnp.bfloat16),
        value_heads,
        preferred_element_type=jnp.float32,
    )
    return (numerator, denominator + jnp.sum(weights, axis=2))


def blockwise(step_fn, running, pieces, first_row, block_rows):
    total_rows = pieces[0].shape[0]
    if total_rows > block_rows and total_rows % block_rows == 0:
        number = total_rows // block_rows
        stacked_first = pieces[0].reshape(number, block_rows, pieces[0].shape[1])
        stacked_second = pieces[1].reshape(number, block_rows, pieces[1].shape[1])
        block_starts = first_row + block_rows * jnp.arange(number, dtype=jnp.int32)

        def advance(state, items):
            return (step_fn(state, (items[0], items[1]), items[2]), None)

        running, _ = lax.scan(advance, running, (stacked_first, stacked_second, block_starts))
        return running
    return step_fn(running, pieces, first_row)


def backward_block(running, items, query_sp, query_pos, grad_sp, shift_sp, geometry):
    key_block, value_block, first_row = items
    score_scale = geometry[5]
    weights, key_heads = key_weights(query_sp, query_pos, key_block, first_row, geometry)
    key_count = key_block.shape[0]
    value_heads = value_block.reshape(key_heads.shape)
    pressure = jnp.einsum("ihd,jhd->hij", grad_sp, value_heads, preferred_element_type=jnp.float32)
    slopes = (weights * (pressure - shift_sp[:, :, None])).astype(jnp.bfloat16)
    running = (
        running
        + jnp.einsum("hij,jhd->ihd", slopes, key_heads, preferred_element_type=jnp.float32)
        * score_scale
    )
    grad_keys = (
        jnp.einsum("hij,ihd->jhd", slopes, query_sp, preferred_element_type=jnp.float32)
        * score_scale
    )
    grad_values = jnp.einsum(
        "hij,ihd->jhd", weights.astype(jnp.bfloat16), grad_sp, preferred_element_type=jnp.float32
    )
    return (running, (grad_keys.reshape(key_count, -1), grad_values.reshape(key_count, -1)))


def local_weights(query_heads, key_heads, score_scale):
    local_len = query_heads.shape[0]
    scores = (
        jnp.einsum("ihd,jhd->hij", query_heads, key_heads, preferred_element_type=jnp.float32)
        * score_scale
    )
    positions = jnp.arange(local_len, dtype=jnp.int32)
    causal = positions[:, None] >= positions[None, :]
    return jnp.where(causal[None], jnp.exp(scores), 0.0)


def on_device(
    tokens,
    cotangent,
    entry_weight,
    exit_weight,
    up_weight,
    down_weight,
    first_gain,
    first_bias,
    second_gain,
    second_bias,
    dilations,
    offsets,
):
    local_len, width_model = tokens.shape
    head_count = offsets.shape[1]
    head_size = width_model // head_count
    score_scale = head_size ** (-0.5)
    capacity = local_len // RATE_MIN
    group_idx = lax.axis_index("grp")
    seq_index = lax.axis_index("seq")
    seq_count = lax.axis_size("seq")
    dilation = lax.dynamic_index_in_dim(dilations, group_idx, 0, keepdims=False)
    head_offs = lax.dynamic_index_in_dim(offsets, group_idx, 0, keepdims=False)
    segment = local_len * seq_count * dilation // RATE_MAX
    step_ids = jnp.arange(capacity, dtype=jnp.int32)
    row_live = step_ids < local_len // dilation
    local_rows = jnp.minimum(head_offs[:, None] + dilation * step_ids[None, :], local_len - 1)
    query_pos = jnp.where(
        row_live[None, :],
        seq_index * local_len + head_offs[:, None] + dilation * step_ids[None, :],
        -1,
    )
    geometry = (local_len, capacity, dilation, segment, head_offs, score_scale)
    head_shape = (local_len, head_count, head_size)
    selector = local_rows[:, :, None] == jnp.arange(local_len, dtype=jnp.int32)[None, None, :]
    select_low = selector.astype(jnp.bfloat16)
    select_full = selector.astype(jnp.float32)

    def pick(array_in):
        return jnp.einsum(
            "hci,ihd->chd", select_low, array_in, preferred_element_type=jnp.float32
        ).astype(jnp.bfloat16)

    def place_back(sparse_in):
        return jnp.einsum("hci,chd->ihd", select_full, sparse_in, precision=PRECISE)

    inputs = tokens.astype(jnp.float32)
    normed_one, plain_one, inverse_one = norm_forward(inputs, first_gain, first_bias)
    normed_low = normed_one.astype(jnp.bfloat16)
    packed = jnp.dot(normed_low, entry_weight, preferred_element_type=jnp.float32).astype(
        jnp.bfloat16
    )
    query_heads = packed[:, :width_model].reshape(head_shape)
    key_heads = packed[:, width_model : 2 * width_model].reshape(head_shape)
    value_heads = packed[:, 2 * width_model :].reshape(head_shape)
    query_sp = pick(query_heads)
    key_sp = pick(key_heads).reshape(capacity, width_model)
    value_sp = pick(value_heads).reshape(capacity, width_model)
    empty_state = (
        jnp.zeros((head_count, capacity, head_size), jnp.float32),
        jnp.zeros((head_count, capacity), jnp.float32),
    )
    forward_step = partial(forward_block, query_sp=query_sp, query_pos=query_pos, geometry=geometry)
    numerator, denominator = blockwise(
        forward_step,
        empty_state,
        (
            lax.all_gather(key_sp, "seq", axis=0, tiled=True),
            lax.all_gather(value_sp, "seq", axis=0, tiled=True),
        ),
        jnp.int32(0),
        8 * capacity,
    )

    def local_part(query_in, key_in, value_in):
        weights = local_weights(query_in, key_in, score_scale)
        local_num = jnp.einsum(
            "hij,jhd->ihd",
            weights.astype(jnp.bfloat16),
            value_in,
            preferred_element_type=jnp.float32,
        )
        return (local_num, jnp.sum(weights, axis=2).T)

    def local_none(query_in, key_in, value_in):
        return (jnp.zeros(head_shape, jnp.float32), jnp.zeros((local_len, head_count), jnp.float32))

    local_num, local_den = lax.cond(
        group_idx == 0, local_part, local_none, query_heads, key_heads, value_heads
    )
    numerator_full = (
        jnp.einsum("hci,hcd->ihd", select_full, numerator, precision=PRECISE) + local_num
    )
    denominator_full = (
        jnp.einsum("hci,hc->ih", select_full, denominator, precision=PRECISE) + local_den
    )
    merged_num, merged_den = lax.psum(
        (numerator_full.reshape(local_len, width_model), denominator_full), "grp"
    )
    attention = merged_num.reshape(head_shape) / merged_den[:, :, None]
    mixed = attention.reshape(local_len, width_model).astype(jnp.bfloat16)
    middle = inputs + jnp.dot(mixed, exit_weight, preferred_element_type=jnp.float32)
    normed_two, plain_two, inverse_two = norm_forward(middle, second_gain, second_bias)
    normed_two_low = normed_two.astype(jnp.bfloat16)
    hidden = jnp.dot(normed_two_low, up_weight, preferred_element_type=jnp.float32)
    active = jax.nn.gelu(hidden, approximate=False).astype(jnp.bfloat16)
    output = (middle + jnp.dot(active, down_weight, preferred_element_type=jnp.float32)).astype(
        jnp.bfloat16
    )
    down_grad = jnp.dot(active.T, cotangent, preferred_element_type=jnp.float32)
    grad_active = jnp.dot(cotangent, down_weight.T, preferred_element_type=jnp.float32)
    _, gelu_pull = jax.vjp(partial(jax.nn.gelu, approximate=False), hidden)
    grad_hidden = gelu_pull(grad_active)[0].astype(jnp.bfloat16)
    up_grad = jnp.dot(normed_two_low.T, grad_hidden, preferred_element_type=jnp.float32)
    grad_normed_two = jnp.dot(grad_hidden, up_weight.T, preferred_element_type=jnp.float32)
    grad_plain_two, second_gain_grad, second_bias_grad = norm_backward(
        grad_normed_two, plain_two, inverse_two, second_gain
    )
    grad_middle = cotangent.astype(jnp.float32) + grad_plain_two
    grad_branch = grad_middle.astype(jnp.bfloat16)
    exit_grad = jnp.dot(mixed.T, grad_branch, preferred_element_type=jnp.float32)
    grad_mixed_low = lax.optimization_barrier(
        jnp.dot(grad_branch, exit_weight.T, preferred_element_type=jnp.float32).astype(jnp.bfloat16)
    )
    grad_mixed = grad_mixed_low.astype(jnp.float32).reshape(head_shape)
    grad_numer = (grad_mixed / merged_den[:, :, None]).astype(jnp.bfloat16)
    row_shift = jnp.sum(grad_mixed * attention, axis=2) / merged_den
    grad_sp = pick(grad_numer)
    shift_sp = jnp.einsum("hci,ih->hc", select_full, row_shift, precision=PRECISE)
    back_keys, back_values = (
        lax.all_gather(key_sp, "seq", axis=0, tiled=True),
        lax.all_gather(value_sp, "seq", axis=0, tiled=True),
    )
    block_rows = 8 * capacity
    number = back_keys.shape[0] // block_rows
    stacked_keys = back_keys.reshape(number, block_rows, width_model)
    stacked_values = back_values.reshape(number, block_rows, width_model)
    block_starts = block_rows * jnp.arange(number, dtype=jnp.int32)
    empty_query = jnp.zeros((capacity, head_count, head_size), jnp.float32)
    back_step = partial(
        backward_block,
        query_sp=query_sp,
        query_pos=query_pos,
        grad_sp=grad_sp,
        shift_sp=shift_sp,
        geometry=geometry,
    )
    grad_query_sp, (grad_key_all, grad_value_all) = lax.scan(
        back_step, empty_query, (stacked_keys, stacked_values, block_starts)
    )
    own_keys, own_values = (
        lax.psum_scatter(
            grad_key_all.reshape(-1, width_model), "seq", scatter_dimension=0, tiled=True
        ),
        lax.psum_scatter(
            grad_value_all.reshape(-1, width_model), "seq", scatter_dimension=0, tiled=True
        ),
    )

    def local_grads(query_in, key_in, value_in, grad_in, shift_in):
        weights = local_weights(query_in, key_in, score_scale)
        pressure = jnp.einsum("ihd,jhd->hij", grad_in, value_in, preferred_element_type=jnp.float32)
        slopes = (weights * (pressure - shift_in.T[:, :, None])).astype(jnp.bfloat16)
        grad_query = (
            jnp.einsum("hij,jhd->ihd", slopes, key_in, preferred_element_type=jnp.float32)
            * score_scale
        )
        grad_key = (
            jnp.einsum("hij,ihd->jhd", slopes, query_in, preferred_element_type=jnp.float32)
            * score_scale
        )
        grad_value = jnp.einsum(
            "hij,ihd->jhd",
            weights.astype(jnp.bfloat16),
            grad_in,
            preferred_element_type=jnp.float32,
        )
        return (grad_query, grad_key, grad_value)

    def local_skip(query_in, key_in, value_in, grad_in, shift_in):
        zeros_heads = jnp.zeros(head_shape, jnp.float32)
        return (zeros_heads, zeros_heads, zeros_heads)

    local_dq, local_dk, local_dv = lax.cond(
        group_idx == 0,
        local_grads,
        local_skip,
        query_heads,
        key_heads,
        value_heads,
        grad_numer,
        row_shift,
    )
    grad_query_full = place_back(grad_query_sp) + local_dq
    grad_key_full = place_back(own_keys.reshape(capacity, head_count, head_size)) + local_dk
    grad_value_full = place_back(own_values.reshape(capacity, head_count, head_size)) + local_dv
    grad_packed = jnp.concatenate(
        [
            grad_query_full.reshape(local_len, width_model),
            grad_key_full.reshape(local_len, width_model),
            grad_value_full.reshape(local_len, width_model),
        ],
        axis=1,
    )
    summed = lax.psum(grad_packed, "grp").astype(jnp.bfloat16)
    entry_grad = jnp.dot(normed_low.T, summed, preferred_element_type=jnp.float32)
    grad_normed_one = jnp.dot(summed, entry_weight.T, preferred_element_type=jnp.float32)
    grad_plain_one, first_gain_grad, first_bias_grad = norm_backward(
        grad_normed_one, plain_one, inverse_one, first_gain
    )
    token_grad = (grad_middle + grad_plain_one).astype(jnp.bfloat16)
    shards = (
        lax.psum_scatter(entry_grad, "seq", scatter_dimension=0, tiled=True),
        lax.psum_scatter(exit_grad, "seq", scatter_dimension=0, tiled=True),
        lax.psum_scatter(up_grad, "seq", scatter_dimension=0, tiled=True),
        lax.psum_scatter(down_grad, "seq", scatter_dimension=0, tiled=True),
        lax.psum_scatter(first_gain_grad, "seq", scatter_dimension=0, tiled=True),
        lax.psum_scatter(first_bias_grad, "seq", scatter_dimension=0, tiled=True),
        lax.psum_scatter(second_gain_grad, "seq", scatter_dimension=0, tiled=True),
        lax.psum_scatter(second_bias_grad, "seq", scatter_dimension=0, tiled=True),
    )
    return (
        output,
        token_grad,
        shards[0],
        shards[1],
        shards[2],
        shards[3],
        shards[4],
        shards[5],
        shards[6],
        shards[7],
    )


MESH = pl.DeviceIdType.MESH
LANES = 128
LOG2E = 1.4426950408889634
F32 = jnp.float32
BF16 = jnp.bfloat16


def dot_nn(left, right):
    return lax.dot_general(left, right, (((1,), (0,)), ((), ())), preferred_element_type=F32)


def dot_nt(left, right):
    return lax.dot_general(left, right, (((1,), (1,)), ((), ())), preferred_element_type=F32)


def dot_tn(left, right):
    return lax.dot_general(left, right, (((0,), (0,)), ((), ())), preferred_element_type=F32)


def lane_ids(width):
    return lax.broadcasted_iota(jnp.int32, (1, width), 1)


def slot_mask(slot, width=256):
    ids = lane_ids(width)
    return jnp.where((ids >= 64 * slot) & (ids < 64 * slot + 64), 1.0, 0.0).astype(F32)


def join_halves(low_part, high_part):
    return jnp.where(lane_ids(LANES) < 64, low_part, high_part)


def swap_halves(tile):
    return pltpu.roll(tile, 64, axis=1)


def layer_kernel(
    sizes,
    dil_ref,
    off_ref,
    tok_ref,
    cot_ref,
    gain1_ref,
    bias1_ref,
    gain2_ref,
    bias2_ref,
    entry_hbm,
    exit_hbm,
    up_hbm,
    down_hbm,
    out_ref,
    tgrad_ref,
    oentry_ref,
    oexit_ref,
    oup_ref,
    odown_ref,
    ostat_ref,
    win,
    exit_all,
    exit_win,
    up_all,
    down_all,
    n1,
    n2,
    middle,
    gmid,
    gbranch,
    mixed,
    active,
    ghid,
    gn2,
    member,
    masks,
    kv,
    qb,
    dob,
    qmask,
    shift,
    invden,
    att,
    acc_a,
    acc_b,
    acc_c,
    zmix,
    drecv,
    tz,
    stat,
    stat_z,
    pc_up,
    r1_up,
    r2_up,
    ag_up,
    pc_down,
    r1_down,
    r2_down,
    ag_down,
    pc_eq,
    r1_eq,
    r2_eq,
    ag_eq,
    pc_ekv,
    r1_ekv,
    r2_ekv,
    ag_ekv,
    load_sem,
    kv_ssem,
    kv_rsem,
    q_ssem,
    q_rsem,
    do_ssem,
    do_rsem,
    zm_ssem,
    zm_rsem,
    zd_ssem,
    zd_rsem,
    zt_ssem,
    zt_rsem,
    rs_s1,
    rs_r1,
    rs_s2,
    rs_r2,
    rs_zs,
    rs_zr,
    st_ssem,
    st_rsem,
    sz_ssem,
    sz_rsem,
):
    T, D, HEADS, E, FF, NSEQ, NGRP = sizes
    scale = E ** (-0.5)
    exp_scale = scale * LOG2E
    s = lax.axis_index("seq")
    g = lax.axis_index("grp")
    chip = s // 2
    core = s % 2
    sib = s + 1 - 2 * core
    odd = g % 2
    chips = NSEQ // 2
    part = D // NGRP
    is_odd = odd == 1
    gain1 = gain1_ref[...].reshape(1, D)
    bias1 = bias1_ref[...].reshape(1, D)
    gain2 = gain2_ref[...].reshape(1, D)
    bias2 = bias2_ref[...].reshape(1, D)

    def to_seq(peer, src, dst, ssem, rsem):
        return pltpu.make_async_remote_copy(
            src_ref=src,
            dst_ref=dst,
            send_sem=ssem,
            recv_sem=rsem,
            device_id={"seq": peer},
            device_id_type=MESH,
        )

    def to_grp(peer, src, dst, ssem, rsem):
        return pltpu.make_async_remote_copy(
            src_ref=src,
            dst_ref=dst,
            send_sem=ssem,
            recv_sem=rsem,
            device_id={"grp": peer},
            device_id_type=MESH,
        )

    loads = []
    for t in range(3):
        first = pl.multiple_of(t * D + part * g - 64 * odd, LANES)
        loads.append(
            pltpu.make_async_copy(entry_hbm.at[:, pl.ds(first, 256)], win.at[t], load_sem.at[t])
        )
    loads.append(pltpu.make_async_copy(down_hbm, down_all, load_sem.at[3]))
    loads.append(pltpu.make_async_copy(exit_hbm, exit_all, load_sem.at[4]))
    loads.append(
        pltpu.make_async_copy(
            exit_hbm.at[pl.ds(pl.multiple_of(part * g, 64), part), :],
            exit_win.at[pl.ds(64, part), :],
            load_sem.at[5],
        )
    )
    loads.append(pltpu.make_async_copy(up_hbm, up_all, load_sem.at[6]))
    for load in loads:
        load.start()

    barrier = pltpu.get_barrier_semaphore()
    for step in range(1, NSEQ):
        pl.semaphore_signal(
            barrier, inc=1, device_id={"seq": lax.rem(s + step, NSEQ)}, device_id_type=MESH
        )
    for step in range(1, NGRP):
        pl.semaphore_signal(
            barrier, inc=1, device_id={"grp": lax.rem(g + step, NGRP)}, device_id_type=MESH
        )

    rows = 96

    def norm_one(i, carry):
        at = pl.ds(pl.multiple_of(i * rows, rows), rows)
        value = tok_ref[at, :].astype(F32)
        centered = value - jnp.mean(value, axis=1, keepdims=True)
        inverse = lax.rsqrt(jnp.mean(centered * centered, axis=1, keepdims=True) + EPS)
        n1[at, :] = (centered * inverse * gain1 + bias1).astype(BF16)
        return carry

    lax.fori_loop(0, T // rows, norm_one, 0)
    exit_win[0:64, :] = jnp.zeros((64, D), BF16)

    for t in range(3):
        loads[t].wait()
    lane256 = lane_ids(256)
    q_raw = dot_nn(n1[...], win[0])
    k_raw = dot_nn(n1[...], win[1])
    v_raw = dot_nn(n1[...], win[2])
    q_own = jnp.where(is_odd, pltpu.roll(q_raw, 192, axis=1), q_raw)
    k_own = jnp.where(is_odd, pltpu.roll(k_raw, 192, axis=1), k_raw)
    v_own = jnp.where(is_odd, v_raw, pltpu.roll(v_raw, 64, axis=1))
    q_own = jnp.where(lane256 < 192, q_own, 0.0)
    qb[s] = q_own.astype(BF16)
    for h in range(3):
        qmask[h] = (q_own * slot_mask(h)).astype(BF16)
    kv[s, :, 0:128] = k_own[:, 0:128].astype(BF16)
    kv[s, :, 128:256] = join_halves(k_own[:, 128:256], v_own[:, 0:128]).astype(BF16)
    kv[s, :, 256:384] = v_own[:, 128:256].astype(BF16)

    pl.semaphore_wait(barrier, NSEQ - 1 + NGRP - 1)

    launched = {}

    def launch(name, copies):
        for cond, copy in copies():
            pl.when(cond)(copy.start)
        launched[name] = copies

    always = core >= 0

    def spread(name, buffer, ssem, rsem, upward):
        def copies():
            found = []
            for d in range(1, chips):
                peer = lax.rem(s + (2 * d if upward else NSEQ - 2 * d), NSEQ)
                cond = chip + d < chips if upward else chip >= d
                found.append(
                    (cond, to_seq(peer, buffer.at[s], buffer.at[s], ssem.at[d - 1], rsem.at[s]))
                )
            found.append((always, to_seq(sib, buffer.at[s], buffer.at[s], ssem.at[3], rsem.at[s])))
            return found

        launch(name, copies)

    spread("kv", kv, kv_ssem, kv_rsem, True)
    spread("q", qb, q_ssem, q_rsem, False)

    lane128 = lane_ids(LANES)
    rate_row = jnp.ones((1, LANES), F32)
    for i in range(NGRP):
        rate_row = jnp.where(lane128 == i, dil_ref[i].astype(F32), rate_row)
    local_pos = lax.broadcasted_iota(jnp.int32, (T, 1), 0).astype(F32)
    residue = local_pos - rate_row * jnp.floor((local_pos + 0.5) / rate_row)
    for h in range(3):
        off_row = jnp.full((1, LANES), -1.0, F32)
        for i in range(NGRP):
            off_row = jnp.where(
                lane128 == i, off_ref[i, 3 * g + h].astype(F32), off_row
            )
        member[h] = jnp.where(residue == off_row, 1.0, 0.0).astype(BF16)
    per_segment = rate_row * (T * NSEQ // RATE_MAX)

    def segment_of(block):
        return jnp.floor((jnp.full((1, LANES), block * T, jnp.int32).astype(F32) + 0.5) / per_segment)

    own_segment = segment_of(s)

    pair_width = 2 * T

    def pair_lanes(cc):
        return pl.ds(pl.multiple_of(cc * pair_width, LANES), pair_width)

    def build_mask(cc, carry):
        for h in range(3):
            blocks = []
            for i in range(2):
                same = jnp.where(segment_of(2 * cc + i) == own_segment, 1.0, 0.0)
                blocks.append((member[h].astype(F32) * same).astype(BF16))
            count = dot_nt(member[h], jnp.concatenate(blocks, axis=0))
            masks[h, :, pair_lanes(cc)] = count.astype(BF16)
        return carry

    lax.fori_loop(0, chips, build_mask, 0)
    own_id = lax.broadcasted_iota(jnp.int32, (T, pair_width), 0) + core * T
    pair_id = lax.broadcasted_iota(jnp.int32, (T, pair_width), 1)
    own_block = (pair_id >= core * T) & (pair_id < core * T + T)
    for h in range(3):
        count = masks[h, :, pair_lanes(chip)].astype(F32) + jnp.where(own_block, 1.0, 0.0)
        masks[h, :, pair_lanes(chip)] = jnp.where(pair_id <= own_id, count, 0.0).astype(BF16)
        masks[h, :, pair_lanes(chips)] = jnp.where(own_id <= pair_id, count, 0.0).astype(BF16)

    half = T // 2
    width = part + 64
    piece = D // NSEQ

    def pack_half(tile, high):
        top, bottom = tile[0:half], tile[half:T]
        if high:
            return join_halves(swap_halves(top), bottom).astype(BF16)
        return join_halves(top, swap_halves(bottom)).astype(BF16)

    right, left = lax.rem(g + 1, NGRP), lax.rem(g + NGRP - 1, NGRP)

    def chain_start(name, at, ssem, rsem):
        launch(
            name + "0",
            lambda: [
                (g + 1 < NGRP, to_grp(right, at(g), at(g), ssem().at[0, 0], rsem().at[g])),
                (g >= 1, to_grp(left, at(g), at(g), ssem().at[0, 1], rsem().at[g])),
            ],
        )

    def chain_step(d, name, at, ssem, rsem):
        def slots():
            return lax.rem(g - d + NGRP, NGRP), lax.rem(g + d, NGRP)

        def copies():
            lower, upper = slots()
            return [
                (
                    (g - d >= 0) & (g + 1 < NGRP),
                    to_grp(right, at(lower), at(lower), ssem().at[d, 0], rsem().at[lower]),
                ),
                (
                    (g + d < NGRP) & (g >= 1),
                    to_grp(left, at(upper), at(upper), ssem().at[d, 1], rsem().at[upper]),
                ),
            ]

        lower, upper = slots()
        pl.when(g - d >= 0)(
            to_grp(right, at(lower), at(lower), ssem().at[0, 0], rsem().at[lower]).wait_recv
        )
        pl.when(g + d < NGRP)(
            to_grp(left, at(upper), at(upper), ssem().at[0, 1], rsem().at[upper]).wait_recv
        )
        if d < NGRP - 1:
            launch(name + str(d), copies)

    def direct_start(name, at, ssem, rsem):
        def copies():
            found = []
            for step in range(1, NGRP):
                peer = lax.rem(g + step, NGRP)
                found.append((always, to_grp(peer, at(g), at(g), ssem.at[step - 1], rsem.at[g])))
            return found

        launch(name, copies)

    def direct_wait(name, at, ssem, rsem):
        for step in range(1, NGRP):
            slot = lax.rem(g + step, NGRP)
            to_grp(slot, at(slot), at(slot), ssem.at[0], rsem.at[slot]).wait_recv()

    acc_a[...] = jnp.zeros_like(acc_a)
    shift[...] = jnp.zeros_like(shift)

    def pair_of(ref, cc, first, last):
        return ref[pl.ds(2 * cc, 2), :, first:last].reshape(pair_width, last - first)

    def weights_of(score, count):
        count = count.astype(F32)
        return jnp.where(count > 0.5, jnp.exp2(score * exp_scale) * count, 0.0)

    def wait_pair(buffer, ssem, rsem, j, cc):
        mine, other = 2 * cc + core, 2 * cc + 1 - core

        @pl.when(j > 0)
        def _():
            to_seq(sib, buffer.at[mine], buffer.at[mine], ssem.at[0], rsem.at[mine]).wait_recv()
            to_seq(sib, buffer.at[mine], buffer.at[mine], ssem.at[3 + j], rsem.at[mine]).start()

        to_seq(sib, buffer.at[other], buffer.at[other], ssem.at[0], rsem.at[other]).wait_recv()

    def forward_step(j, carry):
        cc = chip - j
        wait_pair(kv, kv_ssem, kv_rsem, j, cc)
        keys = pair_of(kv, cc, 0, 256)
        values = pair_of(kv, cc, 128, 384)
        for h in range(3):
            weight = weights_of(dot_nt(qmask[h], keys), masks[h, :, pair_lanes(cc)])
            row_sum = weight[:, 0:LANES]
            for i in range(1, pair_width // LANES):
                row_sum = row_sum + weight[:, LANES * i : LANES * i + LANES]
            shift[h] += row_sum
            low_weight = weight.astype(BF16)
            masks[h, :, pair_lanes(cc)] = low_weight
            acc_a[...] += dot_nn(low_weight, values) * slot_mask(h + 1)
        return carry

    lax.fori_loop(0, chip + 1, forward_step, 0)
    inverse = jnp.zeros((T, 256), F32)
    for h in range(3):
        inverse += slot_mask(h + 1) / jnp.sum(shift[h], axis=1, keepdims=True)
    att_own = acc_a[...] * inverse
    invden[...] = inverse
    att[...] = att_own
    for h in range(3):
        tile = att_own[:, 0:128] if h == 0 else att_own[:, 128:256]
        zmix[g, h] = pack_half(tile, h != 1)
    mixed_gather = ("mixed", lambda i: zmix.at[i], zm_ssem, zm_rsem)
    direct_start(*mixed_gather)

    for d in range(1, chips):

        @pl.when(chip + d < chips)
        def _(d=d):
            slot = lax.rem(s + 2 * d, NSEQ)
            to_seq(sib, qb.at[slot], qb.at[slot], q_ssem.at[0], q_rsem.at[slot]).wait_recv()

    def hand_on(buffer, ssem, rsem, upward):
        found = []
        for d in range(1, chips):
            slot = lax.rem(s + (NSEQ - 2 * d if upward else 2 * d), NSEQ)
            cond = chip >= d if upward else chip + d < chips
            found.append(
                (cond, to_seq(sib, buffer.at[slot], buffer.at[slot], ssem.at[3 + d], rsem.at[slot]))
            )
        return found

    launch("q on", lambda: hand_on(qb, q_ssem, q_rsem, False))
    launched["kv on"] = lambda: hand_on(kv, kv_ssem, kv_rsem, True)
    launched["do on"] = lambda: hand_on(dob, do_ssem, do_rsem, False)

    loads[3].wait()

    def cot_times_down(i, carry):
        at = pl.ds(pl.multiple_of(i * T, T), T)
        ghid[:, at] = dot_nt(cot_ref[...], down_all[at, :]).astype(BF16)
        return carry

    lax.fori_loop(0, FF // T, cot_times_down, 0)
    direct_wait(*mixed_gather)
    for tile in range(D // LANES):
        (g_a, h_a), (g_b, h_b) = divmod(2 * tile, 3), divmod(2 * tile + 1, 3)
        first_head = zmix[g_a, h_a].astype(F32)
        second_head = zmix[g_b, h_b].astype(F32)
        cols = slice(tile * LANES, tile * LANES + LANES)
        mixed[0:half, cols] = join_halves(first_head, swap_halves(second_head)).astype(BF16)
        mixed[half:T, cols] = join_halves(swap_halves(first_head), second_head).astype(BF16)

    loads[4].wait()
    middle[...] = tok_ref[...].astype(F32) + dot_nn(mixed[...], exit_all[...])

    def norm_two(i, carry):
        at = pl.ds(pl.multiple_of(i * rows, rows), rows)
        value = middle[at, :]
        centered = value - jnp.mean(value, axis=1, keepdims=True)
        inverse = lax.rsqrt(jnp.mean(centered * centered, axis=1, keepdims=True) + EPS)
        plain = centered * inverse
        n2[at, :] = (plain * gain2 + bias2).astype(BF16)
        return carry

    lax.fori_loop(0, T // rows, norm_two, 0)

    def reduce_start(i, pieces, first_in, cond=None, tag=""):
        launch(
            f"first{i}{tag}",
            lambda: [
                (
                    always if cond is None else cond(),
                    to_seq(sib, pieces.at[1 - core], first_in, rs_s1.at[i], rs_r1.at[i]),
                )
            ],
        )

    def reduce_pass(i, pieces, first_in, second_in, cond=None, tag=""):
        def given():
            return always if cond is None else cond()

        @pl.when(given())
        def _():
            to_seq(sib, pieces.at[core], first_in, rs_s1.at[i], rs_r1.at[i]).wait_recv()
            for cc in range(chips):
                pieces[core, cc] = (
                    pieces[core, cc].astype(F32) + first_in[cc].astype(F32)
                ).astype(BF16)

        def copies():
            found = []
            for d in range(1, chips):
                to_chip = lax.rem(chip + d, chips)
                copy = to_seq(
                    2 * to_chip + core,
                    pieces.at[core, to_chip],
                    second_in.at[chip],
                    rs_s2.at[i, d - 1],
                    rs_r2.at[i, chip],
                )
                found.append((given(), copy))
            return found

        launch(f"second{i}{tag}", copies)

    def weight_gather(i, gathered):
        return ("weight" + str(i), lambda j: gathered.at[j], lambda: rs_zs.at[i], lambda: rs_zr.at[i])

    def reduce_end(i, pieces, second_in, gathered):
        result = pieces[core, chip].astype(F32)
        for d in range(1, chips):
            slot = lax.rem(chip + d, chips)
            to_seq(
                sib, second_in.at[slot], second_in.at[slot], rs_s1.at[i], rs_r2.at[i, slot]
            ).wait_recv()
            result = result + second_in[slot].astype(F32)
        gathered[g] = result.astype(BF16)
        chain_start(*weight_gather(i, gathered))

    loads[6].wait()
    cot_turned = jnp.transpose(
        cot_ref[:, pl.ds(pl.multiple_of(lax.rem(g, 3) * width, LANES), width)].astype(F32)
    ).astype(BF16)

    def feed_forward(i, carry):
        c = lax.rem(g + i, NGRP)
        at = pl.ds(pl.multiple_of(c * D, LANES), D)
        hidden = dot_nn(n2[...], up_all[:, at])
        cdf = 0.5 + 0.5 * lax.erf(hidden * (0.5**0.5))
        low_active = (hidden * cdf).astype(BF16)
        active[:, at] = low_active
        density = jnp.exp2(hidden * hidden * (-0.5 * LOG2E)) * 0.3989422804014327
        ghid[:, at] = (ghid[:, at].astype(F32) * (cdf + hidden * density)).astype(BF16)

        @pl.when(g < 3)
        def _():
            turned = dot_nn(cot_turned, active[:, at]).astype(BF16)
            pc_down[0, c] = turned[:, 0:T]
            pc_down[1, c] = turned[:, T : 2 * T]

        @pl.when(i == 0)
        def _():
            for j in range(2):
                up_grad = dot_tn(n2[...], ghid[:, pl.ds(pl.multiple_of(g * D + T * j, LANES), T)])
                for t in range(NSEQ):
                    pc_up[t % 2, t // 2, :, T * j : T * j + T] = up_grad[
                        piece * t : piece * t + piece, :
                    ].astype(BF16)
            reduce_start(0, pc_up, r1_up)

        @pl.when(i == 1)
        def _():
            reduce_pass(0, pc_up, r1_up, r2_up)

        return carry

    lax.fori_loop(0, NGRP, feed_forward, 0)
    reduce_start(1, pc_down, r1_down, lambda: g < 3, "down")

    def back_through_up(i, carry):
        at = pl.ds(pl.multiple_of(i * 256, 256), 256)
        gn2[:, at] = dot_nt(ghid[...], up_all[at, :])
        return carry

    lax.fori_loop(0, D // 256, back_through_up, 0)
    reduce_pass(1, pc_down, r1_down, r2_down, lambda: g < 3, "down")

    stat[s] = jnp.zeros((8, D), F32)

    def norm_two_back(i, carry):
        at = pl.ds(pl.multiple_of(i * rows, rows), rows)
        upstream = gn2[at, :]
        value = middle[at, :]
        centered = value - jnp.mean(value, axis=1, keepdims=True)
        inverse = lax.rsqrt(jnp.mean(centered * centered, axis=1, keepdims=True) + EPS)
        plain = centered * inverse
        scaled = upstream * gain2
        inner = (
            scaled
            - jnp.mean(scaled, axis=1, keepdims=True)
            - plain * jnp.mean(scaled * plain, axis=1, keepdims=True)
        )
        grad = cot_ref[at, :].astype(F32) + inverse * inner
        gmid[at, :] = grad
        gbranch[at, :] = grad.astype(BF16)
        stat[s, 0:1, :] += jnp.sum(upstream * plain, axis=0, keepdims=True)
        stat[s, 1:2, :] += jnp.sum(upstream, axis=0, keepdims=True)
        return carry

    lax.fori_loop(0, T // rows, norm_two_back, 0)

    loads[5].wait()
    gmix = dot_nt(gbranch[...], exit_win[...]).astype(BF16).astype(F32)
    numer_grad = gmix * invden[...]
    product = numer_grad * att[...]
    for h in range(3):
        value = jnp.sum(product * slot_mask(h + 1), axis=1, keepdims=True)
        shift[h] = jnp.broadcast_to(value, (T, LANES))
        high = value.astype(BF16).astype(F32)
        low = value - high
        numer_grad = jnp.where(lane256 == 2 * h, high, numer_grad)
        numer_grad = jnp.where(lane256 == 2 * h + 1, low, numer_grad)
    dob[s] = numer_grad.astype(BF16)

    spread("do", dob, do_ssem, do_rsem, False)

    reduce_end(0, pc_up, r2_up, ag_up)

    @pl.when(g == 3)
    def _():
        exit_grad = dot_tn(mixed[...], gbranch[...]).astype(BF16)
        for t in range(NSEQ):
            for i in range(2):
                pc_down[t % 2, t // 2, piece * i : piece * i + piece, :] = exit_grad[
                    piece * t : piece * t + piece, T * i : T * i + T
                ]
            pc_down[t % 2, t // 2, 2 * piece : width, :] = jnp.zeros((width - 2 * piece, T), BF16)

    reduce_start(1, pc_down, r1_down, lambda: g == 3, "exit")
    reduce_pass(1, pc_down, r1_down, r2_down, lambda: g == 3, "exit")

    for h in range(3):
        qmask[h] = (dob[s].astype(F32) * slot_mask(h + 1)).astype(BF16)
    acc_a[...] = jnp.zeros_like(acc_a)

    def query_side(cc, carry):
        keys = pair_of(kv, cc, 0, 256)
        values = pair_of(kv, cc, 128, 384)
        for h in range(3):
            row_shift = jnp.concatenate([shift[h]] * (pair_width // LANES), axis=1)
            pressure = dot_nt(qmask[h], values) - row_shift
            slope = (masks[h, :, pair_lanes(cc)].astype(F32) * pressure).astype(BF16)
            acc_a[...] += dot_nn(slope, keys) * slot_mask(h)
        return carry

    lax.fori_loop(0, chip + 1, query_side, 0)
    dq = acc_a[...] * scale

    def weight_pieces(pieces, grad):
        for t in range(NSEQ):
            pieces[t % 2, t // 2] = grad[piece * t : piece * t + piece, :].astype(BF16)

    weight_pieces(pc_eq, dot_tn(n1[...], dq.astype(BF16)))
    reduce_start(2, pc_eq, r1_eq)
    chain_step(1, *weight_gather(0, ag_up))

    v_tile = kv[s, :, 128:384].astype(F32)
    k_tile = kv[s, :, 0:256].astype(F32)
    for h in range(3):
        qmask[h] = (k_tile * slot_mask(h)).astype(BF16)
        minus = jnp.where((lane256 == 2 * h) | (lane256 == 2 * h + 1), -1.0, 0.0)
        qmask[3 + h] = (v_tile * slot_mask(h + 1) + minus).astype(BF16)
    acc_b[...] = jnp.zeros_like(acc_b)
    acc_c[...] = jnp.zeros_like(acc_c)

    def key_side(j, carry):
        cc = chip + j
        wait_pair(dob, do_ssem, do_rsem, j, cc)
        other = 2 * cc + 1 - core
        to_seq(sib, qb.at[other], qb.at[other], q_ssem.at[0], q_rsem.at[other]).wait_recv()
        queries = pair_of(qb, cc, 0, 256)
        grads = pair_of(dob, cc, 0, 256)
        for h in range(3):
            count = masks[h, :, pair_lanes(jnp.where(j == 0, chips, cc))]
            weight = weights_of(dot_nt(qmask[h], queries), count)
            slope = (weight * dot_nt(qmask[3 + h], grads)).astype(BF16)
            acc_b[...] += dot_nn(slope, queries) * slot_mask(h)
            acc_c[...] += dot_nn(weight.astype(BF16), grads) * slot_mask(h + 1)

        @pl.when(j == 0)
        def _():
            reduce_pass(2, pc_eq, r1_eq, r2_eq)
            chain_step(2, *weight_gather(0, ag_up))

        @pl.when((j == 1) | ((j == 0) & (chip == chips - 1)))
        def _():
            reduce_end(1, pc_down, r2_down, ag_down)

        return carry

    lax.fori_loop(0, chips - chip, key_side, 0)

    dk, dv = acc_b[...] * scale, acc_c[...]
    part_sum = dot_nt(jnp.where(is_odd, pltpu.roll(dq, 64, axis=1), dq).astype(BF16), win[0])
    part_sum += dot_nt(jnp.where(is_odd, pltpu.roll(dk, 64, axis=1), dk).astype(BF16), win[1])
    part_sum += dot_nt(jnp.where(is_odd, dv, pltpu.roll(dv, 192, axis=1)).astype(BF16), win[2])
    gn2[...] = part_sum
    n2[...] = part_sum.astype(BF16)
    own_rows = pl.ds(pl.multiple_of(g * piece, piece), piece)

    def row_copies():
        found = []
        for step in range(1, NGRP):
            peer = lax.rem(g + step, NGRP)
            rows_of = pl.ds(pl.multiple_of(peer * piece, piece), piece)
            copy = to_grp(peer, n2.at[rows_of, :], drecv.at[g], zd_ssem.at[step - 1], zd_rsem.at[g])
            found.append((always, copy))
        return found

    launch("rows", row_copies)

    dpack = ghid.at[:, 0:384]
    dpack[:, 0:128] = dk[:, 0:128].astype(BF16)
    dpack[:, 128:256] = join_halves(dk[:, 128:256], dv[:, 0:128]).astype(BF16)
    dpack[:, 256:384] = dv[:, 128:256].astype(BF16)
    weight_pieces(pc_ekv, dot_tn(n1[...], dpack[...]))
    reduce_start(3, pc_ekv, r1_ekv)
    chain_step(1, *weight_gather(1, ag_down))
    reduce_end(2, pc_eq, r2_eq, ag_eq)

    def through_down(i, carry):
        at = pl.ds(pl.multiple_of(i * 256, 256), 256)
        out_ref[:, at] = (middle[:, at] + dot_nn(active[...], down_all[:, at])).astype(BF16)
        return carry

    lax.fori_loop(0, D // 256, through_down, 0)
    reduce_pass(3, pc_ekv, r1_ekv, r2_ekv)
    chain_step(2, *weight_gather(1, ag_down))
    chain_step(1, *weight_gather(2, ag_eq))

    upstream = gn2[own_rows, :]
    for step in range(1, NGRP):
        slot = lax.rem(g + step, NGRP)
        to_grp(slot, drecv.at[slot], drecv.at[slot], zd_ssem.at[0], zd_rsem.at[slot]).wait_recv()
        upstream = upstream + drecv[slot].astype(F32)
    value = tok_ref[own_rows, :].astype(F32)
    centered = value - jnp.mean(value, axis=1, keepdims=True)
    inverse = lax.rsqrt(jnp.mean(centered * centered, axis=1, keepdims=True) + EPS)
    plain = centered * inverse
    scaled = upstream * gain1
    inner = (
        scaled
        - jnp.mean(scaled, axis=1, keepdims=True)
        - plain * jnp.mean(scaled * plain, axis=1, keepdims=True)
    )
    tz[g] = (gmid[own_rows, :] + inverse * inner).astype(BF16)
    token_gather = ("token", lambda i: tz.at[i], zt_ssem, zt_rsem)
    direct_start(*token_gather)
    stat[s, 2:3, :] = jnp.sum(upstream * plain, axis=0, keepdims=True)
    stat[s, 3:4, :] = jnp.sum(upstream, axis=0, keepdims=True)

    def stat_copies():
        found = []
        for step in range(1, NSEQ):
            peer = lax.rem(s + step, NSEQ)
            copy = to_seq(peer, stat.at[s], stat.at[s], st_ssem.at[step - 1], st_rsem.at[s])
            found.append((always, copy))
        return found

    launch("stat", stat_copies)
    reduce_end(3, pc_ekv, r2_ekv, ag_ekv)
    chain_step(2, *weight_gather(2, ag_eq))

    for step in range(1, NSEQ):
        slot = lax.rem(s + step, NSEQ)
        to_seq(sib, stat.at[slot], stat.at[slot], st_ssem.at[0], st_rsem.at[slot]).wait_recv()
    total_stat = stat[0]
    for i in range(1, NSEQ):
        total_stat = total_stat + stat[i]
    stat_z[g] = total_stat
    direct_start("stat z", lambda i: stat_z.at[i], sz_ssem, sz_rsem)

    chain_step(3, *weight_gather(0, ag_up))
    chain_step(1, *weight_gather(3, ag_ekv))
    for i in range(NGRP):
        oup_ref[:, D * i : D * i + D] = ag_up[i]
    chain_step(3, *weight_gather(1, ag_down))
    chain_step(2, *weight_gather(3, ag_ekv))
    for i in range(3):
        odown_ref[:, width * i : width * i + width] = jnp.transpose(ag_down[i].astype(F32)).astype(BF16)
    for i in range(2):
        oexit_ref[:, T * i : T * i + T] = ag_down[3, piece * i : piece * i + piece, :]
    chain_step(3, *weight_gather(2, ag_eq))

    def place_entry(first, tiles):
        for tile, value in enumerate(tiles):
            at = first + tile * LANES
            oentry_ref[:, at : at + LANES] = value.astype(BF16)

    for pair in range(NGRP // 2):
        a = ag_eq[2 * pair].astype(F32)
        b = ag_eq[2 * pair + 1].astype(F32)
        turned = swap_halves(b[:, 0:128])
        place_entry(
            pair * 2 * part,
            (
                a[:, 0:128],
                join_halves(a[:, 128:256], turned),
                join_halves(turned, swap_halves(b[:, 128:256])),
            ),
        )
    direct_wait(*token_gather)
    for i in range(NGRP):
        tgrad_ref[piece * i : piece * i + piece, :] = tz[i]
    total_stat = jnp.zeros((8, D), F32)
    for step in range(1, NGRP):
        slot = lax.rem(g + step, NGRP)
        to_grp(slot, stat_z.at[slot], stat_z.at[slot], sz_ssem.at[0], sz_rsem.at[slot]).wait_recv()
    for i in range(NGRP):
        total_stat = total_stat + stat_z[i]
    row_id = lax.broadcasted_iota(jnp.int32, (8, 1), 0)
    ostat_ref[...] = jnp.where(row_id < 2, stat_z[g], total_stat)
    chain_step(3, *weight_gather(3, ag_ekv))
    for pair in range(NGRP // 2):
        a = ag_ekv[2 * pair].astype(F32)
        b = ag_ekv[2 * pair + 1].astype(F32)
        turned = swap_halves(b[:, 0:128])
        place_entry(
            D + pair * 2 * part,
            (
                a[:, 0:128],
                join_halves(a[:, 128:256], turned),
                join_halves(turned, swap_halves(b[:, 128:256])),
            ),
        )
        turned = swap_halves(a[:, 256:384])
        place_entry(
            2 * D + pair * 2 * part,
            (
                join_halves(swap_halves(a[:, 128:256]), turned),
                join_halves(turned, b[:, 128:256]),
                b[:, 256:384],
            ),
        )

    for copies in launched.values():
        for cond, copy in copies():
            pl.when(cond)(copy.wait_send)


def finish_kernel(
    out_in,
    tgrad_in,
    entry_in,
    exit_in,
    up_in,
    down_in,
    stat_in,
    out_hbm,
    tgrad_hbm,
    entry_hbm,
    exit_hbm,
    up_hbm,
    down_hbm,
    fgain_ref,
    fbias_ref,
    sgain_ref,
    sbias_ref,
    out_low,
    tgrad_low,
    down_low,
    up_low,
    entry_low,
    exit_low,
    stat_low,
    down_full,
    up_full,
    entry_full,
    exit_full,
    sems,
):
    plans = (
        (down_in, down_low, down_full, down_hbm),
        (up_in, up_low, up_full, up_hbm),
        (entry_in, entry_low, entry_full, entry_hbm),
        (exit_in, exit_low, exit_full, exit_hbm),
        (out_in, out_low, out_low, out_hbm),
        (tgrad_in, tgrad_low, tgrad_low, tgrad_hbm),
    )
    loads = [
        pltpu.make_async_copy(source, low, sems.at[6 + i])
        for i, (source, low, _, _) in enumerate(plans)
    ]
    stat_load = pltpu.make_async_copy(stat_in, stat_low, sems.at[12])
    for copy in [*loads, stat_load]:
        copy.start()
    copies = []
    for i, (_, low, full, target) in enumerate(plans):
        loads[i].wait()
        if full is not low:
            full[...] = low[...].astype(F32)
        copy = pltpu.make_async_copy(full, target, sems.at[i])
        copy.start()
        copies.append(copy)
    stat_load.wait()
    width = stat_low.shape[1]
    part = fgain_ref.shape[0]
    first = lax.axis_index("seq") * part
    turned = pltpu.roll(stat_low[...], lax.rem(width - first, width), axis=1)
    fgain_ref[...] = turned[2:3, 0:part].reshape(part)
    fbias_ref[...] = turned[3:4, 0:part].reshape(part)
    sgain_ref[...] = turned[0:1, 0:part].reshape(part)
    sbias_ref[...] = turned[1:2, 0:part].reshape(part)
    for copy in copies:
        copy.wait()


def fast_on_device(
    seq_count,
    tokens,
    cotangent,
    entry_weight,
    exit_weight,
    up_weight,
    down_weight,
    first_gain,
    first_bias,
    second_gain,
    second_bias,
    dilations,
    offsets,
):
    T, D = tokens.shape
    NGRP, HEADS = offsets.shape
    FF = up_weight.shape[1]
    E = D // HEADS
    NSEQ = seq_count
    chips = NSEQ // 2
    sizes = (T, D, HEADS, E, FF, NSEQ, NGRP)
    piece = D // NSEQ
    vmem = pl.BlockSpec(memory_space=pltpu.VMEM)
    smem = pl.BlockSpec(memory_space=pltpu.SMEM)
    anywhere = pl.BlockSpec(memory_space=pl.ANY)
    dma = pltpu.SemaphoreType.DMA
    scratch = [
        pltpu.VMEM((3, D, 256), BF16),
        pltpu.VMEM((D, D), BF16),
        pltpu.VMEM((256, D), BF16),
        pltpu.VMEM((D, FF), BF16),
        pltpu.VMEM((FF, D), BF16),
        pltpu.VMEM((T, D), BF16),
        pltpu.VMEM((T, D), BF16),
        pltpu.VMEM((T, D), F32),
        pltpu.VMEM((T, D), F32),
        pltpu.VMEM((T, D), BF16),
        pltpu.VMEM((T, D), BF16),
        pltpu.VMEM((T, FF), BF16),
        pltpu.VMEM((T, FF), BF16),
        pltpu.VMEM((T, D), F32),
        pltpu.VMEM((3, T, LANES), BF16),
        pltpu.VMEM((3, T, (NSEQ + 2) * T), BF16),
        pltpu.VMEM((NSEQ, T, 384), BF16),
        pltpu.VMEM((NSEQ, T, 256), BF16),
        pltpu.VMEM((NSEQ, T, 256), BF16),
        pltpu.VMEM((6, T, 256), BF16),
        pltpu.VMEM((3, T, LANES), F32),
        pltpu.VMEM((T, 256), F32),
        pltpu.VMEM((T, 256), F32),
        pltpu.VMEM((T, 256), F32),
        pltpu.VMEM((T, 256), F32),
        pltpu.VMEM((T, 256), F32),
        pltpu.VMEM((NGRP, 3, T // 2, LANES), BF16),
        pltpu.VMEM((NGRP, piece, D), BF16),
        pltpu.VMEM((NGRP, piece, D), BF16),
        pltpu.VMEM((NSEQ, 8, D), F32),
        pltpu.VMEM((NGRP, 8, D), F32),
    ]
    for rows, cols in ((piece, D), (256, T), (piece, 256), (piece, 384)):
        scratch += [
            pltpu.VMEM((2, chips, rows, cols), BF16),
            pltpu.VMEM((chips, rows, cols), BF16),
            pltpu.VMEM((chips, rows, cols), BF16),
            pltpu.VMEM((NGRP, rows, cols), BF16),
        ]
    scratch += [
        dma((7,)),
        dma((7,)),
        dma((NSEQ,)),
        dma((7,)),
        dma((NSEQ,)),
        dma((7,)),
        dma((NSEQ,)),
        dma((NGRP - 1,)),
        dma((NGRP,)),
        dma((NGRP - 1,)),
        dma((NGRP,)),
        dma((NGRP - 1,)),
        dma((NGRP,)),
        dma((4,)),
        dma((4,)),
        dma((4, 3)),
        dma((4, chips)),
        dma((4, 3, 2)),
        dma((4, NGRP)),
        dma((NSEQ - 1,)),
        dma((NSEQ,)),
        dma((NGRP - 1,)),
        dma((NGRP,)),
    ]
    out_shape = (
        jax.ShapeDtypeStruct((T, D), BF16),
        jax.ShapeDtypeStruct((T, D), BF16),
        jax.ShapeDtypeStruct((piece, 3 * D), BF16),
        jax.ShapeDtypeStruct((piece, D), BF16),
        jax.ShapeDtypeStruct((piece, FF), BF16),
        jax.ShapeDtypeStruct((T, D), BF16),
        jax.ShapeDtypeStruct((8, D), F32),
    )
    output, token_grad, entry_grad, exit_grad, up_grad, down_grad, stats = pl.pallas_call(
        partial(layer_kernel, sizes),
        out_shape=out_shape,
        in_specs=[smem] * 2 + [vmem] * 6 + [anywhere] * 4,
        out_specs=tuple([vmem] * 7),
        scratch_shapes=scratch,
        compiler_params=pltpu.CompilerParams(
            collective_id=0, has_side_effects=True, vmem_limit_bytes=63 * 1024 * 1024
        ),
        name="layer",
    )(
        dilations,
        offsets,
        tokens,
        cotangent,
        first_gain,
        first_bias,
        second_gain,
        second_bias,
        entry_weight,
        exit_weight,
        up_weight,
        down_weight,
    )
    part = piece
    finish_shape = (
        jax.ShapeDtypeStruct((T, D), BF16),
        jax.ShapeDtypeStruct((T, D), BF16),
        jax.ShapeDtypeStruct((part, 3 * D), F32),
        jax.ShapeDtypeStruct((part, D), F32),
        jax.ShapeDtypeStruct((part, FF), F32),
        jax.ShapeDtypeStruct((T, D), F32),
    ) + tuple([jax.ShapeDtypeStruct((part,), F32)] * 4)
    return pl.pallas_call(
        finish_kernel,
        out_shape=finish_shape,
        in_specs=[anywhere] * 7,
        out_specs=tuple([anywhere] * 6 + [vmem] * 4),
        scratch_shapes=[
            pltpu.VMEM((T, D), BF16),
            pltpu.VMEM((T, D), BF16),
            pltpu.VMEM((T, D), BF16),
            pltpu.VMEM((part, FF), BF16),
            pltpu.VMEM((part, 3 * D), BF16),
            pltpu.VMEM((part, D), BF16),
            pltpu.VMEM((8, D), F32),
            pltpu.VMEM((T, D), F32),
            pltpu.VMEM((part, FF), F32),
            pltpu.VMEM((part, 3 * D), F32),
            pltpu.VMEM((part, D), F32),
            dma((13,)),
        ],
        compiler_params=pltpu.CompilerParams(vmem_limit_bytes=62 * 1024 * 1024),
        name="finish",
    )(output, token_grad, entry_grad, exit_grad, up_grad, down_grad, stats)


def solution(mesh):
    seq_count = mesh.shape["seq"]
    fast = seq_count == 8 and mesh.shape["grp"] == 4
    return jax.shard_map(
        partial(fast_on_device, seq_count) if fast else on_device,
        mesh=mesh,
        in_specs=(P("seq", None), P("seq", None), P(), P(), P(), P(), P(), P(), P(), P(), P(), P()),
        out_specs=(
            P("seq", None),
            P("seq", None),
            P("seq", None),
            P("seq", None),
            P("seq", None),
            P("seq", None),
            P("seq"),
            P("seq"),
            P("seq"),
            P("seq"),
        ),
        check_vma=False,
    )
```

```python
from functools import partial

import jax
import jax.numpy as jnp
from jax import lax
from jax.experimental import pallas as pl
from jax.experimental.pallas import tpu as pltpu
from jax.sharding import PartitionSpec as P

RATE_MIN = 2
RATE_MAX = 8


EPS = 1e-05
PRECISE = lax.Precision.HIGHEST


def norm_forward(values, gain_vec, bias_vec):
    centered = values - jnp.mean(values, axis=1, keepdims=True)
    inverse = lax.rsqrt(jnp.mean(centered * centered, axis=1, keepdims=True) + EPS)
    plain = centered * inverse
    return (plain * gain_vec + bias_vec, plain, inverse)


def norm_backward(upstream, plain, inverse, gain_vec):
    scaled = upstream * gain_vec
    inner = (
        scaled
        - jnp.mean(scaled, axis=1, keepdims=True)
        - plain * jnp.mean(scaled * plain, axis=1, keepdims=True)
    )
    return (inverse * inner, jnp.sum(upstream * plain, axis=0), jnp.sum(upstream, axis=0))


def key_weights(query_sp, query_pos, key_block, first_row, geometry):
    local_len, capacity, dilation, segment, head_offs, score_scale = geometry
    key_count = key_block.shape[0]
    key_heads = key_block.reshape(key_count, query_sp.shape[1], query_sp.shape[2])
    scores = (
        jnp.einsum("ihd,jhd->hij", query_sp, key_heads, preferred_element_type=jnp.float32)
        * score_scale
    )
    key_index = first_row + jnp.arange(key_count, dtype=jnp.int32)
    source = key_index // capacity
    within = key_index - source * capacity
    key_pos = source[None, :] * local_len + head_offs[:, None] + dilation * within[None, :]
    key_live = within < local_len // dilation
    earlier = key_pos[:, None, :] <= query_pos[:, :, None]
    segment_match = key_pos[:, None, :] // segment == query_pos[:, :, None] // segment
    allowed = earlier & segment_match & key_live[None, None, :]
    return (jnp.where(allowed, jnp.exp(scores), 0.0), key_heads)


def forward_block(running, pieces, first_row, query_sp, query_pos, geometry):
    numerator, denominator = running
    key_block, value_block = pieces
    weights, key_heads = key_weights(query_sp, query_pos, key_block, first_row, geometry)
    value_heads = value_block.reshape(key_heads.shape)
    numerator = numerator + jnp.einsum(
        "hij,jhd->hid",
        weights.astype(jnp.bfloat16),
        value_heads,
        preferred_element_type=jnp.float32,
    )
    return (numerator, denominator + jnp.sum(weights, axis=2))


def blockwise(step_fn, running, pieces, first_row, block_rows):
    total_rows = pieces[0].shape[0]
    if total_rows > block_rows and total_rows % block_rows == 0:
        number = total_rows // block_rows
        stacked_first = pieces[0].reshape(number, block_rows, pieces[0].shape[1])
        stacked_second = pieces[1].reshape(number, block_rows, pieces[1].shape[1])
        block_starts = first_row + block_rows * jnp.arange(number, dtype=jnp.int32)

        def advance(state, items):
            return (step_fn(state, (items[0], items[1]), items[2]), None)

        running, _ = lax.scan(advance, running, (stacked_first, stacked_second, block_starts))
        return running
    return step_fn(running, pieces, first_row)


def backward_block(running, items, query_sp, query_pos, grad_sp, shift_sp, geometry):
    key_block, value_block, first_row = items
    score_scale = geometry[5]
    weights, key_heads = key_weights(query_sp, query_pos, key_block, first_row, geometry)
    key_count = key_block.shape[0]
    value_heads = value_block.reshape(key_heads.shape)
    pressure = jnp.einsum("ihd,jhd->hij", grad_sp, value_heads, preferred_element_type=jnp.float32)
    slopes = (weights * (pressure - shift_sp[:, :, None])).astype(jnp.bfloat16)
    running = (
        running
        + jnp.einsum("hij,jhd->ihd", slopes, key_heads, preferred_element_type=jnp.float32)
        * score_scale
    )
    grad_keys = (
        jnp.einsum("hij,ihd->jhd", slopes, query_sp, preferred_element_type=jnp.float32)
        * score_scale
    )
    grad_values = jnp.einsum(
        "hij,ihd->jhd", weights.astype(jnp.bfloat16), grad_sp, preferred_element_type=jnp.float32
    )
    return (running, (grad_keys.reshape(key_count, -1), grad_values.reshape(key_count, -1)))


def local_weights(query_heads, key_heads, score_scale):
    local_len = query_heads.shape[0]
    scores = (
        jnp.einsum("ihd,jhd->hij", query_heads, key_heads, preferred_element_type=jnp.float32)
        * score_scale
    )
    positions = jnp.arange(local_len, dtype=jnp.int32)
    causal = positions[:, None] >= positions[None, :]
    return jnp.where(causal[None], jnp.exp(scores), 0.0)


def on_device(
    tokens,
    cotangent,
    entry_weight,
    exit_weight,
    up_weight,
    down_weight,
    first_gain,
    first_bias,
    second_gain,
    second_bias,
    dilations,
    offsets,
):
    local_len, width_model = tokens.shape
    head_count = offsets.shape[1]
    head_size = width_model // head_count
    score_scale = head_size ** (-0.5)
    capacity = local_len // RATE_MIN
    group_idx = lax.axis_index("grp")
    seq_index = lax.axis_index("seq")
    seq_count = lax.axis_size("seq")
    dilation = lax.dynamic_index_in_dim(dilations, group_idx, 0, keepdims=False)
    head_offs = lax.dynamic_index_in_dim(offsets, group_idx, 0, keepdims=False)
    segment = local_len * seq_count * dilation // RATE_MAX
    step_ids = jnp.arange(capacity, dtype=jnp.int32)
    row_live = step_ids < local_len // dilation
    local_rows = jnp.minimum(head_offs[:, None] + dilation * step_ids[None, :], local_len - 1)
    query_pos = jnp.where(
        row_live[None, :],
        seq_index * local_len + head_offs[:, None] + dilation * step_ids[None, :],
        -1,
    )
    geometry = (local_len, capacity, dilation, segment, head_offs, score_scale)
    head_shape = (local_len, head_count, head_size)
    selector = local_rows[:, :, None] == jnp.arange(local_len, dtype=jnp.int32)[None, None, :]
    select_low = selector.astype(jnp.bfloat16)
    select_full = selector.astype(jnp.float32)

    def pick(array_in):
        return jnp.einsum(
            "hci,ihd->chd", select_low, array_in, preferred_element_type=jnp.float32
        ).astype(jnp.bfloat16)

    def place_back(sparse_in):
        return jnp.einsum("hci,chd->ihd", select_full, sparse_in, precision=PRECISE)

    inputs = tokens.astype(jnp.float32)
    normed_one, plain_one, inverse_one = norm_forward(inputs, first_gain, first_bias)
    normed_low = normed_one.astype(jnp.bfloat16)
    packed = jnp.dot(normed_low, entry_weight, preferred_element_type=jnp.float32).astype(
        jnp.bfloat16
    )
    query_heads = packed[:, :width_model].reshape(head_shape)
    key_heads = packed[:, width_model : 2 * width_model].reshape(head_shape)
    value_heads = packed[:, 2 * width_model :].reshape(head_shape)
    query_sp = pick(query_heads)
    key_sp = pick(key_heads).reshape(capacity, width_model)
    value_sp = pick(value_heads).reshape(capacity, width_model)
    empty_state = (
        jnp.zeros((head_count, capacity, head_size), jnp.float32),
        jnp.zeros((head_count, capacity), jnp.float32),
    )
    forward_step = partial(forward_block, query_sp=query_sp, query_pos=query_pos, geometry=geometry)
    numerator, denominator = blockwise(
        forward_step,
        empty_state,
        (
            lax.all_gather(key_sp, "seq", axis=0, tiled=True),
            lax.all_gather(value_sp, "seq", axis=0, tiled=True),
        ),
        jnp.int32(0),
        8 * capacity,
    )

    def local_part(query_in, key_in, value_in):
        weights = local_weights(query_in, key_in, score_scale)
        local_num = jnp.einsum(
            "hij,jhd->ihd",
            weights.astype(jnp.bfloat16),
            value_in,
            preferred_element_type=jnp.float32,
        )
        return (local_num, jnp.sum(weights, axis=2).T)

    def local_none(query_in, key_in, value_in):
        return (jnp.zeros(head_shape, jnp.float32), jnp.zeros((local_len, head_count), jnp.float32))

    local_num, local_den = lax.cond(
        group_idx == 0, local_part, local_none, query_heads, key_heads, value_heads
    )
    numerator_full = (
        jnp.einsum("hci,hcd->ihd", select_full, numerator, precision=PRECISE) + local_num
    )
    denominator_full = (
        jnp.einsum("hci,hc->ih", select_full, denominator, precision=PRECISE) + local_den
    )
    merged_num, merged_den = lax.psum(
        (numerator_full.reshape(local_len, width_model), denominator_full), "grp"
    )
    attention = merged_num.reshape(head_shape) / merged_den[:, :, None]
    mixed = attention.reshape(local_len, width_model).astype(jnp.bfloat16)
    middle = inputs + jnp.dot(mixed, exit_weight, preferred_element_type=jnp.float32)
    normed_two, plain_two, inverse_two = norm_forward(middle, second_gain, second_bias)
    normed_two_low = normed_two.astype(jnp.bfloat16)
    hidden = jnp.dot(normed_two_low, up_weight, preferred_element_type=jnp.float32)
    active = jax.nn.gelu(hidden, approximate=False).astype(jnp.bfloat16)
    output = (middle + jnp.dot(active, down_weight, preferred_element_type=jnp.float32)).astype(
        jnp.bfloat16
    )
    down_grad = jnp.dot(active.T, cotangent, preferred_element_type=jnp.float32)
    grad_active = jnp.dot(cotangent, down_weight.T, preferred_element_type=jnp.float32)
    _, gelu_pull = jax.vjp(partial(jax.nn.gelu, approximate=False), hidden)
    grad_hidden = gelu_pull(grad_active)[0].astype(jnp.bfloat16)
    up_grad = jnp.dot(normed_two_low.T, grad_hidden, preferred_element_type=jnp.float32)
    grad_normed_two = jnp.dot(grad_hidden, up_weight.T, preferred_element_type=jnp.float32)
    grad_plain_two, second_gain_grad, second_bias_grad = norm_backward(
        grad_normed_two, plain_two, inverse_two, second_gain
    )
    grad_middle = cotangent.astype(jnp.float32) + grad_plain_two
    grad_branch = grad_middle.astype(jnp.bfloat16)
    exit_grad = jnp.dot(mixed.T, grad_branch, preferred_element_type=jnp.float32)
    grad_mixed_low = lax.optimization_barrier(
        jnp.dot(grad_branch, exit_weight.T, preferred_element_type=jnp.float32).astype(jnp.bfloat16)
    )
    grad_mixed = grad_mixed_low.astype(jnp.float32).reshape(head_shape)
    grad_numer = (grad_mixed / merged_den[:, :, None]).astype(jnp.bfloat16)
    row_shift = jnp.sum(grad_mixed * attention, axis=2) / merged_den
    grad_sp = pick(grad_numer)
    shift_sp = jnp.einsum("hci,ih->hc", select_full, row_shift, precision=PRECISE)
    back_keys, back_values = (
        lax.all_gather(key_sp, "seq", axis=0, tiled=True),
        lax.all_gather(value_sp, "seq", axis=0, tiled=True),
    )
    block_rows = 8 * capacity
    number = back_keys.shape[0] // block_rows
    stacked_keys = back_keys.reshape(number, block_rows, width_model)
    stacked_values = back_values.reshape(number, block_rows, width_model)
    block_starts = block_rows * jnp.arange(number, dtype=jnp.int32)
    empty_query = jnp.zeros((capacity, head_count, head_size), jnp.float32)
    back_step = partial(
        backward_block,
        query_sp=query_sp,
        query_pos=query_pos,
        grad_sp=grad_sp,
        shift_sp=shift_sp,
        geometry=geometry,
    )
    grad_query_sp, (grad_key_all, grad_value_all) = lax.scan(
        back_step, empty_query, (stacked_keys, stacked_values, block_starts)
    )
    own_keys, own_values = (
        lax.psum_scatter(
            grad_key_all.reshape(-1, width_model), "seq", scatter_dimension=0, tiled=True
        ),
        lax.psum_scatter(
            grad_value_all.reshape(-1, width_model), "seq", scatter_dimension=0, tiled=True
        ),
    )

    def local_grads(query_in, key_in, value_in, grad_in, shift_in):
        weights = local_weights(query_in, key_in, score_scale)
        pressure = jnp.einsum("ihd,jhd->hij", grad_in, value_in, preferred_element_type=jnp.float32)
        slopes = (weights * (pressure - shift_in.T[:, :, None])).astype(jnp.bfloat16)
        grad_query = (
            jnp.einsum("hij,jhd->ihd", slopes, key_in, preferred_element_type=jnp.float32)
            * score_scale
        )
        grad_key = (
            jnp.einsum("hij,ihd->jhd", slopes, query_in, preferred_element_type=jnp.float32)
            * score_scale
        )
        grad_value = jnp.einsum(
            "hij,ihd->jhd",
            weights.astype(jnp.bfloat16),
            grad_in,
            preferred_element_type=jnp.float32,
        )
        return (grad_query, grad_key, grad_value)

    def local_skip(query_in, key_in, value_in, grad_in, shift_in):
        zeros_heads = jnp.zeros(head_shape, jnp.float32)
        return (zeros_heads, zeros_heads, zeros_heads)

    local_dq, local_dk, local_dv = lax.cond(
        group_idx == 0,
        local_grads,
        local_skip,
        query_heads,
        key_heads,
        value_heads,
        grad_numer,
        row_shift,
    )
    grad_query_full = place_back(grad_query_sp) + local_dq
    grad_key_full = place_back(own_keys.reshape(capacity, head_count, head_size)) + local_dk
    grad_value_full = place_back(own_values.reshape(capacity, head_count, head_size)) + local_dv
    grad_packed = jnp.concatenate(
        [
            grad_query_full.reshape(local_len, width_model),
            grad_key_full.reshape(local_len, width_model),
            grad_value_full.reshape(local_len, width_model),
        ],
        axis=1,
    )
    summed = lax.psum(grad_packed, "grp").astype(jnp.bfloat16)
    entry_grad = jnp.dot(normed_low.T, summed, preferred_element_type=jnp.float32)
    grad_normed_one = jnp.dot(summed, entry_weight.T, preferred_element_type=jnp.float32)
    grad_plain_one, first_gain_grad, first_bias_grad = norm_backward(
        grad_normed_one, plain_one, inverse_one, first_gain
    )
    token_grad = (grad_middle + grad_plain_one).astype(jnp.bfloat16)
    shards = (
        lax.psum_scatter(entry_grad, "seq", scatter_dimension=0, tiled=True),
        lax.psum_scatter(exit_grad, "seq", scatter_dimension=0, tiled=True),
        lax.psum_scatter(up_grad, "seq", scatter_dimension=0, tiled=True),
        lax.psum_scatter(down_grad, "seq", scatter_dimension=0, tiled=True),
        lax.psum_scatter(first_gain_grad, "seq", scatter_dimension=0, tiled=True),
        lax.psum_scatter(first_bias_grad, "seq", scatter_dimension=0, tiled=True),
        lax.psum_scatter(second_gain_grad, "seq", scatter_dimension=0, tiled=True),
        lax.psum_scatter(second_bias_grad, "seq", scatter_dimension=0, tiled=True),
    )
    return (
        output,
        token_grad,
        shards[0],
        shards[1],
        shards[2],
        shards[3],
        shards[4],
        shards[5],
        shards[6],
        shards[7],
    )


MESH = pl.DeviceIdType.MESH
LANES = 128
LOG2E = 1.4426950408889634
F32 = jnp.float32
BF16 = jnp.bfloat16


def dot_nn(left, right):
    return lax.dot_general(left, right, (((1,), (0,)), ((), ())), preferred_element_type=F32)


def dot_nt(left, right):
    return lax.dot_general(left, right, (((1,), (1,)), ((), ())), preferred_element_type=F32)


def dot_tn(left, right):
    return lax.dot_general(left, right, (((0,), (0,)), ((), ())), preferred_element_type=F32)


def lane_ids(width):
    return lax.broadcasted_iota(jnp.int32, (1, width), 1)


def slot_mask(slot, width=256):
    ids = lane_ids(width)
    return jnp.where((ids >= 64 * slot) & (ids < 64 * slot + 64), 1.0, 0.0).astype(F32)


def join_halves(low_part, high_part):
    return jnp.where(lane_ids(LANES) < 64, low_part, high_part)


def swap_halves(tile):
    return pltpu.roll(tile, 64, axis=1)


def layer_kernel(
    sizes,
    dil_ref,
    off_ref,
    tok_ref,
    cot_ref,
    gain1_ref,
    bias1_ref,
    gain2_ref,
    bias2_ref,
    entry_hbm,
    exit_hbm,
    up_hbm,
    down_hbm,
    out_ref,
    tgrad_ref,
    oentry_ref,
    oexit_ref,
    oup_ref,
    odown_ref,
    ostat_ref,
    win,
    exit_all,
    up_all,
    down_all,
    n1,
    n2,
    middle,
    gmid,
    gbranch,
    mixed,
    active,
    ghid,
    gn2,
    member,
    masks,
    kv,
    qb,
    dob,
    qmask,
    shift,
    invden,
    att,
    acc_a,
    acc_b,
    acc_c,
    zmix,
    drecv,
    tz,
    stat,
    stat_z,
    r1_exit,
    r2_exit,
    r1_down,
    r2_down,
    pc_up,
    r1_up,
    r2_up,
    ag_up,
    pc_eq,
    r1_eq,
    r2_eq,
    ag_eq,
    pc_ekv,
    r1_ekv,
    r2_ekv,
    ag_ekv,
    load_sem,
    kv_ssem,
    kv_rsem,
    q_ssem,
    q_rsem,
    do_ssem,
    do_rsem,
    zm_ssem,
    zm_rsem,
    zd_ssem,
    zd_rsem,
    zt_ssem,
    zt_rsem,
    rs_s1,
    rs_r1,
    rs_s2,
    rs_r2,
    rs_zs,
    rs_zr,
    st_ssem,
    st_rsem,
    sz_ssem,
    sz_rsem,
):
    T, D, HEADS, E, FF, NSEQ, NGRP = sizes
    scale = E ** (-0.5)
    exp_scale = scale * LOG2E
    s = lax.axis_index("seq")
    g = lax.axis_index("grp")
    chip = s // 2
    core = s % 2
    sib = s + 1 - 2 * core
    odd = g % 2
    chips = NSEQ // 2
    part = D // NGRP
    is_odd = odd == 1
    gain1 = gain1_ref[...].reshape(1, D)
    bias1 = bias1_ref[...].reshape(1, D)
    gain2 = gain2_ref[...].reshape(1, D)
    bias2 = bias2_ref[...].reshape(1, D)

    def to_seq(peer, src, dst, ssem, rsem):
        return pltpu.make_async_remote_copy(
            src_ref=src,
            dst_ref=dst,
            send_sem=ssem,
            recv_sem=rsem,
            device_id={"seq": peer},
            device_id_type=MESH,
        )

    def to_grp(peer, src, dst, ssem, rsem):
        return pltpu.make_async_remote_copy(
            src_ref=src,
            dst_ref=dst,
            send_sem=ssem,
            recv_sem=rsem,
            device_id={"grp": peer},
            device_id_type=MESH,
        )

    loads = []
    for t in range(3):
        first = pl.multiple_of(t * D + part * g - 64 * odd, LANES)
        loads.append(
            pltpu.make_async_copy(entry_hbm.at[:, pl.ds(first, 256)], win.at[t], load_sem.at[t])
        )
    loads.append(pltpu.make_async_copy(down_hbm, down_all, load_sem.at[3]))
    loads.append(pltpu.make_async_copy(exit_hbm, exit_all, load_sem.at[4]))
    loads.append(pltpu.make_async_copy(up_hbm, up_all, load_sem.at[5]))
    for load in loads[:3]:
        load.start()

    barrier = pltpu.get_barrier_semaphore()
    for step in range(1, NSEQ):
        pl.semaphore_signal(
            barrier, inc=1, device_id={"seq": lax.rem(s + step, NSEQ)}, device_id_type=MESH
        )
    for step in range(1, NGRP):
        pl.semaphore_signal(
            barrier, inc=1, device_id={"grp": lax.rem(g + step, NGRP)}, device_id_type=MESH
        )

    rows = D // NSEQ

    def norm_one(i, carry):
        at = pl.ds(pl.multiple_of(i * rows, rows), rows)
        value = tok_ref[at, :].astype(F32)
        centered = value - jnp.mean(value, axis=1, keepdims=True)
        inverse = lax.rsqrt(jnp.mean(centered * centered, axis=1, keepdims=True) + EPS)
        n1[at, :] = (centered * inverse * gain1 + bias1).astype(BF16)
        return carry

    lax.fori_loop(0, T // rows, norm_one, 0)

    for load in loads[:3]:
        load.wait()
    for load in loads[3:]:
        load.start()
    lane256 = lane_ids(256)
    q_raw = dot_nn(n1[...], win[0])
    k_raw = dot_nn(n1[...], win[1])
    v_raw = dot_nn(n1[...], win[2])
    q_own = jnp.where(is_odd, pltpu.roll(q_raw, 192, axis=1), q_raw)
    k_own = jnp.where(is_odd, pltpu.roll(k_raw, 192, axis=1), k_raw)
    v_own = jnp.where(is_odd, v_raw, pltpu.roll(v_raw, 64, axis=1))
    q_own = jnp.where(lane256 < 192, q_own, 0.0)
    qb[s] = q_own.astype(BF16)
    for h in range(3):
        qmask[h] = (q_own * slot_mask(h)).astype(BF16)
    kv[s, :, 0:128] = k_own[:, 0:128].astype(BF16)
    kv[s, :, 128:256] = join_halves(k_own[:, 128:256], v_own[:, 0:128]).astype(BF16)
    kv[s, :, 256:384] = v_own[:, 128:256].astype(BF16)

    pl.semaphore_wait(barrier, NSEQ - 1 + NGRP - 1)

    launched = {}

    def launch(name, copies):
        for cond, copy in copies():
            pl.when(cond)(copy.start)
        launched[name] = copies

    always = core >= 0

    def spread(name, buffer, ssem, rsem, upward):
        def copies():
            found = []
            for d in range(1, chips):
                peer = lax.rem(s + (2 * d if upward else NSEQ - 2 * d), NSEQ)
                cond = chip + d < chips if upward else chip >= d
                found.append(
                    (cond, to_seq(peer, buffer.at[s], buffer.at[s], ssem.at[d - 1], rsem.at[s]))
                )
            found.append((always, to_seq(sib, buffer.at[s], buffer.at[s], ssem.at[3], rsem.at[s])))
            return found

        launch(name, copies)

    spread("kv", kv, kv_ssem, kv_rsem, True)
    spread("q", qb, q_ssem, q_rsem, False)

    lane128 = lane_ids(LANES)
    rate_row = jnp.ones((1, LANES), F32)
    for i in range(NGRP):
        rate_row = jnp.where(lane128 == i, dil_ref[i].astype(F32), rate_row)
    local_pos = lax.broadcasted_iota(jnp.int32, (T, 1), 0).astype(F32)
    residue = local_pos - rate_row * jnp.floor((local_pos + 0.5) / rate_row)
    for h in range(3):
        off_row = jnp.full((1, LANES), -1.0, F32)
        for i in range(NGRP):
            off_row = jnp.where(
                lane128 == i, off_ref[i, 3 * g + h].astype(F32), off_row
            )
        member[h] = jnp.where(residue == off_row, 1.0, 0.0).astype(BF16)
    per_segment = rate_row * (T * NSEQ // RATE_MAX)

    def segment_of(block):
        return jnp.floor((jnp.full((1, LANES), block * T, jnp.int32).astype(F32) + 0.5) / per_segment)

    own_segment = segment_of(s)

    pair_width = 2 * T

    def pair_lanes(cc):
        return pl.ds(pl.multiple_of(cc * pair_width, LANES), pair_width)

    def build_mask(cc, carry):
        for h in range(3):
            blocks = []
            for i in range(2):
                same = jnp.where(segment_of(2 * cc + i) == own_segment, 1.0, 0.0)
                blocks.append((member[h].astype(F32) * same).astype(BF16))
            count = dot_nt(member[h], jnp.concatenate(blocks, axis=0))
            masks[h, :, pair_lanes(cc)] = count.astype(BF16)
        return carry

    lax.fori_loop(0, chips, build_mask, 0)
    own_id = lax.broadcasted_iota(jnp.int32, (T, pair_width), 0) + core * T
    pair_id = lax.broadcasted_iota(jnp.int32, (T, pair_width), 1)
    own_block = (pair_id >= core * T) & (pair_id < core * T + T)
    for h in range(3):
        count = masks[h, :, pair_lanes(chip)].astype(F32) + jnp.where(own_block, 1.0, 0.0)
        masks[h, :, pair_lanes(chip)] = jnp.where(pair_id <= own_id, count, 0.0).astype(BF16)
        masks[h, :, pair_lanes(chips)] = jnp.where(own_id <= pair_id, count, 0.0).astype(BF16)

    half = T // 2
    piece = D // NSEQ

    def pack_half(tile, high):
        top, bottom = tile[0:half], tile[half:T]
        if high:
            return join_halves(swap_halves(top), bottom).astype(BF16)
        return join_halves(top, swap_halves(bottom)).astype(BF16)

    right, left = lax.rem(g + 1, NGRP), lax.rem(g + NGRP - 1, NGRP)

    def chain_start(name, at, ssem, rsem):
        launch(
            name + "0",
            lambda: [
                (g + 1 < NGRP, to_grp(right, at(g), at(g), ssem().at[0, 0], rsem().at[g])),
                (g >= 1, to_grp(left, at(g), at(g), ssem().at[0, 1], rsem().at[g])),
            ],
        )

    def chain_step(d, name, at, ssem, rsem):
        def slots():
            return lax.rem(g - d + NGRP, NGRP), lax.rem(g + d, NGRP)

        def copies():
            lower, upper = slots()
            return [
                (
                    (g - d >= 0) & (g + 1 < NGRP),
                    to_grp(right, at(lower), at(lower), ssem().at[d, 0], rsem().at[lower]),
                ),
                (
                    (g + d < NGRP) & (g >= 1),
                    to_grp(left, at(upper), at(upper), ssem().at[d, 1], rsem().at[upper]),
                ),
            ]

        lower, upper = slots()
        pl.when(g - d >= 0)(
            to_grp(right, at(lower), at(lower), ssem().at[0, 0], rsem().at[lower]).wait_recv
        )
        pl.when(g + d < NGRP)(
            to_grp(left, at(upper), at(upper), ssem().at[0, 1], rsem().at[upper]).wait_recv
        )
        if d < NGRP - 1:
            launch(name + str(d), copies)

    def weight_direct(name, at, ssem, rsem):
        def copies():
            found = []
            for step in range(1, NGRP):
                peer = lax.rem(g + step, NGRP)
                found.append((always, to_grp(peer, at(g), at(g), ssem().at[step - 1, 0], rsem().at[g])))
            return found

        launch(name, copies)

    def weight_wait(name, at, ssem, rsem):
        for step in range(1, NGRP):
            slot = lax.rem(g + step, NGRP)
            to_grp(slot, at(slot), at(slot), ssem().at[0, 0], rsem().at[slot]).wait_recv()

    def chain_parts(name, views, ssem, rsem):
        return [
            (name + str(i), view, lambda i=i: ssem.at[i], lambda i=i: rsem.at[i])
            for i, view in enumerate(views)
        ]

    def chain_finish(parts):
        for d in range(1, NGRP):
            for part_of in parts:
                chain_step(d, *part_of)

    def direct_start(name, at, ssem, rsem):
        def copies():
            found = []
            for step in range(1, NGRP):
                peer = lax.rem(g + step, NGRP)
                found.append((always, to_grp(peer, at(g), at(g), ssem.at[step - 1], rsem.at[g])))
            return found

        launch(name, copies)

    def direct_wait(name, at, ssem, rsem):
        for step in range(1, NGRP):
            slot = lax.rem(g + step, NGRP)
            to_grp(slot, at(slot), at(slot), ssem.at[0], rsem.at[slot]).wait_recv()

    loads[3].wait()

    def cot_times_down(i, carry):
        at = pl.ds(pl.multiple_of(i * T, T), T)
        ghid[:, at] = dot_nt(cot_ref[...], down_all[at, :]).astype(BF16)
        return carry

    lax.fori_loop(0, FF // T, cot_times_down, 0)

    acc_a[...] = jnp.zeros_like(acc_a)
    shift[...] = jnp.zeros_like(shift)

    def pair_of(ref, cc, first, last):
        return ref[pl.ds(2 * cc, 2), :, first:last].reshape(pair_width, last - first)

    def weights_of(score, count):
        count = count.astype(F32)
        return jnp.where(count > 0.5, jnp.exp2(score * exp_scale) * count, 0.0)

    def wait_pair(buffer, ssem, rsem, j, cc):
        mine, other = 2 * cc + core, 2 * cc + 1 - core

        @pl.when(j > 0)
        def _():
            to_seq(sib, buffer.at[mine], buffer.at[mine], ssem.at[0], rsem.at[mine]).wait_recv()
            to_seq(sib, buffer.at[mine], buffer.at[mine], ssem.at[3 + j], rsem.at[mine]).start()

        to_seq(sib, buffer.at[other], buffer.at[other], ssem.at[0], rsem.at[other]).wait_recv()

    def forward_step(j, carry):
        cc = chip - j
        wait_pair(kv, kv_ssem, kv_rsem, j, cc)
        keys = pair_of(kv, cc, 0, 256)
        values = pair_of(kv, cc, 128, 384)
        for h in range(3):
            weight = weights_of(dot_nt(qmask[h], keys), masks[h, :, pair_lanes(cc)])
            row_sum = weight[:, 0:LANES]
            for i in range(1, pair_width // LANES):
                row_sum = row_sum + weight[:, LANES * i : LANES * i + LANES]
            shift[h] += row_sum
            low_weight = weight.astype(BF16)
            masks[h, :, pair_lanes(cc)] = low_weight
            acc_a[...] += dot_nn(low_weight, values) * slot_mask(h + 1)
        return carry

    lax.fori_loop(0, chip + 1, forward_step, 0)
    inverse = jnp.zeros((T, 256), F32)
    for h in range(3):
        inverse += slot_mask(h + 1) / jnp.sum(shift[h], axis=1, keepdims=True)
    att_own = acc_a[...] * inverse
    invden[...] = inverse
    att[...] = att_own
    for h in range(3):
        tile = att_own[:, 0:128] if h == 0 else att_own[:, 128:256]
        zmix[g, h] = pack_half(tile, h != 1)
    quarter = half // 2
    mixed_gather = chain_parts(
        "mixed",
        (lambda i: zmix.at[i, :, 0:quarter], lambda i: zmix.at[i, :, quarter:half]),
        zm_ssem,
        zm_rsem,
    )
    for part_of in mixed_gather:
        chain_start(*part_of)

    for d in range(1, chips):

        @pl.when(chip + d < chips)
        def _(d=d):
            slot = lax.rem(s + 2 * d, NSEQ)
            to_seq(sib, qb.at[slot], qb.at[slot], q_ssem.at[0], q_rsem.at[slot]).wait_recv()

    def hand_on(buffer, ssem, rsem, upward):
        found = []
        for d in range(1, chips):
            slot = lax.rem(s + (NSEQ - 2 * d if upward else 2 * d), NSEQ)
            cond = chip >= d if upward else chip + d < chips
            found.append(
                (cond, to_seq(sib, buffer.at[slot], buffer.at[slot], ssem.at[3 + d], rsem.at[slot]))
            )
        return found

    launch("q on", lambda: hand_on(qb, q_ssem, q_rsem, False))
    launched["kv on"] = lambda: hand_on(kv, kv_ssem, kv_rsem, True)
    launched["do on"] = lambda: hand_on(dob, do_ssem, do_rsem, False)

    chain_finish(mixed_gather)
    for tile in range(D // LANES):
        (g_a, h_a), (g_b, h_b) = divmod(2 * tile, 3), divmod(2 * tile + 1, 3)
        first_head = zmix[g_a, h_a].astype(F32)
        second_head = zmix[g_b, h_b].astype(F32)
        cols = slice(tile * LANES, tile * LANES + LANES)
        mixed[0:half, cols] = join_halves(first_head, swap_halves(second_head)).astype(BF16)
        mixed[half:T, cols] = join_halves(swap_halves(first_head), second_head).astype(BF16)

    loads[4].wait()
    middle[...] = tok_ref[...].astype(F32) + dot_nn(mixed[...], exit_all[...])

    def norm_two(i, carry):
        at = pl.ds(pl.multiple_of(i * rows, rows), rows)
        value = middle[at, :]
        centered = value - jnp.mean(value, axis=1, keepdims=True)
        inverse = lax.rsqrt(jnp.mean(centered * centered, axis=1, keepdims=True) + EPS)
        plain = centered * inverse
        n2[at, :] = (plain * gain2 + bias2).astype(BF16)
        return carry

    lax.fori_loop(0, T // rows, norm_two, 0)

    class Stacked:
        def __init__(self, pieces, first_in, second_in):
            self.pieces, self.first_in, self.second_in = pieces, first_in, second_in

        def whole(self, k):
            return self.pieces.at[k]

        def block(self, k, cc):
            return self.pieces.at[k, cc]

        def first(self, cc):
            return self.first_in.at[cc]

    class Tiled(Stacked):
        def rows(self, k):
            count = self.first_in.shape[0]
            return pl.ds(pl.multiple_of(count * k, count), count)

        def cols(self, cc):
            return pl.ds(pl.multiple_of(D * cc, LANES), D)

        def whole(self, k):
            return self.pieces.at[self.rows(k), :]

        def block(self, k, cc):
            return self.pieces.at[self.rows(k), self.cols(cc)]

        def first(self, cc):
            return self.first_in.at[:, self.cols(cc)]

    sum_up = Stacked(pc_up, r1_up, r2_up)
    sum_down = Tiled(up_all, r1_down, r2_down)
    sum_eq = Stacked(pc_eq, r1_eq, r2_eq)
    sum_ekv = Stacked(pc_ekv, r1_ekv, r2_ekv)
    sum_exit = Tiled(ghid, r1_exit, r2_exit)

    def reduce_start(i, parts):
        launch(
            f"first{i}",
            lambda: [
                (
                    always,
                    to_seq(sib, parts.whole(1 - core), parts.first_in, rs_s1.at[i], rs_r1.at[i]),
                )
            ],
        )

    def reduce_pass(i, parts):
        to_seq(sib, parts.whole(core), parts.first_in, rs_s1.at[i], rs_r1.at[i]).wait_recv()

        def add(cc, carry):
            block = parts.block(core, cc)
            block[...] = (block[...].astype(F32) + parts.first(cc)[...].astype(F32)).astype(BF16)
            return carry

        lax.fori_loop(0, chips, add, 0)

        def copies():
            found = []
            for d in range(1, chips):
                to_chip = lax.rem(chip + d, chips)
                copy = to_seq(
                    2 * to_chip + core,
                    parts.block(core, to_chip),
                    parts.second_in.at[chips - d - 1],
                    rs_s2.at[i, d - 1],
                    rs_r2.at[i, chips - d - 1],
                )
                found.append((always, copy))
            return found

        launch(f"second{i}", copies)

    def reduce_end(i, parts):
        result = parts.block(core, chip)[...].astype(F32)
        for d in range(1, chips):
            landed = parts.second_in.at[d - 1]
            to_seq(sib, landed, landed, rs_s1.at[i], rs_r2.at[i, d - 1]).wait_recv()
            result = result + landed[...].astype(F32)
        return result.astype(BF16)

    def weight_gather(i, gathered):
        return ("weight" + str(i), lambda j: gathered.at[j], lambda: rs_zs.at[i], lambda: rs_zr.at[i])

    def gather_sum(i, parts, gathered):
        gathered[g] = reduce_end(i, parts)
        weight_direct(*weight_gather(i, gathered))

    loads[5].wait()
    def feed_forward(i, carry):
        c = lax.rem(g + i, NGRP)
        at = pl.ds(pl.multiple_of(c * D, LANES), D)
        hidden = dot_nn(n2[...], up_all[:, at])
        cdf = 0.5 + 0.5 * lax.erf(hidden * (0.5**0.5))
        low_active = (hidden * cdf).astype(BF16)
        active[:, at] = low_active
        density = jnp.exp2(hidden * hidden * (-0.5 * LOG2E)) * 0.3989422804014327
        ghid[:, at] = (ghid[:, at].astype(F32) * (cdf + hidden * density)).astype(BF16)

        @pl.when(i == 0)
        def _():
            for j in range(2):
                up_grad = dot_tn(n2[...], ghid[:, pl.ds(pl.multiple_of(g * D + T * j, LANES), T)])
                for t in range(NSEQ):
                    pc_up[t % 2, t // 2, :, T * j : T * j + T] = up_grad[
                        piece * t : piece * t + piece, :
                    ].astype(BF16)
            reduce_start(0, sum_up)

        @pl.when(i == 1)
        def _():
            reduce_pass(0, sum_up)

        return carry

    lax.fori_loop(0, NGRP, feed_forward, 0)

    def back_through_up(i, carry):
        at = pl.ds(pl.multiple_of(i * 256, 256), 256)
        gn2[:, at] = dot_nt(ghid[...], up_all[at, :])
        return carry

    lax.fori_loop(0, D // 256, back_through_up, 0)

    stat[s] = jnp.zeros((8, D), F32)

    def norm_two_back(i, carry):
        at = pl.ds(pl.multiple_of(i * rows, rows), rows)
        upstream = gn2[at, :]
        value = middle[at, :]
        centered = value - jnp.mean(value, axis=1, keepdims=True)
        inverse = lax.rsqrt(jnp.mean(centered * centered, axis=1, keepdims=True) + EPS)
        plain = centered * inverse
        scaled = upstream * gain2
        inner = (
            scaled
            - jnp.mean(scaled, axis=1, keepdims=True)
            - plain * jnp.mean(scaled * plain, axis=1, keepdims=True)
        )
        grad = cot_ref[at, :].astype(F32) + inverse * inner

        @pl.when(i == g)
        def _():
            gmid[...] = grad

        gbranch[at, :] = grad.astype(BF16)
        stat[s, 0:1, :] += jnp.sum(upstream * plain, axis=0, keepdims=True)
        stat[s, 1:2, :] += jnp.sum(upstream, axis=0, keepdims=True)
        return carry

    lax.fori_loop(0, T // rows, norm_two_back, 0)

    window = pl.ds(pl.multiple_of(jnp.maximum(part * g - 64, 0), 64), 256)
    gmix = dot_nt(gbranch[...], exit_all[window, :])
    gmix = jnp.where(g == 0, pltpu.roll(gmix, 64, axis=1), gmix)
    gmix = jnp.where(lane256 < 64, 0.0, gmix).astype(BF16).astype(F32)
    numer_grad = gmix * invden[...]
    product = numer_grad * att[...]
    for h in range(3):
        value = jnp.sum(product * slot_mask(h + 1), axis=1, keepdims=True)
        shift[h] = jnp.broadcast_to(value, (T, LANES))
        high = value.astype(BF16).astype(F32)
        low = value - high
        numer_grad = jnp.where(lane256 == 2 * h, high, numer_grad)
        numer_grad = jnp.where(lane256 == 2 * h + 1, low, numer_grad)
    dob[s] = numer_grad.astype(BF16)

    spread("do", dob, do_ssem, do_rsem, False)


    def down_piece(t, carry):
        at = pl.ds(pl.multiple_of(t * T, T), T)
        sum_down.block(t % 2, t // 2)[...] = dot_tn(active[:, at], cot_ref[...]).astype(BF16)
        return carry

    lax.fori_loop(0, NSEQ, down_piece, 0)
    reduce_start(1, sum_down)
    for i in range(2):
        exit_grad = dot_tn(mixed[...], gbranch[:, T * i : T * i + T]).astype(BF16)
        for t in range(NSEQ):
            first, low = D * (t // 2) + T * i, piece * (t % 2)
            ghid[low : low + piece, first : first + T] = exit_grad[piece * t : piece * t + piece, :]
    reduce_start(4, sum_exit)

    for h in range(3):
        qmask[h] = (dob[s].astype(F32) * slot_mask(h + 1)).astype(BF16)
    acc_a[...] = jnp.zeros_like(acc_a)

    def query_side(cc, carry):
        keys = pair_of(kv, cc, 0, 256)
        values = pair_of(kv, cc, 128, 384)
        for h in range(3):
            row_shift = jnp.concatenate([shift[h]] * (pair_width // LANES), axis=1)
            pressure = dot_nt(qmask[h], values) - row_shift
            slope = (masks[h, :, pair_lanes(cc)].astype(F32) * pressure).astype(BF16)
            acc_a[...] += dot_nn(slope, keys) * slot_mask(h)
        return carry

    lax.fori_loop(0, chip + 1, query_side, 0)
    dq = acc_a[...] * scale
    gather_sum(0, sum_up, ag_up)

    def weight_pieces(pieces, grad):
        for t in range(NSEQ):
            pieces[t % 2, t // 2] = grad[piece * t : piece * t + piece, :].astype(BF16)

    weight_pieces(pc_eq, dot_tn(n1[...], dq.astype(BF16)))
    reduce_start(2, sum_eq)

    reduce_pass(4, sum_exit)

    v_tile = kv[s, :, 128:384].astype(F32)
    k_tile = kv[s, :, 0:256].astype(F32)
    for h in range(3):
        qmask[h] = (k_tile * slot_mask(h)).astype(BF16)
        minus = jnp.where((lane256 == 2 * h) | (lane256 == 2 * h + 1), -1.0, 0.0)
        qmask[3 + h] = (v_tile * slot_mask(h + 1) + minus).astype(BF16)
    acc_b[...] = jnp.zeros_like(acc_b)
    acc_c[...] = jnp.zeros_like(acc_c)

    def key_side(j, carry):
        cc = chip + j
        wait_pair(dob, do_ssem, do_rsem, j, cc)
        other = 2 * cc + 1 - core
        to_seq(sib, qb.at[other], qb.at[other], q_ssem.at[0], q_rsem.at[other]).wait_recv()
        queries = pair_of(qb, cc, 0, 256)
        grads = pair_of(dob, cc, 0, 256)
        for h in range(3):
            count = masks[h, :, pair_lanes(jnp.where(j == 0, chips, cc))]
            weight = weights_of(dot_nt(qmask[h], queries), count)
            slope = (weight * dot_nt(qmask[3 + h], grads)).astype(BF16)
            acc_b[...] += dot_nn(slope, queries) * slot_mask(h)
            acc_c[...] += dot_nn(weight.astype(BF16), grads) * slot_mask(h + 1)

        @pl.when(j == 0)
        def _():
            reduce_pass(2, sum_eq)

        return carry

    lax.fori_loop(0, chips - chip, key_side, 0)

    dk, dv = acc_b[...] * scale, acc_c[...]
    part_sum = dot_nt(jnp.where(is_odd, pltpu.roll(dq, 64, axis=1), dq).astype(BF16), win[0])
    part_sum += dot_nt(jnp.where(is_odd, pltpu.roll(dk, 64, axis=1), dk).astype(BF16), win[1])
    part_sum += dot_nt(jnp.where(is_odd, dv, pltpu.roll(dv, 192, axis=1)).astype(BF16), win[2])
    gn2[...] = part_sum
    n2[...] = part_sum.astype(BF16)
    own_rows = pl.ds(pl.multiple_of(g * piece, piece), piece)

    def row_copies():
        found = []
        for step in range(1, NGRP):
            peer = lax.rem(g + step, NGRP)
            rows_of = pl.ds(pl.multiple_of(peer * piece, piece), piece)
            copy = to_grp(peer, n2.at[rows_of, :], drecv.at[g], zd_ssem.at[step - 1], zd_rsem.at[g])
            found.append((always, copy))
        return found

    launch("rows", row_copies)

    def norm_one_sums(i, carry):
        at = pl.ds(pl.multiple_of(i * rows, rows), rows)
        value = tok_ref[at, :].astype(F32)
        centered = value - jnp.mean(value, axis=1, keepdims=True)
        inverse = lax.rsqrt(jnp.mean(centered * centered, axis=1, keepdims=True) + EPS)
        stat[s, 2:3, :] += jnp.sum(gn2[at, :] * (centered * inverse), axis=0, keepdims=True)
        stat[s, 3:4, :] += jnp.sum(gn2[at, :], axis=0, keepdims=True)
        return carry

    lax.fori_loop(0, T // rows, norm_one_sums, 0)

    def stat_copies():
        found = []
        for step in range(1, NSEQ):
            peer = lax.rem(s + step, NSEQ)
            copy = to_seq(peer, stat.at[s], stat.at[s], st_ssem.at[step - 1], st_rsem.at[s])
            found.append((always, copy))
        return found

    launch("stat", stat_copies)

    dpack = exit_all.at[0:T, 0:384]
    dpack[:, 0:128] = dk[:, 0:128].astype(BF16)
    dpack[:, 128:256] = join_halves(dk[:, 128:256], dv[:, 0:128]).astype(BF16)
    dpack[:, 256:384] = dv[:, 128:256].astype(BF16)
    weight_pieces(pc_ekv, dot_tn(n1[...], dpack[...]))
    reduce_start(3, sum_ekv)
    gather_sum(2, sum_eq, ag_eq)

    def through_down(i, carry):
        at = pl.ds(pl.multiple_of(i * 256, 256), 256)
        out_ref[:, at] = (middle[:, at] + dot_nn(active[...], down_all[:, at])).astype(BF16)
        return carry

    lax.fori_loop(0, D // 256, through_down, 0)
    reduce_pass(3, sum_ekv)
    reduce_pass(1, sum_down)

    upstream = gn2[own_rows, :]
    for step in range(1, NGRP):
        slot = lax.rem(g + step, NGRP)
        to_grp(slot, drecv.at[slot], drecv.at[slot], zd_ssem.at[0], zd_rsem.at[slot]).wait_recv()
        upstream = upstream + drecv[slot].astype(F32)
    value = tok_ref[own_rows, :].astype(F32)
    centered = value - jnp.mean(value, axis=1, keepdims=True)
    inverse = lax.rsqrt(jnp.mean(centered * centered, axis=1, keepdims=True) + EPS)
    plain = centered * inverse
    scaled = upstream * gain1
    inner = (
        scaled
        - jnp.mean(scaled, axis=1, keepdims=True)
        - plain * jnp.mean(scaled * plain, axis=1, keepdims=True)
    )
    tz[g] = (gmid[...] + inverse * inner).astype(BF16)
    middle_row = piece // 2
    token_gather = chain_parts(
        "token",
        (lambda i: tz.at[i, 0:middle_row], lambda i: tz.at[i, middle_row:piece]),
        zt_ssem,
        zt_rsem,
    )
    for part_of in token_gather:
        chain_start(*part_of)

    gather_sum(3, sum_ekv, ag_ekv)

    chain_finish(token_gather)

    for step in range(1, NSEQ):
        slot = lax.rem(s + step, NSEQ)
        to_seq(sib, stat.at[slot], stat.at[slot], st_ssem.at[0], st_rsem.at[slot]).wait_recv()
    total_stat = stat[0]
    for i in range(1, NSEQ):
        total_stat = total_stat + stat[i]
    stat_z[g] = total_stat
    direct_start("stat z", lambda i: stat_z.at[i], sz_ssem, sz_rsem)

    weight_wait(*weight_gather(0, ag_up))
    pass
    for i in range(NGRP):
        oup_ref[:, D * i : D * i + D] = ag_up[i]
    pass
    oexit_ref[...] = reduce_end(4, sum_exit)
    weight_wait(*weight_gather(2, ag_eq))

    def place_entry(first, tiles):
        for tile, value in enumerate(tiles):
            at = first + tile * LANES
            oentry_ref[:, at : at + LANES] = value.astype(BF16)

    for pair in range(NGRP // 2):
        a = ag_eq[2 * pair].astype(F32)
        b = ag_eq[2 * pair + 1].astype(F32)
        turned = swap_halves(b[:, 0:128])
        place_entry(
            pair * 2 * part,
            (
                a[:, 0:128],
                join_halves(a[:, 128:256], turned),
                join_halves(turned, swap_halves(b[:, 128:256])),
            ),
        )
    odown_ref[...] = reduce_end(1, sum_down)
    for i in range(NGRP):
        tgrad_ref[piece * i : piece * i + piece, :] = tz[i]
    total_stat = jnp.zeros((8, D), F32)
    for step in range(1, NGRP):
        slot = lax.rem(g + step, NGRP)
        to_grp(slot, stat_z.at[slot], stat_z.at[slot], sz_ssem.at[0], sz_rsem.at[slot]).wait_recv()
    for i in range(NGRP):
        total_stat = total_stat + stat_z[i]
    row_id = lax.broadcasted_iota(jnp.int32, (8, 1), 0)
    ostat_ref[...] = jnp.where(row_id < 2, stat_z[g], total_stat)
    weight_wait(*weight_gather(3, ag_ekv))
    for pair in range(NGRP // 2):
        a = ag_ekv[2 * pair].astype(F32)
        b = ag_ekv[2 * pair + 1].astype(F32)
        turned = swap_halves(b[:, 0:128])
        place_entry(
            D + pair * 2 * part,
            (
                a[:, 0:128],
                join_halves(a[:, 128:256], turned),
                join_halves(turned, swap_halves(b[:, 128:256])),
            ),
        )
        turned = swap_halves(a[:, 256:384])
        place_entry(
            2 * D + pair * 2 * part,
            (
                join_halves(swap_halves(a[:, 128:256]), turned),
                join_halves(turned, b[:, 128:256]),
                b[:, 256:384],
            ),
        )

    for copies in launched.values():
        for cond, copy in copies():
            pl.when(cond)(copy.wait_send)


def finish_kernel(
    out_in,
    tgrad_in,
    entry_in,
    exit_in,
    up_in,
    down_in,
    stat_in,
    out_hbm,
    tgrad_hbm,
    entry_hbm,
    exit_hbm,
    up_hbm,
    down_hbm,
    fgain_ref,
    fbias_ref,
    sgain_ref,
    sbias_ref,
    out_low,
    tgrad_low,
    down_low,
    up_low,
    entry_low,
    exit_low,
    stat_low,
    down_full,
    up_full,
    entry_full,
    exit_full,
    sems,
):
    plans = (
        (down_in, down_low, down_full, down_hbm),
        (up_in, up_low, up_full, up_hbm),
        (entry_in, entry_low, entry_full, entry_hbm),
        (exit_in, exit_low, exit_full, exit_hbm),
        (out_in, out_low, out_low, out_hbm),
        (tgrad_in, tgrad_low, tgrad_low, tgrad_hbm),
    )
    loads = [
        pltpu.make_async_copy(source, low, sems.at[6 + i])
        for i, (source, low, _, _) in enumerate(plans)
    ]
    stat_load = pltpu.make_async_copy(stat_in, stat_low, sems.at[12])
    for copy in [*loads, stat_load]:
        copy.start()
    copies = []
    for i, (_, low, full, target) in enumerate(plans):
        loads[i].wait()
        if full is not low:
            full[...] = low[...].astype(F32)
        copy = pltpu.make_async_copy(full, target, sems.at[i])
        copy.start()
        copies.append(copy)
    stat_load.wait()
    width = stat_low.shape[1]
    part = fgain_ref.shape[0]
    first = lax.axis_index("seq") * part
    turned = pltpu.roll(stat_low[...], lax.rem(width - first, width), axis=1)
    fgain_ref[...] = turned[2:3, 0:part].reshape(part)
    fbias_ref[...] = turned[3:4, 0:part].reshape(part)
    sgain_ref[...] = turned[0:1, 0:part].reshape(part)
    sbias_ref[...] = turned[1:2, 0:part].reshape(part)
    for copy in copies:
        copy.wait()


def fast_on_device(
    seq_count,
    tokens,
    cotangent,
    entry_weight,
    exit_weight,
    up_weight,
    down_weight,
    first_gain,
    first_bias,
    second_gain,
    second_bias,
    dilations,
    offsets,
):
    T, D = tokens.shape
    NGRP, HEADS = offsets.shape
    FF = up_weight.shape[1]
    E = D // HEADS
    NSEQ = seq_count
    chips = NSEQ // 2
    sizes = (T, D, HEADS, E, FF, NSEQ, NGRP)
    piece = D // NSEQ
    vmem = pl.BlockSpec(memory_space=pltpu.VMEM)
    smem = pl.BlockSpec(memory_space=pltpu.SMEM)
    anywhere = pl.BlockSpec(memory_space=pl.ANY)
    dma = pltpu.SemaphoreType.DMA
    scratch = [
        pltpu.VMEM((3, D, 256), BF16),
        pltpu.VMEM((D, D), BF16),
        pltpu.VMEM((D, FF), BF16),
        pltpu.VMEM((FF, D), BF16),
        pltpu.VMEM((T, D), BF16),
        pltpu.VMEM((T, D), BF16),
        pltpu.VMEM((T, D), F32),
        pltpu.VMEM((piece, D), F32),
        pltpu.VMEM((T, D), BF16),
        pltpu.VMEM((T, D), BF16),
        pltpu.VMEM((T, FF), BF16),
        pltpu.VMEM((T, FF), BF16),
        pltpu.VMEM((T, D), F32),
        pltpu.VMEM((3, T, LANES), BF16),
        pltpu.VMEM((3, T, (NSEQ + 2) * T), BF16),
        pltpu.VMEM((NSEQ, T, 384), BF16),
        pltpu.VMEM((NSEQ, T, 256), BF16),
        pltpu.VMEM((NSEQ, T, 256), BF16),
        pltpu.VMEM((6, T, 256), BF16),
        pltpu.VMEM((3, T, LANES), F32),
        pltpu.VMEM((T, 256), F32),
        pltpu.VMEM((T, 256), F32),
        pltpu.VMEM((T, 256), F32),
        pltpu.VMEM((T, 256), F32),
        pltpu.VMEM((T, 256), F32),
        pltpu.VMEM((NGRP, 3, T // 2, LANES), BF16),
        pltpu.VMEM((NGRP, piece, D), BF16),
        pltpu.VMEM((NGRP, piece, D), BF16),
        pltpu.VMEM((NSEQ, 8, D), F32),
        pltpu.VMEM((NGRP, 8, D), F32),
    ]
    scratch += [
        pltpu.VMEM((piece, chips * D), BF16),
        pltpu.VMEM((chips - 1, piece, D), BF16),
        pltpu.VMEM((T, chips * D), BF16),
        pltpu.VMEM((chips - 1, T, D), BF16),
    ]
    for rows, cols in ((piece, D), (piece, 256), (piece, 384)):
        scratch += [
            pltpu.VMEM((2, chips, rows, cols), BF16),
            pltpu.VMEM((chips, rows, cols), BF16),
            pltpu.VMEM((chips - 1, rows, cols), BF16),
            pltpu.VMEM((NGRP, rows, cols), BF16),
        ]
    scratch += [
        dma((7,)),
        dma((7,)),
        dma((NSEQ,)),
        dma((7,)),
        dma((NSEQ,)),
        dma((7,)),
        dma((NSEQ,)),
        dma((2, 3, 2)),
        dma((2, NGRP)),
        dma((NGRP - 1,)),
        dma((NGRP,)),
        dma((2, 3, 2)),
        dma((2, NGRP)),
        dma((5,)),
        dma((5,)),
        dma((5, 3)),
        dma((5, chips - 1)),
        dma((4, 3, 2)),
        dma((4, NGRP)),
        dma((NSEQ - 1,)),
        dma((NSEQ,)),
        dma((NGRP - 1,)),
        dma((NGRP,)),
    ]
    out_shape = (
        jax.ShapeDtypeStruct((T, D), BF16),
        jax.ShapeDtypeStruct((T, D), BF16),
        jax.ShapeDtypeStruct((piece, 3 * D), BF16),
        jax.ShapeDtypeStruct((piece, D), BF16),
        jax.ShapeDtypeStruct((piece, FF), BF16),
        jax.ShapeDtypeStruct((T, D), BF16),
        jax.ShapeDtypeStruct((8, D), F32),
    )
    output, token_grad, entry_grad, exit_grad, up_grad, down_grad, stats = pl.pallas_call(
        partial(layer_kernel, sizes),
        out_shape=out_shape,
        in_specs=[smem] * 2 + [vmem] * 6 + [anywhere] * 4,
        out_specs=tuple([vmem] * 7),
        scratch_shapes=scratch,
        compiler_params=pltpu.CompilerParams(
            collective_id=0, has_side_effects=True, vmem_limit_bytes=63 * 1024 * 1024
        ),
        name="layer",
    )(
        dilations,
        offsets,
        tokens,
        cotangent,
        first_gain,
        first_bias,
        second_gain,
        second_bias,
        entry_weight,
        exit_weight,
        up_weight,
        down_weight,
    )
    part = piece
    finish_shape = (
        jax.ShapeDtypeStruct((T, D), BF16),
        jax.ShapeDtypeStruct((T, D), BF16),
        jax.ShapeDtypeStruct((part, 3 * D), F32),
        jax.ShapeDtypeStruct((part, D), F32),
        jax.ShapeDtypeStruct((part, FF), F32),
        jax.ShapeDtypeStruct((T, D), F32),
    ) + tuple([jax.ShapeDtypeStruct((part,), F32)] * 4)
    return pl.pallas_call(
        finish_kernel,
        out_shape=finish_shape,
        in_specs=[anywhere] * 7,
        out_specs=tuple([anywhere] * 6 + [vmem] * 4),
        scratch_shapes=[
            pltpu.VMEM((T, D), BF16),
            pltpu.VMEM((T, D), BF16),
            pltpu.VMEM((T, D), BF16),
            pltpu.VMEM((part, FF), BF16),
            pltpu.VMEM((part, 3 * D), BF16),
            pltpu.VMEM((part, D), BF16),
            pltpu.VMEM((8, D), F32),
            pltpu.VMEM((T, D), F32),
            pltpu.VMEM((part, FF), F32),
            pltpu.VMEM((part, 3 * D), F32),
            pltpu.VMEM((part, D), F32),
            dma((13,)),
        ],
        compiler_params=pltpu.CompilerParams(vmem_limit_bytes=62 * 1024 * 1024),
        name="finish",
    )(output, token_grad, entry_grad, exit_grad, up_grad, down_grad, stats)


def solution(mesh):
    seq_count = mesh.shape["seq"]
    fast = seq_count == 8 and mesh.shape["grp"] == 4
    return jax.shard_map(
        partial(fast_on_device, seq_count) if fast else on_device,
        mesh=mesh,
        in_specs=(P("seq", None), P("seq", None), P(), P(), P(), P(), P(), P(), P(), P(), P(), P()),
        out_specs=(
            P("seq", None),
            P("seq", None),
            P("seq", None),
            P("seq", None),
            P("seq", None),
            P("seq", None),
            P("seq"),
            P("seq"),
            P("seq"),
            P("seq"),
        ),
        check_vma=False,
    )
```

```python
from functools import partial

import jax
import jax.numpy as jnp
from jax import lax
from jax.experimental import pallas as pl
from jax.experimental.pallas import tpu as pltpu
from jax.sharding import PartitionSpec as P

RATE_MIN = 2
RATE_MAX = 8


EPS = 1e-05
PRECISE = lax.Precision.HIGHEST


def norm_forward(values, gain_vec, bias_vec):
    centered = values - jnp.mean(values, axis=1, keepdims=True)
    inverse = lax.rsqrt(jnp.mean(centered * centered, axis=1, keepdims=True) + EPS)
    plain = centered * inverse
    return (plain * gain_vec + bias_vec, plain, inverse)


def norm_backward(upstream, plain, inverse, gain_vec):
    scaled = upstream * gain_vec
    inner = (
        scaled
        - jnp.mean(scaled, axis=1, keepdims=True)
        - plain * jnp.mean(scaled * plain, axis=1, keepdims=True)
    )
    return (inverse * inner, jnp.sum(upstream * plain, axis=0), jnp.sum(upstream, axis=0))


def key_weights(query_sp, query_pos, key_block, first_row, geometry):
    local_len, capacity, dilation, segment, head_offs, score_scale = geometry
    key_count = key_block.shape[0]
    key_heads = key_block.reshape(key_count, query_sp.shape[1], query_sp.shape[2])
    scores = (
        jnp.einsum("ihd,jhd->hij", query_sp, key_heads, preferred_element_type=jnp.float32)
        * score_scale
    )
    key_index = first_row + jnp.arange(key_count, dtype=jnp.int32)
    source = key_index // capacity
    within = key_index - source * capacity
    key_pos = source[None, :] * local_len + head_offs[:, None] + dilation * within[None, :]
    key_live = within < local_len // dilation
    earlier = key_pos[:, None, :] <= query_pos[:, :, None]
    segment_match = key_pos[:, None, :] // segment == query_pos[:, :, None] // segment
    allowed = earlier & segment_match & key_live[None, None, :]
    return (jnp.where(allowed, jnp.exp(scores), 0.0), key_heads)


def forward_block(running, pieces, first_row, query_sp, query_pos, geometry):
    numerator, denominator = running
    key_block, value_block = pieces
    weights, key_heads = key_weights(query_sp, query_pos, key_block, first_row, geometry)
    value_heads = value_block.reshape(key_heads.shape)
    numerator = numerator + jnp.einsum(
        "hij,jhd->hid",
        weights.astype(jnp.bfloat16),
        value_heads,
        preferred_element_type=jnp.float32,
    )
    return (numerator, denominator + jnp.sum(weights, axis=2))


def blockwise(step_fn, running, pieces, first_row, block_rows):
    total_rows = pieces[0].shape[0]
    if total_rows > block_rows and total_rows % block_rows == 0:
        number = total_rows // block_rows
        stacked_first = pieces[0].reshape(number, block_rows, pieces[0].shape[1])
        stacked_second = pieces[1].reshape(number, block_rows, pieces[1].shape[1])
        block_starts = first_row + block_rows * jnp.arange(number, dtype=jnp.int32)

        def advance(state, items):
            return (step_fn(state, (items[0], items[1]), items[2]), None)

        running, _ = lax.scan(advance, running, (stacked_first, stacked_second, block_starts))
        return running
    return step_fn(running, pieces, first_row)


def backward_block(running, items, query_sp, query_pos, grad_sp, shift_sp, geometry):
    key_block, value_block, first_row = items
    score_scale = geometry[5]
    weights, key_heads = key_weights(query_sp, query_pos, key_block, first_row, geometry)
    key_count = key_block.shape[0]
    value_heads = value_block.reshape(key_heads.shape)
    pressure = jnp.einsum("ihd,jhd->hij", grad_sp, value_heads, preferred_element_type=jnp.float32)
    slopes = (weights * (pressure - shift_sp[:, :, None])).astype(jnp.bfloat16)
    running = (
        running
        + jnp.einsum("hij,jhd->ihd", slopes, key_heads, preferred_element_type=jnp.float32)
        * score_scale
    )
    grad_keys = (
        jnp.einsum("hij,ihd->jhd", slopes, query_sp, preferred_element_type=jnp.float32)
        * score_scale
    )
    grad_values = jnp.einsum(
        "hij,ihd->jhd", weights.astype(jnp.bfloat16), grad_sp, preferred_element_type=jnp.float32
    )
    return (running, (grad_keys.reshape(key_count, -1), grad_values.reshape(key_count, -1)))


def local_weights(query_heads, key_heads, score_scale):
    local_len = query_heads.shape[0]
    scores = (
        jnp.einsum("ihd,jhd->hij", query_heads, key_heads, preferred_element_type=jnp.float32)
        * score_scale
    )
    positions = jnp.arange(local_len, dtype=jnp.int32)
    causal = positions[:, None] >= positions[None, :]
    return jnp.where(causal[None], jnp.exp(scores), 0.0)


def on_device(
    tokens,
    cotangent,
    entry_weight,
    exit_weight,
    up_weight,
    down_weight,
    first_gain,
    first_bias,
    second_gain,
    second_bias,
    dilations,
    offsets,
):
    local_len, width_model = tokens.shape
    head_count = offsets.shape[1]
    head_size = width_model // head_count
    score_scale = head_size ** (-0.5)
    capacity = local_len // RATE_MIN
    group_idx = lax.axis_index("grp")
    seq_index = lax.axis_index("seq")
    seq_count = lax.axis_size("seq")
    dilation = lax.dynamic_index_in_dim(dilations, group_idx, 0, keepdims=False)
    head_offs = lax.dynamic_index_in_dim(offsets, group_idx, 0, keepdims=False)
    segment = local_len * seq_count * dilation // RATE_MAX
    step_ids = jnp.arange(capacity, dtype=jnp.int32)
    row_live = step_ids < local_len // dilation
    local_rows = jnp.minimum(head_offs[:, None] + dilation * step_ids[None, :], local_len - 1)
    query_pos = jnp.where(
        row_live[None, :],
        seq_index * local_len + head_offs[:, None] + dilation * step_ids[None, :],
        -1,
    )
    geometry = (local_len, capacity, dilation, segment, head_offs, score_scale)
    head_shape = (local_len, head_count, head_size)
    selector = local_rows[:, :, None] == jnp.arange(local_len, dtype=jnp.int32)[None, None, :]
    select_low = selector.astype(jnp.bfloat16)
    select_full = selector.astype(jnp.float32)

    def pick(array_in):
        return jnp.einsum(
            "hci,ihd->chd", select_low, array_in, preferred_element_type=jnp.float32
        ).astype(jnp.bfloat16)

    def place_back(sparse_in):
        return jnp.einsum("hci,chd->ihd", select_full, sparse_in, precision=PRECISE)

    inputs = tokens.astype(jnp.float32)
    normed_one, plain_one, inverse_one = norm_forward(inputs, first_gain, first_bias)
    normed_low = normed_one.astype(jnp.bfloat16)
    packed = jnp.dot(normed_low, entry_weight, preferred_element_type=jnp.float32).astype(
        jnp.bfloat16
    )
    query_heads = packed[:, :width_model].reshape(head_shape)
    key_heads = packed[:, width_model : 2 * width_model].reshape(head_shape)
    value_heads = packed[:, 2 * width_model :].reshape(head_shape)
    query_sp = pick(query_heads)
    key_sp = pick(key_heads).reshape(capacity, width_model)
    value_sp = pick(value_heads).reshape(capacity, width_model)
    empty_state = (
        jnp.zeros((head_count, capacity, head_size), jnp.float32),
        jnp.zeros((head_count, capacity), jnp.float32),
    )
    forward_step = partial(forward_block, query_sp=query_sp, query_pos=query_pos, geometry=geometry)
    numerator, denominator = blockwise(
        forward_step,
        empty_state,
        (
            lax.all_gather(key_sp, "seq", axis=0, tiled=True),
            lax.all_gather(value_sp, "seq", axis=0, tiled=True),
        ),
        jnp.int32(0),
        8 * capacity,
    )

    def local_part(query_in, key_in, value_in):
        weights = local_weights(query_in, key_in, score_scale)
        local_num = jnp.einsum(
            "hij,jhd->ihd",
            weights.astype(jnp.bfloat16),
            value_in,
            preferred_element_type=jnp.float32,
        )
        return (local_num, jnp.sum(weights, axis=2).T)

    def local_none(query_in, key_in, value_in):
        return (jnp.zeros(head_shape, jnp.float32), jnp.zeros((local_len, head_count), jnp.float32))

    local_num, local_den = lax.cond(
        group_idx == 0, local_part, local_none, query_heads, key_heads, value_heads
    )
    numerator_full = (
        jnp.einsum("hci,hcd->ihd", select_full, numerator, precision=PRECISE) + local_num
    )
    denominator_full = (
        jnp.einsum("hci,hc->ih", select_full, denominator, precision=PRECISE) + local_den
    )
    merged_num, merged_den = lax.psum(
        (numerator_full.reshape(local_len, width_model), denominator_full), "grp"
    )
    attention = merged_num.reshape(head_shape) / merged_den[:, :, None]
    mixed = attention.reshape(local_len, width_model).astype(jnp.bfloat16)
    middle = inputs + jnp.dot(mixed, exit_weight, preferred_element_type=jnp.float32)
    normed_two, plain_two, inverse_two = norm_forward(middle, second_gain, second_bias)
    normed_two_low = normed_two.astype(jnp.bfloat16)
    hidden = jnp.dot(normed_two_low, up_weight, preferred_element_type=jnp.float32)
    active = jax.nn.gelu(hidden, approximate=False).astype(jnp.bfloat16)
    output = (middle + jnp.dot(active, down_weight, preferred_element_type=jnp.float32)).astype(
        jnp.bfloat16
    )
    down_grad = jnp.dot(active.T, cotangent, preferred_element_type=jnp.float32)
    grad_active = jnp.dot(cotangent, down_weight.T, preferred_element_type=jnp.float32)
    _, gelu_pull = jax.vjp(partial(jax.nn.gelu, approximate=False), hidden)
    grad_hidden = gelu_pull(grad_active)[0].astype(jnp.bfloat16)
    up_grad = jnp.dot(normed_two_low.T, grad_hidden, preferred_element_type=jnp.float32)
    grad_normed_two = jnp.dot(grad_hidden, up_weight.T, preferred_element_type=jnp.float32)
    grad_plain_two, second_gain_grad, second_bias_grad = norm_backward(
        grad_normed_two, plain_two, inverse_two, second_gain
    )
    grad_middle = cotangent.astype(jnp.float32) + grad_plain_two
    grad_branch = grad_middle.astype(jnp.bfloat16)
    exit_grad = jnp.dot(mixed.T, grad_branch, preferred_element_type=jnp.float32)
    grad_mixed_low = lax.optimization_barrier(
        jnp.dot(grad_branch, exit_weight.T, preferred_element_type=jnp.float32).astype(jnp.bfloat16)
    )
    grad_mixed = grad_mixed_low.astype(jnp.float32).reshape(head_shape)
    grad_numer = (grad_mixed / merged_den[:, :, None]).astype(jnp.bfloat16)
    row_shift = jnp.sum(grad_mixed * attention, axis=2) / merged_den
    grad_sp = pick(grad_numer)
    shift_sp = jnp.einsum("hci,ih->hc", select_full, row_shift, precision=PRECISE)
    back_keys, back_values = (
        lax.all_gather(key_sp, "seq", axis=0, tiled=True),
        lax.all_gather(value_sp, "seq", axis=0, tiled=True),
    )
    block_rows = 8 * capacity
    number = back_keys.shape[0] // block_rows
    stacked_keys = back_keys.reshape(number, block_rows, width_model)
    stacked_values = back_values.reshape(number, block_rows, width_model)
    block_starts = block_rows * jnp.arange(number, dtype=jnp.int32)
    empty_query = jnp.zeros((capacity, head_count, head_size), jnp.float32)
    back_step = partial(
        backward_block,
        query_sp=query_sp,
        query_pos=query_pos,
        grad_sp=grad_sp,
        shift_sp=shift_sp,
        geometry=geometry,
    )
    grad_query_sp, (grad_key_all, grad_value_all) = lax.scan(
        back_step, empty_query, (stacked_keys, stacked_values, block_starts)
    )
    own_keys, own_values = (
        lax.psum_scatter(
            grad_key_all.reshape(-1, width_model), "seq", scatter_dimension=0, tiled=True
        ),
        lax.psum_scatter(
            grad_value_all.reshape(-1, width_model), "seq", scatter_dimension=0, tiled=True
        ),
    )

    def local_grads(query_in, key_in, value_in, grad_in, shift_in):
        weights = local_weights(query_in, key_in, score_scale)
        pressure = jnp.einsum("ihd,jhd->hij", grad_in, value_in, preferred_element_type=jnp.float32)
        slopes = (weights * (pressure - shift_in.T[:, :, None])).astype(jnp.bfloat16)
        grad_query = (
            jnp.einsum("hij,jhd->ihd", slopes, key_in, preferred_element_type=jnp.float32)
            * score_scale
        )
        grad_key = (
            jnp.einsum("hij,ihd->jhd", slopes, query_in, preferred_element_type=jnp.float32)
            * score_scale
        )
        grad_value = jnp.einsum(
            "hij,ihd->jhd",
            weights.astype(jnp.bfloat16),
            grad_in,
            preferred_element_type=jnp.float32,
        )
        return (grad_query, grad_key, grad_value)

    def local_skip(query_in, key_in, value_in, grad_in, shift_in):
        zeros_heads = jnp.zeros(head_shape, jnp.float32)
        return (zeros_heads, zeros_heads, zeros_heads)

    local_dq, local_dk, local_dv = lax.cond(
        group_idx == 0,
        local_grads,
        local_skip,
        query_heads,
        key_heads,
        value_heads,
        grad_numer,
        row_shift,
    )
    grad_query_full = place_back(grad_query_sp) + local_dq
    grad_key_full = place_back(own_keys.reshape(capacity, head_count, head_size)) + local_dk
    grad_value_full = place_back(own_values.reshape(capacity, head_count, head_size)) + local_dv
    grad_packed = jnp.concatenate(
        [
            grad_query_full.reshape(local_len, width_model),
            grad_key_full.reshape(local_len, width_model),
            grad_value_full.reshape(local_len, width_model),
        ],
        axis=1,
    )
    summed = lax.psum(grad_packed, "grp").astype(jnp.bfloat16)
    entry_grad = jnp.dot(normed_low.T, summed, preferred_element_type=jnp.float32)
    grad_normed_one = jnp.dot(summed, entry_weight.T, preferred_element_type=jnp.float32)
    grad_plain_one, first_gain_grad, first_bias_grad = norm_backward(
        grad_normed_one, plain_one, inverse_one, first_gain
    )
    token_grad = (grad_middle + grad_plain_one).astype(jnp.bfloat16)
    shards = (
        lax.psum_scatter(entry_grad, "seq", scatter_dimension=0, tiled=True),
        lax.psum_scatter(exit_grad, "seq", scatter_dimension=0, tiled=True),
        lax.psum_scatter(up_grad, "seq", scatter_dimension=0, tiled=True),
        lax.psum_scatter(down_grad, "seq", scatter_dimension=0, tiled=True),
        lax.psum_scatter(first_gain_grad, "seq", scatter_dimension=0, tiled=True),
        lax.psum_scatter(first_bias_grad, "seq", scatter_dimension=0, tiled=True),
        lax.psum_scatter(second_gain_grad, "seq", scatter_dimension=0, tiled=True),
        lax.psum_scatter(second_bias_grad, "seq", scatter_dimension=0, tiled=True),
    )
    return (
        output,
        token_grad,
        shards[0],
        shards[1],
        shards[2],
        shards[3],
        shards[4],
        shards[5],
        shards[6],
        shards[7],
    )


MESH = pl.DeviceIdType.MESH
LANES = 128
LOG2E = 1.4426950408889634
F32 = jnp.float32
BF16 = jnp.bfloat16


def dot_nn(left, right):
    return lax.dot_general(left, right, (((1,), (0,)), ((), ())), preferred_element_type=F32)


def dot_nt(left, right):
    return lax.dot_general(left, right, (((1,), (1,)), ((), ())), preferred_element_type=F32)


def dot_tn(left, right):
    return lax.dot_general(left, right, (((0,), (0,)), ((), ())), preferred_element_type=F32)


def lane_ids(width):
    return lax.broadcasted_iota(jnp.int32, (1, width), 1)


def slot_mask(slot, width=256):
    ids = lane_ids(width)
    return jnp.where((ids >= 64 * slot) & (ids < 64 * slot + 64), 1.0, 0.0).astype(F32)


def join_halves(low_part, high_part):
    return jnp.where(lane_ids(LANES) < 64, low_part, high_part)


def swap_halves(tile):
    return pltpu.roll(tile, 64, axis=1)


def layer_kernel(
    sizes,
    dil_ref,
    off_ref,
    tok_ref,
    cot_ref,
    gain1_ref,
    bias1_ref,
    gain2_ref,
    bias2_ref,
    entry_hbm,
    exit_hbm,
    up_hbm,
    down_hbm,
    out_ref,
    tgrad_ref,
    oentry_ref,
    oexit_ref,
    oup_ref,
    odown_ref,
    ostat_ref,
    win,
    exit_all,
    up_all,
    down_all,
    n1,
    n2,
    middle,
    gmid,
    gbranch,
    mixed,
    active,
    ghid,
    gn2,
    member,
    masks,
    kv,
    qb,
    dob,
    qmask,
    shift,
    invden,
    att,
    acc_a,
    acc_b,
    acc_c,
    zmix,
    drecv,
    tz,
    stat,
    stat_z,
    r1_exit,
    r2_exit,
    r1_down,
    r2_down,
    pc_up,
    r1_up,
    r2_up,
    ag_up,
    pc_eq,
    r1_eq,
    r2_eq,
    ag_eq,
    pc_ekv,
    r1_ekv,
    r2_ekv,
    ag_ekv,
    load_sem,
    kv_ssem,
    kv_rsem,
    q_ssem,
    q_rsem,
    do_ssem,
    do_rsem,
    zm_ssem,
    zm_rsem,
    zd_ssem,
    zd_rsem,
    zt_ssem,
    zt_rsem,
    rs_s1,
    rs_r1,
    rs_s2,
    rs_r2,
    rs_zs,
    rs_zr,
    st_ssem,
    st_rsem,
    sz_ssem,
    sz_rsem,
):
    T, D, HEADS, E, FF, NSEQ, NGRP = sizes
    scale = E ** (-0.5)
    exp_scale = scale * LOG2E
    s = lax.axis_index("seq")
    g = lax.axis_index("grp")
    chip = s // 2
    core = s % 2
    sib = s + 1 - 2 * core
    odd = g % 2
    chips = NSEQ // 2
    part = D // NGRP
    is_odd = odd == 1
    gain1 = gain1_ref[...].reshape(1, D)
    bias1 = bias1_ref[...].reshape(1, D)
    gain2 = gain2_ref[...].reshape(1, D)
    bias2 = bias2_ref[...].reshape(1, D)

    def to_seq(peer, src, dst, ssem, rsem):
        return pltpu.make_async_remote_copy(
            src_ref=src,
            dst_ref=dst,
            send_sem=ssem,
            recv_sem=rsem,
            device_id={"seq": peer},
            device_id_type=MESH,
        )

    def to_grp(peer, src, dst, ssem, rsem):
        return pltpu.make_async_remote_copy(
            src_ref=src,
            dst_ref=dst,
            send_sem=ssem,
            recv_sem=rsem,
            device_id={"grp": peer},
            device_id_type=MESH,
        )

    loads = []
    for t in range(3):
        first = pl.multiple_of(t * D + part * g - 64 * odd, LANES)
        loads.append(
            pltpu.make_async_copy(entry_hbm.at[:, pl.ds(first, 256)], win.at[t], load_sem.at[t])
        )
    loads.append(pltpu.make_async_copy(down_hbm, down_all, load_sem.at[3]))
    loads.append(pltpu.make_async_copy(exit_hbm, exit_all, load_sem.at[4]))
    loads.append(pltpu.make_async_copy(up_hbm, up_all, load_sem.at[5]))
    for load in loads[:3]:
        load.start()

    barrier = pltpu.get_barrier_semaphore()
    for step in range(1, NSEQ):
        pl.semaphore_signal(
            barrier, inc=1, device_id={"seq": lax.rem(s + step, NSEQ)}, device_id_type=MESH
        )
    for step in range(1, NGRP):
        pl.semaphore_signal(
            barrier, inc=1, device_id={"grp": lax.rem(g + step, NGRP)}, device_id_type=MESH
        )

    rows = D // NSEQ

    def norm_one(i, carry):
        at = pl.ds(pl.multiple_of(i * rows, rows), rows)
        value = tok_ref[at, :].astype(F32)
        centered = value - jnp.mean(value, axis=1, keepdims=True)
        inverse = lax.rsqrt(jnp.mean(centered * centered, axis=1, keepdims=True) + EPS)
        n1[at, :] = (centered * inverse * gain1 + bias1).astype(BF16)
        return carry

    lax.fori_loop(0, T // rows, norm_one, 0)

    for load in loads[:3]:
        load.wait()
    for load in loads[3:]:
        load.start()
    lane256 = lane_ids(256)
    q_raw = dot_nn(n1[...], win[0])
    k_raw = dot_nn(n1[...], win[1])
    v_raw = dot_nn(n1[...], win[2])
    q_own = jnp.where(is_odd, pltpu.roll(q_raw, 192, axis=1), q_raw)
    k_own = jnp.where(is_odd, pltpu.roll(k_raw, 192, axis=1), k_raw)
    v_own = jnp.where(is_odd, v_raw, pltpu.roll(v_raw, 64, axis=1))
    q_own = jnp.where(lane256 < 192, q_own, 0.0)
    qb[s] = q_own.astype(BF16)
    for h in range(3):
        qmask[h] = (q_own * slot_mask(h)).astype(BF16)
    kv[s, :, 0:128] = k_own[:, 0:128].astype(BF16)
    kv[s, :, 128:256] = join_halves(k_own[:, 128:256], v_own[:, 0:128]).astype(BF16)
    kv[s, :, 256:384] = v_own[:, 128:256].astype(BF16)

    pl.semaphore_wait(barrier, NSEQ - 1 + NGRP - 1)

    launched = {}

    def launch(name, copies):
        for cond, copy in copies():
            pl.when(cond)(copy.start)
        launched[name] = copies

    always = core >= 0

    def spread(name, buffer, ssem, rsem, upward):
        def copies():
            found = []
            for d in range(1, chips):
                peer = lax.rem(s + (2 * d if upward else NSEQ - 2 * d), NSEQ)
                cond = chip + d < chips if upward else chip >= d
                found.append(
                    (cond, to_seq(peer, buffer.at[s], buffer.at[s], ssem.at[d - 1], rsem.at[s]))
                )
            found.append((always, to_seq(sib, buffer.at[s], buffer.at[s], ssem.at[3], rsem.at[s])))
            return found

        launch(name, copies)

    spread("kv", kv, kv_ssem, kv_rsem, True)
    spread("q", qb, q_ssem, q_rsem, False)

    lane128 = lane_ids(LANES)
    rate_row = jnp.ones((1, LANES), F32)
    for i in range(NGRP):
        rate_row = jnp.where(lane128 == i, dil_ref[i].astype(F32), rate_row)
    local_pos = lax.broadcasted_iota(jnp.int32, (T, 1), 0).astype(F32)
    residue = local_pos - rate_row * jnp.floor((local_pos + 0.5) / rate_row)
    for h in range(3):
        off_row = jnp.full((1, LANES), -1.0, F32)
        for i in range(NGRP):
            off_row = jnp.where(
                lane128 == i, off_ref[i, 3 * g + h].astype(F32), off_row
            )
        member[h] = jnp.where(residue == off_row, 1.0, 0.0).astype(BF16)
    per_segment = rate_row * (T * NSEQ // RATE_MAX)

    def segment_of(block):
        return jnp.floor((jnp.full((1, LANES), block * T, jnp.int32).astype(F32) + 0.5) / per_segment)

    own_segment = segment_of(s)

    pair_width = 2 * T

    def pair_lanes(cc):
        return pl.ds(pl.multiple_of(cc * pair_width, LANES), pair_width)

    def build_mask(cc, carry):
        for h in range(3):
            blocks = []
            for i in range(2):
                same = jnp.where(segment_of(2 * cc + i) == own_segment, 1.0, 0.0)
                blocks.append((member[h].astype(F32) * same).astype(BF16))
            count = dot_nt(member[h], jnp.concatenate(blocks, axis=0))
            masks[h, :, pair_lanes(cc)] = count.astype(BF16)
        return carry

    lax.fori_loop(0, chips, build_mask, 0)
    own_id = lax.broadcasted_iota(jnp.int32, (T, pair_width), 0) + core * T
    pair_id = lax.broadcasted_iota(jnp.int32, (T, pair_width), 1)
    own_block = (pair_id >= core * T) & (pair_id < core * T + T)
    for h in range(3):
        count = masks[h, :, pair_lanes(chip)].astype(F32) + jnp.where(own_block, 1.0, 0.0)
        masks[h, :, pair_lanes(chip)] = jnp.where(pair_id <= own_id, count, 0.0).astype(BF16)
        masks[h, :, pair_lanes(chips)] = jnp.where(own_id <= pair_id, count, 0.0).astype(BF16)

    half = T // 2
    piece = D // NSEQ

    def pack_half(tile, high):
        top, bottom = tile[0:half], tile[half:T]
        if high:
            return join_halves(swap_halves(top), bottom).astype(BF16)
        return join_halves(top, swap_halves(bottom)).astype(BF16)

    right, left = lax.rem(g + 1, NGRP), lax.rem(g + NGRP - 1, NGRP)

    def chain_start(name, at, ssem, rsem):
        launch(
            name + "0",
            lambda: [
                (g + 1 < NGRP, to_grp(right, at(g), at(g), ssem().at[0, 0], rsem().at[g])),
                (g >= 1, to_grp(left, at(g), at(g), ssem().at[0, 1], rsem().at[g])),
            ],
        )

    def chain_step(d, name, at, ssem, rsem):
        def slots():
            return lax.rem(g - d + NGRP, NGRP), lax.rem(g + d, NGRP)

        def copies():
            lower, upper = slots()
            return [
                (
                    (g - d >= 0) & (g + 1 < NGRP),
                    to_grp(right, at(lower), at(lower), ssem().at[d, 0], rsem().at[lower]),
                ),
                (
                    (g + d < NGRP) & (g >= 1),
                    to_grp(left, at(upper), at(upper), ssem().at[d, 1], rsem().at[upper]),
                ),
            ]

        lower, upper = slots()
        pl.when(g - d >= 0)(
            to_grp(right, at(lower), at(lower), ssem().at[0, 0], rsem().at[lower]).wait_recv
        )
        pl.when(g + d < NGRP)(
            to_grp(left, at(upper), at(upper), ssem().at[0, 1], rsem().at[upper]).wait_recv
        )
        if d < NGRP - 1:
            launch(name + str(d), copies)

    def weight_direct(name, at, ssem, rsem):
        def copies():
            found = []
            for step in range(1, NGRP):
                peer = lax.rem(g + step, NGRP)
                found.append((always, to_grp(peer, at(g), at(g), ssem().at[step - 1, 0], rsem().at[g])))
            return found

        launch(name, copies)

    def weight_wait(name, at, ssem, rsem):
        for step in range(1, NGRP):
            slot = lax.rem(g + step, NGRP)
            to_grp(slot, at(slot), at(slot), ssem().at[0, 0], rsem().at[slot]).wait_recv()

    def chain_parts(name, views, ssem, rsem):
        return [
            (name + str(i), view, lambda i=i: ssem.at[i], lambda i=i: rsem.at[i])
            for i, view in enumerate(views)
        ]

    def chain_finish(parts):
        for d in range(1, NGRP):
            for part_of in parts:
                chain_step(d, *part_of)

    def near_start(name, at, ssem, rsem):
        def copies():
            found = []
            for i, step in enumerate((1, -1, 2, -2)):
                peer = g + step
                to = lax.rem(peer + NGRP, NGRP)
                sem = ssem().at[i // 2, i % 2]
                found.append(((peer >= 0) & (peer < NGRP), to_grp(to, at(g), at(g), sem, rsem().at[g])))
            return found

        launch(name, copies)

    def near_forward(name, at, ssem, rsem):
        ends = ((NGRP - 2, 0, NGRP - 1), (1, NGRP - 1, 0))

        def copies():
            return [
                (g == near, to_grp(end, at(far), at(far), ssem().at[2, 0], rsem().at[far]))
                for near, far, end in ends
            ]

        for near, far, end in ends:
            pl.when(g == near)(
                to_grp(end, at(far), at(far), ssem().at[2, 0], rsem().at[far]).wait_recv
            )
        launch(name + "on", copies)

    def near_wait(name, at, ssem, rsem):
        for slot in range(NGRP):
            handed = ((g == NGRP - 2) & (slot == 0)) | ((g == 1) & (slot == NGRP - 1))
            pl.when((g != slot) & jnp.logical_not(handed))(
                to_grp(
                    lax.rem(g + 1, NGRP), at(slot), at(slot), ssem().at[0, 0], rsem().at[slot]
                ).wait_recv
            )

    def direct_start(name, at, ssem, rsem):
        def copies():
            found = []
            for step in range(1, NGRP):
                peer = lax.rem(g + step, NGRP)
                found.append((always, to_grp(peer, at(g), at(g), ssem.at[step - 1], rsem.at[g])))
            return found

        launch(name, copies)

    def direct_wait(name, at, ssem, rsem):
        for step in range(1, NGRP):
            slot = lax.rem(g + step, NGRP)
            to_grp(slot, at(slot), at(slot), ssem.at[0], rsem.at[slot]).wait_recv()

    loads[3].wait()

    def cot_times_down(i, carry):
        at = pl.ds(pl.multiple_of(i * T, T), T)
        ghid[:, at] = dot_nt(cot_ref[...], down_all[at, :]).astype(BF16)
        return carry

    lax.fori_loop(0, FF // T, cot_times_down, 0)

    acc_a[...] = jnp.zeros_like(acc_a)
    shift[...] = jnp.zeros_like(shift)

    def pair_of(ref, cc, first, last):
        return ref[pl.ds(2 * cc, 2), :, first:last].reshape(pair_width, last - first)

    def weights_of(score, count):
        count = count.astype(F32)
        return jnp.where(count > 0.5, jnp.exp2(score * exp_scale) * count, 0.0)

    def wait_pair(buffer, ssem, rsem, j, cc):
        mine, other = 2 * cc + core, 2 * cc + 1 - core

        @pl.when(j > 0)
        def _():
            to_seq(sib, buffer.at[mine], buffer.at[mine], ssem.at[0], rsem.at[mine]).wait_recv()
            to_seq(sib, buffer.at[mine], buffer.at[mine], ssem.at[3 + j], rsem.at[mine]).start()

        to_seq(sib, buffer.at[other], buffer.at[other], ssem.at[0], rsem.at[other]).wait_recv()

    def forward_step(j, carry):
        cc = chip - j
        wait_pair(kv, kv_ssem, kv_rsem, j, cc)
        keys = pair_of(kv, cc, 0, 256)
        values = pair_of(kv, cc, 128, 384)
        for h in range(3):
            weight = weights_of(dot_nt(qmask[h], keys), masks[h, :, pair_lanes(cc)])
            row_sum = weight[:, 0:LANES]
            for i in range(1, pair_width // LANES):
                row_sum = row_sum + weight[:, LANES * i : LANES * i + LANES]
            shift[h] += row_sum
            low_weight = weight.astype(BF16)
            masks[h, :, pair_lanes(cc)] = low_weight
            acc_a[...] += dot_nn(low_weight, values) * slot_mask(h + 1)
        return carry

    lax.fori_loop(0, chip + 1, forward_step, 0)
    inverse = jnp.zeros((T, 256), F32)
    for h in range(3):
        inverse += slot_mask(h + 1) / jnp.sum(shift[h], axis=1, keepdims=True)
    att_own = acc_a[...] * inverse
    invden[...] = inverse
    att[...] = att_own
    for h in range(3):
        tile = att_own[:, 0:128] if h == 0 else att_own[:, 128:256]
        zmix[g, h] = pack_half(tile, h != 1)
    quarter = half // 2
    mixed_gather = chain_parts(
        "mixed",
        (lambda i: zmix.at[i, :, 0:quarter], lambda i: zmix.at[i, :, quarter:half]),
        zm_ssem,
        zm_rsem,
    )
    for part_of in mixed_gather:
        chain_start(*part_of)

    for d in range(1, chips):

        @pl.when(chip + d < chips)
        def _(d=d):
            slot = lax.rem(s + 2 * d, NSEQ)
            to_seq(sib, qb.at[slot], qb.at[slot], q_ssem.at[0], q_rsem.at[slot]).wait_recv()

    def hand_on(buffer, ssem, rsem, upward):
        found = []
        for d in range(1, chips):
            slot = lax.rem(s + (NSEQ - 2 * d if upward else 2 * d), NSEQ)
            cond = chip >= d if upward else chip + d < chips
            found.append(
                (cond, to_seq(sib, buffer.at[slot], buffer.at[slot], ssem.at[3 + d], rsem.at[slot]))
            )
        return found

    launch("q on", lambda: hand_on(qb, q_ssem, q_rsem, False))
    launched["kv on"] = lambda: hand_on(kv, kv_ssem, kv_rsem, True)
    launched["do on"] = lambda: hand_on(dob, do_ssem, do_rsem, False)

    chain_finish(mixed_gather)
    for tile in range(D // LANES):
        (g_a, h_a), (g_b, h_b) = divmod(2 * tile, 3), divmod(2 * tile + 1, 3)
        first_head = zmix[g_a, h_a].astype(F32)
        second_head = zmix[g_b, h_b].astype(F32)
        cols = slice(tile * LANES, tile * LANES + LANES)
        mixed[0:half, cols] = join_halves(first_head, swap_halves(second_head)).astype(BF16)
        mixed[half:T, cols] = join_halves(swap_halves(first_head), second_head).astype(BF16)

    loads[4].wait()
    middle[...] = tok_ref[...].astype(F32) + dot_nn(mixed[...], exit_all[...])

    def norm_two(i, carry):
        at = pl.ds(pl.multiple_of(i * rows, rows), rows)
        value = middle[at, :]
        centered = value - jnp.mean(value, axis=1, keepdims=True)
        inverse = lax.rsqrt(jnp.mean(centered * centered, axis=1, keepdims=True) + EPS)
        plain = centered * inverse
        n2[at, :] = (plain * gain2 + bias2).astype(BF16)
        return carry

    lax.fori_loop(0, T // rows, norm_two, 0)

    class Stacked:
        def __init__(self, pieces, first_in, second_in):
            self.pieces, self.first_in, self.second_in = pieces, first_in, second_in

        def whole(self, k):
            return self.pieces.at[k]

        def block(self, k, cc):
            return self.pieces.at[k, cc]

        def first(self, cc):
            return self.first_in.at[cc]

    class Tiled(Stacked):
        def rows(self, k):
            count = self.first_in.shape[0]
            return pl.ds(pl.multiple_of(count * k, count), count)

        def cols(self, cc):
            return pl.ds(pl.multiple_of(D * cc, LANES), D)

        def whole(self, k):
            return self.pieces.at[self.rows(k), :]

        def block(self, k, cc):
            return self.pieces.at[self.rows(k), self.cols(cc)]

        def first(self, cc):
            return self.first_in.at[:, self.cols(cc)]

    sum_up = Stacked(pc_up, r1_up, r2_up)
    sum_down = Tiled(up_all, r1_down, r2_down)
    sum_eq = Stacked(pc_eq, r1_eq, r2_eq)
    sum_ekv = Stacked(pc_ekv, r1_ekv, r2_ekv)
    sum_exit = Tiled(ghid, r1_exit, r2_exit)

    def reduce_start(i, parts):
        launch(
            f"first{i}",
            lambda: [
                (
                    always,
                    to_seq(sib, parts.whole(1 - core), parts.first_in, rs_s1.at[i], rs_r1.at[i]),
                )
            ],
        )

    def reduce_pass(i, parts):
        to_seq(sib, parts.whole(core), parts.first_in, rs_s1.at[i], rs_r1.at[i]).wait_recv()

        def add(cc, carry):
            block = parts.block(core, cc)
            block[...] = (block[...].astype(F32) + parts.first(cc)[...].astype(F32)).astype(BF16)
            return carry

        lax.fori_loop(0, chips, add, 0)

        def copies():
            found = []
            for d in range(1, chips):
                to_chip = lax.rem(chip + d, chips)
                copy = to_seq(
                    2 * to_chip + core,
                    parts.block(core, to_chip),
                    parts.second_in.at[chips - d - 1],
                    rs_s2.at[i, d - 1],
                    rs_r2.at[i, chips - d - 1],
                )
                found.append((always, copy))
            return found

        launch(f"second{i}", copies)

    def reduce_end(i, parts):
        result = parts.block(core, chip)[...].astype(F32)
        for d in range(1, chips):
            landed = parts.second_in.at[d - 1]
            to_seq(sib, landed, landed, rs_s1.at[i], rs_r2.at[i, d - 1]).wait_recv()
            result = result + landed[...].astype(F32)
        return result.astype(BF16)

    def weight_gather(i, gathered):
        return ("weight" + str(i), lambda j: gathered.at[j], lambda: rs_zs.at[i], lambda: rs_zr.at[i])

    def gather_sum(i, parts, gathered):
        gathered[g] = reduce_end(i, parts)
        start = near_start if i in (0, 2, 3) else weight_direct
        start(*weight_gather(i, gathered))

    loads[5].wait()
    def feed_forward(i, carry):
        c = lax.rem(g + i, NGRP)
        at = pl.ds(pl.multiple_of(c * D, LANES), D)
        hidden = dot_nn(n2[...], up_all[:, at])
        cdf = 0.5 + 0.5 * lax.erf(hidden * (0.5**0.5))
        low_active = (hidden * cdf).astype(BF16)
        active[:, at] = low_active
        density = jnp.exp2(hidden * hidden * (-0.5 * LOG2E)) * 0.3989422804014327
        ghid[:, at] = (ghid[:, at].astype(F32) * (cdf + hidden * density)).astype(BF16)

        @pl.when(i == 0)
        def _():
            for j in range(2):
                up_grad = dot_tn(n2[...], ghid[:, pl.ds(pl.multiple_of(g * D + T * j, LANES), T)])
                for t in range(NSEQ):
                    pc_up[t % 2, t // 2, :, T * j : T * j + T] = up_grad[
                        piece * t : piece * t + piece, :
                    ].astype(BF16)
            reduce_start(0, sum_up)

        @pl.when(i == 1)
        def _():
            reduce_pass(0, sum_up)

        return carry

    lax.fori_loop(0, NGRP, feed_forward, 0)

    def back_through_up(i, carry):
        at = pl.ds(pl.multiple_of(i * 256, 256), 256)
        gn2[:, at] = dot_nt(ghid[...], up_all[at, :])
        return carry

    lax.fori_loop(0, D // 256, back_through_up, 0)

    stat[s] = jnp.zeros((8, D), F32)

    def norm_two_back(i, carry):
        at = pl.ds(pl.multiple_of(i * rows, rows), rows)
        upstream = gn2[at, :]
        value = middle[at, :]
        centered = value - jnp.mean(value, axis=1, keepdims=True)
        inverse = lax.rsqrt(jnp.mean(centered * centered, axis=1, keepdims=True) + EPS)
        plain = centered * inverse
        scaled = upstream * gain2
        inner = (
            scaled
            - jnp.mean(scaled, axis=1, keepdims=True)
            - plain * jnp.mean(scaled * plain, axis=1, keepdims=True)
        )
        grad = cot_ref[at, :].astype(F32) + inverse * inner

        @pl.when(i == g)
        def _():
            gmid[...] = grad

        gbranch[at, :] = grad.astype(BF16)
        stat[s, 0:1, :] += jnp.sum(upstream * plain, axis=0, keepdims=True)
        stat[s, 1:2, :] += jnp.sum(upstream, axis=0, keepdims=True)
        return carry

    lax.fori_loop(0, T // rows, norm_two_back, 0)

    window = pl.ds(pl.multiple_of(jnp.maximum(part * g - 64, 0), 64), 256)
    gmix = dot_nt(gbranch[...], exit_all[window, :])
    gmix = jnp.where(g == 0, pltpu.roll(gmix, 64, axis=1), gmix)
    gmix = jnp.where(lane256 < 64, 0.0, gmix).astype(BF16).astype(F32)
    numer_grad = gmix * invden[...]
    product = numer_grad * att[...]
    for h in range(3):
        value = jnp.sum(product * slot_mask(h + 1), axis=1, keepdims=True)
        shift[h] = jnp.broadcast_to(value, (T, LANES))
        high = value.astype(BF16).astype(F32)
        low = value - high
        numer_grad = jnp.where(lane256 == 2 * h, high, numer_grad)
        numer_grad = jnp.where(lane256 == 2 * h + 1, low, numer_grad)
    dob[s] = numer_grad.astype(BF16)

    spread("do", dob, do_ssem, do_rsem, False)


    def down_piece(t, carry):
        at = pl.ds(pl.multiple_of(t * T, T), T)
        sum_down.block(t % 2, t // 2)[...] = dot_tn(active[:, at], cot_ref[...]).astype(BF16)
        return carry

    lax.fori_loop(0, NSEQ, down_piece, 0)
    reduce_start(1, sum_down)
    for i in range(2):
        exit_grad = dot_tn(mixed[...], gbranch[:, T * i : T * i + T]).astype(BF16)
        for t in range(NSEQ):
            first, low = D * (t // 2) + T * i, piece * (t % 2)
            ghid[low : low + piece, first : first + T] = exit_grad[piece * t : piece * t + piece, :]
    reduce_start(4, sum_exit)

    for h in range(3):
        qmask[h] = (dob[s].astype(F32) * slot_mask(h + 1)).astype(BF16)
    acc_a[...] = jnp.zeros_like(acc_a)

    def query_side(cc, carry):
        keys = pair_of(kv, cc, 0, 256)
        values = pair_of(kv, cc, 128, 384)
        for h in range(3):
            row_shift = jnp.concatenate([shift[h]] * (pair_width // LANES), axis=1)
            pressure = dot_nt(qmask[h], values) - row_shift
            slope = (masks[h, :, pair_lanes(cc)].astype(F32) * pressure).astype(BF16)
            acc_a[...] += dot_nn(slope, keys) * slot_mask(h)
        return carry

    lax.fori_loop(0, chip + 1, query_side, 0)
    dq = acc_a[...] * scale
    gather_sum(0, sum_up, ag_up)

    def weight_pieces(pieces, grad):
        for t in range(NSEQ):
            pieces[t % 2, t // 2] = grad[piece * t : piece * t + piece, :].astype(BF16)

    weight_pieces(pc_eq, dot_tn(n1[...], dq.astype(BF16)))
    reduce_start(2, sum_eq)

    reduce_pass(4, sum_exit)

    v_tile = kv[s, :, 128:384].astype(F32)
    k_tile = kv[s, :, 0:256].astype(F32)
    for h in range(3):
        qmask[h] = (k_tile * slot_mask(h)).astype(BF16)
        minus = jnp.where((lane256 == 2 * h) | (lane256 == 2 * h + 1), -1.0, 0.0)
        qmask[3 + h] = (v_tile * slot_mask(h + 1) + minus).astype(BF16)
    acc_b[...] = jnp.zeros_like(acc_b)
    acc_c[...] = jnp.zeros_like(acc_c)

    def key_side(j, carry):
        cc = chip + j
        wait_pair(dob, do_ssem, do_rsem, j, cc)
        other = 2 * cc + 1 - core
        to_seq(sib, qb.at[other], qb.at[other], q_ssem.at[0], q_rsem.at[other]).wait_recv()
        queries = pair_of(qb, cc, 0, 256)
        grads = pair_of(dob, cc, 0, 256)
        for h in range(3):
            count = masks[h, :, pair_lanes(jnp.where(j == 0, chips, cc))]
            weight = weights_of(dot_nt(qmask[h], queries), count)
            slope = (weight * dot_nt(qmask[3 + h], grads)).astype(BF16)
            acc_b[...] += dot_nn(slope, queries) * slot_mask(h)
            acc_c[...] += dot_nn(weight.astype(BF16), grads) * slot_mask(h + 1)

        @pl.when(j == 0)
        def _():
            reduce_pass(2, sum_eq)

        return carry

    lax.fori_loop(0, chips - chip, key_side, 0)

    dk, dv = acc_b[...] * scale, acc_c[...]
    part_sum = dot_nt(jnp.where(is_odd, pltpu.roll(dq, 64, axis=1), dq).astype(BF16), win[0])
    part_sum += dot_nt(jnp.where(is_odd, pltpu.roll(dk, 64, axis=1), dk).astype(BF16), win[1])
    part_sum += dot_nt(jnp.where(is_odd, dv, pltpu.roll(dv, 192, axis=1)).astype(BF16), win[2])
    gn2[...] = part_sum
    n2[...] = part_sum.astype(BF16)
    own_rows = pl.ds(pl.multiple_of(g * piece, piece), piece)

    def row_copies():
        found = []
        for step in range(1, NGRP):
            peer = lax.rem(g + step, NGRP)
            rows_of = pl.ds(pl.multiple_of(peer * piece, piece), piece)
            copy = to_grp(peer, n2.at[rows_of, :], drecv.at[g], zd_ssem.at[step - 1], zd_rsem.at[g])
            found.append((always, copy))
        return found

    launch("rows", row_copies)
    near_forward(*weight_gather(0, ag_up))

    def norm_one_sums(i, carry):
        at = pl.ds(pl.multiple_of(i * rows, rows), rows)
        value = tok_ref[at, :].astype(F32)
        centered = value - jnp.mean(value, axis=1, keepdims=True)
        inverse = lax.rsqrt(jnp.mean(centered * centered, axis=1, keepdims=True) + EPS)
        stat[s, 2:3, :] += jnp.sum(gn2[at, :] * (centered * inverse), axis=0, keepdims=True)
        stat[s, 3:4, :] += jnp.sum(gn2[at, :], axis=0, keepdims=True)
        return carry

    lax.fori_loop(0, T // rows, norm_one_sums, 0)

    def stat_copies():
        found = []
        for step in range(1, NSEQ):
            peer = lax.rem(s + step, NSEQ)
            copy = to_seq(peer, stat.at[s], stat.at[s], st_ssem.at[step - 1], st_rsem.at[s])
            found.append((always, copy))
        return found

    launch("stat", stat_copies)

    dpack = exit_all.at[0:T, 0:384]
    dpack[:, 0:128] = dk[:, 0:128].astype(BF16)
    dpack[:, 128:256] = join_halves(dk[:, 128:256], dv[:, 0:128]).astype(BF16)
    dpack[:, 256:384] = dv[:, 128:256].astype(BF16)
    weight_pieces(pc_ekv, dot_tn(n1[...], dpack[...]))
    reduce_start(3, sum_ekv)
    gather_sum(2, sum_eq, ag_eq)

    reduce_pass(3, sum_ekv)
    reduce_pass(1, sum_down)

    def through_down(i, carry):
        at = pl.ds(pl.multiple_of(i * 256, 256), 256)
        out_ref[:, at] = (middle[:, at] + dot_nn(active[...], down_all[:, at])).astype(BF16)
        return carry

    lax.fori_loop(0, D // 256, through_down, 0)

    upstream = gn2[own_rows, :]
    for step in range(1, NGRP):
        slot = lax.rem(g + step, NGRP)
        to_grp(slot, drecv.at[slot], drecv.at[slot], zd_ssem.at[0], zd_rsem.at[slot]).wait_recv()
        upstream = upstream + drecv[slot].astype(F32)
    value = tok_ref[own_rows, :].astype(F32)
    centered = value - jnp.mean(value, axis=1, keepdims=True)
    inverse = lax.rsqrt(jnp.mean(centered * centered, axis=1, keepdims=True) + EPS)
    plain = centered * inverse
    scaled = upstream * gain1
    inner = (
        scaled
        - jnp.mean(scaled, axis=1, keepdims=True)
        - plain * jnp.mean(scaled * plain, axis=1, keepdims=True)
    )
    tz[g] = (gmid[...] + inverse * inner).astype(BF16)
    middle_row = piece // 2
    token_gather = chain_parts(
        "token",
        (lambda i: tz.at[i, 0:middle_row], lambda i: tz.at[i, middle_row:piece]),
        zt_ssem,
        zt_rsem,
    )
    for part_of in token_gather:
        chain_start(*part_of)

    gather_sum(3, sum_ekv, ag_ekv)
    near_forward(*weight_gather(2, ag_eq))

    chain_finish(token_gather)
    near_forward(*weight_gather(3, ag_ekv))

    for step in range(1, NSEQ):
        slot = lax.rem(s + step, NSEQ)
        to_seq(sib, stat.at[slot], stat.at[slot], st_ssem.at[0], st_rsem.at[slot]).wait_recv()
    total_stat = stat[0]
    for i in range(1, NSEQ):
        total_stat = total_stat + stat[i]
    stat_z[g] = total_stat
    direct_start("stat z", lambda i: stat_z.at[i], sz_ssem, sz_rsem)

    near_wait(*weight_gather(0, ag_up))
    pass
    for i in range(NGRP):
        oup_ref[:, D * i : D * i + D] = ag_up[i]
    pass
    oexit_ref[...] = reduce_end(4, sum_exit)
    near_wait(*weight_gather(2, ag_eq))

    def place_entry(first, tiles):
        for tile, value in enumerate(tiles):
            at = first + tile * LANES
            oentry_ref[:, at : at + LANES] = value.astype(BF16)

    for pair in range(NGRP // 2):
        a = ag_eq[2 * pair].astype(F32)
        b = ag_eq[2 * pair + 1].astype(F32)
        turned = swap_halves(b[:, 0:128])
        place_entry(
            pair * 2 * part,
            (
                a[:, 0:128],
                join_halves(a[:, 128:256], turned),
                join_halves(turned, swap_halves(b[:, 128:256])),
            ),
        )
    odown_ref[...] = reduce_end(1, sum_down)
    for i in range(NGRP):
        tgrad_ref[piece * i : piece * i + piece, :] = tz[i]
    total_stat = jnp.zeros((8, D), F32)
    for step in range(1, NGRP):
        slot = lax.rem(g + step, NGRP)
        to_grp(slot, stat_z.at[slot], stat_z.at[slot], sz_ssem.at[0], sz_rsem.at[slot]).wait_recv()
    for i in range(NGRP):
        total_stat = total_stat + stat_z[i]
    row_id = lax.broadcasted_iota(jnp.int32, (8, 1), 0)
    ostat_ref[...] = jnp.where(row_id < 2, stat_z[g], total_stat)
    near_wait(*weight_gather(3, ag_ekv))
    for pair in range(NGRP // 2):
        a = ag_ekv[2 * pair].astype(F32)
        b = ag_ekv[2 * pair + 1].astype(F32)
        turned = swap_halves(b[:, 0:128])
        place_entry(
            D + pair * 2 * part,
            (
                a[:, 0:128],
                join_halves(a[:, 128:256], turned),
                join_halves(turned, swap_halves(b[:, 128:256])),
            ),
        )
        turned = swap_halves(a[:, 256:384])
        place_entry(
            2 * D + pair * 2 * part,
            (
                join_halves(swap_halves(a[:, 128:256]), turned),
                join_halves(turned, b[:, 128:256]),
                b[:, 256:384],
            ),
        )

    for copies in launched.values():
        for cond, copy in copies():
            pl.when(cond)(copy.wait_send)


def finish_kernel(
    out_in,
    tgrad_in,
    entry_in,
    exit_in,
    up_in,
    down_in,
    stat_in,
    out_hbm,
    tgrad_hbm,
    entry_hbm,
    exit_hbm,
    up_hbm,
    down_hbm,
    fgain_ref,
    fbias_ref,
    sgain_ref,
    sbias_ref,
    out_low,
    tgrad_low,
    down_low,
    up_low,
    entry_low,
    exit_low,
    stat_low,
    down_full,
    up_full,
    entry_full,
    exit_full,
    sems,
):
    plans = (
        (down_in, down_low, down_full, down_hbm),
        (up_in, up_low, up_full, up_hbm),
        (entry_in, entry_low, entry_full, entry_hbm),
        (exit_in, exit_low, exit_full, exit_hbm),
        (out_in, out_low, out_low, out_hbm),
        (tgrad_in, tgrad_low, tgrad_low, tgrad_hbm),
    )
    loads = [
        pltpu.make_async_copy(source, low, sems.at[6 + i])
        for i, (source, low, _, _) in enumerate(plans)
    ]
    stat_load = pltpu.make_async_copy(stat_in, stat_low, sems.at[12])
    for copy in [*loads, stat_load]:
        copy.start()
    copies = []
    for i, (_, low, full, target) in enumerate(plans):
        loads[i].wait()
        if full is not low:
            full[...] = low[...].astype(F32)
        copy = pltpu.make_async_copy(full, target, sems.at[i])
        copy.start()
        copies.append(copy)
    stat_load.wait()
    width = stat_low.shape[1]
    part = fgain_ref.shape[0]
    first = lax.axis_index("seq") * part
    turned = pltpu.roll(stat_low[...], lax.rem(width - first, width), axis=1)
    fgain_ref[...] = turned[2:3, 0:part].reshape(part)
    fbias_ref[...] = turned[3:4, 0:part].reshape(part)
    sgain_ref[...] = turned[0:1, 0:part].reshape(part)
    sbias_ref[...] = turned[1:2, 0:part].reshape(part)
    for copy in copies:
        copy.wait()


def fast_on_device(
    seq_count,
    tokens,
    cotangent,
    entry_weight,
    exit_weight,
    up_weight,
    down_weight,
    first_gain,
    first_bias,
    second_gain,
    second_bias,
    dilations,
    offsets,
):
    T, D = tokens.shape
    NGRP, HEADS = offsets.shape
    FF = up_weight.shape[1]
    E = D // HEADS
    NSEQ = seq_count
    chips = NSEQ // 2
    sizes = (T, D, HEADS, E, FF, NSEQ, NGRP)
    piece = D // NSEQ
    vmem = pl.BlockSpec(memory_space=pltpu.VMEM)
    smem = pl.BlockSpec(memory_space=pltpu.SMEM)
    anywhere = pl.BlockSpec(memory_space=pl.ANY)
    dma = pltpu.SemaphoreType.DMA
    scratch = [
        pltpu.VMEM((3, D, 256), BF16),
        pltpu.VMEM((D, D), BF16),
        pltpu.VMEM((D, FF), BF16),
        pltpu.VMEM((FF, D), BF16),
        pltpu.VMEM((T, D), BF16),
        pltpu.VMEM((T, D), BF16),
        pltpu.VMEM((T, D), F32),
        pltpu.VMEM((piece, D), F32),
        pltpu.VMEM((T, D), BF16),
        pltpu.VMEM((T, D), BF16),
        pltpu.VMEM((T, FF), BF16),
        pltpu.VMEM((T, FF), BF16),
        pltpu.VMEM((T, D), F32),
        pltpu.VMEM((3, T, LANES), BF16),
        pltpu.VMEM((3, T, (NSEQ + 2) * T), BF16),
        pltpu.VMEM((NSEQ, T, 384), BF16),
        pltpu.VMEM((NSEQ, T, 256), BF16),
        pltpu.VMEM((NSEQ, T, 256), BF16),
        pltpu.VMEM((6, T, 256), BF16),
        pltpu.VMEM((3, T, LANES), F32),
        pltpu.VMEM((T, 256), F32),
        pltpu.VMEM((T, 256), F32),
        pltpu.VMEM((T, 256), F32),
        pltpu.VMEM((T, 256), F32),
        pltpu.VMEM((T, 256), F32),
        pltpu.VMEM((NGRP, 3, T // 2, LANES), BF16),
        pltpu.VMEM((NGRP, piece, D), BF16),
        pltpu.VMEM((NGRP, piece, D), BF16),
        pltpu.VMEM((NSEQ, 8, D), F32),
        pltpu.VMEM((NGRP, 8, D), F32),
    ]
    scratch += [
        pltpu.VMEM((piece, chips * D), BF16),
        pltpu.VMEM((chips - 1, piece, D), BF16),
        pltpu.VMEM((T, chips * D), BF16),
        pltpu.VMEM((chips - 1, T, D), BF16),
    ]
    for rows, cols in ((piece, D), (piece, 256), (piece, 384)):
        scratch += [
            pltpu.VMEM((2, chips, rows, cols), BF16),
            pltpu.VMEM((chips, rows, cols), BF16),
            pltpu.VMEM((chips - 1, rows, cols), BF16),
            pltpu.VMEM((NGRP, rows, cols), BF16),
        ]
    scratch += [
        dma((7,)),
        dma((7,)),
        dma((NSEQ,)),
        dma((7,)),
        dma((NSEQ,)),
        dma((7,)),
        dma((NSEQ,)),
        dma((2, 3, 2)),
        dma((2, NGRP)),
        dma((NGRP - 1,)),
        dma((NGRP,)),
        dma((2, 3, 2)),
        dma((2, NGRP)),
        dma((5,)),
        dma((5,)),
        dma((5, 3)),
        dma((5, chips - 1)),
        dma((4, 3, 2)),
        dma((4, NGRP)),
        dma((NSEQ - 1,)),
        dma((NSEQ,)),
        dma((NGRP - 1,)),
        dma((NGRP,)),
    ]
    out_shape = (
        jax.ShapeDtypeStruct((T, D), BF16),
        jax.ShapeDtypeStruct((T, D), BF16),
        jax.ShapeDtypeStruct((piece, 3 * D), BF16),
        jax.ShapeDtypeStruct((piece, D), BF16),
        jax.ShapeDtypeStruct((piece, FF), BF16),
        jax.ShapeDtypeStruct((T, D), BF16),
        jax.ShapeDtypeStruct((8, D), F32),
    )
    output, token_grad, entry_grad, exit_grad, up_grad, down_grad, stats = pl.pallas_call(
        partial(layer_kernel, sizes),
        out_shape=out_shape,
        in_specs=[smem] * 2 + [vmem] * 6 + [anywhere] * 4,
        out_specs=tuple([vmem] * 7),
        scratch_shapes=scratch,
        compiler_params=pltpu.CompilerParams(
            collective_id=0, has_side_effects=True, vmem_limit_bytes=63 * 1024 * 1024
        ),
        name="layer",
    )(
        dilations,
        offsets,
        tokens,
        cotangent,
        first_gain,
        first_bias,
        second_gain,
        second_bias,
        entry_weight,
        exit_weight,
        up_weight,
        down_weight,
    )
    part = piece
    finish_shape = (
        jax.ShapeDtypeStruct((T, D), BF16),
        jax.ShapeDtypeStruct((T, D), BF16),
        jax.ShapeDtypeStruct((part, 3 * D), F32),
        jax.ShapeDtypeStruct((part, D), F32),
        jax.ShapeDtypeStruct((part, FF), F32),
        jax.ShapeDtypeStruct((T, D), F32),
    ) + tuple([jax.ShapeDtypeStruct((part,), F32)] * 4)
    return pl.pallas_call(
        finish_kernel,
        out_shape=finish_shape,
        in_specs=[anywhere] * 7,
        out_specs=tuple([anywhere] * 6 + [vmem] * 4),
        scratch_shapes=[
            pltpu.VMEM((T, D), BF16),
            pltpu.VMEM((T, D), BF16),
            pltpu.VMEM((T, D), BF16),
            pltpu.VMEM((part, FF), BF16),
            pltpu.VMEM((part, 3 * D), BF16),
            pltpu.VMEM((part, D), BF16),
            pltpu.VMEM((8, D), F32),
            pltpu.VMEM((T, D), F32),
            pltpu.VMEM((part, FF), F32),
            pltpu.VMEM((part, 3 * D), F32),
            pltpu.VMEM((part, D), F32),
            dma((13,)),
        ],
        compiler_params=pltpu.CompilerParams(vmem_limit_bytes=62 * 1024 * 1024),
        name="finish",
    )(output, token_grad, entry_grad, exit_grad, up_grad, down_grad, stats)


def solution(mesh):
    seq_count = mesh.shape["seq"]
    fast = seq_count == 8 and mesh.shape["grp"] == 4
    return jax.shard_map(
        partial(fast_on_device, seq_count) if fast else on_device,
        mesh=mesh,
        in_specs=(P("seq", None), P("seq", None), P(), P(), P(), P(), P(), P(), P(), P(), P(), P()),
        out_specs=(
            P("seq", None),
            P("seq", None),
            P("seq", None),
            P("seq", None),
            P("seq", None),
            P("seq", None),
            P("seq"),
            P("seq"),
            P("seq"),
            P("seq"),
        ),
        check_vma=False,
    )
```

```python
from functools import partial

import jax
import jax.numpy as jnp
from jax import lax
from jax.experimental import pallas as pl
from jax.experimental.pallas import tpu as pltpu
from jax.sharding import PartitionSpec as P

RATE_MIN = 2
RATE_MAX = 8


EPS = 1e-05
PRECISE = lax.Precision.HIGHEST


def norm_forward(values, gain_vec, bias_vec):
    centered = values - jnp.mean(values, axis=1, keepdims=True)
    inverse = lax.rsqrt(jnp.mean(centered * centered, axis=1, keepdims=True) + EPS)
    plain = centered * inverse
    return (plain * gain_vec + bias_vec, plain, inverse)


def norm_backward(upstream, plain, inverse, gain_vec):
    scaled = upstream * gain_vec
    inner = (
        scaled
        - jnp.mean(scaled, axis=1, keepdims=True)
        - plain * jnp.mean(scaled * plain, axis=1, keepdims=True)
    )
    return (inverse * inner, jnp.sum(upstream * plain, axis=0), jnp.sum(upstream, axis=0))


def key_weights(query_sp, query_pos, key_block, first_row, geometry):
    local_len, capacity, dilation, segment, head_offs, score_scale = geometry
    key_count = key_block.shape[0]
    key_heads = key_block.reshape(key_count, query_sp.shape[1], query_sp.shape[2])
    scores = (
        jnp.einsum("ihd,jhd->hij", query_sp, key_heads, preferred_element_type=jnp.float32)
        * score_scale
    )
    key_index = first_row + jnp.arange(key_count, dtype=jnp.int32)
    source = key_index // capacity
    within = key_index - source * capacity
    key_pos = source[None, :] * local_len + head_offs[:, None] + dilation * within[None, :]
    key_live = within < local_len // dilation
    earlier = key_pos[:, None, :] <= query_pos[:, :, None]
    segment_match = key_pos[:, None, :] // segment == query_pos[:, :, None] // segment
    allowed = earlier & segment_match & key_live[None, None, :]
    return (jnp.where(allowed, jnp.exp(scores), 0.0), key_heads)


def forward_block(running, pieces, first_row, query_sp, query_pos, geometry):
    numerator, denominator = running
    key_block, value_block = pieces
    weights, key_heads = key_weights(query_sp, query_pos, key_block, first_row, geometry)
    value_heads = value_block.reshape(key_heads.shape)
    numerator = numerator + jnp.einsum(
        "hij,jhd->hid",
        weights.astype(jnp.bfloat16),
        value_heads,
        preferred_element_type=jnp.float32,
    )
    return (numerator, denominator + jnp.sum(weights, axis=2))


def blockwise(step_fn, running, pieces, first_row, block_rows):
    total_rows = pieces[0].shape[0]
    if total_rows > block_rows and total_rows % block_rows == 0:
        number = total_rows // block_rows
        stacked_first = pieces[0].reshape(number, block_rows, pieces[0].shape[1])
        stacked_second = pieces[1].reshape(number, block_rows, pieces[1].shape[1])
        block_starts = first_row + block_rows * jnp.arange(number, dtype=jnp.int32)

        def advance(state, items):
            return (step_fn(state, (items[0], items[1]), items[2]), None)

        running, _ = lax.scan(advance, running, (stacked_first, stacked_second, block_starts))
        return running
    return step_fn(running, pieces, first_row)


def backward_block(running, items, query_sp, query_pos, grad_sp, shift_sp, geometry):
    key_block, value_block, first_row = items
    score_scale = geometry[5]
    weights, key_heads = key_weights(query_sp, query_pos, key_block, first_row, geometry)
    key_count = key_block.shape[0]
    value_heads = value_block.reshape(key_heads.shape)
    pressure = jnp.einsum("ihd,jhd->hij", grad_sp, value_heads, preferred_element_type=jnp.float32)
    slopes = (weights * (pressure - shift_sp[:, :, None])).astype(jnp.bfloat16)
    running = (
        running
        + jnp.einsum("hij,jhd->ihd", slopes, key_heads, preferred_element_type=jnp.float32)
        * score_scale
    )
    grad_keys = (
        jnp.einsum("hij,ihd->jhd", slopes, query_sp, preferred_element_type=jnp.float32)
        * score_scale
    )
    grad_values = jnp.einsum(
        "hij,ihd->jhd", weights.astype(jnp.bfloat16), grad_sp, preferred_element_type=jnp.float32
    )
    return (running, (grad_keys.reshape(key_count, -1), grad_values.reshape(key_count, -1)))


def local_weights(query_heads, key_heads, score_scale):
    local_len = query_heads.shape[0]
    scores = (
        jnp.einsum("ihd,jhd->hij", query_heads, key_heads, preferred_element_type=jnp.float32)
        * score_scale
    )
    positions = jnp.arange(local_len, dtype=jnp.int32)
    causal = positions[:, None] >= positions[None, :]
    return jnp.where(causal[None], jnp.exp(scores), 0.0)


def on_device(
    tokens,
    cotangent,
    entry_weight,
    exit_weight,
    up_weight,
    down_weight,
    first_gain,
    first_bias,
    second_gain,
    second_bias,
    dilations,
    offsets,
):
    local_len, width_model = tokens.shape
    head_count = offsets.shape[1]
    head_size = width_model // head_count
    score_scale = head_size ** (-0.5)
    capacity = local_len // RATE_MIN
    group_idx = lax.axis_index("grp")
    seq_index = lax.axis_index("seq")
    seq_count = lax.axis_size("seq")
    dilation = lax.dynamic_index_in_dim(dilations, group_idx, 0, keepdims=False)
    head_offs = lax.dynamic_index_in_dim(offsets, group_idx, 0, keepdims=False)
    segment = local_len * seq_count * dilation // RATE_MAX
    step_ids = jnp.arange(capacity, dtype=jnp.int32)
    row_live = step_ids < local_len // dilation
    local_rows = jnp.minimum(head_offs[:, None] + dilation * step_ids[None, :], local_len - 1)
    query_pos = jnp.where(
        row_live[None, :],
        seq_index * local_len + head_offs[:, None] + dilation * step_ids[None, :],
        -1,
    )
    geometry = (local_len, capacity, dilation, segment, head_offs, score_scale)
    head_shape = (local_len, head_count, head_size)
    selector = local_rows[:, :, None] == jnp.arange(local_len, dtype=jnp.int32)[None, None, :]
    select_low = selector.astype(jnp.bfloat16)
    select_full = selector.astype(jnp.float32)

    def pick(array_in):
        return jnp.einsum(
            "hci,ihd->chd", select_low, array_in, preferred_element_type=jnp.float32
        ).astype(jnp.bfloat16)

    def place_back(sparse_in):
        return jnp.einsum("hci,chd->ihd", select_full, sparse_in, precision=PRECISE)

    inputs = tokens.astype(jnp.float32)
    normed_one, plain_one, inverse_one = norm_forward(inputs, first_gain, first_bias)
    normed_low = normed_one.astype(jnp.bfloat16)
    packed = jnp.dot(normed_low, entry_weight, preferred_element_type=jnp.float32).astype(
        jnp.bfloat16
    )
    query_heads = packed[:, :width_model].reshape(head_shape)
    key_heads = packed[:, width_model : 2 * width_model].reshape(head_shape)
    value_heads = packed[:, 2 * width_model :].reshape(head_shape)
    query_sp = pick(query_heads)
    key_sp = pick(key_heads).reshape(capacity, width_model)
    value_sp = pick(value_heads).reshape(capacity, width_model)
    empty_state = (
        jnp.zeros((head_count, capacity, head_size), jnp.float32),
        jnp.zeros((head_count, capacity), jnp.float32),
    )
    forward_step = partial(forward_block, query_sp=query_sp, query_pos=query_pos, geometry=geometry)
    numerator, denominator = blockwise(
        forward_step,
        empty_state,
        (
            lax.all_gather(key_sp, "seq", axis=0, tiled=True),
            lax.all_gather(value_sp, "seq", axis=0, tiled=True),
        ),
        jnp.int32(0),
        8 * capacity,
    )

    def local_part(query_in, key_in, value_in):
        weights = local_weights(query_in, key_in, score_scale)
        local_num = jnp.einsum(
            "hij,jhd->ihd",
            weights.astype(jnp.bfloat16),
            value_in,
            preferred_element_type=jnp.float32,
        )
        return (local_num, jnp.sum(weights, axis=2).T)

    def local_none(query_in, key_in, value_in):
        return (jnp.zeros(head_shape, jnp.float32), jnp.zeros((local_len, head_count), jnp.float32))

    local_num, local_den = lax.cond(
        group_idx == 0, local_part, local_none, query_heads, key_heads, value_heads
    )
    numerator_full = (
        jnp.einsum("hci,hcd->ihd", select_full, numerator, precision=PRECISE) + local_num
    )
    denominator_full = (
        jnp.einsum("hci,hc->ih", select_full, denominator, precision=PRECISE) + local_den
    )
    merged_num, merged_den = lax.psum(
        (numerator_full.reshape(local_len, width_model), denominator_full), "grp"
    )
    attention = merged_num.reshape(head_shape) / merged_den[:, :, None]
    mixed = attention.reshape(local_len, width_model).astype(jnp.bfloat16)
    middle = inputs + jnp.dot(mixed, exit_weight, preferred_element_type=jnp.float32)
    normed_two, plain_two, inverse_two = norm_forward(middle, second_gain, second_bias)
    normed_two_low = normed_two.astype(jnp.bfloat16)
    hidden = jnp.dot(normed_two_low, up_weight, preferred_element_type=jnp.float32)
    active = jax.nn.gelu(hidden, approximate=False).astype(jnp.bfloat16)
    output = (middle + jnp.dot(active, down_weight, preferred_element_type=jnp.float32)).astype(
        jnp.bfloat16
    )
    down_grad = jnp.dot(active.T, cotangent, preferred_element_type=jnp.float32)
    grad_active = jnp.dot(cotangent, down_weight.T, preferred_element_type=jnp.float32)
    _, gelu_pull = jax.vjp(partial(jax.nn.gelu, approximate=False), hidden)
    grad_hidden = gelu_pull(grad_active)[0].astype(jnp.bfloat16)
    up_grad = jnp.dot(normed_two_low.T, grad_hidden, preferred_element_type=jnp.float32)
    grad_normed_two = jnp.dot(grad_hidden, up_weight.T, preferred_element_type=jnp.float32)
    grad_plain_two, second_gain_grad, second_bias_grad = norm_backward(
        grad_normed_two, plain_two, inverse_two, second_gain
    )
    grad_middle = cotangent.astype(jnp.float32) + grad_plain_two
    grad_branch = grad_middle.astype(jnp.bfloat16)
    exit_grad = jnp.dot(mixed.T, grad_branch, preferred_element_type=jnp.float32)
    grad_mixed_low = lax.optimization_barrier(
        jnp.dot(grad_branch, exit_weight.T, preferred_element_type=jnp.float32).astype(jnp.bfloat16)
    )
    grad_mixed = grad_mixed_low.astype(jnp.float32).reshape(head_shape)
    grad_numer = (grad_mixed / merged_den[:, :, None]).astype(jnp.bfloat16)
    row_shift = jnp.sum(grad_mixed * attention, axis=2) / merged_den
    grad_sp = pick(grad_numer)
    shift_sp = jnp.einsum("hci,ih->hc", select_full, row_shift, precision=PRECISE)
    back_keys, back_values = (
        lax.all_gather(key_sp, "seq", axis=0, tiled=True),
        lax.all_gather(value_sp, "seq", axis=0, tiled=True),
    )
    block_rows = 8 * capacity
    number = back_keys.shape[0] // block_rows
    stacked_keys = back_keys.reshape(number, block_rows, width_model)
    stacked_values = back_values.reshape(number, block_rows, width_model)
    block_starts = block_rows * jnp.arange(number, dtype=jnp.int32)
    empty_query = jnp.zeros((capacity, head_count, head_size), jnp.float32)
    back_step = partial(
        backward_block,
        query_sp=query_sp,
        query_pos=query_pos,
        grad_sp=grad_sp,
        shift_sp=shift_sp,
        geometry=geometry,
    )
    grad_query_sp, (grad_key_all, grad_value_all) = lax.scan(
        back_step, empty_query, (stacked_keys, stacked_values, block_starts)
    )
    own_keys, own_values = (
        lax.psum_scatter(
            grad_key_all.reshape(-1, width_model), "seq", scatter_dimension=0, tiled=True
        ),
        lax.psum_scatter(
            grad_value_all.reshape(-1, width_model), "seq", scatter_dimension=0, tiled=True
        ),
    )

    def local_grads(query_in, key_in, value_in, grad_in, shift_in):
        weights = local_weights(query_in, key_in, score_scale)
        pressure = jnp.einsum("ihd,jhd->hij", grad_in, value_in, preferred_element_type=jnp.float32)
        slopes = (weights * (pressure - shift_in.T[:, :, None])).astype(jnp.bfloat16)
        grad_query = (
            jnp.einsum("hij,jhd->ihd", slopes, key_in, preferred_element_type=jnp.float32)
            * score_scale
        )
        grad_key = (
            jnp.einsum("hij,ihd->jhd", slopes, query_in, preferred_element_type=jnp.float32)
            * score_scale
        )
        grad_value = jnp.einsum(
            "hij,ihd->jhd",
            weights.astype(jnp.bfloat16),
            grad_in,
            preferred_element_type=jnp.float32,
        )
        return (grad_query, grad_key, grad_value)

    def local_skip(query_in, key_in, value_in, grad_in, shift_in):
        zeros_heads = jnp.zeros(head_shape, jnp.float32)
        return (zeros_heads, zeros_heads, zeros_heads)

    local_dq, local_dk, local_dv = lax.cond(
        group_idx == 0,
        local_grads,
        local_skip,
        query_heads,
        key_heads,
        value_heads,
        grad_numer,
        row_shift,
    )
    grad_query_full = place_back(grad_query_sp) + local_dq
    grad_key_full = place_back(own_keys.reshape(capacity, head_count, head_size)) + local_dk
    grad_value_full = place_back(own_values.reshape(capacity, head_count, head_size)) + local_dv
    grad_packed = jnp.concatenate(
        [
            grad_query_full.reshape(local_len, width_model),
            grad_key_full.reshape(local_len, width_model),
            grad_value_full.reshape(local_len, width_model),
        ],
        axis=1,
    )
    summed = lax.psum(grad_packed, "grp").astype(jnp.bfloat16)
    entry_grad = jnp.dot(normed_low.T, summed, preferred_element_type=jnp.float32)
    grad_normed_one = jnp.dot(summed, entry_weight.T, preferred_element_type=jnp.float32)
    grad_plain_one, first_gain_grad, first_bias_grad = norm_backward(
        grad_normed_one, plain_one, inverse_one, first_gain
    )
    token_grad = (grad_middle + grad_plain_one).astype(jnp.bfloat16)
    shards = (
        lax.psum_scatter(entry_grad, "seq", scatter_dimension=0, tiled=True),
        lax.psum_scatter(exit_grad, "seq", scatter_dimension=0, tiled=True),
        lax.psum_scatter(up_grad, "seq", scatter_dimension=0, tiled=True),
        lax.psum_scatter(down_grad, "seq", scatter_dimension=0, tiled=True),
        lax.psum_scatter(first_gain_grad, "seq", scatter_dimension=0, tiled=True),
        lax.psum_scatter(first_bias_grad, "seq", scatter_dimension=0, tiled=True),
        lax.psum_scatter(second_gain_grad, "seq", scatter_dimension=0, tiled=True),
        lax.psum_scatter(second_bias_grad, "seq", scatter_dimension=0, tiled=True),
    )
    return (
        output,
        token_grad,
        shards[0],
        shards[1],
        shards[2],
        shards[3],
        shards[4],
        shards[5],
        shards[6],
        shards[7],
    )


MESH = pl.DeviceIdType.MESH
LANES = 128
LOG2E = 1.4426950408889634
F32 = jnp.float32
BF16 = jnp.bfloat16


def dot_nn(left, right):
    return lax.dot_general(left, right, (((1,), (0,)), ((), ())), preferred_element_type=F32)


def dot_nt(left, right):
    return lax.dot_general(left, right, (((1,), (1,)), ((), ())), preferred_element_type=F32)


def dot_tn(left, right):
    return lax.dot_general(left, right, (((0,), (0,)), ((), ())), preferred_element_type=F32)


def lane_ids(width):
    return lax.broadcasted_iota(jnp.int32, (1, width), 1)


def slot_mask(slot, width=256):
    ids = lane_ids(width)
    return jnp.where((ids >= 64 * slot) & (ids < 64 * slot + 64), 1.0, 0.0).astype(F32)


def join_halves(low_part, high_part):
    return jnp.where(lane_ids(LANES) < 64, low_part, high_part)


def swap_halves(tile):
    return pltpu.roll(tile, 64, axis=1)


def layer_kernel(
    sizes,
    dil_ref,
    off_ref,
    tok_ref,
    cot_ref,
    gain1_ref,
    bias1_ref,
    gain2_ref,
    bias2_ref,
    entry_hbm,
    exit_hbm,
    up_hbm,
    down_hbm,
    out_ref,
    tgrad_ref,
    oentry_ref,
    oexit_ref,
    oup_ref,
    odown_ref,
    ostat_ref,
    win,
    exit_all,
    up_all,
    down_all,
    n1,
    n2,
    middle,
    gmid,
    gbranch,
    mixed,
    active,
    ghid,
    gn2,
    member,
    masks,
    kv,
    qb,
    dob,
    qmask,
    shift,
    invden,
    att,
    acc_a,
    acc_b,
    acc_c,
    zmix,
    drecv,
    tz,
    stat,
    stat_z,
    r1_exit,
    r2_exit,
    r1_down,
    r2_down,
    pc_up,
    r1_up,
    r2_up,
    ag_up,
    pc_eq,
    r1_eq,
    r2_eq,
    ag_eq,
    pc_ekv,
    r1_ekv,
    r2_ekv,
    ag_ekv,
    load_sem,
    kv_ssem,
    kv_rsem,
    q_ssem,
    q_rsem,
    do_ssem,
    do_rsem,
    zm_ssem,
    zm_rsem,
    zd_ssem,
    zd_rsem,
    zt_ssem,
    zt_rsem,
    rs_s1,
    rs_r1,
    rs_s2,
    rs_r2,
    rs_zs,
    rs_zr,
    st_ssem,
    st_rsem,
    sz_ssem,
    sz_rsem,
):
    T, D, HEADS, E, FF, NSEQ, NGRP = sizes
    scale = E ** (-0.5)
    exp_scale = scale * LOG2E
    s = lax.axis_index("seq")
    g = lax.axis_index("grp")
    chip = s // 2
    core = s % 2
    sib = s + 1 - 2 * core
    odd = g % 2
    chips = NSEQ // 2
    part = D // NGRP
    is_odd = odd == 1
    gain1 = gain1_ref[...].reshape(1, D)
    bias1 = bias1_ref[...].reshape(1, D)
    gain2 = gain2_ref[...].reshape(1, D)
    bias2 = bias2_ref[...].reshape(1, D)

    def to_seq(peer, src, dst, ssem, rsem):
        return pltpu.make_async_remote_copy(
            src_ref=src,
            dst_ref=dst,
            send_sem=ssem,
            recv_sem=rsem,
            device_id={"seq": peer},
            device_id_type=MESH,
        )

    def to_grp(peer, src, dst, ssem, rsem):
        return pltpu.make_async_remote_copy(
            src_ref=src,
            dst_ref=dst,
            send_sem=ssem,
            recv_sem=rsem,
            device_id={"grp": peer},
            device_id_type=MESH,
        )

    loads = []
    for t in range(3):
        first = pl.multiple_of(t * D + part * g - 64 * odd, LANES)
        loads.append(
            pltpu.make_async_copy(entry_hbm.at[:, pl.ds(first, 256)], win.at[t], load_sem.at[t])
        )
    loads.append(pltpu.make_async_copy(down_hbm, down_all, load_sem.at[3]))
    loads.append(pltpu.make_async_copy(exit_hbm, exit_all, load_sem.at[4]))
    loads.append(pltpu.make_async_copy(up_hbm, up_all, load_sem.at[5]))
    for load in loads[:3]:
        load.start()

    barrier = pltpu.get_barrier_semaphore()
    for step in range(1, NSEQ):
        pl.semaphore_signal(
            barrier, inc=1, device_id={"seq": lax.rem(s + step, NSEQ)}, device_id_type=MESH
        )
    for step in range(1, NGRP):
        pl.semaphore_signal(
            barrier, inc=1, device_id={"grp": lax.rem(g + step, NGRP)}, device_id_type=MESH
        )

    rows = D // NSEQ

    def norm_one(i, carry):
        at = pl.ds(pl.multiple_of(i * rows, rows), rows)
        value = tok_ref[at, :].astype(F32)
        centered = value - jnp.mean(value, axis=1, keepdims=True)
        inverse = lax.rsqrt(jnp.mean(centered * centered, axis=1, keepdims=True) + EPS)
        n1[at, :] = (centered * inverse * gain1 + bias1).astype(BF16)
        return carry

    lax.fori_loop(0, T // rows, norm_one, 0)

    for load in loads[:3]:
        load.wait()
    for load in loads[3:]:
        load.start()
    lane256 = lane_ids(256)
    q_raw = dot_nn(n1[...], win[0])
    k_raw = dot_nn(n1[...], win[1])
    v_raw = dot_nn(n1[...], win[2])
    q_own = jnp.where(is_odd, pltpu.roll(q_raw, 192, axis=1), q_raw)
    k_own = jnp.where(is_odd, pltpu.roll(k_raw, 192, axis=1), k_raw)
    v_own = jnp.where(is_odd, v_raw, pltpu.roll(v_raw, 64, axis=1))
    q_own = jnp.where(lane256 < 192, q_own, 0.0)
    qb[s] = q_own.astype(BF16)
    for h in range(3):
        qmask[h] = (q_own * slot_mask(h)).astype(BF16)
    kv[s, :, 0:128] = k_own[:, 0:128].astype(BF16)
    kv[s, :, 128:256] = join_halves(k_own[:, 128:256], v_own[:, 0:128]).astype(BF16)
    kv[s, :, 256:384] = v_own[:, 128:256].astype(BF16)

    pl.semaphore_wait(barrier, NSEQ - 1 + NGRP - 1)

    launched = {}

    def launch(name, copies):
        for cond, copy in copies():
            pl.when(cond)(copy.start)
        launched[name] = copies

    always = core >= 0

    def spread(name, buffer, ssem, rsem, upward):
        def copies():
            found = []
            for d in range(1, chips):
                peer = lax.rem(s + (2 * d if upward else NSEQ - 2 * d), NSEQ)
                cond = chip + d < chips if upward else chip >= d
                found.append(
                    (cond, to_seq(peer, buffer.at[s], buffer.at[s], ssem.at[d - 1], rsem.at[s]))
                )
            found.append((always, to_seq(sib, buffer.at[s], buffer.at[s], ssem.at[3], rsem.at[s])))
            return found

        launch(name, copies)

    spread("kv", kv, kv_ssem, kv_rsem, True)
    spread("q", qb, q_ssem, q_rsem, False)

    lane128 = lane_ids(LANES)
    rate_row = jnp.ones((1, LANES), F32)
    for i in range(NGRP):
        rate_row = jnp.where(lane128 == i, dil_ref[i].astype(F32), rate_row)
    local_pos = lax.broadcasted_iota(jnp.int32, (T, 1), 0).astype(F32)
    residue = local_pos - rate_row * jnp.floor((local_pos + 0.5) / rate_row)
    for h in range(3):
        off_row = jnp.full((1, LANES), -1.0, F32)
        for i in range(NGRP):
            off_row = jnp.where(
                lane128 == i, off_ref[i, 3 * g + h].astype(F32), off_row
            )
        member[h] = jnp.where(residue == off_row, 1.0, 0.0).astype(BF16)
    per_segment = rate_row * (T * NSEQ // RATE_MAX)

    def segment_of(block):
        return jnp.floor((jnp.full((1, LANES), block * T, jnp.int32).astype(F32) + 0.5) / per_segment)

    own_segment = segment_of(s)

    pair_width = 2 * T

    def pair_lanes(cc):
        return pl.ds(pl.multiple_of(cc * pair_width, LANES), pair_width)

    def build_mask(cc, carry):
        for h in range(3):
            blocks = []
            for i in range(2):
                same = jnp.where(segment_of(2 * cc + i) == own_segment, 1.0, 0.0)
                blocks.append((member[h].astype(F32) * same).astype(BF16))
            count = dot_nt(member[h], jnp.concatenate(blocks, axis=0))
            masks[h, :, pair_lanes(cc)] = count.astype(BF16)
        return carry

    lax.fori_loop(0, chips, build_mask, 0)
    own_id = lax.broadcasted_iota(jnp.int32, (T, pair_width), 0) + core * T
    pair_id = lax.broadcasted_iota(jnp.int32, (T, pair_width), 1)
    own_block = (pair_id >= core * T) & (pair_id < core * T + T)
    for h in range(3):
        count = masks[h, :, pair_lanes(chip)].astype(F32) + jnp.where(own_block, 1.0, 0.0)
        masks[h, :, pair_lanes(chip)] = jnp.where(pair_id <= own_id, count, 0.0).astype(BF16)
        masks[h, :, pair_lanes(chips)] = jnp.where(own_id <= pair_id, count, 0.0).astype(BF16)

    half = T // 2
    piece = D // NSEQ

    def pack_half(tile, high):
        top, bottom = tile[0:half], tile[half:T]
        if high:
            return join_halves(swap_halves(top), bottom).astype(BF16)
        return join_halves(top, swap_halves(bottom)).astype(BF16)

    right, left = lax.rem(g + 1, NGRP), lax.rem(g + NGRP - 1, NGRP)

    def chain_start(name, at, ssem, rsem):
        launch(
            name + "0",
            lambda: [
                (g + 1 < NGRP, to_grp(right, at(g), at(g), ssem().at[0, 0], rsem().at[g])),
                (g >= 1, to_grp(left, at(g), at(g), ssem().at[0, 1], rsem().at[g])),
            ],
        )

    def chain_step(d, name, at, ssem, rsem):
        def slots():
            return lax.rem(g - d + NGRP, NGRP), lax.rem(g + d, NGRP)

        def copies():
            lower, upper = slots()
            return [
                (
                    (g - d >= 0) & (g + 1 < NGRP),
                    to_grp(right, at(lower), at(lower), ssem().at[d, 0], rsem().at[lower]),
                ),
                (
                    (g + d < NGRP) & (g >= 1),
                    to_grp(left, at(upper), at(upper), ssem().at[d, 1], rsem().at[upper]),
                ),
            ]

        lower, upper = slots()
        pl.when(g - d >= 0)(
            to_grp(right, at(lower), at(lower), ssem().at[0, 0], rsem().at[lower]).wait_recv
        )
        pl.when(g + d < NGRP)(
            to_grp(left, at(upper), at(upper), ssem().at[0, 1], rsem().at[upper]).wait_recv
        )
        if d < NGRP - 1:
            launch(name + str(d), copies)

    def chain_parts(name, views, ssem, rsem):
        return [
            (name + str(i), view, lambda i=i: ssem.at[i], lambda i=i: rsem.at[i])
            for i, view in enumerate(views)
        ]

    def chain_finish(parts):
        for d in range(1, NGRP):
            for part_of in parts:
                chain_step(d, *part_of)

    def near_start(name, at, ssem, rsem):
        def copies():
            found = []
            for i, step in enumerate((1, -1, 2, -2)):
                peer = g + step
                to = lax.rem(peer + NGRP, NGRP)
                sem = ssem().at[i // 2, i % 2]
                found.append(((peer >= 0) & (peer < NGRP), to_grp(to, at(g), at(g), sem, rsem().at[g])))
            return found

        launch(name, copies)

    def near_forward(name, at, ssem, rsem):
        ends = ((NGRP - 2, 0, NGRP - 1), (1, NGRP - 1, 0))

        def copies():
            return [
                (g == near, to_grp(end, at(far), at(far), ssem().at[2, 0], rsem().at[far]))
                for near, far, end in ends
            ]

        for near, far, end in ends:
            pl.when(g == near)(
                to_grp(end, at(far), at(far), ssem().at[2, 0], rsem().at[far]).wait_recv
            )
        launch(name + "on", copies)

    def near_wait(name, at, ssem, rsem):
        for slot in range(NGRP):
            handed = ((g == NGRP - 2) & (slot == 0)) | ((g == 1) & (slot == NGRP - 1))
            pl.when((g != slot) & jnp.logical_not(handed))(
                to_grp(
                    lax.rem(g + 1, NGRP), at(slot), at(slot), ssem().at[0, 0], rsem().at[slot]
                ).wait_recv
            )

    def direct_start(name, at, ssem, rsem):
        def copies():
            found = []
            for step in range(1, NGRP):
                peer = lax.rem(g + step, NGRP)
                found.append((always, to_grp(peer, at(g), at(g), ssem.at[step - 1], rsem.at[g])))
            return found

        launch(name, copies)

    def direct_wait(name, at, ssem, rsem):
        for step in range(1, NGRP):
            slot = lax.rem(g + step, NGRP)
            to_grp(slot, at(slot), at(slot), ssem.at[0], rsem.at[slot]).wait_recv()

    loads[3].wait()

    def cot_times_down(i, carry):
        at = pl.ds(pl.multiple_of(i * T, T), T)
        ghid[:, at] = dot_nt(cot_ref[...], down_all[at, :]).astype(BF16)
        return carry

    lax.fori_loop(0, FF // T, cot_times_down, 0)

    acc_a[...] = jnp.zeros_like(acc_a)
    shift[...] = jnp.zeros_like(shift)

    def pair_of(ref, cc, first, last):
        return ref[pl.ds(2 * cc, 2), :, first:last].reshape(pair_width, last - first)

    def weights_of(score, count):
        count = count.astype(F32)
        return jnp.where(count > 0.5, jnp.exp2(score * exp_scale) * count, 0.0)

    def wait_pair(buffer, ssem, rsem, j, cc):
        mine, other = 2 * cc + core, 2 * cc + 1 - core

        @pl.when(j > 0)
        def _():
            to_seq(sib, buffer.at[mine], buffer.at[mine], ssem.at[0], rsem.at[mine]).wait_recv()
            to_seq(sib, buffer.at[mine], buffer.at[mine], ssem.at[3 + j], rsem.at[mine]).start()

        to_seq(sib, buffer.at[other], buffer.at[other], ssem.at[0], rsem.at[other]).wait_recv()

    def forward_step(j, carry):
        cc = chip - j
        wait_pair(kv, kv_ssem, kv_rsem, j, cc)
        keys = pair_of(kv, cc, 0, 256)
        values = pair_of(kv, cc, 128, 384)
        for h in range(3):
            weight = weights_of(dot_nt(qmask[h], keys), masks[h, :, pair_lanes(cc)])
            row_sum = weight[:, 0:LANES]
            for i in range(1, pair_width // LANES):
                row_sum = row_sum + weight[:, LANES * i : LANES * i + LANES]
            shift[h] += row_sum
            low_weight = weight.astype(BF16)
            masks[h, :, pair_lanes(cc)] = low_weight
            acc_a[...] += dot_nn(low_weight, values) * slot_mask(h + 1)
        return carry

    lax.fori_loop(0, chip + 1, forward_step, 0)
    inverse = jnp.zeros((T, 256), F32)
    for h in range(3):
        inverse += slot_mask(h + 1) / jnp.sum(shift[h], axis=1, keepdims=True)
    att_own = acc_a[...] * inverse
    invden[...] = inverse
    att[...] = att_own
    for h in range(3):
        tile = att_own[:, 0:128] if h == 0 else att_own[:, 128:256]
        zmix[g, h] = pack_half(tile, h != 1)
    mixed_gather = chain_parts(
        "mixed",
        [lambda i, n=n: zmix.at[i, :, n * half // 3 : (n + 1) * half // 3] for n in range(3)],
        zm_ssem,
        zm_rsem,
    )
    for part_of in mixed_gather:
        chain_start(*part_of)

    for d in range(1, chips):

        @pl.when(chip + d < chips)
        def _(d=d):
            slot = lax.rem(s + 2 * d, NSEQ)
            to_seq(sib, qb.at[slot], qb.at[slot], q_ssem.at[0], q_rsem.at[slot]).wait_recv()

    def hand_on(buffer, ssem, rsem, upward):
        found = []
        for d in range(1, chips):
            slot = lax.rem(s + (NSEQ - 2 * d if upward else 2 * d), NSEQ)
            cond = chip >= d if upward else chip + d < chips
            found.append(
                (cond, to_seq(sib, buffer.at[slot], buffer.at[slot], ssem.at[3 + d], rsem.at[slot]))
            )
        return found

    launch("q on", lambda: hand_on(qb, q_ssem, q_rsem, False))
    launched["kv on"] = lambda: hand_on(kv, kv_ssem, kv_rsem, True)
    launched["do on"] = lambda: hand_on(dob, do_ssem, do_rsem, False)

    chain_finish(mixed_gather)
    for tile in range(D // LANES):
        (g_a, h_a), (g_b, h_b) = divmod(2 * tile, 3), divmod(2 * tile + 1, 3)
        first_head = zmix[g_a, h_a].astype(F32)
        second_head = zmix[g_b, h_b].astype(F32)
        cols = slice(tile * LANES, tile * LANES + LANES)
        mixed[0:half, cols] = join_halves(first_head, swap_halves(second_head)).astype(BF16)
        mixed[half:T, cols] = join_halves(swap_halves(first_head), second_head).astype(BF16)

    loads[4].wait()
    middle[...] = tok_ref[...].astype(F32) + dot_nn(mixed[...], exit_all[...])

    def norm_two(i, carry):
        at = pl.ds(pl.multiple_of(i * rows, rows), rows)
        value = middle[at, :]
        centered = value - jnp.mean(value, axis=1, keepdims=True)
        inverse = lax.rsqrt(jnp.mean(centered * centered, axis=1, keepdims=True) + EPS)
        plain = centered * inverse
        n2[at, :] = (plain * gain2 + bias2).astype(BF16)
        return carry

    lax.fori_loop(0, T // rows, norm_two, 0)

    class Stacked:
        def __init__(self, pieces, first_in, second_in):
            self.pieces, self.first_in, self.second_in = pieces, first_in, second_in

        def whole(self, k):
            return self.pieces.at[k]

        def block(self, k, cc):
            return self.pieces.at[k, cc]

        def first(self, cc):
            return self.first_in.at[cc]

    class Tiled(Stacked):
        def rows(self, k):
            count = self.first_in.shape[0]
            return pl.ds(pl.multiple_of(count * k, count), count)

        def cols(self, cc):
            return pl.ds(pl.multiple_of(D * cc, LANES), D)

        def whole(self, k):
            return self.pieces.at[self.rows(k), :]

        def block(self, k, cc):
            return self.pieces.at[self.rows(k), self.cols(cc)]

        def first(self, cc):
            return self.first_in.at[:, self.cols(cc)]

    sum_up = Stacked(pc_up, r1_up, r2_up)
    sum_down = Tiled(up_all, r1_down, r2_down)
    sum_eq = Stacked(pc_eq, r1_eq, r2_eq)
    sum_ekv = Stacked(pc_ekv, r1_ekv, r2_ekv)
    sum_exit = Tiled(ghid, r1_exit, r2_exit)

    def reduce_start(i, parts):
        launch(
            f"first{i}",
            lambda: [
                (
                    always,
                    to_seq(sib, parts.whole(1 - core), parts.first_in, rs_s1.at[i], rs_r1.at[i]),
                )
            ],
        )

    def reduce_pass(i, parts):
        to_seq(sib, parts.whole(core), parts.first_in, rs_s1.at[i], rs_r1.at[i]).wait_recv()

        def add(cc, carry):
            block = parts.block(core, cc)
            block[...] = (block[...].astype(F32) + parts.first(cc)[...].astype(F32)).astype(BF16)
            return carry

        lax.fori_loop(0, chips, add, 0)

        def copies():
            found = []
            for d in range(1, chips):
                to_chip = lax.rem(chip + d, chips)
                copy = to_seq(
                    2 * to_chip + core,
                    parts.block(core, to_chip),
                    parts.second_in.at[chips - d - 1],
                    rs_s2.at[i, d - 1],
                    rs_r2.at[i, chips - d - 1],
                )
                found.append((always, copy))
            return found

        launch(f"second{i}", copies)

    def reduce_end(i, parts):
        result = parts.block(core, chip)[...].astype(F32)
        for d in range(1, chips):
            landed = parts.second_in.at[d - 1]
            to_seq(sib, landed, landed, rs_s1.at[i], rs_r2.at[i, d - 1]).wait_recv()
            result = result + landed[...].astype(F32)
        return result.astype(BF16)

    def weight_gather(i, gathered):
        return ("weight" + str(i), lambda j: gathered.at[j], lambda: rs_zs.at[i], lambda: rs_zr.at[i])

    def gather_sum(i, parts, gathered):
        gathered[g] = reduce_end(i, parts)
        near_start(*weight_gather(i, gathered))

    loads[5].wait()
    def feed_forward(i, carry):
        c = lax.rem(g + i, NGRP)
        at = pl.ds(pl.multiple_of(c * D, LANES), D)
        hidden = dot_nn(n2[...], up_all[:, at])
        cdf = 0.5 + 0.5 * lax.erf(hidden * (0.5**0.5))
        low_active = (hidden * cdf).astype(BF16)
        active[:, at] = low_active
        density = jnp.exp2(hidden * hidden * (-0.5 * LOG2E)) * 0.3989422804014327
        ghid[:, at] = (ghid[:, at].astype(F32) * (cdf + hidden * density)).astype(BF16)

        @pl.when(i == 0)
        def _():
            for j in range(2):
                up_grad = dot_tn(n2[...], ghid[:, pl.ds(pl.multiple_of(g * D + T * j, LANES), T)])
                for t in range(NSEQ):
                    pc_up[t % 2, t // 2, :, T * j : T * j + T] = up_grad[
                        piece * t : piece * t + piece, :
                    ].astype(BF16)
            reduce_start(0, sum_up)

        @pl.when(i == 1)
        def _():
            reduce_pass(0, sum_up)

        return carry

    lax.fori_loop(0, NGRP, feed_forward, 0)

    def back_through_up(i, carry):
        at = pl.ds(pl.multiple_of(i * 256, 256), 256)
        gn2[:, at] = dot_nt(ghid[...], up_all[at, :])
        return carry

    lax.fori_loop(0, D // 256, back_through_up, 0)

    stat[s] = jnp.zeros((8, D), F32)

    def norm_two_back(i, carry):
        at = pl.ds(pl.multiple_of(i * rows, rows), rows)
        upstream = gn2[at, :]
        value = middle[at, :]
        centered = value - jnp.mean(value, axis=1, keepdims=True)
        inverse = lax.rsqrt(jnp.mean(centered * centered, axis=1, keepdims=True) + EPS)
        plain = centered * inverse
        scaled = upstream * gain2
        inner = (
            scaled
            - jnp.mean(scaled, axis=1, keepdims=True)
            - plain * jnp.mean(scaled * plain, axis=1, keepdims=True)
        )
        grad = cot_ref[at, :].astype(F32) + inverse * inner

        @pl.when(i == g)
        def _():
            gmid[...] = grad

        gbranch[at, :] = grad.astype(BF16)
        stat[s, 0:1, :] += jnp.sum(upstream * plain, axis=0, keepdims=True)
        stat[s, 1:2, :] += jnp.sum(upstream, axis=0, keepdims=True)
        return carry

    lax.fori_loop(0, T // rows, norm_two_back, 0)

    window = pl.ds(pl.multiple_of(jnp.maximum(part * g - 64, 0), 64), 256)
    gmix = dot_nt(gbranch[...], exit_all[window, :])
    gmix = jnp.where(g == 0, pltpu.roll(gmix, 64, axis=1), gmix)
    gmix = jnp.where(lane256 < 64, 0.0, gmix).astype(BF16).astype(F32)
    numer_grad = gmix * invden[...]
    product = numer_grad * att[...]
    for h in range(3):
        value = jnp.sum(product * slot_mask(h + 1), axis=1, keepdims=True)
        shift[h] = jnp.broadcast_to(value, (T, LANES))
        high = value.astype(BF16).astype(F32)
        low = value - high
        numer_grad = jnp.where(lane256 == 2 * h, high, numer_grad)
        numer_grad = jnp.where(lane256 == 2 * h + 1, low, numer_grad)
    dob[s] = numer_grad.astype(BF16)

    spread("do", dob, do_ssem, do_rsem, False)


    def down_piece(t, carry):
        at = pl.ds(pl.multiple_of(t * T, T), T)
        sum_down.block(t % 2, t // 2)[...] = dot_tn(active[:, at], cot_ref[...]).astype(BF16)
        return carry

    lax.fori_loop(0, NSEQ, down_piece, 0)
    reduce_start(1, sum_down)
    for i in range(2):
        exit_grad = dot_tn(mixed[...], gbranch[:, T * i : T * i + T]).astype(BF16)
        for t in range(NSEQ):
            first, low = D * (t // 2) + T * i, piece * (t % 2)
            ghid[low : low + piece, first : first + T] = exit_grad[piece * t : piece * t + piece, :]
    reduce_start(4, sum_exit)

    for h in range(3):
        qmask[h] = (dob[s].astype(F32) * slot_mask(h + 1)).astype(BF16)
    acc_a[...] = jnp.zeros_like(acc_a)

    def query_side(cc, carry):
        keys = pair_of(kv, cc, 0, 256)
        values = pair_of(kv, cc, 128, 384)
        for h in range(3):
            row_shift = jnp.concatenate([shift[h]] * (pair_width // LANES), axis=1)
            pressure = dot_nt(qmask[h], values) - row_shift
            slope = (masks[h, :, pair_lanes(cc)].astype(F32) * pressure).astype(BF16)
            acc_a[...] += dot_nn(slope, keys) * slot_mask(h)
        return carry

    lax.fori_loop(0, chip + 1, query_side, 0)
    dq = acc_a[...] * scale
    gather_sum(0, sum_up, ag_up)

    def weight_pieces(pieces, grad):
        for t in range(NSEQ):
            pieces[t % 2, t // 2] = grad[piece * t : piece * t + piece, :].astype(BF16)

    weight_pieces(pc_eq, dot_tn(n1[...], dq.astype(BF16)))
    reduce_start(2, sum_eq)

    reduce_pass(4, sum_exit)

    v_tile = kv[s, :, 128:384].astype(F32)
    k_tile = kv[s, :, 0:256].astype(F32)
    for h in range(3):
        qmask[h] = (k_tile * slot_mask(h)).astype(BF16)
        minus = jnp.where((lane256 == 2 * h) | (lane256 == 2 * h + 1), -1.0, 0.0)
        qmask[3 + h] = (v_tile * slot_mask(h + 1) + minus).astype(BF16)
    acc_b[...] = jnp.zeros_like(acc_b)
    acc_c[...] = jnp.zeros_like(acc_c)

    def key_side(j, carry):
        cc = chip + j
        wait_pair(dob, do_ssem, do_rsem, j, cc)
        other = 2 * cc + 1 - core
        to_seq(sib, qb.at[other], qb.at[other], q_ssem.at[0], q_rsem.at[other]).wait_recv()
        queries = pair_of(qb, cc, 0, 256)
        grads = pair_of(dob, cc, 0, 256)
        for h in range(3):
            count = masks[h, :, pair_lanes(jnp.where(j == 0, chips, cc))]
            weight = weights_of(dot_nt(qmask[h], queries), count)
            slope = (weight * dot_nt(qmask[3 + h], grads)).astype(BF16)
            acc_b[...] += dot_nn(slope, queries) * slot_mask(h)
            acc_c[...] += dot_nn(weight.astype(BF16), grads) * slot_mask(h + 1)

        @pl.when(j == 0)
        def _():
            reduce_pass(2, sum_eq)

        return carry

    lax.fori_loop(0, chips - chip, key_side, 0)

    dk, dv = acc_b[...] * scale, acc_c[...]
    part_sum = dot_nt(jnp.where(is_odd, pltpu.roll(dq, 64, axis=1), dq).astype(BF16), win[0])
    part_sum += dot_nt(jnp.where(is_odd, pltpu.roll(dk, 64, axis=1), dk).astype(BF16), win[1])
    part_sum += dot_nt(jnp.where(is_odd, dv, pltpu.roll(dv, 192, axis=1)).astype(BF16), win[2])
    gn2[...] = part_sum
    n2[...] = part_sum.astype(BF16)
    own_rows = pl.ds(pl.multiple_of(g * piece, piece), piece)

    def row_copies():
        found = []
        for step in range(1, NGRP):
            peer = lax.rem(g + step, NGRP)
            rows_of = pl.ds(pl.multiple_of(peer * piece, piece), piece)
            copy = to_grp(peer, n2.at[rows_of, :], drecv.at[g], zd_ssem.at[step - 1], zd_rsem.at[g])
            found.append((always, copy))
        return found

    launch("rows", row_copies)

    def norm_one_sums(i, carry):
        at = pl.ds(pl.multiple_of(i * rows, rows), rows)
        value = tok_ref[at, :].astype(F32)
        centered = value - jnp.mean(value, axis=1, keepdims=True)
        inverse = lax.rsqrt(jnp.mean(centered * centered, axis=1, keepdims=True) + EPS)
        stat[s, 2:3, :] += jnp.sum(gn2[at, :] * (centered * inverse), axis=0, keepdims=True)
        stat[s, 3:4, :] += jnp.sum(gn2[at, :], axis=0, keepdims=True)
        return carry

    lax.fori_loop(0, T // rows, norm_one_sums, 0)

    def stat_copies():
        found = []
        for step in range(1, NSEQ):
            peer = lax.rem(s + step, NSEQ)
            copy = to_seq(peer, stat.at[s], stat.at[s], st_ssem.at[step - 1], st_rsem.at[s])
            found.append((always, copy))
        return found

    launch("stat", stat_copies)

    dpack = exit_all.at[0:T, 0:384]
    dpack[:, 0:128] = dk[:, 0:128].astype(BF16)
    dpack[:, 128:256] = join_halves(dk[:, 128:256], dv[:, 0:128]).astype(BF16)
    dpack[:, 256:384] = dv[:, 128:256].astype(BF16)
    weight_pieces(pc_ekv, dot_tn(n1[...], dpack[...]))
    reduce_start(3, sum_ekv)
    gather_sum(2, sum_eq, ag_eq)

    reduce_pass(3, sum_ekv)
    near_forward(*weight_gather(0, ag_up))
    reduce_pass(1, sum_down)

    def through_down(i, carry):
        at = pl.ds(pl.multiple_of(i * 256, 256), 256)
        out_ref[:, at] = (middle[:, at] + dot_nn(active[...], down_all[:, at])).astype(BF16)
        return carry

    lax.fori_loop(0, D // 256, through_down, 0)

    upstream = gn2[own_rows, :]
    for step in range(1, NGRP):
        slot = lax.rem(g + step, NGRP)
        to_grp(slot, drecv.at[slot], drecv.at[slot], zd_ssem.at[0], zd_rsem.at[slot]).wait_recv()
        upstream = upstream + drecv[slot].astype(F32)
    value = tok_ref[own_rows, :].astype(F32)
    centered = value - jnp.mean(value, axis=1, keepdims=True)
    inverse = lax.rsqrt(jnp.mean(centered * centered, axis=1, keepdims=True) + EPS)
    plain = centered * inverse
    scaled = upstream * gain1
    inner = (
        scaled
        - jnp.mean(scaled, axis=1, keepdims=True)
        - plain * jnp.mean(scaled * plain, axis=1, keepdims=True)
    )
    tz[g] = (gmid[...] + inverse * inner).astype(BF16)
    middle_row = piece // 2
    token_gather = chain_parts(
        "token",
        (lambda i: tz.at[i, 0:middle_row], lambda i: tz.at[i, middle_row:piece]),
        zt_ssem,
        zt_rsem,
    )
    for part_of in token_gather:
        chain_start(*part_of)

    gather_sum(3, sum_ekv, ag_ekv)
    near_forward(*weight_gather(2, ag_eq))

    chain_finish(token_gather)
    near_forward(*weight_gather(3, ag_ekv))

    for step in range(1, NSEQ):
        slot = lax.rem(s + step, NSEQ)
        to_seq(sib, stat.at[slot], stat.at[slot], st_ssem.at[0], st_rsem.at[slot]).wait_recv()
    total_stat = stat[0]
    for i in range(1, NSEQ):
        total_stat = total_stat + stat[i]
    stat_z[g] = total_stat
    direct_start("stat z", lambda i: stat_z.at[i], sz_ssem, sz_rsem)

    near_wait(*weight_gather(0, ag_up))
    pass
    for i in range(NGRP):
        oup_ref[:, D * i : D * i + D] = ag_up[i]
    pass
    oexit_ref[...] = reduce_end(4, sum_exit)
    near_wait(*weight_gather(2, ag_eq))

    def place_entry(first, tiles):
        for tile, value in enumerate(tiles):
            at = first + tile * LANES
            oentry_ref[:, at : at + LANES] = value.astype(BF16)

    for pair in range(NGRP // 2):
        a = ag_eq[2 * pair].astype(F32)
        b = ag_eq[2 * pair + 1].astype(F32)
        turned = swap_halves(b[:, 0:128])
        place_entry(
            pair * 2 * part,
            (
                a[:, 0:128],
                join_halves(a[:, 128:256], turned),
                join_halves(turned, swap_halves(b[:, 128:256])),
            ),
        )
    odown_ref[...] = reduce_end(1, sum_down)
    for i in range(NGRP):
        tgrad_ref[piece * i : piece * i + piece, :] = tz[i]
    total_stat = jnp.zeros((8, D), F32)
    for step in range(1, NGRP):
        slot = lax.rem(g + step, NGRP)
        to_grp(slot, stat_z.at[slot], stat_z.at[slot], sz_ssem.at[0], sz_rsem.at[slot]).wait_recv()
    for i in range(NGRP):
        total_stat = total_stat + stat_z[i]
    row_id = lax.broadcasted_iota(jnp.int32, (8, 1), 0)
    ostat_ref[...] = jnp.where(row_id < 2, stat_z[g], total_stat)
    near_wait(*weight_gather(3, ag_ekv))
    for pair in range(NGRP // 2):
        a = ag_ekv[2 * pair].astype(F32)
        b = ag_ekv[2 * pair + 1].astype(F32)
        turned = swap_halves(b[:, 0:128])
        place_entry(
            D + pair * 2 * part,
            (
                a[:, 0:128],
                join_halves(a[:, 128:256], turned),
                join_halves(turned, swap_halves(b[:, 128:256])),
            ),
        )
        turned = swap_halves(a[:, 256:384])
        place_entry(
            2 * D + pair * 2 * part,
            (
                join_halves(swap_halves(a[:, 128:256]), turned),
                join_halves(turned, b[:, 128:256]),
                b[:, 256:384],
            ),
        )

    for copies in launched.values():
        for cond, copy in copies():
            pl.when(cond)(copy.wait_send)


def finish_kernel(
    out_in,
    tgrad_in,
    entry_in,
    exit_in,
    up_in,
    down_in,
    stat_in,
    out_hbm,
    tgrad_hbm,
    entry_hbm,
    exit_hbm,
    up_hbm,
    down_hbm,
    fgain_ref,
    fbias_ref,
    sgain_ref,
    sbias_ref,
    out_low,
    tgrad_low,
    down_low,
    up_low,
    entry_low,
    exit_low,
    stat_low,
    down_full,
    up_full,
    entry_full,
    exit_full,
    sems,
):
    plans = (
        (down_in, down_low, down_full, down_hbm),
        (up_in, up_low, up_full, up_hbm),
        (entry_in, entry_low, entry_full, entry_hbm),
        (exit_in, exit_low, exit_full, exit_hbm),
        (out_in, out_low, out_low, out_hbm),
        (tgrad_in, tgrad_low, tgrad_low, tgrad_hbm),
    )
    loads = [
        pltpu.make_async_copy(source, low, sems.at[6 + i])
        for i, (source, low, _, _) in enumerate(plans)
    ]
    stat_load = pltpu.make_async_copy(stat_in, stat_low, sems.at[12])
    for copy in [*loads, stat_load]:
        copy.start()
    copies = []
    for i, (_, low, full, target) in enumerate(plans):
        loads[i].wait()
        if full is not low:
            full[...] = low[...].astype(F32)
        copy = pltpu.make_async_copy(full, target, sems.at[i])
        copy.start()
        copies.append(copy)
    stat_load.wait()
    width = stat_low.shape[1]
    part = fgain_ref.shape[0]
    first = lax.axis_index("seq") * part
    turned = pltpu.roll(stat_low[...], lax.rem(width - first, width), axis=1)
    fgain_ref[...] = turned[2:3, 0:part].reshape(part)
    fbias_ref[...] = turned[3:4, 0:part].reshape(part)
    sgain_ref[...] = turned[0:1, 0:part].reshape(part)
    sbias_ref[...] = turned[1:2, 0:part].reshape(part)
    for copy in copies:
        copy.wait()


def fast_on_device(
    seq_count,
    tokens,
    cotangent,
    entry_weight,
    exit_weight,
    up_weight,
    down_weight,
    first_gain,
    first_bias,
    second_gain,
    second_bias,
    dilations,
    offsets,
):
    T, D = tokens.shape
    NGRP, HEADS = offsets.shape
    FF = up_weight.shape[1]
    E = D // HEADS
    NSEQ = seq_count
    chips = NSEQ // 2
    sizes = (T, D, HEADS, E, FF, NSEQ, NGRP)
    piece = D // NSEQ
    vmem = pl.BlockSpec(memory_space=pltpu.VMEM)
    smem = pl.BlockSpec(memory_space=pltpu.SMEM)
    anywhere = pl.BlockSpec(memory_space=pl.ANY)
    dma = pltpu.SemaphoreType.DMA
    scratch = [
        pltpu.VMEM((3, D, 256), BF16),
        pltpu.VMEM((D, D), BF16),
        pltpu.VMEM((D, FF), BF16),
        pltpu.VMEM((FF, D), BF16),
        pltpu.VMEM((T, D), BF16),
        pltpu.VMEM((T, D), BF16),
        pltpu.VMEM((T, D), F32),
        pltpu.VMEM((piece, D), F32),
        pltpu.VMEM((T, D), BF16),
        pltpu.VMEM((T, D), BF16),
        pltpu.VMEM((T, FF), BF16),
        pltpu.VMEM((T, FF), BF16),
        pltpu.VMEM((T, D), F32),
        pltpu.VMEM((3, T, LANES), BF16),
        pltpu.VMEM((3, T, (NSEQ + 2) * T), BF16),
        pltpu.VMEM((NSEQ, T, 384), BF16),
        pltpu.VMEM((NSEQ, T, 256), BF16),
        pltpu.VMEM((NSEQ, T, 256), BF16),
        pltpu.VMEM((6, T, 256), BF16),
        pltpu.VMEM((3, T, LANES), F32),
        pltpu.VMEM((T, 256), F32),
        pltpu.VMEM((T, 256), F32),
        pltpu.VMEM((T, 256), F32),
        pltpu.VMEM((T, 256), F32),
        pltpu.VMEM((T, 256), F32),
        pltpu.VMEM((NGRP, 3, T // 2, LANES), BF16),
        pltpu.VMEM((NGRP, piece, D), BF16),
        pltpu.VMEM((NGRP, piece, D), BF16),
        pltpu.VMEM((NSEQ, 8, D), F32),
        pltpu.VMEM((NGRP, 8, D), F32),
    ]
    scratch += [
        pltpu.VMEM((piece, chips * D), BF16),
        pltpu.VMEM((chips - 1, piece, D), BF16),
        pltpu.VMEM((T, chips * D), BF16),
        pltpu.VMEM((chips - 1, T, D), BF16),
    ]
    for rows, cols in ((piece, D), (piece, 256), (piece, 384)):
        scratch += [
            pltpu.VMEM((2, chips, rows, cols), BF16),
            pltpu.VMEM((chips, rows, cols), BF16),
            pltpu.VMEM((chips - 1, rows, cols), BF16),
            pltpu.VMEM((NGRP, rows, cols), BF16),
        ]
    scratch += [
        dma((7,)),
        dma((7,)),
        dma((NSEQ,)),
        dma((7,)),
        dma((NSEQ,)),
        dma((7,)),
        dma((NSEQ,)),
        dma((3, 3, 2)),
        dma((3, NGRP)),
        dma((NGRP - 1,)),
        dma((NGRP,)),
        dma((2, 3, 2)),
        dma((2, NGRP)),
        dma((5,)),
        dma((5,)),
        dma((5, 3)),
        dma((5, chips - 1)),
        dma((4, 3, 2)),
        dma((4, NGRP)),
        dma((NSEQ - 1,)),
        dma((NSEQ,)),
        dma((NGRP - 1,)),
        dma((NGRP,)),
    ]
    out_shape = (
        jax.ShapeDtypeStruct((T, D), BF16),
        jax.ShapeDtypeStruct((T, D), BF16),
        jax.ShapeDtypeStruct((piece, 3 * D), BF16),
        jax.ShapeDtypeStruct((piece, D), BF16),
        jax.ShapeDtypeStruct((piece, FF), BF16),
        jax.ShapeDtypeStruct((T, D), BF16),
        jax.ShapeDtypeStruct((8, D), F32),
    )
    output, token_grad, entry_grad, exit_grad, up_grad, down_grad, stats = pl.pallas_call(
        partial(layer_kernel, sizes),
        out_shape=out_shape,
        in_specs=[smem] * 2 + [vmem] * 6 + [anywhere] * 4,
        out_specs=tuple([vmem] * 7),
        scratch_shapes=scratch,
        compiler_params=pltpu.CompilerParams(
            collective_id=0, has_side_effects=True, vmem_limit_bytes=63 * 1024 * 1024
        ),
        name="layer",
    )(
        dilations,
        offsets,
        tokens,
        cotangent,
        first_gain,
        first_bias,
        second_gain,
        second_bias,
        entry_weight,
        exit_weight,
        up_weight,
        down_weight,
    )
    part = piece
    finish_shape = (
        jax.ShapeDtypeStruct((T, D), BF16),
        jax.ShapeDtypeStruct((T, D), BF16),
        jax.ShapeDtypeStruct((part, 3 * D), F32),
        jax.ShapeDtypeStruct((part, D), F32),
        jax.ShapeDtypeStruct((part, FF), F32),
        jax.ShapeDtypeStruct((T, D), F32),
    ) + tuple([jax.ShapeDtypeStruct((part,), F32)] * 4)
    return pl.pallas_call(
        finish_kernel,
        out_shape=finish_shape,
        in_specs=[anywhere] * 7,
        out_specs=tuple([anywhere] * 6 + [vmem] * 4),
        scratch_shapes=[
            pltpu.VMEM((T, D), BF16),
            pltpu.VMEM((T, D), BF16),
            pltpu.VMEM((T, D), BF16),
            pltpu.VMEM((part, FF), BF16),
            pltpu.VMEM((part, 3 * D), BF16),
            pltpu.VMEM((part, D), BF16),
            pltpu.VMEM((8, D), F32),
            pltpu.VMEM((T, D), F32),
            pltpu.VMEM((part, FF), F32),
            pltpu.VMEM((part, 3 * D), F32),
            pltpu.VMEM((part, D), F32),
            dma((13,)),
        ],
        compiler_params=pltpu.CompilerParams(vmem_limit_bytes=62 * 1024 * 1024),
        name="finish",
    )(output, token_grad, entry_grad, exit_grad, up_grad, down_grad, stats)


def solution(mesh):
    seq_count = mesh.shape["seq"]
    fast = seq_count == 8 and mesh.shape["grp"] == 4
    return jax.shard_map(
        partial(fast_on_device, seq_count) if fast else on_device,
        mesh=mesh,
        in_specs=(P("seq", None), P("seq", None), P(), P(), P(), P(), P(), P(), P(), P(), P(), P()),
        out_specs=(
            P("seq", None),
            P("seq", None),
            P("seq", None),
            P("seq", None),
            P("seq", None),
            P("seq", None),
            P("seq"),
            P("seq"),
            P("seq"),
            P("seq"),
        ),
        check_vma=False,
    )
```

```python
from functools import partial

import jax
import jax.numpy as jnp
from jax import lax
from jax.experimental import pallas as pl
from jax.experimental.pallas import tpu as pltpu
from jax.sharding import PartitionSpec as P

RATE_MIN = 2
RATE_MAX = 8


EPS = 1e-05
PRECISE = lax.Precision.HIGHEST


def norm_forward(values, gain_vec, bias_vec):
    centered = values - jnp.mean(values, axis=1, keepdims=True)
    inverse = lax.rsqrt(jnp.mean(centered * centered, axis=1, keepdims=True) + EPS)
    plain = centered * inverse
    return (plain * gain_vec + bias_vec, plain, inverse)


def norm_backward(upstream, plain, inverse, gain_vec):
    scaled = upstream * gain_vec
    inner = (
        scaled
        - jnp.mean(scaled, axis=1, keepdims=True)
        - plain * jnp.mean(scaled * plain, axis=1, keepdims=True)
    )
    return (inverse * inner, jnp.sum(upstream * plain, axis=0), jnp.sum(upstream, axis=0))


def key_weights(query_sp, query_pos, key_block, first_row, geometry):
    local_len, capacity, dilation, segment, head_offs, score_scale = geometry
    key_count = key_block.shape[0]
    key_heads = key_block.reshape(key_count, query_sp.shape[1], query_sp.shape[2])
    scores = (
        jnp.einsum("ihd,jhd->hij", query_sp, key_heads, preferred_element_type=jnp.float32)
        * score_scale
    )
    key_index = first_row + jnp.arange(key_count, dtype=jnp.int32)
    source = key_index // capacity
    within = key_index - source * capacity
    key_pos = source[None, :] * local_len + head_offs[:, None] + dilation * within[None, :]
    key_live = within < local_len // dilation
    earlier = key_pos[:, None, :] <= query_pos[:, :, None]
    segment_match = key_pos[:, None, :] // segment == query_pos[:, :, None] // segment
    allowed = earlier & segment_match & key_live[None, None, :]
    return (jnp.where(allowed, jnp.exp(scores), 0.0), key_heads)


def forward_block(running, pieces, first_row, query_sp, query_pos, geometry):
    numerator, denominator = running
    key_block, value_block = pieces
    weights, key_heads = key_weights(query_sp, query_pos, key_block, first_row, geometry)
    value_heads = value_block.reshape(key_heads.shape)
    numerator = numerator + jnp.einsum(
        "hij,jhd->hid",
        weights.astype(jnp.bfloat16),
        value_heads,
        preferred_element_type=jnp.float32,
    )
    return (numerator, denominator + jnp.sum(weights, axis=2))


def blockwise(step_fn, running, pieces, first_row, block_rows):
    total_rows = pieces[0].shape[0]
    if total_rows > block_rows and total_rows % block_rows == 0:
        number = total_rows // block_rows
        stacked_first = pieces[0].reshape(number, block_rows, pieces[0].shape[1])
        stacked_second = pieces[1].reshape(number, block_rows, pieces[1].shape[1])
        block_starts = first_row + block_rows * jnp.arange(number, dtype=jnp.int32)

        def advance(state, items):
            return (step_fn(state, (items[0], items[1]), items[2]), None)

        running, _ = lax.scan(advance, running, (stacked_first, stacked_second, block_starts))
        return running
    return step_fn(running, pieces, first_row)


def backward_block(running, items, query_sp, query_pos, grad_sp, shift_sp, geometry):
    key_block, value_block, first_row = items
    score_scale = geometry[5]
    weights, key_heads = key_weights(query_sp, query_pos, key_block, first_row, geometry)
    key_count = key_block.shape[0]
    value_heads = value_block.reshape(key_heads.shape)
    pressure = jnp.einsum("ihd,jhd->hij", grad_sp, value_heads, preferred_element_type=jnp.float32)
    slopes = (weights * (pressure - shift_sp[:, :, None])).astype(jnp.bfloat16)
    running = (
        running
        + jnp.einsum("hij,jhd->ihd", slopes, key_heads, preferred_element_type=jnp.float32)
        * score_scale
    )
    grad_keys = (
        jnp.einsum("hij,ihd->jhd", slopes, query_sp, preferred_element_type=jnp.float32)
        * score_scale
    )
    grad_values = jnp.einsum(
        "hij,ihd->jhd", weights.astype(jnp.bfloat16), grad_sp, preferred_element_type=jnp.float32
    )
    return (running, (grad_keys.reshape(key_count, -1), grad_values.reshape(key_count, -1)))


def local_weights(query_heads, key_heads, score_scale):
    local_len = query_heads.shape[0]
    scores = (
        jnp.einsum("ihd,jhd->hij", query_heads, key_heads, preferred_element_type=jnp.float32)
        * score_scale
    )
    positions = jnp.arange(local_len, dtype=jnp.int32)
    causal = positions[:, None] >= positions[None, :]
    return jnp.where(causal[None], jnp.exp(scores), 0.0)


def on_device(
    tokens,
    cotangent,
    entry_weight,
    exit_weight,
    up_weight,
    down_weight,
    first_gain,
    first_bias,
    second_gain,
    second_bias,
    dilations,
    offsets,
):
    local_len, width_model = tokens.shape
    head_count = offsets.shape[1]
    head_size = width_model // head_count
    score_scale = head_size ** (-0.5)
    capacity = local_len // RATE_MIN
    group_idx = lax.axis_index("grp")
    seq_index = lax.axis_index("seq")
    seq_count = lax.axis_size("seq")
    dilation = lax.dynamic_index_in_dim(dilations, group_idx, 0, keepdims=False)
    head_offs = lax.dynamic_index_in_dim(offsets, group_idx, 0, keepdims=False)
    segment = local_len * seq_count * dilation // RATE_MAX
    step_ids = jnp.arange(capacity, dtype=jnp.int32)
    row_live = step_ids < local_len // dilation
    local_rows = jnp.minimum(head_offs[:, None] + dilation * step_ids[None, :], local_len - 1)
    query_pos = jnp.where(
        row_live[None, :],
        seq_index * local_len + head_offs[:, None] + dilation * step_ids[None, :],
        -1,
    )
    geometry = (local_len, capacity, dilation, segment, head_offs, score_scale)
    head_shape = (local_len, head_count, head_size)
    selector = local_rows[:, :, None] == jnp.arange(local_len, dtype=jnp.int32)[None, None, :]
    select_low = selector.astype(jnp.bfloat16)
    select_full = selector.astype(jnp.float32)

    def pick(array_in):
        return jnp.einsum(
            "hci,ihd->chd", select_low, array_in, preferred_element_type=jnp.float32
        ).astype(jnp.bfloat16)

    def place_back(sparse_in):
        return jnp.einsum("hci,chd->ihd", select_full, sparse_in, precision=PRECISE)

    inputs = tokens.astype(jnp.float32)
    normed_one, plain_one, inverse_one = norm_forward(inputs, first_gain, first_bias)
    normed_low = normed_one.astype(jnp.bfloat16)
    packed = jnp.dot(normed_low, entry_weight, preferred_element_type=jnp.float32).astype(
        jnp.bfloat16
    )
    query_heads = packed[:, :width_model].reshape(head_shape)
    key_heads = packed[:, width_model : 2 * width_model].reshape(head_shape)
    value_heads = packed[:, 2 * width_model :].reshape(head_shape)
    query_sp = pick(query_heads)
    key_sp = pick(key_heads).reshape(capacity, width_model)
    value_sp = pick(value_heads).reshape(capacity, width_model)
    empty_state = (
        jnp.zeros((head_count, capacity, head_size), jnp.float32),
        jnp.zeros((head_count, capacity), jnp.float32),
    )
    forward_step = partial(forward_block, query_sp=query_sp, query_pos=query_pos, geometry=geometry)
    numerator, denominator = blockwise(
        forward_step,
        empty_state,
        (
            lax.all_gather(key_sp, "seq", axis=0, tiled=True),
            lax.all_gather(value_sp, "seq", axis=0, tiled=True),
        ),
        jnp.int32(0),
        8 * capacity,
    )

    def local_part(query_in, key_in, value_in):
        weights = local_weights(query_in, key_in, score_scale)
        local_num = jnp.einsum(
            "hij,jhd->ihd",
            weights.astype(jnp.bfloat16),
            value_in,
            preferred_element_type=jnp.float32,
        )
        return (local_num, jnp.sum(weights, axis=2).T)

    def local_none(query_in, key_in, value_in):
        return (jnp.zeros(head_shape, jnp.float32), jnp.zeros((local_len, head_count), jnp.float32))

    local_num, local_den = lax.cond(
        group_idx == 0, local_part, local_none, query_heads, key_heads, value_heads
    )
    numerator_full = (
        jnp.einsum("hci,hcd->ihd", select_full, numerator, precision=PRECISE) + local_num
    )
    denominator_full = (
        jnp.einsum("hci,hc->ih", select_full, denominator, precision=PRECISE) + local_den
    )
    merged_num, merged_den = lax.psum(
        (numerator_full.reshape(local_len, width_model), denominator_full), "grp"
    )
    attention = merged_num.reshape(head_shape) / merged_den[:, :, None]
    mixed = attention.reshape(local_len, width_model).astype(jnp.bfloat16)
    middle = inputs + jnp.dot(mixed, exit_weight, preferred_element_type=jnp.float32)
    normed_two, plain_two, inverse_two = norm_forward(middle, second_gain, second_bias)
    normed_two_low = normed_two.astype(jnp.bfloat16)
    hidden = jnp.dot(normed_two_low, up_weight, preferred_element_type=jnp.float32)
    active = jax.nn.gelu(hidden, approximate=False).astype(jnp.bfloat16)
    output = (middle + jnp.dot(active, down_weight, preferred_element_type=jnp.float32)).astype(
        jnp.bfloat16
    )
    down_grad = jnp.dot(active.T, cotangent, preferred_element_type=jnp.float32)
    grad_active = jnp.dot(cotangent, down_weight.T, preferred_element_type=jnp.float32)
    _, gelu_pull = jax.vjp(partial(jax.nn.gelu, approximate=False), hidden)
    grad_hidden = gelu_pull(grad_active)[0].astype(jnp.bfloat16)
    up_grad = jnp.dot(normed_two_low.T, grad_hidden, preferred_element_type=jnp.float32)
    grad_normed_two = jnp.dot(grad_hidden, up_weight.T, preferred_element_type=jnp.float32)
    grad_plain_two, second_gain_grad, second_bias_grad = norm_backward(
        grad_normed_two, plain_two, inverse_two, second_gain
    )
    grad_middle = cotangent.astype(jnp.float32) + grad_plain_two
    grad_branch = grad_middle.astype(jnp.bfloat16)
    exit_grad = jnp.dot(mixed.T, grad_branch, preferred_element_type=jnp.float32)
    grad_mixed_low = lax.optimization_barrier(
        jnp.dot(grad_branch, exit_weight.T, preferred_element_type=jnp.float32).astype(jnp.bfloat16)
    )
    grad_mixed = grad_mixed_low.astype(jnp.float32).reshape(head_shape)
    grad_numer = (grad_mixed / merged_den[:, :, None]).astype(jnp.bfloat16)
    row_shift = jnp.sum(grad_mixed * attention, axis=2) / merged_den
    grad_sp = pick(grad_numer)
    shift_sp = jnp.einsum("hci,ih->hc", select_full, row_shift, precision=PRECISE)
    back_keys, back_values = (
        lax.all_gather(key_sp, "seq", axis=0, tiled=True),
        lax.all_gather(value_sp, "seq", axis=0, tiled=True),
    )
    block_rows = 8 * capacity
    number = back_keys.shape[0] // block_rows
    stacked_keys = back_keys.reshape(number, block_rows, width_model)
    stacked_values = back_values.reshape(number, block_rows, width_model)
    block_starts = block_rows * jnp.arange(number, dtype=jnp.int32)
    empty_query = jnp.zeros((capacity, head_count, head_size), jnp.float32)
    back_step = partial(
        backward_block,
        query_sp=query_sp,
        query_pos=query_pos,
        grad_sp=grad_sp,
        shift_sp=shift_sp,
        geometry=geometry,
    )
    grad_query_sp, (grad_key_all, grad_value_all) = lax.scan(
        back_step, empty_query, (stacked_keys, stacked_values, block_starts)
    )
    own_keys, own_values = (
        lax.psum_scatter(
            grad_key_all.reshape(-1, width_model), "seq", scatter_dimension=0, tiled=True
        ),
        lax.psum_scatter(
            grad_value_all.reshape(-1, width_model), "seq", scatter_dimension=0, tiled=True
        ),
    )

    def local_grads(query_in, key_in, value_in, grad_in, shift_in):
        weights = local_weights(query_in, key_in, score_scale)
        pressure = jnp.einsum("ihd,jhd->hij", grad_in, value_in, preferred_element_type=jnp.float32)
        slopes = (weights * (pressure - shift_in.T[:, :, None])).astype(jnp.bfloat16)
        grad_query = (
            jnp.einsum("hij,jhd->ihd", slopes, key_in, preferred_element_type=jnp.float32)
            * score_scale
        )
        grad_key = (
            jnp.einsum("hij,ihd->jhd", slopes, query_in, preferred_element_type=jnp.float32)
            * score_scale
        )
        grad_value = jnp.einsum(
            "hij,ihd->jhd",
            weights.astype(jnp.bfloat16),
            grad_in,
            preferred_element_type=jnp.float32,
        )
        return (grad_query, grad_key, grad_value)

    def local_skip(query_in, key_in, value_in, grad_in, shift_in):
        zeros_heads = jnp.zeros(head_shape, jnp.float32)
        return (zeros_heads, zeros_heads, zeros_heads)

    local_dq, local_dk, local_dv = lax.cond(
        group_idx == 0,
        local_grads,
        local_skip,
        query_heads,
        key_heads,
        value_heads,
        grad_numer,
        row_shift,
    )
    grad_query_full = place_back(grad_query_sp) + local_dq
    grad_key_full = place_back(own_keys.reshape(capacity, head_count, head_size)) + local_dk
    grad_value_full = place_back(own_values.reshape(capacity, head_count, head_size)) + local_dv
    grad_packed = jnp.concatenate(
        [
            grad_query_full.reshape(local_len, width_model),
            grad_key_full.reshape(local_len, width_model),
            grad_value_full.reshape(local_len, width_model),
        ],
        axis=1,
    )
    summed = lax.psum(grad_packed, "grp").astype(jnp.bfloat16)
    entry_grad = jnp.dot(normed_low.T, summed, preferred_element_type=jnp.float32)
    grad_normed_one = jnp.dot(summed, entry_weight.T, preferred_element_type=jnp.float32)
    grad_plain_one, first_gain_grad, first_bias_grad = norm_backward(
        grad_normed_one, plain_one, inverse_one, first_gain
    )
    token_grad = (grad_middle + grad_plain_one).astype(jnp.bfloat16)
    shards = (
        lax.psum_scatter(entry_grad, "seq", scatter_dimension=0, tiled=True),
        lax.psum_scatter(exit_grad, "seq", scatter_dimension=0, tiled=True),
        lax.psum_scatter(up_grad, "seq", scatter_dimension=0, tiled=True),
        lax.psum_scatter(down_grad, "seq", scatter_dimension=0, tiled=True),
        lax.psum_scatter(first_gain_grad, "seq", scatter_dimension=0, tiled=True),
        lax.psum_scatter(first_bias_grad, "seq", scatter_dimension=0, tiled=True),
        lax.psum_scatter(second_gain_grad, "seq", scatter_dimension=0, tiled=True),
        lax.psum_scatter(second_bias_grad, "seq", scatter_dimension=0, tiled=True),
    )
    return (
        output,
        token_grad,
        shards[0],
        shards[1],
        shards[2],
        shards[3],
        shards[4],
        shards[5],
        shards[6],
        shards[7],
    )


MESH = pl.DeviceIdType.MESH
LANES = 128
LOG2E = 1.4426950408889634
F32 = jnp.float32
BF16 = jnp.bfloat16


def dot_nn(left, right):
    return lax.dot_general(left, right, (((1,), (0,)), ((), ())), preferred_element_type=F32)


def dot_nt(left, right):
    return lax.dot_general(left, right, (((1,), (1,)), ((), ())), preferred_element_type=F32)


def dot_tn(left, right):
    return lax.dot_general(left, right, (((0,), (0,)), ((), ())), preferred_element_type=F32)


def lane_ids(width):
    return lax.broadcasted_iota(jnp.int32, (1, width), 1)


def slot_mask(slot, width=256):
    ids = lane_ids(width)
    return jnp.where((ids >= 64 * slot) & (ids < 64 * slot + 64), 1.0, 0.0).astype(F32)


def join_halves(low_part, high_part):
    return jnp.where(lane_ids(LANES) < 64, low_part, high_part)


def swap_halves(tile):
    return pltpu.roll(tile, 64, axis=1)


def layer_kernel(
    sizes,
    dil_ref,
    off_ref,
    tok_ref,
    cot_ref,
    gain1_ref,
    bias1_ref,
    gain2_ref,
    bias2_ref,
    entry_hbm,
    exit_hbm,
    up_hbm,
    down_hbm,
    out_ref,
    tgrad_ref,
    oentry_ref,
    oexit_ref,
    oup_ref,
    odown_ref,
    ostat_ref,
    win,
    exit_all,
    up_all,
    down_all,
    n1,
    n2,
    middle,
    gmid,
    gbranch,
    mixed,
    active,
    ghid,
    gn2,
    member,
    masks,
    kv,
    qb,
    dob,
    qmask,
    shift,
    invden,
    att,
    acc_a,
    acc_b,
    acc_c,
    zmix,
    drecv,
    tz,
    stat,
    stat_z,
    r1_exit,
    r2_exit,
    r1_down,
    r2_down,
    pc_up,
    r1_up,
    r2_up,
    ag_up,
    pc_eq,
    r1_eq,
    r2_eq,
    ag_eq,
    pc_ekv,
    r1_ekv,
    r2_ekv,
    ag_ekv,
    load_sem,
    kv_ssem,
    kv_rsem,
    q_ssem,
    q_rsem,
    do_ssem,
    do_rsem,
    zm_ssem,
    zm_rsem,
    zd_ssem,
    zd_rsem,
    zt_ssem,
    zt_rsem,
    rs_s1,
    rs_r1,
    rs_s2,
    rs_r2,
    rs_zs,
    rs_zr,
    st_ssem,
    st_rsem,
    sz_ssem,
    sz_rsem,
):
    T, D, HEADS, E, FF, NSEQ, NGRP = sizes
    scale = E ** (-0.5)
    exp_scale = scale * LOG2E
    s = lax.axis_index("seq")
    g = lax.axis_index("grp")
    chip = s // 2
    core = s % 2
    sib = s + 1 - 2 * core
    odd = g % 2
    chips = NSEQ // 2
    part = D // NGRP
    is_odd = odd == 1
    gain1 = gain1_ref[...].reshape(1, D)
    bias1 = bias1_ref[...].reshape(1, D)
    gain2 = gain2_ref[...].reshape(1, D)
    bias2 = bias2_ref[...].reshape(1, D)

    def to_seq(peer, src, dst, ssem, rsem):
        return pltpu.make_async_remote_copy(
            src_ref=src,
            dst_ref=dst,
            send_sem=ssem,
            recv_sem=rsem,
            device_id={"seq": peer},
            device_id_type=MESH,
        )

    def to_grp(peer, src, dst, ssem, rsem):
        return pltpu.make_async_remote_copy(
            src_ref=src,
            dst_ref=dst,
            send_sem=ssem,
            recv_sem=rsem,
            device_id={"grp": peer},
            device_id_type=MESH,
        )

    loads = []
    for t in range(3):
        first = pl.multiple_of(t * D + part * g - 64 * odd, LANES)
        loads.append(
            pltpu.make_async_copy(entry_hbm.at[:, pl.ds(first, 256)], win.at[t], load_sem.at[t])
        )
    loads.append(pltpu.make_async_copy(down_hbm, down_all, load_sem.at[3]))
    loads.append(pltpu.make_async_copy(exit_hbm, exit_all, load_sem.at[4]))
    loads.append(pltpu.make_async_copy(up_hbm, up_all, load_sem.at[5]))
    for load in loads[:3]:
        load.start()

    barrier = pltpu.get_barrier_semaphore()
    for step in range(1, NSEQ):
        pl.semaphore_signal(
            barrier, inc=1, device_id={"seq": lax.rem(s + step, NSEQ)}, device_id_type=MESH
        )
    for step in range(1, NGRP):
        pl.semaphore_signal(
            barrier, inc=1, device_id={"grp": lax.rem(g + step, NGRP)}, device_id_type=MESH
        )

    rows = D // NSEQ

    def norm_one(i, carry):
        at = pl.ds(pl.multiple_of(i * rows, rows), rows)
        value = tok_ref[at, :].astype(F32)
        centered = value - jnp.mean(value, axis=1, keepdims=True)
        inverse = lax.rsqrt(jnp.mean(centered * centered, axis=1, keepdims=True) + EPS)
        n1[at, :] = (centered * inverse * gain1 + bias1).astype(BF16)
        return carry

    lax.fori_loop(0, T // rows, norm_one, 0)

    for load in loads[:3]:
        load.wait()
    for load in loads[3:]:
        load.start()
    lane256 = lane_ids(256)
    q_raw = dot_nn(n1[...], win[0])
    k_raw = dot_nn(n1[...], win[1])
    v_raw = dot_nn(n1[...], win[2])
    q_own = jnp.where(is_odd, pltpu.roll(q_raw, 192, axis=1), q_raw)
    k_own = jnp.where(is_odd, pltpu.roll(k_raw, 192, axis=1), k_raw)
    v_own = jnp.where(is_odd, v_raw, pltpu.roll(v_raw, 64, axis=1))
    q_own = jnp.where(lane256 < 192, q_own, 0.0)
    qb[s] = q_own.astype(BF16)
    for h in range(3):
        qmask[h] = (q_own * slot_mask(h)).astype(BF16)
    kv[s, :, 0:128] = k_own[:, 0:128].astype(BF16)
    kv[s, :, 128:256] = join_halves(k_own[:, 128:256], v_own[:, 0:128]).astype(BF16)
    kv[s, :, 256:384] = v_own[:, 128:256].astype(BF16)

    pl.semaphore_wait(barrier, NSEQ - 1 + NGRP - 1)

    launched = {}

    def launch(name, copies):
        for cond, copy in copies():
            pl.when(cond)(copy.start)
        launched[name] = copies

    always = core >= 0

    def spread(name, buffer, ssem, rsem, upward):
        def copies():
            found = []
            for d in range(1, chips):
                peer = lax.rem(s + (2 * d if upward else NSEQ - 2 * d), NSEQ)
                cond = chip + d < chips if upward else chip >= d
                found.append(
                    (cond, to_seq(peer, buffer.at[s], buffer.at[s], ssem.at[d - 1], rsem.at[s]))
                )
            found.append((always, to_seq(sib, buffer.at[s], buffer.at[s], ssem.at[3], rsem.at[s])))
            return found

        launch(name, copies)

    spread("kv", kv, kv_ssem, kv_rsem, True)
    spread("q", qb, q_ssem, q_rsem, False)

    lane128 = lane_ids(LANES)
    rate_row = jnp.ones((1, LANES), F32)
    for i in range(NGRP):
        rate_row = jnp.where(lane128 == i, dil_ref[i].astype(F32), rate_row)
    local_pos = lax.broadcasted_iota(jnp.int32, (T, 1), 0).astype(F32)
    residue = local_pos - rate_row * jnp.floor((local_pos + 0.5) / rate_row)
    for h in range(3):
        off_row = jnp.full((1, LANES), -1.0, F32)
        for i in range(NGRP):
            off_row = jnp.where(
                lane128 == i, off_ref[i, 3 * g + h].astype(F32), off_row
            )
        member[h] = jnp.where(residue == off_row, 1.0, 0.0).astype(BF16)
    per_segment = rate_row * (T * NSEQ // RATE_MAX)

    def segment_of(block):
        return jnp.floor((jnp.full((1, LANES), block * T, jnp.int32).astype(F32) + 0.5) / per_segment)

    own_segment = segment_of(s)

    pair_width = 2 * T

    def pair_lanes(cc):
        return pl.ds(pl.multiple_of(cc * pair_width, LANES), pair_width)

    def build_mask(cc, carry):
        for h in range(3):
            blocks = []
            for i in range(2):
                same = jnp.where(segment_of(2 * cc + i) == own_segment, 1.0, 0.0)
                blocks.append((member[h].astype(F32) * same).astype(BF16))
            count = dot_nt(member[h], jnp.concatenate(blocks, axis=0))
            masks[h, :, pair_lanes(cc)] = count.astype(BF16)
        return carry

    lax.fori_loop(0, chips, build_mask, 0)
    own_id = lax.broadcasted_iota(jnp.int32, (T, pair_width), 0) + core * T
    pair_id = lax.broadcasted_iota(jnp.int32, (T, pair_width), 1)
    own_block = (pair_id >= core * T) & (pair_id < core * T + T)
    for h in range(3):
        count = masks[h, :, pair_lanes(chip)].astype(F32) + jnp.where(own_block, 1.0, 0.0)
        masks[h, :, pair_lanes(chip)] = jnp.where(pair_id <= own_id, count, 0.0).astype(BF16)
        masks[h, :, pair_lanes(chips)] = jnp.where(own_id <= pair_id, count, 0.0).astype(BF16)

    half = T // 2
    piece = D // NSEQ

    def pack_half(tile, high):
        top, bottom = tile[0:half], tile[half:T]
        if high:
            return join_halves(swap_halves(top), bottom).astype(BF16)
        return join_halves(top, swap_halves(bottom)).astype(BF16)

    right, left = lax.rem(g + 1, NGRP), lax.rem(g + NGRP - 1, NGRP)

    def chain_start(name, at, ssem, rsem):
        launch(
            name + "0",
            lambda: [
                (g + 1 < NGRP, to_grp(right, at(g), at(g), ssem().at[0, 0], rsem().at[g])),
                (g >= 1, to_grp(left, at(g), at(g), ssem().at[0, 1], rsem().at[g])),
            ],
        )

    def chain_step(d, name, at, ssem, rsem):
        def slots():
            return lax.rem(g - d + NGRP, NGRP), lax.rem(g + d, NGRP)

        def copies():
            lower, upper = slots()
            return [
                (
                    (g - d >= 0) & (g + 1 < NGRP),
                    to_grp(right, at(lower), at(lower), ssem().at[d, 0], rsem().at[lower]),
                ),
                (
                    (g + d < NGRP) & (g >= 1),
                    to_grp(left, at(upper), at(upper), ssem().at[d, 1], rsem().at[upper]),
                ),
            ]

        lower, upper = slots()
        pl.when(g - d >= 0)(
            to_grp(right, at(lower), at(lower), ssem().at[0, 0], rsem().at[lower]).wait_recv
        )
        pl.when(g + d < NGRP)(
            to_grp(left, at(upper), at(upper), ssem().at[0, 1], rsem().at[upper]).wait_recv
        )
        if d < NGRP - 1:
            launch(name + str(d), copies)

    def chain_parts(name, views, ssem, rsem):
        return [
            (name + str(i), view, lambda i=i: ssem.at[i], lambda i=i: rsem.at[i])
            for i, view in enumerate(views)
        ]

    def chain_finish(parts):
        for d in range(1, NGRP):
            for part_of in parts:
                chain_step(d, *part_of)

    def near_start(name, at, ssem, rsem):
        def copies():
            found = []
            for i, step in enumerate((1, -1, 2, -2)):
                peer = g + step
                to = lax.rem(peer + NGRP, NGRP)
                sem = ssem().at[i // 2, i % 2]
                found.append(((peer >= 0) & (peer < NGRP), to_grp(to, at(g), at(g), sem, rsem().at[g])))
            return found

        launch(name, copies)

    def near_forward(name, at, ssem, rsem):
        ends = ((NGRP - 2, 0, NGRP - 1), (1, NGRP - 1, 0))

        def copies():
            return [
                (g == near, to_grp(end, at(far), at(far), ssem().at[2, 0], rsem().at[far]))
                for near, far, end in ends
            ]

        for near, far, end in ends:
            pl.when(g == near)(
                to_grp(end, at(far), at(far), ssem().at[2, 0], rsem().at[far]).wait_recv
            )
        launch(name + "on", copies)

    def near_wait(name, at, ssem, rsem):
        for slot in range(NGRP):
            handed = ((g == NGRP - 2) & (slot == 0)) | ((g == 1) & (slot == NGRP - 1))
            pl.when((g != slot) & jnp.logical_not(handed))(
                to_grp(
                    lax.rem(g + 1, NGRP), at(slot), at(slot), ssem().at[0, 0], rsem().at[slot]
                ).wait_recv
            )

    def direct_start(name, at, ssem, rsem):
        def copies():
            found = []
            for step in range(1, NGRP):
                peer = lax.rem(g + step, NGRP)
                found.append((always, to_grp(peer, at(g), at(g), ssem.at[step - 1], rsem.at[g])))
            return found

        launch(name, copies)

    def direct_wait(name, at, ssem, rsem):
        for step in range(1, NGRP):
            slot = lax.rem(g + step, NGRP)
            to_grp(slot, at(slot), at(slot), ssem.at[0], rsem.at[slot]).wait_recv()

    loads[3].wait()

    def cot_times_down(i, carry):
        at = pl.ds(pl.multiple_of(i * T, T), T)
        ghid[:, at] = dot_nt(cot_ref[...], down_all[at, :]).astype(BF16)
        return carry

    lax.fori_loop(0, FF // T, cot_times_down, 0)

    acc_a[...] = jnp.zeros_like(acc_a)
    shift[...] = jnp.zeros_like(shift)

    def pair_of(ref, cc, first, last):
        return ref[pl.ds(2 * cc, 2), :, first:last].reshape(pair_width, last - first)

    def weights_of(score, count):
        count = count.astype(F32)
        return jnp.where(count > 0.5, jnp.exp2(score * exp_scale) * count, 0.0)

    def wait_pair(buffer, ssem, rsem, j, cc):
        mine, other = 2 * cc + core, 2 * cc + 1 - core

        @pl.when(j > 0)
        def _():
            to_seq(sib, buffer.at[mine], buffer.at[mine], ssem.at[0], rsem.at[mine]).wait_recv()
            to_seq(sib, buffer.at[mine], buffer.at[mine], ssem.at[3 + j], rsem.at[mine]).start()

        to_seq(sib, buffer.at[other], buffer.at[other], ssem.at[0], rsem.at[other]).wait_recv()

    def forward_step(j, carry):
        cc = chip - j
        wait_pair(kv, kv_ssem, kv_rsem, j, cc)
        keys = pair_of(kv, cc, 0, 256)
        values = pair_of(kv, cc, 128, 384)
        for h in range(3):
            weight = weights_of(dot_nt(qmask[h], keys), masks[h, :, pair_lanes(cc)])
            row_sum = weight[:, 0:LANES]
            for i in range(1, pair_width // LANES):
                row_sum = row_sum + weight[:, LANES * i : LANES * i + LANES]
            shift[h] += row_sum
            low_weight = weight.astype(BF16)
            masks[h, :, pair_lanes(cc)] = low_weight
            acc_a[...] += dot_nn(low_weight, values) * slot_mask(h + 1)
        return carry

    lax.fori_loop(0, chip + 1, forward_step, 0)
    inverse = jnp.zeros((T, 256), F32)
    for h in range(3):
        inverse += slot_mask(h + 1) / jnp.sum(shift[h], axis=1, keepdims=True)
    att_own = acc_a[...] * inverse
    invden[...] = inverse
    att[...] = att_own
    for h in range(3):
        tile = att_own[:, 0:128] if h == 0 else att_own[:, 128:256]
        zmix[g, h] = pack_half(tile, h != 1)
    mixed_gather = chain_parts(
        "mixed",
        [lambda i, n=n: zmix.at[i, :, n * half // 3 : (n + 1) * half // 3] for n in range(3)],
        zm_ssem,
        zm_rsem,
    )
    for part_of in mixed_gather:
        chain_start(*part_of)

    chain_finish(mixed_gather)
    for tile in range(D // LANES):
        (g_a, h_a), (g_b, h_b) = divmod(2 * tile, 3), divmod(2 * tile + 1, 3)
        first_head = zmix[g_a, h_a].astype(F32)
        second_head = zmix[g_b, h_b].astype(F32)
        cols = slice(tile * LANES, tile * LANES + LANES)
        mixed[0:half, cols] = join_halves(first_head, swap_halves(second_head)).astype(BF16)
        mixed[half:T, cols] = join_halves(swap_halves(first_head), second_head).astype(BF16)

    loads[4].wait()
    middle[...] = tok_ref[...].astype(F32) + dot_nn(mixed[...], exit_all[...])

    def norm_two(i, carry):
        at = pl.ds(pl.multiple_of(i * rows, rows), rows)
        value = middle[at, :]
        centered = value - jnp.mean(value, axis=1, keepdims=True)
        inverse = lax.rsqrt(jnp.mean(centered * centered, axis=1, keepdims=True) + EPS)
        plain = centered * inverse
        n2[at, :] = (plain * gain2 + bias2).astype(BF16)
        return carry

    lax.fori_loop(0, T // rows, norm_two, 0)

    class Stacked:
        def __init__(self, pieces, first_in, second_in):
            self.pieces, self.first_in, self.second_in = pieces, first_in, second_in

        def whole(self, k):
            return self.pieces.at[k]

        def block(self, k, cc):
            return self.pieces.at[k, cc]

        def first(self, cc):
            return self.first_in.at[cc]

    class Tiled(Stacked):
        def rows(self, k):
            count = self.first_in.shape[0]
            return pl.ds(pl.multiple_of(count * k, count), count)

        def cols(self, cc):
            return pl.ds(pl.multiple_of(D * cc, LANES), D)

        def whole(self, k):
            return self.pieces.at[self.rows(k), :]

        def block(self, k, cc):
            return self.pieces.at[self.rows(k), self.cols(cc)]

        def first(self, cc):
            return self.first_in.at[:, self.cols(cc)]

    sum_up = Stacked(pc_up, r1_up, r2_up)
    sum_down = Tiled(up_all, r1_down, r2_down)
    sum_eq = Stacked(pc_eq, r1_eq, r2_eq)
    sum_ekv = Stacked(pc_ekv, r1_ekv, r2_ekv)
    sum_exit = Tiled(ghid, r1_exit, r2_exit)

    def reduce_start(i, parts):
        launch(
            f"first{i}",
            lambda: [
                (
                    always,
                    to_seq(sib, parts.whole(1 - core), parts.first_in, rs_s1.at[i], rs_r1.at[i]),
                )
            ],
        )

    def reduce_pass(i, parts):
        to_seq(sib, parts.whole(core), parts.first_in, rs_s1.at[i], rs_r1.at[i]).wait_recv()

        def add(cc, carry):
            block = parts.block(core, cc)
            block[...] = (block[...].astype(F32) + parts.first(cc)[...].astype(F32)).astype(BF16)
            return carry

        lax.fori_loop(0, chips, add, 0)

        def copies():
            found = []
            for d in range(1, chips):
                to_chip = lax.rem(chip + d, chips)
                copy = to_seq(
                    2 * to_chip + core,
                    parts.block(core, to_chip),
                    parts.second_in.at[chips - d - 1],
                    rs_s2.at[i, d - 1],
                    rs_r2.at[i, chips - d - 1],
                )
                found.append((always, copy))
            return found

        launch(f"second{i}", copies)

    def reduce_end(i, parts):
        result = parts.block(core, chip)[...].astype(F32)
        for d in range(1, chips):
            landed = parts.second_in.at[d - 1]
            to_seq(sib, landed, landed, rs_s1.at[i], rs_r2.at[i, d - 1]).wait_recv()
            result = result + landed[...].astype(F32)
        return result.astype(BF16)

    def weight_gather(i, gathered):
        return ("weight" + str(i), lambda j: gathered.at[j], lambda: rs_zs.at[i], lambda: rs_zr.at[i])

    def gather_sum(i, parts, gathered):
        gathered[g] = reduce_end(i, parts)
        near_start(*weight_gather(i, gathered))

    for d in range(1, chips):

        @pl.when(chip + d < chips)
        def _(d=d):
            slot = lax.rem(s + 2 * d, NSEQ)
            to_seq(sib, qb.at[slot], qb.at[slot], q_ssem.at[0], q_rsem.at[slot]).wait_recv()

    def hand_on(buffer, ssem, rsem, upward):
        found = []
        for d in range(1, chips):
            slot = lax.rem(s + (NSEQ - 2 * d if upward else 2 * d), NSEQ)
            cond = chip >= d if upward else chip + d < chips
            found.append(
                (cond, to_seq(sib, buffer.at[slot], buffer.at[slot], ssem.at[3 + d], rsem.at[slot]))
            )
        return found

    launch("q on", lambda: hand_on(qb, q_ssem, q_rsem, False))
    launched["kv on"] = lambda: hand_on(kv, kv_ssem, kv_rsem, True)
    launched["do on"] = lambda: hand_on(dob, do_ssem, do_rsem, False)

    loads[5].wait()
    def feed_forward(i, carry):
        c = lax.rem(g + i, NGRP)
        at = pl.ds(pl.multiple_of(c * D, LANES), D)
        hidden = dot_nn(n2[...], up_all[:, at])
        cdf = 0.5 + 0.5 * lax.erf(hidden * (0.5**0.5))
        low_active = (hidden * cdf).astype(BF16)
        active[:, at] = low_active
        density = jnp.exp2(hidden * hidden * (-0.5 * LOG2E)) * 0.3989422804014327
        ghid[:, at] = (ghid[:, at].astype(F32) * (cdf + hidden * density)).astype(BF16)

        @pl.when(i == 0)
        def _():
            for j in range(2):
                up_grad = dot_tn(n2[...], ghid[:, pl.ds(pl.multiple_of(g * D + T * j, LANES), T)])
                for t in range(NSEQ):
                    pc_up[t % 2, t // 2, :, T * j : T * j + T] = up_grad[
                        piece * t : piece * t + piece, :
                    ].astype(BF16)
            reduce_start(0, sum_up)

        @pl.when(i == 2)
        def _():
            reduce_pass(0, sum_up)

        return carry

    lax.fori_loop(0, NGRP, feed_forward, 0)

    def back_through_up(i, carry):
        at = pl.ds(pl.multiple_of(i * 256, 256), 256)
        gn2[:, at] = dot_nt(ghid[...], up_all[at, :])
        return carry

    lax.fori_loop(0, D // 256, back_through_up, 0)

    stat[s] = jnp.zeros((8, D), F32)

    def norm_two_back(i, carry):
        at = pl.ds(pl.multiple_of(i * rows, rows), rows)
        upstream = gn2[at, :]
        value = middle[at, :]
        centered = value - jnp.mean(value, axis=1, keepdims=True)
        inverse = lax.rsqrt(jnp.mean(centered * centered, axis=1, keepdims=True) + EPS)
        plain = centered * inverse
        scaled = upstream * gain2
        inner = (
            scaled
            - jnp.mean(scaled, axis=1, keepdims=True)
            - plain * jnp.mean(scaled * plain, axis=1, keepdims=True)
        )
        grad = cot_ref[at, :].astype(F32) + inverse * inner

        @pl.when(i == g)
        def _():
            gmid[...] = grad

        gbranch[at, :] = grad.astype(BF16)
        stat[s, 0:1, :] += jnp.sum(upstream * plain, axis=0, keepdims=True)
        stat[s, 1:2, :] += jnp.sum(upstream, axis=0, keepdims=True)
        return carry

    lax.fori_loop(0, T // rows, norm_two_back, 0)

    window = pl.ds(pl.multiple_of(jnp.maximum(part * g - 64, 0), 64), 256)
    gmix = dot_nt(gbranch[...], exit_all[window, :])
    gmix = jnp.where(g == 0, pltpu.roll(gmix, 64, axis=1), gmix)
    gmix = jnp.where(lane256 < 64, 0.0, gmix).astype(BF16).astype(F32)
    numer_grad = gmix * invden[...]
    product = numer_grad * att[...]
    for h in range(3):
        value = jnp.sum(product * slot_mask(h + 1), axis=1, keepdims=True)
        shift[h] = jnp.broadcast_to(value, (T, LANES))
        high = value.astype(BF16).astype(F32)
        low = value - high
        numer_grad = jnp.where(lane256 == 2 * h, high, numer_grad)
        numer_grad = jnp.where(lane256 == 2 * h + 1, low, numer_grad)
    dob[s] = numer_grad.astype(BF16)

    spread("do", dob, do_ssem, do_rsem, False)


    def down_piece(t, carry):
        at = pl.ds(pl.multiple_of(t * T, T), T)
        sum_down.block(t % 2, t // 2)[...] = dot_tn(active[:, at], cot_ref[...]).astype(BF16)
        return carry

    lax.fori_loop(0, NSEQ, down_piece, 0)
    reduce_start(1, sum_down)
    for i in range(2):
        exit_grad = dot_tn(mixed[...], gbranch[:, T * i : T * i + T]).astype(BF16)
        for t in range(NSEQ):
            first, low = D * (t // 2) + T * i, piece * (t % 2)
            ghid[low : low + piece, first : first + T] = exit_grad[piece * t : piece * t + piece, :]
    reduce_start(4, sum_exit)

    for h in range(3):
        qmask[h] = (dob[s].astype(F32) * slot_mask(h + 1)).astype(BF16)
    acc_a[...] = jnp.zeros_like(acc_a)

    def query_side(cc, carry):
        keys = pair_of(kv, cc, 0, 256)
        values = pair_of(kv, cc, 128, 384)
        for h in range(3):
            row_shift = jnp.concatenate([shift[h]] * (pair_width // LANES), axis=1)
            pressure = dot_nt(qmask[h], values) - row_shift
            slope = (masks[h, :, pair_lanes(cc)].astype(F32) * pressure).astype(BF16)
            acc_a[...] += dot_nn(slope, keys) * slot_mask(h)
        return carry

    lax.fori_loop(0, chip + 1, query_side, 0)
    dq = acc_a[...] * scale
    gather_sum(0, sum_up, ag_up)

    def weight_pieces(pieces, grad):
        for t in range(NSEQ):
            pieces[t % 2, t // 2] = grad[piece * t : piece * t + piece, :].astype(BF16)

    weight_pieces(pc_eq, dot_tn(n1[...], dq.astype(BF16)))
    reduce_start(2, sum_eq)

    reduce_pass(4, sum_exit)

    v_tile = kv[s, :, 128:384].astype(F32)
    k_tile = kv[s, :, 0:256].astype(F32)
    for h in range(3):
        qmask[h] = (k_tile * slot_mask(h)).astype(BF16)
        minus = jnp.where((lane256 == 2 * h) | (lane256 == 2 * h + 1), -1.0, 0.0)
        qmask[3 + h] = (v_tile * slot_mask(h + 1) + minus).astype(BF16)
    acc_b[...] = jnp.zeros_like(acc_b)
    acc_c[...] = jnp.zeros_like(acc_c)

    def key_side(j, carry):
        cc = chip + j
        wait_pair(dob, do_ssem, do_rsem, j, cc)
        other = 2 * cc + 1 - core
        to_seq(sib, qb.at[other], qb.at[other], q_ssem.at[0], q_rsem.at[other]).wait_recv()
        queries = pair_of(qb, cc, 0, 256)
        grads = pair_of(dob, cc, 0, 256)
        for h in range(3):
            count = masks[h, :, pair_lanes(jnp.where(j == 0, chips, cc))]
            weight = weights_of(dot_nt(qmask[h], queries), count)
            slope = (weight * dot_nt(qmask[3 + h], grads)).astype(BF16)
            acc_b[...] += dot_nn(slope, queries) * slot_mask(h)
            acc_c[...] += dot_nn(weight.astype(BF16), grads) * slot_mask(h + 1)

        @pl.when(j == 0)
        def _():
            reduce_pass(2, sum_eq)

        return carry

    lax.fori_loop(0, chips - chip, key_side, 0)

    dk, dv = acc_b[...] * scale, acc_c[...]
    part_sum = dot_nt(jnp.where(is_odd, pltpu.roll(dq, 64, axis=1), dq).astype(BF16), win[0])
    part_sum += dot_nt(jnp.where(is_odd, pltpu.roll(dk, 64, axis=1), dk).astype(BF16), win[1])
    part_sum += dot_nt(jnp.where(is_odd, dv, pltpu.roll(dv, 192, axis=1)).astype(BF16), win[2])
    gn2[...] = part_sum
    n2[...] = part_sum.astype(BF16)
    own_rows = pl.ds(pl.multiple_of(g * piece, piece), piece)

    def row_copies():
        found = []
        for step in range(1, NGRP):
            peer = lax.rem(g + step, NGRP)
            rows_of = pl.ds(pl.multiple_of(peer * piece, piece), piece)
            copy = to_grp(peer, n2.at[rows_of, :], drecv.at[g], zd_ssem.at[step - 1], zd_rsem.at[g])
            found.append((always, copy))
        return found

    launch("rows", row_copies)

    def norm_one_sums(i, carry):
        at = pl.ds(pl.multiple_of(i * rows, rows), rows)
        value = tok_ref[at, :].astype(F32)
        centered = value - jnp.mean(value, axis=1, keepdims=True)
        inverse = lax.rsqrt(jnp.mean(centered * centered, axis=1, keepdims=True) + EPS)
        stat[s, 2:3, :] += jnp.sum(gn2[at, :] * (centered * inverse), axis=0, keepdims=True)
        stat[s, 3:4, :] += jnp.sum(gn2[at, :], axis=0, keepdims=True)
        return carry

    lax.fori_loop(0, T // rows, norm_one_sums, 0)

    def stat_copies():
        found = []
        for step in range(1, NSEQ):
            peer = lax.rem(s + step, NSEQ)
            copy = to_seq(peer, stat.at[s], stat.at[s], st_ssem.at[step - 1], st_rsem.at[s])
            found.append((always, copy))
        return found

    launch("stat", stat_copies)

    dpack = exit_all.at[0:T, 0:384]
    dpack[:, 0:128] = dk[:, 0:128].astype(BF16)
    dpack[:, 128:256] = join_halves(dk[:, 128:256], dv[:, 0:128]).astype(BF16)
    dpack[:, 256:384] = dv[:, 128:256].astype(BF16)
    weight_pieces(pc_ekv, dot_tn(n1[...], dpack[...]))
    reduce_start(3, sum_ekv)
    gather_sum(2, sum_eq, ag_eq)

    reduce_pass(3, sum_ekv)
    near_forward(*weight_gather(0, ag_up))
    reduce_pass(1, sum_down)

    def through_down(i, carry):
        at = pl.ds(pl.multiple_of(i * 256, 256), 256)
        out_ref[:, at] = (middle[:, at] + dot_nn(active[...], down_all[:, at])).astype(BF16)
        return carry

    lax.fori_loop(0, D // 256, through_down, 0)

    upstream = gn2[own_rows, :]
    for step in range(1, NGRP):
        slot = lax.rem(g + step, NGRP)
        to_grp(slot, drecv.at[slot], drecv.at[slot], zd_ssem.at[0], zd_rsem.at[slot]).wait_recv()
        upstream = upstream + drecv[slot].astype(F32)
    value = tok_ref[own_rows, :].astype(F32)
    centered = value - jnp.mean(value, axis=1, keepdims=True)
    inverse = lax.rsqrt(jnp.mean(centered * centered, axis=1, keepdims=True) + EPS)
    plain = centered * inverse
    scaled = upstream * gain1
    inner = (
        scaled
        - jnp.mean(scaled, axis=1, keepdims=True)
        - plain * jnp.mean(scaled * plain, axis=1, keepdims=True)
    )
    tz[g] = (gmid[...] + inverse * inner).astype(BF16)
    middle_row = piece // 2
    token_gather = chain_parts(
        "token",
        (lambda i: tz.at[i, 0:middle_row], lambda i: tz.at[i, middle_row:piece]),
        zt_ssem,
        zt_rsem,
    )
    for part_of in token_gather:
        chain_start(*part_of)

    gather_sum(3, sum_ekv, ag_ekv)
    near_forward(*weight_gather(2, ag_eq))

    chain_finish(token_gather)
    near_forward(*weight_gather(3, ag_ekv))

    for step in range(1, NSEQ):
        slot = lax.rem(s + step, NSEQ)
        to_seq(sib, stat.at[slot], stat.at[slot], st_ssem.at[0], st_rsem.at[slot]).wait_recv()
    total_stat = stat[0]
    for i in range(1, NSEQ):
        total_stat = total_stat + stat[i]
    stat_z[g] = total_stat
    direct_start("stat z", lambda i: stat_z.at[i], sz_ssem, sz_rsem)

    near_wait(*weight_gather(0, ag_up))
    pass
    for i in range(NGRP):
        oup_ref[:, D * i : D * i + D] = ag_up[i]
    pass
    oexit_ref[...] = reduce_end(4, sum_exit)
    near_wait(*weight_gather(2, ag_eq))

    def place_entry(first, tiles):
        for tile, value in enumerate(tiles):
            at = first + tile * LANES
            oentry_ref[:, at : at + LANES] = value.astype(BF16)

    for pair in range(NGRP // 2):
        a = ag_eq[2 * pair].astype(F32)
        b = ag_eq[2 * pair + 1].astype(F32)
        turned = swap_halves(b[:, 0:128])
        place_entry(
            pair * 2 * part,
            (
                a[:, 0:128],
                join_halves(a[:, 128:256], turned),
                join_halves(turned, swap_halves(b[:, 128:256])),
            ),
        )
    odown_ref[...] = reduce_end(1, sum_down)
    for i in range(NGRP):
        tgrad_ref[piece * i : piece * i + piece, :] = tz[i]
    total_stat = jnp.zeros((8, D), F32)
    for step in range(1, NGRP):
        slot = lax.rem(g + step, NGRP)
        to_grp(slot, stat_z.at[slot], stat_z.at[slot], sz_ssem.at[0], sz_rsem.at[slot]).wait_recv()
    for i in range(NGRP):
        total_stat = total_stat + stat_z[i]
    row_id = lax.broadcasted_iota(jnp.int32, (8, 1), 0)
    ostat_ref[...] = jnp.where(row_id < 2, stat_z[g], total_stat)
    near_wait(*weight_gather(3, ag_ekv))
    for pair in range(NGRP // 2):
        a = ag_ekv[2 * pair].astype(F32)
        b = ag_ekv[2 * pair + 1].astype(F32)
        turned = swap_halves(b[:, 0:128])
        place_entry(
            D + pair * 2 * part,
            (
                a[:, 0:128],
                join_halves(a[:, 128:256], turned),
                join_halves(turned, swap_halves(b[:, 128:256])),
            ),
        )
        turned = swap_halves(a[:, 256:384])
        place_entry(
            2 * D + pair * 2 * part,
            (
                join_halves(swap_halves(a[:, 128:256]), turned),
                join_halves(turned, b[:, 128:256]),
                b[:, 256:384],
            ),
        )

    for copies in launched.values():
        for cond, copy in copies():
            pl.when(cond)(copy.wait_send)


def finish_kernel(
    out_in,
    tgrad_in,
    entry_in,
    exit_in,
    up_in,
    down_in,
    stat_in,
    out_hbm,
    tgrad_hbm,
    entry_hbm,
    exit_hbm,
    up_hbm,
    down_hbm,
    fgain_ref,
    fbias_ref,
    sgain_ref,
    sbias_ref,
    out_low,
    tgrad_low,
    down_low,
    up_low,
    entry_low,
    exit_low,
    stat_low,
    down_full,
    up_full,
    entry_full,
    exit_full,
    sems,
):
    plans = (
        (down_in, down_low, down_full, down_hbm),
        (up_in, up_low, up_full, up_hbm),
        (entry_in, entry_low, entry_full, entry_hbm),
        (exit_in, exit_low, exit_full, exit_hbm),
        (out_in, out_low, out_low, out_hbm),
        (tgrad_in, tgrad_low, tgrad_low, tgrad_hbm),
    )
    loads = [
        pltpu.make_async_copy(source, low, sems.at[6 + i])
        for i, (source, low, _, _) in enumerate(plans)
    ]
    stat_load = pltpu.make_async_copy(stat_in, stat_low, sems.at[12])
    for copy in [*loads, stat_load]:
        copy.start()
    copies = []
    for i, (_, low, full, target) in enumerate(plans):
        loads[i].wait()
        if full is not low:
            full[...] = low[...].astype(F32)
        copy = pltpu.make_async_copy(full, target, sems.at[i])
        copy.start()
        copies.append(copy)
    stat_load.wait()
    width = stat_low.shape[1]
    part = fgain_ref.shape[0]
    first = lax.axis_index("seq") * part
    turned = pltpu.roll(stat_low[...], lax.rem(width - first, width), axis=1)
    fgain_ref[...] = turned[2:3, 0:part].reshape(part)
    fbias_ref[...] = turned[3:4, 0:part].reshape(part)
    sgain_ref[...] = turned[0:1, 0:part].reshape(part)
    sbias_ref[...] = turned[1:2, 0:part].reshape(part)
    for copy in copies:
        copy.wait()


def fast_on_device(
    seq_count,
    tokens,
    cotangent,
    entry_weight,
    exit_weight,
    up_weight,
    down_weight,
    first_gain,
    first_bias,
    second_gain,
    second_bias,
    dilations,
    offsets,
):
    T, D = tokens.shape
    NGRP, HEADS = offsets.shape
    FF = up_weight.shape[1]
    E = D // HEADS
    NSEQ = seq_count
    chips = NSEQ // 2
    sizes = (T, D, HEADS, E, FF, NSEQ, NGRP)
    piece = D // NSEQ
    vmem = pl.BlockSpec(memory_space=pltpu.VMEM)
    smem = pl.BlockSpec(memory_space=pltpu.SMEM)
    anywhere = pl.BlockSpec(memory_space=pl.ANY)
    dma = pltpu.SemaphoreType.DMA
    scratch = [
        pltpu.VMEM((3, D, 256), BF16),
        pltpu.VMEM((D, D), BF16),
        pltpu.VMEM((D, FF), BF16),
        pltpu.VMEM((FF, D), BF16),
        pltpu.VMEM((T, D), BF16),
        pltpu.VMEM((T, D), BF16),
        pltpu.VMEM((T, D), F32),
        pltpu.VMEM((piece, D), F32),
        pltpu.VMEM((T, D), BF16),
        pltpu.VMEM((T, D), BF16),
        pltpu.VMEM((T, FF), BF16),
        pltpu.VMEM((T, FF), BF16),
        pltpu.VMEM((T, D), F32),
        pltpu.VMEM((3, T, LANES), BF16),
        pltpu.VMEM((3, T, (NSEQ + 2) * T), BF16),
        pltpu.VMEM((NSEQ, T, 384), BF16),
        pltpu.VMEM((NSEQ, T, 256), BF16),
        pltpu.VMEM((NSEQ, T, 256), BF16),
        pltpu.VMEM((6, T, 256), BF16),
        pltpu.VMEM((3, T, LANES), F32),
        pltpu.VMEM((T, 256), F32),
        pltpu.VMEM((T, 256), F32),
        pltpu.VMEM((T, 256), F32),
        pltpu.VMEM((T, 256), F32),
        pltpu.VMEM((T, 256), F32),
        pltpu.VMEM((NGRP, 3, T // 2, LANES), BF16),
        pltpu.VMEM((NGRP, piece, D), BF16),
        pltpu.VMEM((NGRP, piece, D), BF16),
        pltpu.VMEM((NSEQ, 8, D), F32),
        pltpu.VMEM((NGRP, 8, D), F32),
    ]
    scratch += [
        pltpu.VMEM((piece, chips * D), BF16),
        pltpu.VMEM((chips - 1, piece, D), BF16),
        pltpu.VMEM((T, chips * D), BF16),
        pltpu.VMEM((chips - 1, T, D), BF16),
    ]
    for rows, cols in ((piece, D), (piece, 256), (piece, 384)):
        scratch += [
            pltpu.VMEM((2, chips, rows, cols), BF16),
            pltpu.VMEM((chips, rows, cols), BF16),
            pltpu.VMEM((chips - 1, rows, cols), BF16),
            pltpu.VMEM((NGRP, rows, cols), BF16),
        ]
    scratch += [
        dma((7,)),
        dma((7,)),
        dma((NSEQ,)),
        dma((7,)),
        dma((NSEQ,)),
        dma((7,)),
        dma((NSEQ,)),
        dma((3, 3, 2)),
        dma((3, NGRP)),
        dma((NGRP - 1,)),
        dma((NGRP,)),
        dma((2, 3, 2)),
        dma((2, NGRP)),
        dma((5,)),
        dma((5,)),
        dma((5, 3)),
        dma((5, chips - 1)),
        dma((4, 3, 2)),
        dma((4, NGRP)),
        dma((NSEQ - 1,)),
        dma((NSEQ,)),
        dma((NGRP - 1,)),
        dma((NGRP,)),
    ]
    out_shape = (
        jax.ShapeDtypeStruct((T, D), BF16),
        jax.ShapeDtypeStruct((T, D), BF16),
        jax.ShapeDtypeStruct((piece, 3 * D), BF16),
        jax.ShapeDtypeStruct((piece, D), BF16),
        jax.ShapeDtypeStruct((piece, FF), BF16),
        jax.ShapeDtypeStruct((T, D), BF16),
        jax.ShapeDtypeStruct((8, D), F32),
    )
    output, token_grad, entry_grad, exit_grad, up_grad, down_grad, stats = pl.pallas_call(
        partial(layer_kernel, sizes),
        out_shape=out_shape,
        in_specs=[smem] * 2 + [vmem] * 6 + [anywhere] * 4,
        out_specs=tuple([vmem] * 7),
        scratch_shapes=scratch,
        compiler_params=pltpu.CompilerParams(
            collective_id=0, has_side_effects=True, vmem_limit_bytes=63 * 1024 * 1024
        ),
        name="layer",
    )(
        dilations,
        offsets,
        tokens,
        cotangent,
        first_gain,
        first_bias,
        second_gain,
        second_bias,
        entry_weight,
        exit_weight,
        up_weight,
        down_weight,
    )
    part = piece
    finish_shape = (
        jax.ShapeDtypeStruct((T, D), BF16),
        jax.ShapeDtypeStruct((T, D), BF16),
        jax.ShapeDtypeStruct((part, 3 * D), F32),
        jax.ShapeDtypeStruct((part, D), F32),
        jax.ShapeDtypeStruct((part, FF), F32),
        jax.ShapeDtypeStruct((T, D), F32),
    ) + tuple([jax.ShapeDtypeStruct((part,), F32)] * 4)
    return pl.pallas_call(
        finish_kernel,
        out_shape=finish_shape,
        in_specs=[anywhere] * 7,
        out_specs=tuple([anywhere] * 6 + [vmem] * 4),
        scratch_shapes=[
            pltpu.VMEM((T, D), BF16),
            pltpu.VMEM((T, D), BF16),
            pltpu.VMEM((T, D), BF16),
            pltpu.VMEM((part, FF), BF16),
            pltpu.VMEM((part, 3 * D), BF16),
            pltpu.VMEM((part, D), BF16),
            pltpu.VMEM((8, D), F32),
            pltpu.VMEM((T, D), F32),
            pltpu.VMEM((part, FF), F32),
            pltpu.VMEM((part, 3 * D), F32),
            pltpu.VMEM((part, D), F32),
            dma((13,)),
        ],
        compiler_params=pltpu.CompilerParams(vmem_limit_bytes=62 * 1024 * 1024),
        name="finish",
    )(output, token_grad, entry_grad, exit_grad, up_grad, down_grad, stats)


def solution(mesh):
    seq_count = mesh.shape["seq"]
    fast = seq_count == 8 and mesh.shape["grp"] == 4
    return jax.shard_map(
        partial(fast_on_device, seq_count) if fast else on_device,
        mesh=mesh,
        in_specs=(P("seq", None), P("seq", None), P(), P(), P(), P(), P(), P(), P(), P(), P(), P()),
        out_specs=(
            P("seq", None),
            P("seq", None),
            P("seq", None),
            P("seq", None),
            P("seq", None),
            P("seq", None),
            P("seq"),
            P("seq"),
            P("seq"),
            P("seq"),
        ),
        check_vma=False,
    )
```
